128 devices in a mesh: attn: 8 (over x, z_hi), grp: 2 (over z_lo), tp: 8 (over y, core).
Axes of the slice: x: 4, y: 4, z: 4 (z_hi: 2, z_lo: 2; z = z_hi * 2 + z_lo), core: 2. Of those that a mesh axis runs over, the one named last changes fastest.
Arguments:
- queries: bfloat16 [512, 8192], P(('attn', 'grp', 'tp')), may hold values from -100 to 100
- keys: bfloat16 [512, 1024, 256], P(('attn', 'grp', 'tp')), may hold values from -6 to 6
- values: bfloat16 [512, 1024, 256], P(('attn', 'grp', 'tp')), may hold values from -6 to 6
- lengths: int32 [512], P(('attn', 'grp', 'tp')), may hold values from 256 to 1024, as said below
- resid: bfloat16 [512, 7168], P(('attn', 'grp', 'tp')), may hold values from -6 to 6
- assign: int32 [128, 4], P(('attn', 'grp', 'tp')), may hold values from 0 to 3, each once within a row
- matching: int32 [2, 8, 8], P(None, 'attn', 'tp'), may hold values from 0 to 1
- w_out: bfloat16 [8192, 7168], P(None, ('attn', 'tp')), may hold values from -0.5 to 0.5
- gain: float32 [7168], replicated, may hold values from 0.1 to 1.9
- gate_w: bfloat16 [2, 7168, 18432], P('grp', None, ('attn', 'tp')), may hold values from -0.0625 to 0.0625
- up_w: bfloat16 [2, 7168, 18432], P('grp', None, ('attn', 'tp')), may hold values from -0.0625 to 0.0625
- down_w: bfloat16 [2, 18432, 7168], P('grp', ('attn', 'tp')), may hold values from -0.046875 to 0.046875
Outputs:
- layer_out: bfloat16 [512, 7168], P(('attn', 'grp', 'tp'))
The draws below stay inside these ranges and needn't reach their ends.
Inputs may be any that keep to these rules, and one draw needn't show every extreme that they name: `assign`: each row is an order of the device's 4 requests. `matching`: 1 sends the requests of both devices at one attn, tp position to the other group, so each group serves the requests of exactly half of the devices in each micro-batch. `lengths`: the first request of every device has 1024 live slots.
All inputs are finite; a program needn't handle non-finite values.
Results may differ from the reference program's by a relative error of at most 0.0063.
Values may be sent and summed in bfloat16 or wider, within the bound.
A program may use at most 128 MiB of HBM per device.

```python
import jax
import jax.numpy as jnp
from jax import lax

D = 7168
FF = 18432
HD = 256
HQ = 32
REQ_DEV = 4
CACHE = 1024
MICRO = 2
NDEV = 128
REQUESTS = 512
N_ATTN = 8
N_GRP = 2
N_TP = 8


def first_keys(key):
    return jnp.clip(jax.random.normal(key, (REQUESTS, 2, HD), jnp.float32), -6.0, 6.0)


def draw_keys(key, part):
    leading = first_keys(key)
    key = jax.random.fold_in(key, 11)
    remainder = jnp.clip(jax.random.normal(key, (REQUESTS, CACHE - 2, HD), jnp.float32), -6.0, 6.0)
    return jnp.concatenate([leading, remainder], axis=1).astype(jnp.bfloat16)


def draw_queries(key, part):
    key = jax.random.fold_in(key, 23)
    noise = jnp.clip(jax.random.normal(key, (REQUESTS, HQ, HD), jnp.float32), -6.0, 6.0)
    field = noise
    return field.reshape(REQUESTS, HQ * HD).astype(jnp.bfloat16)


def draw_lengths(key, part):
    key = jax.random.fold_in(key, 37)
    drawn = jax.random.randint(key, (NDEV, REQ_DEV), CACHE // 4, CACHE + 1, jnp.int32)
    drawn = drawn.at[:, 0].set(CACHE)
    return drawn.reshape(NDEV * REQ_DEV)


def with_ends(values, own_key, smallest, high):
    longest = values.shape.index(max(values.shape))
    spots = []
    for shift in (0, 1):
        where = [jax.random.randint(jax.random.fold_in(own_key, axis), (), 0, length) for axis, length in enumerate(values.shape)]
        where[longest] = (where[longest] + shift) % values.shape[longest]
        spots.append(tuple(where))
    return values.at[spots[0]].set(smallest).at[spots[1]].set(high)


def block_levels(stream_key, dims, pieces, least, largest):
    def one(axis_at, parts):
        heights = jax.random.uniform(jax.random.fold_in(jax.random.fold_in(stream_key, 6), axis_at), (parts,), jnp.float32, least / len(pieces), largest / len(pieces))
        return jnp.repeat(jnp.exp(heights), dims[axis_at] // parts).reshape((-1,) + (1,) * (len(dims) - axis_at - 1))

    level = one(*pieces[0])
    for cut in pieces[1:]:
        level = level * one(*cut)
    return level


def normal_values(key, shape, spread, limit, split=(), held_as=jnp.bfloat16):
    values = spread * jax.random.normal(key, shape, jnp.float32)
    if split:
        values = values * block_levels(key, shape, split, -0.22, 0.18)
    return jnp.clip(values, -limit, limit).astype(held_as)


def setup_inputs(seed: int = 0) -> dict:
    streams_of = jax.random.split(jax.random.key(seed), 13)
    return {
        "queries": draw_queries(jax.random.fold_in(streams_of[12], 71), 0),
        "keys": draw_keys(jax.random.fold_in(streams_of[12], 71), 0),
        "values": normal_values(streams_of[2], (REQUESTS, CACHE, HD), 1.0, 6.0, ((0, 128),)),
        "lengths": draw_lengths(jax.random.fold_in(streams_of[12], 71), 0),
        "resid": normal_values(streams_of[4], (REQUESTS, D), 1.0, 6.0, ((0, 128),)),
        "assign": jax.vmap(lambda own: jax.random.permutation(own, REQ_DEV))(jax.random.split(streams_of[5], NDEV)).reshape((NDEV, REQ_DEV)).astype(jnp.int32),
        "matching": with_ends(jax.random.randint(streams_of[6], (MICRO, N_ATTN, N_TP), 0, 2), jax.random.fold_in(streams_of[6], 1), 0, 1).astype(jnp.int32),
        "w_out": normal_values(streams_of[7], (HQ * HD, D), (HQ * HD // 64) ** -0.5, 0.5, ((1, 64),)),
        "gain": jnp.clip(1.0 + 0.18 * jax.random.normal(streams_of[8], (D,), jnp.float32), 0.1, 1.9),
        "gate_w": normal_values(streams_of[9], (N_GRP, D, FF), D ** -0.5, 0.0625, ((0, 2), (2, 64))),
        "up_w": normal_values(streams_of[10], (N_GRP, D, FF), D ** -0.5, 0.0625, ((0, 2), (2, 64))),
        "down_w": normal_values(streams_of[11], (N_GRP, FF, D), FF ** -0.5, 0.046875, ((0, 2), (1, 64))),
    }


def attend_block(block):
    query_rows, key_rows, value_rows, live = block
    count = query_rows.shape[0]
    query_heads = query_rows.reshape(count, HQ, HD).astype(jnp.float32)
    scores = jnp.einsum('rhd,rkd->rhk', query_heads, key_rows.astype(jnp.float32)) * HD ** (-0.5)
    position = lax.broadcasted_iota(jnp.int32, (1, 1, CACHE), 2)
    visible = position < live[:, None, None]
    scores = jnp.where(visible, scores, -1e+30)
    highest = lax.optimization_barrier(jnp.max(scores, axis=-1, keepdims=True))
    expo = jnp.exp(scores - highest)
    probs = (expo / lax.optimization_barrier(jnp.sum(expo, axis=-1, keepdims=True))).astype(jnp.bfloat16)
    context = jnp.einsum('rhk,rkd->rhd', probs.astype(jnp.float32), value_rows.astype(jnp.float32))
    return context.astype(jnp.bfloat16).reshape(count, HQ * HD)

def feed_forward(bundle, w_out, gain, gate_one, up_one, down_one):
    width = HQ * HD
    context = bundle[:, :width]
    residual = bundle[:, width:]
    projected = jnp.dot(context, w_out, preferred_element_type=jnp.float32)
    hidden_state = (residual.astype(jnp.float32) + projected).astype(jnp.bfloat16)
    wide = hidden_state.astype(jnp.float32)
    stat = lax.optimization_barrier(jnp.mean(wide * wide, axis=-1, keepdims=True))
    normed = (wide * lax.rsqrt(stat + 1e-05) * gain).astype(jnp.bfloat16)
    gate_out = jnp.dot(normed, gate_one, preferred_element_type=jnp.float32)
    up_out = jnp.dot(normed, up_one, preferred_element_type=jnp.float32)
    act = (jax.nn.silu(gate_out) * up_out).astype(jnp.bfloat16)
    summed = wide + jnp.dot(act, down_one, preferred_element_type=jnp.float32)
    return summed.astype(jnp.bfloat16)

def reference(queries, keys, values, lengths, resid, assign, matching, w_out, gain, gate_w, up_w, down_w):
    devices = N_ATTN * N_GRP * N_TP
    blocks = (queries.reshape(devices, REQ_DEV, HQ * HD), keys.reshape(devices, REQ_DEV, CACHE, HD), values.reshape(devices, REQ_DEV, CACHE, HD), lengths.reshape(devices, REQ_DEV))
    context = lax.map(attend_block, blocks)
    bundle = jnp.concatenate([context, resid.reshape(devices, REQ_DEV, D)], axis=-1)
    bundle = bundle.reshape(N_ATTN, N_GRP, N_TP, REQ_DEV, HQ * HD + D)
    order = assign.reshape(N_ATTN, N_GRP, N_TP, REQ_DEV).astype(jnp.int32)
    per_batch = REQ_DEV // 2
    results = []
    for batch_index in range(MICRO):
        picks = order[..., batch_index * per_batch:(batch_index + 1) * per_batch]
        chosen = jnp.take_along_axis(bundle, picks[..., None], axis=3)
        crossing = (matching[batch_index] == 1)[:, :, None, None]
        served = []
        for group in range(N_GRP):
            incoming = jnp.where(crossing, chosen[:, 1 - group], chosen[:, group])
            flat = incoming.reshape(N_ATTN * N_TP * per_batch, HQ * HD + D)
            done = feed_forward(flat, w_out, gain, gate_w[group], up_w[group], down_w[group])
            served.append(done.reshape(N_ATTN, N_TP, per_batch, D))
        back = []
        for source in range(N_GRP):
            back.append(jnp.where(crossing, served[1 - source], served[source]))
        results.append(jnp.stack(back, axis=1))
    ordered = jnp.concatenate(results, axis=3)
    inverse = jnp.argsort(order, axis=-1).astype(jnp.int32)
    layer_out = jnp.take_along_axis(ordered, inverse[..., None], axis=3)
    return layer_out.reshape(devices * REQ_DEV, D)
```

```python
import jax
import jax.numpy as jnp
from jax import lax
from jax.experimental import pallas as pl
from jax.experimental.pallas import tpu as pltpu
from jax.sharding import PartitionSpec as P

D = 7168
CW = 8192
FH = 288
COLS = 112
MESH = pl.DeviceIdType.MESH
F32 = jnp.float32
BF16 = jnp.bfloat16
NT = (((1,), (1,)), ((), ()))


def kernel(
    len_ref, assign_ref, match_ref, q_ref, resid_ref, gain_ref, k_hbm, v_hbm, wo_hbm, g_hbm, u_hbm, d_hbm,
    out_ref,
    kc, vc, wo, wg, wu, wd,
    qs, own_b, got_b, cb, sf, gf, ctx_all, ht, acc_g, acc_u, act_s,
    s1f, s1, s1_got, t1, uf, ub, vb, wf,
    p_send, p_sib, p_own, r2, af, qb, r1, tz, rz, ob, oz,
    kv_sem, w_sem, bs_sem, br_sem, cs_sem, cr_sem, ds_sem, dr_sem, rs_sem, rr_sem,
):
    attn, grp, tp = lax.axis_index("attn"), lax.axis_index("grp"), lax.axis_index("tp")
    x, z, y, c = attn // 2, lax.rem(attn, 2), tp // 2, lax.rem(tp, 2)
    zo, co = 1 - z, 1 - c
    a = x * co + y * c
    b = y * co + x * c

    def dev(x_, z_, y_, c_):
        return (lax.rem(x_, 4) * 2 + z_, grp, lax.rem(y_, 4) * 2 + c_)

    a_right, a_left = dev(x + co, z, y + c, c), dev(x + 3 * co, z, y + 3 * c, c)
    b_right, b_left = dev(x + c, z, y + co, c), dev(x + 3 * c, z, y + 3 * co, c)
    z_peer, sibling = dev(x, zo, y, c), dev(x, z, y, co)
    a1, a2, a3 = lax.rem(a + 1, 4), lax.rem(a + 2, 4), lax.rem(a + 3, 4)
    b1, b2, b3 = lax.rem(b + 1, 4), lax.rem(b + 2, 4), lax.rem(b + 3, 4)

    fetch = []
    for r in range(4):
        for src, dst in ((k_hbm, kc), (v_hbm, vc)):
            fetch.append(pltpu.make_async_copy(src.at[r], dst.at[r], kv_sem.at[len(fetch)]))
            fetch[-1].start()
    loads = [
        pltpu.make_async_copy(src, dst, w_sem.at[i])
        for i, (src, dst) in enumerate(((wo_hbm, wo), (g_hbm, wg), (u_hbm, wu), (d_hbm, wd)))
    ]
    for load in loads:
        load.start()

    barrier = pltpu.get_barrier_semaphore()
    partner = (attn, 1 - grp, tp)
    others = [partner]
    for k in range(1, 8):
        others.append((lax.rem(attn + k, 8), grp, tp))
        others.append((attn, grp, lax.rem(tp + k, 8)))
    for other in others:
        pl.semaphore_signal(barrier, inc=1, device_id=other, device_id_type=MESH)

    wide_q = q_ref[...].astype(F32)
    for h in range(32):
        for half in range(2):
            first = h * 256 + half * 128
            qs[half, pl.ds(h, 4, stride=32), :] = wide_q[:, first : first + 128]
    contexts = []
    slot = lax.broadcasted_iota(jnp.int32, (32, 1024), 1)
    for r in range(4):
        fetch[2 * r].wait()
        scores = lax.dot_general(
            jnp.concatenate([qs[half, r * 32 : (r + 1) * 32] for half in range(2)], axis=1).astype(BF16),
            kc[r],
            NT,
            preferred_element_type=F32,
        ) * (256 ** -0.5)
        scores = jnp.where(slot < len_ref[r], scores, -1e30)
        expo = jnp.exp(scores - jnp.max(scores, axis=-1, keepdims=True))
        probs = (expo / jnp.sum(expo, axis=-1, keepdims=True)).astype(BF16)
        fetch[2 * r + 1].wait()
        contexts.append(jnp.dot(probs, vc[r], preferred_element_type=F32))
    for p in range(4):
        chosen = contexts[0]
        for r in range(1, 4):
            chosen = jnp.where(assign_ref[p] == r, contexts[r], chosen)
        own_b[p * 32 : (p + 1) * 32] = chosen.astype(BF16)
    pl.semaphore_wait(barrier, 15)

    started = []

    def push(src, dst, s_sem, r_sem, i, to):
        copy = pltpu.make_async_remote_copy(
            src_ref=src, dst_ref=dst, send_sem=s_sem.at[i], recv_sem=r_sem.at[i],
            device_id=to, device_id_type=MESH,
        )
        copy.start()
        started.append(copy)

    def landed(dst, s_sem, r_sem, i):
        pltpu.make_async_remote_copy(
            src_ref=dst, dst_ref=dst, send_sem=s_sem.at[i], recv_sem=r_sem.at[i],
            device_id=sibling, device_id_type=MESH,
        ).wait_recv()

    def gather(block, slab, s_sem, r_sem, ready):
        def send(ref, i, to):
            push(ref, ref, s_sem, r_sem, i, to)

        def wait(ref, i):
            landed(ref, s_sem, r_sem, i)

        own = block(z, a)
        send(own, 1, a_right)
        send(own, 2, a_left)
        send(own, 0, z_peer)
        wait(block(zo, a), 0)
        send(block(zo, a), 3, a_right)
        send(block(zo, a), 4, a_left)
        wait(block(z, a3), 1)
        send(block(z, a3), 5, a_right)
        wait(block(z, a1), 2)
        wait(block(zo, a1), 4)
        send(block(zo, a1), 6, a_left)
        wait(block(zo, a3), 3)
        wait(block(z, a2), 5)
        ready(z)
        send(slab(z, b), 7, b_right)
        send(slab(z, b), 8, b_left)
        wait(block(zo, a2), 6)
        ready(zo)
        send(slab(zo, b), 9, b_right)
        send(slab(zo, b), 10, b_left)
        send(slab(z, b), 13, sibling)
        send(slab(zo, b), 14, sibling)
        yield
        wait(slab(z, b3), 7)
        send(slab(z, b3), 11, b_right)
        send(slab(z, b3), 15, sibling)
        wait(slab(z, b1), 8)
        send(slab(z, b1), 16, sibling)
        wait(slab(zo, b1), 10)
        send(slab(zo, b1), 12, b_left)
        send(slab(zo, b1), 17, sibling)
        wait(slab(zo, b3), 9)
        send(slab(zo, b3), 18, sibling)
        wait(slab(z, b2), 11)
        send(slab(z, b2), 19, sibling)
        wait(slab(zo, b2), 12)
        send(slab(zo, b2), 20, sibling)
        yield

    def from_sibling(slab, s_sem, r_sem):
        a_s1, a_s2, a_s3 = a1, a2, a3
        for i, (zv, bv) in enumerate(
            ((z, a), (zo, a), (z, a_s3), (z, a_s1), (zo, a_s1), (zo, a_s3), (z, a_s2), (zo, a_s2))
        ):
            landed(slab(zv, bv), s_sem, r_sem, 13 + i)

    push(own_b, got_b, rs_sem, rr_sem, 0, partner)

    wide_r = resid_ref[...].astype(F32)
    ordered = []
    for p in range(4):
        chosen = wide_r[0:1]
        for r in range(1, 4):
            chosen = jnp.where(assign_ref[p] == r, wide_r[r : r + 1], chosen)
        ordered.append(chosen)
    ordered = jnp.concatenate(ordered, axis=0)
    s1f[...] = jnp.zeros_like(s1f)
    for n in range(8):
        for t in range(8):
            first = n * 896 + t * COLS
            s1f[n, (t % 4) * 4 : (t % 4) * 4 + 4, (t // 4) * 128 : (t // 4) * 128 + COLS] = ordered[
                :, first : first + COLS
            ]
    s1[...] = s1f[...].astype(BF16)
    push(s1, s1_got, rs_sem, rr_sem, 1, partner)

    swap0, swap1 = match_ref[0], match_ref[1]
    row = lax.broadcasted_iota(jnp.int32, (128, 256), 0)
    landed(got_b, rs_sem, rr_sem, 0)
    cb[z, a] = jnp.where(jnp.where(row < 64, swap0, swap1) == 1, got_b[...], own_b[...])

    def ctx_slab(plane):
        return lambda zv, bv: ctx_all.at[(plane * 2 + zv) * 4 + bv]

    def ctx_ready(zv):
        for half in range(2):
            sf[half] = cb[zv, :, :, half * 128 : (half + 1) * 128].astype(F32).reshape(512, 128)
        for h in range(32):
            for half in range(2):
                first = h * 256 + half * 128
                ctx_all[(c * 2 + zv) * 4 + b, :, first : first + 128] = sf[
                    half, pl.ds(h, 16, stride=32), :
                ].astype(BF16)

    steps = gather(lambda zv, av: cb.at[zv, av], ctx_slab(c), bs_sem, br_sem, ctx_ready)
    next(steps)

    landed(s1_got, rs_sem, rr_sem, 1)
    row = lax.rem(lax.broadcasted_iota(jnp.int32, (8, 16, 256), 1), 4)
    served = jnp.where(jnp.where(row < 2, swap0, swap1) == 1, s1_got[...], s1[...])
    s1_got[...] = served
    t1[attn] = s1_got[attn]
    for k in range(1, 8):
        to = lax.rem(attn + k, 8)
        push(s1_got.at[to], t1.at[attn], rs_sem, rr_sem, 1 + k, (to, grp, tp))
    loads[1].wait()
    loads[2].wait()

    def scale(i, _):
        cols = pl.ds(pl.multiple_of(i * 512, 512), 512)
        by = gain_ref[:, cols]
        wg[:, cols] = (wg[:, cols].astype(F32) * by).astype(BF16)
        wu[:, cols] = (wu[:, cols].astype(F32) * by).astype(BF16)
        return 0

    lax.fori_loop(0, 7, scale, 0)
    for k in range(1, 8):
        landed(t1.at[lax.rem(attn + 8 - k, 8)], rs_sem, rr_sem, 1 + k)
    for n in range(8):
        part = t1[n].astype(F32)
        for t in range(8):
            uf[t, n * 4 : n * 4 + 4, :] = part[
                (t % 4) * 4 : (t % 4) * 4 + 4, (t // 4) * 128 : (t // 4) * 128 + 128
            ]
    ub[...] = uf[...].astype(BF16)
    vb[tp] = ub[tp]
    for k in range(1, 8):
        to = lax.rem(tp + k, 8)
        push(ub.at[to], vb.at[tp], rs_sem, rr_sem, 8 + k, (attn, grp, to))
    lax.fori_loop(7, 14, scale, 0)
    next(steps)
    for k in range(1, 8):
        landed(vb.at[lax.rem(tp + 8 - k, 8)], rs_sem, rr_sem, 8 + k)
    for t in range(8):
        part = vb[t].astype(F32)
        for n in range(8):
            place = ((t % 2 * 2 + n % 2) * 4 + (n // 2 if t % 2 else t // 2)) * 4
            place = (place + (t // 2 if t % 2 else n // 2)) * 4
            wf[place : place + 4, :] = part[n * 4 : n * 4 + 4]
    resid_t = wf[...].T[:COLS]
    from_sibling(ctx_slab(co), bs_sem, br_sem)
    loads[0].wait()

    def project(i, acc):
        cols = pl.ds(pl.multiple_of(i * 1024, 1024), 1024)
        rows = ctx_all[:, :, cols].reshape(256, 1024)
        return acc + lax.dot_general(wo[:, cols], rows, NT, preferred_element_type=F32)

    proj = lax.fori_loop(0, CW // 1024, project, jnp.zeros((COLS, 256), F32))
    me = ((c * 2 + z) * 4 + b) * 4 + a
    ht[me] = (resid_t + proj).astype(BF16)

    def ht_slab(plane):
        return lambda zv, bv: ht.at[pl.ds(((plane * 2 + zv) * 4 + bv) * 4, 4)]

    steps = gather(
        lambda zv, av: ht.at[((c * 2 + zv) * 4 + b) * 4 + av], ht_slab(c), cs_sem, cr_sem, lambda zv: None
    )
    next(steps)
    next(steps)
    from_sibling(ht_slab(co), cs_sem, cr_sem)

    acc_g[...] = jnp.zeros_like(acc_g)
    acc_u[...] = jnp.zeros_like(acc_u)

    def features(xv, zv):
        parts = []
        for yv in range(4):
            parts.append(ht[(zv * 4 + yv) * 4 + xv])
            parts.append(ht[((2 + zv) * 4 + xv) * 4 + yv])
        return jnp.concatenate(parts, axis=0)

    def expand(i, squares):
        cols = pl.ds(pl.multiple_of(i * 896, 128), 896)
        part = features(i // 2, lax.rem(i, 2))
        acc_g[...] += jnp.dot(wg[:, cols], part, preferred_element_type=F32)
        acc_u[...] += jnp.dot(wu[:, cols], part, preferred_element_type=F32)
        wide = part.astype(F32)
        return squares + jnp.sum((wide * wide).reshape(112, 8, 256), axis=0)

    squares = lax.fori_loop(0, 8, expand, jnp.zeros((8, 256), F32))
    factor = lax.rsqrt(jnp.sum(squares, axis=0, keepdims=True) * (1.0 / D) + 1e-5)
    gate = acc_g[...] * factor
    act = gate / (1.0 + jnp.exp(-gate)) * (acc_u[...] * factor)
    act_s[...] = act.T.astype(BF16)

    loads[3].wait()
    width = 1024
    act_other = act_s[pl.ds(pl.multiple_of(co * 128, 128), 128), :]
    for j in range(D // width):
        cols = pl.ds(j * width, width)
        part = jnp.dot(act_other, wd[:, cols], preferred_element_type=F32)
        p_send[:, :, cols] = part.astype(BF16).reshape(8, 16, width)
        push(p_send.at[:, :, cols], p_sib.at[:, :, cols], ds_sem, dr_sem, j, sibling)
    act_mine = act_s[pl.ds(pl.multiple_of(c * 128, 128), 128), :]
    for j in range(D // width):
        cols = pl.ds(j * width, width)
        part = jnp.dot(act_mine, wd[:, cols], preferred_element_type=F32)
        landed(p_sib.at[:, :, cols], ds_sem, dr_sem, j)
        total = part + p_sib[:, :, cols].reshape(128, width).astype(F32)
        p_own[:, :, cols] = total.astype(BF16).reshape(8, 16, width)

    def reduce_ring(part, spots, left, right, kl, kr, ko, first):
        def send(ref, i, to):
            push(ref, spots.at[i], ds_sem, dr_sem, first + i, to)

        def wait(i):
            landed(spots.at[i], ds_sem, dr_sem, first + i)

        send(part(0, ko), 0, left)
        send(part(1, ko), 1, right)
        send(part(1, kl), 3, left)
        send(part(0, kr), 4, right)
        yield
        for i, p, k, to, j in ((0, 0, kl, left, 2), (1, 1, kr, right, 5)):
            wait(i)
            ref = part(p, k)
            ref[...] = (ref[...].astype(F32) + spots[i].astype(F32)).astype(BF16)
            send(ref, j, to)
        for i in (3, 4, 2, 5):
            wait(i)
        yield

    zs = (z, zo)
    steps = reduce_ring(lambda p, k: p_own.at[zs[p] * 4 + k], r2, b_left, b_right, b3, b1, b2, 7)
    next(steps)

    lane = lax.broadcasted_iota(jnp.int32, (16, 256), 1)
    sub = lax.broadcasted_iota(jnp.int32, (16, 256), 0)
    hidden = jnp.zeros((16, 1792), F32)
    for q in range(4):
        pick = jnp.where(lane == me * 4 + sub - q * 4, 1.0, 0.0)
        pick = jnp.where((sub >= q * 4) & (sub < q * 4 + 4), pick, 0.0).astype(BF16)
        rows = jnp.concatenate([features(q, 0), features(q, 1)], axis=0)
        hidden = hidden + lax.dot_general(pick, rows, NT, preferred_element_type=F32)
    next(steps)
    for p in range(2):
        af[...] = (
            p_own[zs[p] * 4 + b].astype(F32) + r2[2 + p].astype(F32) + r2[4 + p].astype(F32)
        )
        for av in range(4):
            for q in range(4):
                gf[q * 4 : q * 4 + 4, av * 2048 : av * 2048 + 1792] = af[
                    av * 4 : av * 4 + 4, q * 1792 : (q + 1) * 1792
                ]
        for av in range(4):
            qb[p, av] = gf[:, av * 2048 : av * 2048 + 1792].astype(BF16)
    steps = reduce_ring(lambda p, k: qb.at[p, k], r1, a_left, a_right, a3, a1, a2, 13)
    next(steps)
    next(steps)
    tz[...] = (qb[1, a].astype(F32) + r1[3].astype(F32) + r1[5].astype(F32)).astype(BF16)
    push(tz, rz, ds_sem, dr_sem, 19, z_peer)
    mine = qb[0, a].astype(F32) + r1[2].astype(F32) + r1[4].astype(F32)
    landed(rz, ds_sem, dr_sem, 19)
    ob[...] = (hidden + (mine + rz[...].astype(F32))).astype(BF16)

    push(ob, oz, rs_sem, rr_sem, 16, partner)
    landed(oz, rs_sem, rr_sem, 16)
    row = lax.rem(lax.broadcasted_iota(jnp.int32, (16, 1792), 0), 4)
    swapped = jnp.where(row < 2, swap0, swap1) == 1
    final = jnp.where(swapped, oz[...].astype(F32), ob[...].astype(F32))
    request = lax.broadcasted_iota(jnp.int32, (4, 1792), 0)
    for q in range(4):
        rows = jnp.zeros((4, 1792), F32)
        for p in range(4):
            one = jnp.broadcast_to(final[q * 4 + p : q * 4 + p + 1], (4, 1792))
            rows = jnp.where(request == assign_ref[p], one, rows)
        out_ref[:, q * 1792 : (q + 1) * 1792] = rows.astype(BF16)
    for copy in started:
        copy.wait_send()


def per_device(
    queries, keys, values, lengths, resid, assign, matching, w_out, gain, gate_w, up_w, down_w
):
    smem = pl.BlockSpec(memory_space=pltpu.SMEM)
    vmem = pl.BlockSpec(memory_space=pltpu.VMEM)
    hbm = pl.BlockSpec(memory_space=pl.ANY)
    dma = pltpu.SemaphoreType.DMA
    scratch = (
        ((4, 1024, 256), BF16),
        ((4, 1024, 256), BF16),
        ((COLS, CW), BF16),
        ((FH, D), BF16),
        ((FH, D), BF16),
        ((FH, D), BF16),
        ((2, 128, 128), F32),
        ((128, 256), BF16),
        ((128, 256), BF16),
        ((2, 4, 128, 256), BF16),
        ((2, 512, 128), F32),
        ((16, CW), F32),
        ((16, 16, CW), BF16),
        ((64, COLS, 256), BF16),
        ((FH, 256), F32),
        ((FH, 256), F32),
        ((256, FH), BF16),
        ((8, 16, 256), F32),
        ((8, 16, 256), BF16),
        ((8, 16, 256), BF16),
        ((8, 16, 256), BF16),
        ((8, 32, 128), F32),
        ((8, 32, 128), BF16),
        ((8, 32, 128), BF16),
        ((256, 128), F32),
        ((8, 16, D), BF16),
        ((8, 16, D), BF16),
        ((8, 16, D), BF16),
        ((6, 16, D), BF16),
        ((16, D), F32),
        ((2, 4, 16, 1792), BF16),
        ((6, 16, 1792), BF16),
        ((16, 1792), BF16),
        ((16, 1792), BF16),
        ((16, 1792), BF16),
        ((16, 1792), BF16),
    )
    return pl.pallas_call(
        kernel,
        out_shape=jax.ShapeDtypeStruct((4, D), BF16),
        in_specs=[smem] * 3 + [vmem] * 3 + [hbm] * 6,
        out_specs=vmem,
        scratch_shapes=[pltpu.VMEM(shape, dtype) for shape, dtype in scratch]
        + [dma((n,)) for n in (8, 4, 21, 21, 21, 21, 20, 20, 17, 17)],
        compiler_params=pltpu.CompilerParams(
            collective_id=0, has_side_effects=True, vmem_limit_bytes=60 * 1024 * 1024
        ),
    )(
        lengths, assign[0], matching[:, 0, 0], queries, resid, gain[None],
        keys, values, w_out.T, gate_w[0].T, up_w[0].T, down_w[0],
    )


def solution(mesh):
    rows = P(("attn", "grp", "tp"), None)
    cache = P(("attn", "grp", "tp"), None, None)
    placed = (
        rows,
        cache,
        cache,
        P(("attn", "grp", "tp")),
        rows,
        rows,
        P(None, "attn", "tp"),
        P(None, ("attn", "tp")),
        P(),
        P("grp", None, ("attn", "tp")),
        P("grp", None, ("attn", "tp")),
        P("grp", ("attn", "tp"), None),
    )
    return jax.shard_map(
        per_device, mesh=mesh, in_specs=placed, out_specs=rows, check_vma=False
    )
```

```python
import jax
import jax.numpy as jnp
from jax import lax
from jax.experimental import pallas as pl
from jax.experimental.pallas import tpu as pltpu
from jax.sharding import PartitionSpec as P

D = 7168
CW = 8192
FH = 288
COLS = 112
MESH = pl.DeviceIdType.MESH
F32 = jnp.float32
BF16 = jnp.bfloat16
NT = (((1,), (1,)), ((), ()))


def kernel(
    len_ref, assign_ref, match_ref, q_ref, resid_hbm, gain_hbm, k_hbm, v_hbm, wo_hbm, g_hbm, u_hbm, d_hbm,
    out_ref,
    kc, vc, wo, wg, wu, wd, resid_ref, gain_ref,
    qs, own_b, got_b, cb, sf, ctx_all, ht, acc_g, acc_u, act_s,
    s1f, s1, s1_got, t1, uf, ub, vb, wf, wt,
    pf, p_send, p_sib, p_own, r2, qf, qb, r1, t0, tp0, tz, got_peer, got_partner, got_cross, hid, hid_got,
    kv_sem, w_sem, bs_sem, br_sem, cs_sem, cr_sem, ds_sem, dr_sem, rs_sem, rr_sem,
):
    attn, grp, tp = lax.axis_index("attn"), lax.axis_index("grp"), lax.axis_index("tp")
    x, z, y, c = attn // 2, lax.rem(attn, 2), tp // 2, lax.rem(tp, 2)
    zo, co = 1 - z, 1 - c
    zs = (z, zo)
    a = x * co + y * c
    b = y * co + x * c

    def dev(x_, z_, y_, c_):
        return (lax.rem(x_, 4) * 2 + z_, grp, lax.rem(y_, 4) * 2 + c_)

    a_other = [dev(x + k * co, z, y + k * c, c) for k in range(4)]
    b_right, b_left = dev(x + c, z, y + co, c), dev(x + 3 * c, z, y + 3 * co, c)
    z_peer, sibling = dev(x, zo, y, c), dev(x, z, y, co)
    partner = (attn, 1 - grp, tp)
    cross = (x * 2 + zo, 1 - grp, tp)
    ak = [lax.rem(a + k, 4) for k in range(4)]
    b1, b2, b3 = lax.rem(b + 1, 4), lax.rem(b + 2, 4), lax.rem(b + 3, 4)

    fetch = []
    for r in range(4):
        for src, dst in ((k_hbm, kc), (v_hbm, vc)):
            fetch.append(pltpu.make_async_copy(src.at[r], dst.at[r], kv_sem.at[len(fetch)]))
            fetch[-1].start()
    loads = [
        pltpu.make_async_copy(src, dst, w_sem.at[i])
        for i, (src, dst) in enumerate(
            ((resid_hbm, resid_ref), (gain_hbm, gain_ref), (g_hbm, wg), (u_hbm, wu), (wo_hbm, wo), (d_hbm, wd))
        )
    ]
    for load in loads:
        load.start()

    barrier = pltpu.get_barrier_semaphore()
    others = [partner, cross]
    for k in range(1, 8):
        others.append((lax.rem(attn + k, 8), grp, tp))
        others.append((attn, grp, lax.rem(tp + k, 8)))
    for other in others:
        pl.semaphore_signal(barrier, inc=1, device_id=other, device_id_type=MESH)

    started = []

    def push(src, dst, s_sem, r_sem, i, to):
        copy = pltpu.make_async_remote_copy(
            src_ref=src, dst_ref=dst, send_sem=s_sem.at[i], recv_sem=r_sem.at[i],
            device_id=to, device_id_type=MESH,
        )
        copy.start()
        started.append(copy)

    def landed(dst, s_sem, r_sem, i):
        pltpu.make_async_remote_copy(
            src_ref=dst, dst_ref=dst, send_sem=s_sem.at[i], recv_sem=r_sem.at[i],
            device_id=sibling, device_id_type=MESH,
        ).wait_recv()

    wide_q = q_ref[...].astype(F32)
    for h in range(32):
        for half in range(2):
            first = h * 256 + half * 128
            qs[half, pl.ds(h, 4, stride=32), :] = wide_q[:, first : first + 128]
    slot = lax.broadcasted_iota(jnp.int32, (32, 1024), 1)
    swaps = (match_ref[0], match_ref[1])

    def attend(r):
        fetch[2 * r].wait()
        query = jnp.concatenate([qs[half, r * 32 : (r + 1) * 32] for half in range(2)], axis=1).astype(BF16)
        scores = lax.dot_general(query, kc[r], NT, preferred_element_type=F32) * (256 ** -0.5)
        scores = jnp.where(slot < len_ref[r], scores, -1e30)
        expo = jnp.exp(scores - jnp.max(scores, axis=-1, keepdims=True))
        probs = (expo / jnp.sum(expo, axis=-1, keepdims=True)).astype(BF16)
        fetch[2 * r + 1].wait()
        return jnp.dot(probs, vc[r], preferred_element_type=F32)

    contexts = [attend(r) for r in range(4)]
    for p in range(4):
        chosen = contexts[0]
        for r in range(1, 4):
            chosen = jnp.where(assign_ref[p] == r, contexts[r], chosen)
        own_b[p * 32 : p * 32 + 32] = chosen.astype(BF16)
    pl.semaphore_wait(barrier, 16)

    def gather(block, part, other, s_sem, r_sem, ready):
        def send(ref, i, to):
            push(ref, ref, s_sem, r_sem, i, to)

        def wait(ref, i):
            landed(ref, s_sem, r_sem, i)

        def ring_1(p):
            for k in (1, 3, 2):
                send(block(p, a), 3 * p + k, a_other[k])

        def ring_2(p):
            for k in (1, 3, 2):
                wait(block(p, ak[4 - k]), 3 * p + k)
            ready(p)
            first, second = ((7, b_right), (8, b_left)) if p == 0 else ((10, b_left), (9, b_right))
            send(part(p, b), *first)
            send(part(p, b), *second)
            send(part(p, b), 13 + p, sibling)

        ring_1(0)
        send(block(0, a), 0, z_peer)
        yield
        ring_2(0)
        wait(block(1, a), 0)
        ring_1(1)
        yield
        ring_2(1)
        yield
        wait(part(0, b3), 7)
        send(part(0, b3), 11, b_right)
        send(part(0, b3), 15, sibling)
        wait(part(0, b1), 8)
        send(part(0, b1), 16, sibling)
        yield
        wait(part(1, b1), 10)
        send(part(1, b1), 12, b_left)
        send(part(1, b1), 17, sibling)
        wait(part(1, b3), 9)
        send(part(1, b3), 18, sibling)
        yield
        wait(part(0, b2), 11)
        send(part(0, b2), 19, sibling)
        wait(part(1, b2), 12)
        send(part(1, b2), 20, sibling)
        yield
        for i, (zv, k) in enumerate(
            ((z, 0), (zo, 0), (z, 3), (z, 1), (zo, 1), (zo, 3), (z, 2), (zo, 2))
        ):
            wait(other(zv, ak[k]), 13 + i)
        yield

    me = ((c * 2 + z) * 4 + b) * 4 + a

    def residual():
        loads[0].wait()
        wide_r = resid_ref[...].astype(F32)
        ordered = []
        for p in range(4):
            chosen = wide_r[0:1]
            for r in range(1, 4):
                chosen = jnp.where(assign_ref[p] == r, wide_r[r : r + 1], chosen)
            ordered.append(chosen)
        ordered = jnp.concatenate(ordered, axis=0)
        s1f[...] = jnp.zeros_like(s1f)
        for n in range(8):
            for t in range(8):
                first = n * 896 + t * COLS
                s1f[n, (t % 4) * 4 : (t % 4) * 4 + 4, (t // 4) * 128 : (t // 4) * 128 + COLS] = ordered[
                    :, first : first + COLS
                ]
        s1[...] = s1f[...].astype(BF16)
        push(s1, s1_got, rs_sem, rr_sem, 1, partner)
        yield
        landed(s1_got, rs_sem, rr_sem, 1)
        row = lax.rem(lax.broadcasted_iota(jnp.int32, (8, 16, 256), 1), 4)
        served = jnp.where(jnp.where(row < 2, swaps[0], swaps[1]) == 1, s1_got[...], s1[...])
        s1_got[...] = served
        t1[attn] = s1_got[attn]
        for k in range(1, 8):
            to = lax.rem(attn + k, 8)
            push(s1_got.at[to], t1.at[attn], rs_sem, rr_sem, 1 + k, (to, grp, tp))
        yield
        for k in range(1, 8):
            landed(t1.at[lax.rem(attn + 8 - k, 8)], rs_sem, rr_sem, 1 + k)
        for n in range(8):
            part = t1[n].astype(F32)
            for t in range(8):
                uf[t, n * 4 : n * 4 + 4, :] = part[
                    (t % 4) * 4 : (t % 4) * 4 + 4, (t // 4) * 128 : (t // 4) * 128 + 128
                ]
        ub[...] = uf[...].astype(BF16)
        vb[tp] = ub[tp]
        for k in range(1, 8):
            to = lax.rem(tp + k, 8)
            push(ub.at[to], vb.at[tp], rs_sem, rr_sem, 8 + k, (attn, grp, to))
        yield
        for k in range(1, 8):
            landed(vb.at[lax.rem(tp + 8 - k, 8)], rs_sem, rr_sem, 8 + k)
        for t in range(8):
            part = vb[t].astype(F32)
            for n in range(8):
                plane, zv = t % 2, n % 2
                bv, av = (n // 2, t // 2) if plane else (t // 2, n // 2)
                place = (((plane * 2 + zv) * 4 + bv) * 4 + av) * 4
                wf[place : place + 4, :] = part[n * 4 : n * 4 + 4]
        wt[...] = wf[...].T
        yield

    def scaling():
        for i in (1, 2, 3):
            loads[i].wait()

        def scale(i, _):
            cols = pl.ds(pl.multiple_of(i * 512, 512), 512)
            by = gain_ref[:, cols]
            wg[:, cols] = (wg[:, cols].astype(F32) * by).astype(BF16)
            wu[:, cols] = (wu[:, cols].astype(F32) * by).astype(BF16)
            return 0

        for first, last in ((0, 5), (5, 10), (10, 14)):
            lax.fori_loop(first, last, scale, 0)
            yield

    push(own_b, got_b, rs_sem, rr_sem, 0, partner)
    residual_steps, scaling_steps = residual(), scaling()
    next(residual_steps)
    row = lax.broadcasted_iota(jnp.int32, (128, 256), 0)
    landed(got_b, rs_sem, rr_sem, 0)
    cb[z, a] = jnp.where(jnp.where(row < 64, swaps[0], swaps[1]) == 1, got_b[...], own_b[...])

    def ready(p):
        for half in range(2):
            sf[half] = cb[zs[p], :, :, half * 128 : (half + 1) * 128].astype(F32).reshape(512, 128)
        for h in range(32):
            for half in range(2):
                first = h * 256 + half * 128
                ctx_all[(c * 2 + zs[p]) * 4 + b, :, first : first + 128] = sf[
                    half, pl.ds(h, 16, stride=32), :
                ].astype(BF16)

    steps = gather(
        lambda p, av: cb.at[zs[p], av],
        lambda p, bv: ctx_all.at[(c * 2 + zs[p]) * 4 + bv],
        lambda zv, bv: ctx_all.at[(co * 2 + zv) * 4 + bv],
        bs_sem,
        br_sem,
        ready,
    )
    next(steps)
    next(residual_steps)
    next(steps)
    next(scaling_steps)
    next(steps)
    next(residual_steps)
    next(scaling_steps)
    next(steps)
    next(scaling_steps)
    next(steps)
    next(residual_steps)
    next(steps)
    loads[4].wait()

    def project(plane):
        def step(i, acc):
            cols = pl.ds(pl.multiple_of(i * 1024, 1024), 1024)
            rows = ctx_all[pl.ds(plane * 8, 8), :, cols].reshape(128, 1024)
            return acc + lax.dot_general(wo[:, cols], rows, NT, preferred_element_type=F32)

        total = lax.fori_loop(0, CW // 1024, step, jnp.zeros((COLS, 128), F32))
        lanes = pl.ds(pl.multiple_of(plane * 128, 128), 128)
        ht[me, :, lanes] = (wt[:COLS, lanes] + total).astype(BF16)

    project(c)
    next(steps)
    project(co)

    steps = gather(
        lambda p, av: ht.at[((c * 2 + zs[p]) * 4 + b) * 4 + av],
        lambda p, bv: ht.at[pl.ds(((c * 2 + zs[p]) * 4 + bv) * 4, 4)],
        lambda zv, bv: ht.at[pl.ds(((co * 2 + zv) * 4 + bv) * 4, 4)],
        cs_sem,
        cr_sem,
        lambda p: None,
    )
    for _ in range(7):
        next(steps)

    def features(xv, zv):
        parts = []
        for yv in range(4):
            parts.append(ht[(zv * 4 + yv) * 4 + xv])
            parts.append(ht[((2 + zv) * 4 + xv) * 4 + yv])
        return jnp.concatenate(parts, axis=0)

    acc_g[...] = jnp.zeros_like(acc_g)
    acc_u[...] = jnp.zeros_like(acc_u)

    def expand(i, squares):
        cols = pl.ds(pl.multiple_of(i * 896, 128), 896)
        part = features(i // 2, lax.rem(i, 2))
        acc_g[...] += jnp.dot(wg[:, cols], part, preferred_element_type=F32)
        acc_u[...] += jnp.dot(wu[:, cols], part, preferred_element_type=F32)
        wide = part.astype(F32)
        return squares + jnp.sum((wide * wide).reshape(112, 8, 256), axis=0)

    squares = lax.fori_loop(0, 8, expand, jnp.zeros((8, 256), F32))
    factor = lax.rsqrt(jnp.sum(squares, axis=0, keepdims=True) * (1.0 / D) + 1e-5)
    gate = acc_g[...] * factor
    act = gate / (1.0 + jnp.exp(-gate)) * (acc_u[...] * factor)
    act_s[...] = act.T.astype(BF16)

    loads[5].wait()
    lhs = jnp.concatenate(
        [act_s[pl.ds(pl.multiple_of(k * 128, 128), 128), :] for k in (co, c)], axis=0
    )

    def reduction(h):
        for j in range(2):
            cols = pl.ds(j * 1792, 1792)
            part = jnp.dot(lhs, wd[:, pl.ds(h * 3584 + j * 1792, 1792)], preferred_element_type=F32)
            p_send[h, :, :, cols] = part[:128].astype(BF16).reshape(8, 16, 1792)
            pf[h, :, :, cols] = part[128:].reshape(8, 16, 1792)
        push(p_send.at[h], p_sib.at[h], ds_sem, dr_sem, h, sibling)
        yield
        landed(p_sib.at[h], ds_sem, dr_sem, h)
        p_own[h] = (pf[h] + p_sib[h].astype(F32)).astype(BF16)

        def slab(p, k):
            return p_own.at[h, zs[p] * 4 + k]

        def send(ref, i, to):
            push(ref, r2.at[h, i], ds_sem, dr_sem, 2 + 6 * h + i, to)

        def wait(i):
            landed(r2.at[h, i], ds_sem, dr_sem, 2 + 6 * h + i)

        send(slab(0, b2), 0, b_left)
        send(slab(1, b2), 1, b_right)
        send(slab(1, b3), 3, b_left)
        send(slab(0, b1), 4, b_right)
        yield
        for i, p, k, to, j in ((0, 0, b3, b_left, 2), (1, 1, b1, b_right, 5)):
            wait(i)
            ref = slab(p, k)
            ref[...] = (ref[...].astype(F32) + r2[h, i].astype(F32)).astype(BF16)
            send(ref, j, to)
        yield
        for i in (3, 4, 2, 5):
            wait(i)
        for p in (1, 0):
            total = (
                p_own[h, zs[p] * 4 + b].astype(F32) + r2[h, 2 + p].astype(F32) + r2[h, 4 + p].astype(F32)
            )
            for av in range(4):
                for q in range(4):
                    qf[av, q * 4 : q * 4 + 4, :] = total[av * 4 : av * 4 + 4, q * 896 : (q + 1) * 896]
            qb[h, p] = qf[...].astype(BF16)
            for k in (1, 3, 2):
                push(
                    qb.at[h, p, ak[k]], r1.at[h, p, k - 1], ds_sem, dr_sem, 13 + 6 * h + 3 * p + k, a_other[k]
                )
        yield
        sums = []
        for p in (1, 0):
            total = qb[h, p, a].astype(F32)
            for k in (1, 3, 2):
                landed(r1.at[h, p, k - 1], ds_sem, dr_sem, 13 + 6 * h + 3 * p + k)
                total = total + r1[h, p, k - 1].astype(F32)
            sums.append(total)
            if p == 1:
                tz[h] = total.astype(BF16)
                push(tz.at[h], got_peer.at[h], ds_sem, dr_sem, 26 + 3 * h, z_peer)
                push(tz.at[h], got_cross.at[h], ds_sem, dr_sem, 27 + 3 * h, cross)
        tp0[h] = sums[1].astype(BF16)
        push(tp0.at[h], got_partner.at[h], ds_sem, dr_sem, 28 + 3 * h, partner)
        t0[h] = sums[1]
        yield
        landed(got_partner.at[h], ds_sem, dr_sem, 28 + 3 * h)
        landed(got_cross.at[h], ds_sem, dr_sem, 27 + 3 * h)
        landed(got_peer.at[h], ds_sem, dr_sem, 26 + 3 * h)
        stayed = hid[h].astype(F32) + (t0[h] + got_peer[h].astype(F32))
        moved = hid_got[h].astype(F32) + (got_partner[h].astype(F32) + got_cross[h].astype(F32))
        row = lax.rem(lax.broadcasted_iota(jnp.int32, (16, 896), 0), 4)
        final = jnp.where(jnp.where(row < 2, swaps[0], swaps[1]) == 1, moved, stayed)
        request = lax.broadcasted_iota(jnp.int32, (4, 896), 0)
        for q in range(4):
            rows = jnp.zeros((4, 896), F32)
            for p in range(4):
                one = jnp.broadcast_to(final[q * 4 + p : q * 4 + p + 1], (4, 896))
                rows = jnp.where(request == assign_ref[p], one, rows)
            out_ref[:, h * 3584 + q * 896 : h * 3584 + (q + 1) * 896] = rows.astype(BF16)
        yield

    def own_hidden(h):
        lane = lax.broadcasted_iota(jnp.int32, (16, 256), 1)
        sub = lax.broadcasted_iota(jnp.int32, (16, 256), 0)
        rows = jnp.zeros((16, 896), F32)
        for q in range(4):
            pick = jnp.where(lane == me * 4 + sub - q * 4, 1.0, 0.0)
            pick = jnp.where((sub >= q * 4) & (sub < q * 4 + 4), pick, 0.0).astype(BF16)
            rows = rows + lax.dot_general(
                pick, features(2 * h + q // 2, q % 2), NT, preferred_element_type=F32
            )
        hid[h] = rows.astype(BF16)
        push(hid.at[h], hid_got.at[h], rs_sem, rr_sem, 16 + h, partner)

    halves = (reduction(0), reduction(1))
    for _ in range(2):
        for half in halves:
            next(half)
    own_hidden(0)
    next(halves[0])
    own_hidden(1)
    next(halves[1])
    for _ in range(2):
        for half in halves:
            next(half)
    for h in range(2):
        landed(hid_got.at[h], rs_sem, rr_sem, 16 + h)
    for half in halves:
        next(half)
    for copy in started:
        copy.wait_send()


def per_device(
    queries, keys, values, lengths, resid, assign, matching, w_out, gain, gate_w, up_w, down_w
):
    smem = pl.BlockSpec(memory_space=pltpu.SMEM)
    vmem = pl.BlockSpec(memory_space=pltpu.VMEM)
    hbm = pl.BlockSpec(memory_space=pl.ANY)
    dma = pltpu.SemaphoreType.DMA
    scratch = (
        ((4, 1024, 256), BF16),
        ((4, 1024, 256), BF16),
        ((COLS, CW), BF16),
        ((FH, D), BF16),
        ((FH, D), BF16),
        ((FH, D), BF16),
        ((4, D), BF16),
        ((1, D), F32),
        ((2, 128, 128), F32),
        ((128, 256), BF16),
        ((128, 256), BF16),
        ((2, 4, 128, 256), BF16),
        ((2, 512, 128), F32),
        ((16, 16, CW), BF16),
        ((64, COLS, 256), BF16),
        ((FH, 256), F32),
        ((FH, 256), F32),
        ((256, FH), BF16),
        ((8, 16, 256), F32),
        ((8, 16, 256), BF16),
        ((8, 16, 256), BF16),
        ((8, 16, 256), BF16),
        ((8, 32, 128), F32),
        ((8, 32, 128), BF16),
        ((8, 32, 128), BF16),
        ((256, 128), F32),
        ((128, 256), F32),
        ((2, 8, 16, D // 2), F32),
        ((2, 8, 16, D // 2), BF16),
        ((2, 8, 16, D // 2), BF16),
        ((2, 8, 16, D // 2), BF16),
        ((2, 6, 16, D // 2), BF16),
        ((4, 16, 896), F32),
        ((2, 2, 4, 16, 896), BF16),
        ((2, 2, 3, 16, 896), BF16),
        ((2, 16, 896), F32),
    ) + (((2, 16, 896), BF16),) * 7
    return pl.pallas_call(
        kernel,
        out_shape=jax.ShapeDtypeStruct((4, D), BF16),
        in_specs=[smem] * 3 + [vmem] + [hbm] * 8,
        out_specs=vmem,
        scratch_shapes=[pltpu.VMEM(shape, dtype) for shape, dtype in scratch]
        + [dma((n,)) for n in (8, 6, 21, 21, 21, 21, 32, 32, 18, 18)],
        compiler_params=pltpu.CompilerParams(
            collective_id=0, has_side_effects=True, vmem_limit_bytes=60 * 1024 * 1024
        ),
    )(
        lengths, assign[0], matching[:, 0, 0], queries, resid, gain[None],
        keys, values, w_out.T, gate_w[0].T, up_w[0].T, down_w[0],
    )


def solution(mesh):
    rows = P(("attn", "grp", "tp"), None)
    cache = P(("attn", "grp", "tp"), None, None)
    placed = (
        rows,
        cache,
        cache,
        P(("attn", "grp", "tp")),
        rows,
        rows,
        P(None, "attn", "tp"),
        P(None, ("attn", "tp")),
        P(),
        P("grp", None, ("attn", "tp")),
        P("grp", None, ("attn", "tp")),
        P("grp", ("attn", "tp"), None),
    )
    return jax.shard_map(
        per_device, mesh=mesh, in_specs=placed, out_specs=rows, check_vma=False
    )
```

```python
import jax
import jax.numpy as jnp
from jax import lax
from jax.experimental import pallas as pl
from jax.experimental.pallas import tpu as pltpu
from jax.sharding import PartitionSpec as P

D = 7168
CW = 8192
FH = 288
COLS = 112
MESH = pl.DeviceIdType.MESH
F32 = jnp.float32
BF16 = jnp.bfloat16
NT = (((1,), (1,)), ((), ()))


def kernel(
    len_ref, assign_ref, match_ref, q_ref, resid_hbm, gain_hbm, k_hbm, v_hbm, wo_hbm, g_hbm, u_hbm, d_hbm,
    out_ref,
    kc, vc, wo, wg, wu, wg2, wu2, wd, resid_ref, gain_ref,
    qs, own_b, got_b, cb, sf, ctx_all, ht, acc_g, acc_u, squares, act_out, act_in,
    s1f, s1, s1_got, t1, uf, ub, vb, wf, wt,
    p_own, r2, qf, qb, r1, t0, tp0, tz, got_peer, got_partner, got_cross, hid, hid_got,
    kv_sem, w_sem, bs_sem, br_sem, cs_sem, cr_sem, ds_sem, dr_sem, rs_sem, rr_sem,
):
    attn, grp, tp = lax.axis_index("attn"), lax.axis_index("grp"), lax.axis_index("tp")
    x, z, y, c = attn // 2, lax.rem(attn, 2), tp // 2, lax.rem(tp, 2)
    zo, co = 1 - z, 1 - c
    zs = (z, zo)
    a = x * co + y * c
    b = y * co + x * c

    def dev(x_, z_, y_, c_):
        return (lax.rem(x_, 4) * 2 + z_, grp, lax.rem(y_, 4) * 2 + c_)

    a_other = [dev(x + k * co, z, y + k * c, c) for k in range(4)]
    b_right, b_left = dev(x + c, z, y + co, c), dev(x + 3 * c, z, y + 3 * co, c)
    z_peer, sibling = dev(x, zo, y, c), dev(x, z, y, co)
    partner = (attn, 1 - grp, tp)
    cross = (x * 2 + zo, 1 - grp, tp)
    ak = [lax.rem(a + k, 4) for k in range(4)]
    b1, b2, b3 = lax.rem(b + 1, 4), lax.rem(b + 2, 4), lax.rem(b + 3, 4)

    fetch = []
    for r in range(4):
        for src, dst in ((k_hbm, kc), (v_hbm, vc)):
            fetch.append(pltpu.make_async_copy(src.at[r], dst.at[r], kv_sem.at[len(fetch)]))
            fetch[-1].start()
    loads = [
        pltpu.make_async_copy(src, dst, w_sem.at[i])
        for i, (src, dst) in enumerate(
            ((resid_hbm, resid_ref), (gain_hbm, gain_ref), (g_hbm, wg), (u_hbm, wu), (wo_hbm, wo), (d_hbm, wd.at[pl.ds(0, FH)]))
        )
    ]
    for load in loads:
        load.start()

    barrier = pltpu.get_barrier_semaphore()
    others = [partner, cross]
    for k in range(1, 8):
        others.append((lax.rem(attn + k, 8), grp, tp))
        others.append((attn, grp, lax.rem(tp + k, 8)))
    for other in others:
        pl.semaphore_signal(barrier, inc=1, device_id=other, device_id_type=MESH)

    started = []

    def push(src, dst, s_sem, r_sem, i, to):
        copy = pltpu.make_async_remote_copy(
            src_ref=src, dst_ref=dst, send_sem=s_sem.at[i], recv_sem=r_sem.at[i],
            device_id=to, device_id_type=MESH,
        )
        copy.start()
        started.append(copy)

    def landed(dst, s_sem, r_sem, i):
        pltpu.make_async_remote_copy(
            src_ref=dst, dst_ref=dst, send_sem=s_sem.at[i], recv_sem=r_sem.at[i],
            device_id=sibling, device_id_type=MESH,
        ).wait_recv()

    wide_q = q_ref[...].astype(F32)
    for h in range(32):
        for half in range(2):
            first = h * 256 + half * 128
            qs[half, pl.ds(h, 4, stride=32), :] = wide_q[:, first : first + 128]
    slot = lax.broadcasted_iota(jnp.int32, (32, 1024), 1)
    swaps = (match_ref[0], match_ref[1])

    def attend(r):
        fetch[2 * r].wait()
        query = jnp.concatenate([qs[half, r * 32 : (r + 1) * 32] for half in range(2)], axis=1).astype(BF16)
        scores = lax.dot_general(query, kc[r], NT, preferred_element_type=F32) * (256 ** -0.5)
        scores = jnp.where(slot < len_ref[r], scores, -1e30)
        expo = jnp.exp(scores - jnp.max(scores, axis=-1, keepdims=True))
        probs = (expo / jnp.sum(expo, axis=-1, keepdims=True)).astype(BF16)
        fetch[2 * r + 1].wait()
        return jnp.dot(probs, vc[r], preferred_element_type=F32)

    contexts = [attend(r) for r in range(4)]
    for p in range(4):
        chosen = contexts[0]
        for r in range(1, 4):
            chosen = jnp.where(assign_ref[p] == r, contexts[r], chosen)
        own_b[p * 32 : p * 32 + 32] = chosen.astype(BF16)
    pl.semaphore_wait(barrier, 16)

    def gather(block, part, other, s_sem, r_sem, ready, base=0):
        def send(ref, i, to):
            push(ref, ref, s_sem, r_sem, base + i, to)

        def wait(ref, i):
            landed(ref, s_sem, r_sem, base + i)

        def ring_1(p):
            for k in (1, 3, 2):
                send(block(p, a), 3 * p + k, a_other[k])

        def ring_2(p):
            for k in (1, 3, 2):
                wait(block(p, ak[4 - k]), 3 * p + k)
            ready(p)
            first, second = ((7, b_right), (8, b_left)) if p == 0 else ((10, b_left), (9, b_right))
            send(part(p, b), *first)
            send(part(p, b), *second)
            send(part(p, b), 13 + p, sibling)

        ring_1(0)
        send(block(0, a), 0, z_peer)
        yield
        ring_2(0)
        wait(block(1, a), 0)
        ring_1(1)
        yield
        ring_2(1)
        yield
        wait(part(0, b3), 7)
        send(part(0, b3), 11, b_right)
        send(part(0, b3), 15, sibling)
        wait(part(0, b1), 8)
        send(part(0, b1), 16, sibling)
        yield
        wait(part(1, b1), 10)
        send(part(1, b1), 12, b_left)
        send(part(1, b1), 17, sibling)
        wait(part(1, b3), 9)
        send(part(1, b3), 18, sibling)
        yield
        wait(part(0, b2), 11)
        send(part(0, b2), 19, sibling)
        wait(part(1, b2), 12)
        send(part(1, b2), 20, sibling)
        yield
        for i, (zv, k) in enumerate(
            ((z, 0), (zo, 0), (z, 3), (z, 1), (zo, 1), (zo, 3), (z, 2), (zo, 2))
        ):
            wait(other(zv, ak[k]), 13 + i)
        yield

    me = ((c * 2 + z) * 4 + b) * 4 + a
    me_row = ((z * 4 + b) * 4 + a) * 4

    def residual():
        loads[0].wait()
        wide_r = resid_ref[...].astype(F32)
        ordered = []
        for p in range(4):
            chosen = wide_r[0:1]
            for r in range(1, 4):
                chosen = jnp.where(assign_ref[p] == r, wide_r[r : r + 1], chosen)
            ordered.append(chosen)
        ordered = jnp.concatenate(ordered, axis=0)
        s1f[...] = jnp.zeros_like(s1f)
        for n in range(8):
            for t in range(8):
                first = n * 896 + t * COLS
                s1f[n, (t % 4) * 4 : (t % 4) * 4 + 4, (t // 4) * 128 : (t // 4) * 128 + COLS] = ordered[
                    :, first : first + COLS
                ]
        s1[...] = s1f[...].astype(BF16)
        push(s1, s1_got, rs_sem, rr_sem, 1, partner)
        yield
        landed(s1_got, rs_sem, rr_sem, 1)
        row = lax.rem(lax.broadcasted_iota(jnp.int32, (8, 16, 256), 1), 4)
        served = jnp.where(jnp.where(row < 2, swaps[0], swaps[1]) == 1, s1_got[...], s1[...])
        s1_got[...] = served
        t1[attn] = s1_got[attn]
        for k in range(1, 8):
            to = lax.rem(attn + k, 8)
            push(s1_got.at[to], t1.at[attn], rs_sem, rr_sem, 1 + k, (to, grp, tp))
        yield
        for k in range(1, 8):
            landed(t1.at[lax.rem(attn + 8 - k, 8)], rs_sem, rr_sem, 1 + k)
        for n in range(8):
            part = t1[n].astype(F32)
            for t in range(8):
                uf[t, n * 4 : n * 4 + 4, :] = part[
                    (t % 4) * 4 : (t % 4) * 4 + 4, (t // 4) * 128 : (t // 4) * 128 + 128
                ]
        ub[...] = uf[...].astype(BF16)
        vb[tp] = ub[tp]
        for k in range(1, 8):
            to = lax.rem(tp + k, 8)
            push(ub.at[to], vb.at[tp], rs_sem, rr_sem, 8 + k, (attn, grp, to))
        yield
        for k in range(1, 8):
            landed(vb.at[lax.rem(tp + 8 - k, 8)], rs_sem, rr_sem, 8 + k)
        for t in range(8):
            part = vb[t].astype(F32)
            for n in range(8):
                plane, zv = t % 2, n % 2
                bv, av = (n // 2, t // 2) if plane else (t // 2, n // 2)
                place = (((plane * 2 + zv) * 4 + bv) * 4 + av) * 4
                wf[place : place + 4, :] = part[n * 4 : n * 4 + 4]
        wt[...] = wf[...].T
        yield

    def scaling():
        for i in (1, 2, 3):
            loads[i].wait()

        def scale(i, _):
            rows = pl.ds(pl.multiple_of(i * 16, 16), 16)
            for src, dst in ((wg, wg2), (wu, wu2)):
                wide = (src[rows, :].astype(F32) * gain_ref[...]).astype(BF16)
                for cv in range(2):
                    for xv in range(4):
                        first = [xv * 1792 + (zv * 8 + yv * 2 + cv) * COLS for zv in range(2) for yv in range(4)]
                        dst[cv, rows, xv * 896 : (xv + 1) * 896] = jnp.concatenate(
                            [wide[:, f : f + COLS] for f in first], axis=1
                        )
            return 0

        for part in range(3):
            lax.fori_loop(part * 6, part * 6 + 6, scale, 0)
            yield

    push(own_b, got_b, rs_sem, rr_sem, 0, partner)
    push(d_hbm, wd.at[pl.ds(FH, FH)], rs_sem, rr_sem, 18, sibling)
    residual_steps, scaling_steps = residual(), scaling()
    next(residual_steps)
    row = lax.broadcasted_iota(jnp.int32, (128, 256), 0)
    landed(got_b, rs_sem, rr_sem, 0)
    cb[z, a] = jnp.where(jnp.where(row < 64, swaps[0], swaps[1]) == 1, got_b[...], own_b[...])

    def ready(p):
        for half in range(2):
            sf[half] = cb[zs[p], :, :, half * 128 : (half + 1) * 128].astype(F32).reshape(512, 128)
        for h in range(32):
            for half in range(2):
                first = h * 256 + half * 128
                ctx_all[(c * 2 + zs[p]) * 4 + b, :, first : first + 128] = sf[
                    half, pl.ds(h, 16, stride=32), :
                ].astype(BF16)

    steps = gather(
        lambda p, av: cb.at[zs[p], av],
        lambda p, bv: ctx_all.at[(c * 2 + zs[p]) * 4 + bv],
        lambda zv, bv: ctx_all.at[(co * 2 + zv) * 4 + bv],
        bs_sem,
        br_sem,
        ready,
    )
    next(steps)
    next(residual_steps)
    next(steps)
    next(scaling_steps)
    next(steps)
    next(residual_steps)
    next(scaling_steps)
    next(steps)
    next(scaling_steps)
    next(steps)
    next(residual_steps)
    next(steps)
    loads[4].wait()

    def project(plane):
        def step(i, acc):
            cols = pl.ds(pl.multiple_of(i * 1024, 1024), 1024)
            rows = ctx_all[pl.ds(plane * 8, 8), :, cols].reshape(128, 1024)
            return acc + lax.dot_general(wo[:, cols], rows, NT, preferred_element_type=F32)

        total = lax.fori_loop(0, CW // 1024, step, jnp.zeros((COLS, 128), F32))
        lanes = pl.ds(pl.multiple_of(plane * 128, 128), 128)
        ht[plane, me] = (wt[:COLS, lanes] + total).astype(BF16)

    def gather_hidden(i):
        half = (c, co)[i]
        return gather(
            lambda p, av: ht.at[half, ((c * 2 + zs[p]) * 4 + b) * 4 + av],
            lambda p, bv: ht.at[half, pl.ds(((c * 2 + zs[p]) * 4 + bv) * 4, 4)],
            lambda zv, bv: ht.at[(co, c)[i], pl.ds(((co * 2 + zv) * 4 + bv) * 4, 4)],
            cs_sem,
            cr_sem,
            lambda p: None,
            21 * i,
        )

    early, late = gather_hidden(0), gather_hidden(1)

    def features(plane, half, xv):
        parts = []
        for zv in range(2):
            for yv in range(4):
                bv, av = yv * (1 - plane) + xv * plane, xv * (1 - plane) + yv * plane
                parts.append(ht[half, ((plane * 2 + zv) * 4 + bv) * 4 + av])
        return jnp.concatenate(parts, axis=0)

    def expand(plane, i):
        half = (c, co)[i]

        def step(xv, total):
            cols = pl.ds(pl.multiple_of(xv * 896, 128), 896)
            part = features(plane, half, xv)
            acc_g[i] += jnp.dot(wg2[plane, :, cols], part, preferred_element_type=F32)
            acc_u[i] += jnp.dot(wu2[plane, :, cols], part, preferred_element_type=F32)
            wide = part.astype(F32)
            return total + jnp.sum((wide * wide).reshape(112, 8, 128), axis=0)

        squares[i] += lax.fori_loop(0, 4, step, jnp.zeros((8, 128), F32))

    def activate(i):
        factor = lax.rsqrt(jnp.sum(squares[i], axis=0, keepdims=True) * (1.0 / D) + 1e-5)
        gate = acc_g[i] * factor
        act = gate / (1.0 + jnp.exp(-gate)) * (acc_u[i] * factor)
        return act.T.astype(BF16)

    project(c)
    next(early)
    next(steps)
    project(co)
    next(late)
    acc_g[...] = jnp.zeros_like(acc_g)
    acc_u[...] = jnp.zeros_like(acc_u)
    squares[...] = jnp.zeros_like(squares)
    for _ in range(4):
        next(early)
        next(late)
    next(early)
    expand(c, 0)
    next(late)
    next(early)
    expand(co, 1)
    expand(c, 1)
    act_out[...] = activate(1)
    push(act_out, act_in, rs_sem, rr_sem, 19, sibling)
    next(late)
    expand(co, 0)

    act_own = activate(0)
    loads[5].wait()
    landed(wd.at[pl.ds(FH, FH)], rs_sem, rr_sem, 18)
    landed(act_in, rs_sem, rr_sem, 19)
    lhs = jnp.concatenate([act_own, act_in[...]], axis=1)

    def reduction(h):
        for j in range(2):
            cols = pl.ds(j * 1792, 1792)
            part = jnp.dot(lhs, wd[:, pl.ds(h * 3584 + j * 1792, 1792)], preferred_element_type=F32)
            p_own[h, :, :, cols] = part.astype(BF16).reshape(8, 16, 1792)

        def slab(p, k):
            return p_own.at[h, zs[p] * 4 + k]

        def send(ref, i, to):
            push(ref, r2.at[h, i], ds_sem, dr_sem, 2 + 6 * h + i, to)

        def wait(i):
            landed(r2.at[h, i], ds_sem, dr_sem, 2 + 6 * h + i)

        send(slab(0, b2), 0, b_left)
        send(slab(1, b2), 1, b_right)
        send(slab(1, b3), 3, b_left)
        send(slab(0, b1), 4, b_right)
        yield
        for i, p, k, to, j in ((0, 0, b3, b_left, 2), (1, 1, b1, b_right, 5)):
            wait(i)
            ref = slab(p, k)
            ref[...] = (ref[...].astype(F32) + r2[h, i].astype(F32)).astype(BF16)
            send(ref, j, to)
        yield
        for i in (3, 4, 2, 5):
            wait(i)
        for p in (1, 0):
            total = (
                p_own[h, zs[p] * 4 + b].astype(F32) + r2[h, 2 + p].astype(F32) + r2[h, 4 + p].astype(F32)
            )
            for av in range(4):
                for q in range(4):
                    qf[av, q * 4 : q * 4 + 4, :] = total[av * 4 : av * 4 + 4, q * 896 : (q + 1) * 896]
            qb[h, p] = qf[...].astype(BF16)
            for k in (1, 3, 2):
                push(
                    qb.at[h, p, ak[k]], r1.at[h, p, k - 1], ds_sem, dr_sem, 13 + 6 * h + 3 * p + k, a_other[k]
                )
        yield
        sums = []
        for p in (1, 0):
            total = qb[h, p, a].astype(F32)
            for k in (1, 3, 2):
                landed(r1.at[h, p, k - 1], ds_sem, dr_sem, 13 + 6 * h + 3 * p + k)
                total = total + r1[h, p, k - 1].astype(F32)
            sums.append(total)
            if p == 1:
                tz[h] = total.astype(BF16)
                push(tz.at[h], got_peer.at[h], ds_sem, dr_sem, 26 + 3 * h, z_peer)
                push(tz.at[h], got_cross.at[h], ds_sem, dr_sem, 27 + 3 * h, cross)
        tp0[h] = sums[1].astype(BF16)
        push(tp0.at[h], got_partner.at[h], ds_sem, dr_sem, 28 + 3 * h, partner)
        t0[h] = sums[1]
        yield
        landed(got_partner.at[h], ds_sem, dr_sem, 28 + 3 * h)
        landed(got_cross.at[h], ds_sem, dr_sem, 27 + 3 * h)
        landed(got_peer.at[h], ds_sem, dr_sem, 26 + 3 * h)
        stayed = hid[h].astype(F32) + (t0[h] + got_peer[h].astype(F32))
        moved = hid_got[h].astype(F32) + (got_partner[h].astype(F32) + got_cross[h].astype(F32))
        row = lax.rem(lax.broadcasted_iota(jnp.int32, (16, 896), 0), 4)
        final = jnp.where(jnp.where(row < 2, swaps[0], swaps[1]) == 1, moved, stayed)
        request = lax.broadcasted_iota(jnp.int32, (4, 896), 0)
        for q in range(4):
            rows = jnp.zeros((4, 896), F32)
            for p in range(4):
                one = jnp.broadcast_to(final[q * 4 + p : q * 4 + p + 1], (4, 896))
                rows = jnp.where(request == assign_ref[p], one, rows)
            out_ref[:, h * 3584 + q * 896 : h * 3584 + (q + 1) * 896] = rows.astype(BF16)
        yield

    def own_hidden(h):
        lane = lax.broadcasted_iota(jnp.int32, (16, 128), 1)
        sub = lax.broadcasted_iota(jnp.int32, (16, 128), 0)
        rows = jnp.zeros((16, 896), F32)
        for q in range(4):
            pick = jnp.where(lane == me_row + sub - q * 4, 1.0, 0.0)
            pick = jnp.where((sub >= q * 4) & (sub < q * 4 + 4), pick, 0.0).astype(BF16)
            xv, zv = 2 * h + q // 2, q % 2
            parts = []
            for yv in range(4):
                parts.append(ht[c, (zv * 4 + yv) * 4 + xv])
                parts.append(ht[c, ((2 + zv) * 4 + xv) * 4 + yv])
            rows = rows + lax.dot_general(
                pick, jnp.concatenate(parts, axis=0), NT, preferred_element_type=F32
            )
        hid[h] = rows.astype(BF16)
        push(hid.at[h], hid_got.at[h], rs_sem, rr_sem, 16 + h, partner)

    halves = (reduction(0), reduction(1))
    for half in halves:
        next(half)
    own_hidden(0)
    next(halves[0])
    own_hidden(1)
    next(halves[1])
    for _ in range(2):
        for half in halves:
            next(half)
    for h in range(2):
        landed(hid_got.at[h], rs_sem, rr_sem, 16 + h)
    for half in halves:
        next(half)
    for copy in started:
        copy.wait_send()


def per_device(
    queries, keys, values, lengths, resid, assign, matching, w_out, gain, gate_w, up_w, down_w
):
    smem = pl.BlockSpec(memory_space=pltpu.SMEM)
    vmem = pl.BlockSpec(memory_space=pltpu.VMEM)
    hbm = pl.BlockSpec(memory_space=pl.ANY)
    dma = pltpu.SemaphoreType.DMA
    scratch = (
        ((4, 1024, 256), BF16),
        ((4, 1024, 256), BF16),
        ((COLS, CW), BF16),
        ((FH, D), BF16),
        ((FH, D), BF16),
        ((2, FH, D // 2), BF16),
        ((2, FH, D // 2), BF16),
        ((2 * FH, D), BF16),
        ((4, D), BF16),
        ((1, D), F32),
        ((2, 128, 128), F32),
        ((128, 256), BF16),
        ((128, 256), BF16),
        ((2, 4, 128, 256), BF16),
        ((2, 512, 128), F32),
        ((16, 16, CW), BF16),
        ((2, 64, COLS, 128), BF16),
        ((2, FH, 128), F32),
        ((2, FH, 128), F32),
        ((2, 8, 128), F32),
        ((128, FH), BF16),
        ((128, FH), BF16),
        ((8, 16, 256), F32),
        ((8, 16, 256), BF16),
        ((8, 16, 256), BF16),
        ((8, 16, 256), BF16),
        ((8, 32, 128), F32),
        ((8, 32, 128), BF16),
        ((8, 32, 128), BF16),
        ((256, 128), F32),
        ((128, 256), F32),
        ((2, 8, 16, D // 2), BF16),
        ((2, 6, 16, D // 2), BF16),
        ((4, 16, 896), F32),
        ((2, 2, 4, 16, 896), BF16),
        ((2, 2, 3, 16, 896), BF16),
        ((2, 16, 896), F32),
    ) + (((2, 16, 896), BF16),) * 7
    return pl.pallas_call(
        kernel,
        out_shape=jax.ShapeDtypeStruct((4, D), BF16),
        in_specs=[smem] * 3 + [vmem] + [hbm] * 8,
        out_specs=vmem,
        scratch_shapes=[pltpu.VMEM(shape, dtype) for shape, dtype in scratch]
        + [dma((n,)) for n in (8, 6, 21, 21, 42, 42, 32, 32, 20, 20)],
        compiler_params=pltpu.CompilerParams(
            collective_id=0, has_side_effects=True, vmem_limit_bytes=60 * 1024 * 1024
        ),
    )(
        lengths, assign[0], matching[:, 0, 0], queries, resid, gain[None],
        keys, values, w_out.T, gate_w[0].T, up_w[0].T, down_w[0],
    )


def solution(mesh):
    rows = P(("attn", "grp", "tp"), None)
    cache = P(("attn", "grp", "tp"), None, None)
    placed = (
        rows,
        cache,
        cache,
        P(("attn", "grp", "tp")),
        rows,
        rows,
        P(None, "attn", "tp"),
        P(None, ("attn", "tp")),
        P(),
        P("grp", None, ("attn", "tp")),
        P("grp", None, ("attn", "tp")),
        P("grp", ("attn", "tp"), None),
    )
    return jax.shard_map(
        per_device, mesh=mesh, in_specs=placed, out_specs=rows, check_vma=False
    )
```

```python
import jax
import jax.numpy as jnp
from jax import lax
from jax.experimental import pallas as pl
from jax.experimental.pallas import tpu as pltpu
from jax.sharding import PartitionSpec as P

D = 7168
CW = 8192
FH = 288
COLS = 112
MESH = pl.DeviceIdType.MESH
F32 = jnp.float32
BF16 = jnp.bfloat16
NT = (((1,), (1,)), ((), ()))


def kernel(
    len_ref, assign_ref, match_ref, q_ref, resid_hbm, gain_hbm, k_hbm, v_hbm, wo_hbm, g_hbm, u_hbm, d_hbm,
    out_ref,
    kc, vc, wo, wg, wu, wg2, wu2, wd, resid_ref, gain_ref,
    qs, own_b, got_b, cb, sf, ctx_all, ht, acc_g, acc_u, squares, act_out, act_in,
    s1f, s1, s1_got, t1, uf, ub, vb, wf, wt,
    p_own, r2, qf, qb, r1, t0, tp0, tz, got_peer, got_partner, got_cross, hid, hid_got,
    kv_sem, w_sem, bs_sem, br_sem, cs_sem, cr_sem, ds_sem, dr_sem, rs_sem, rr_sem,
):
    attn, grp, tp = lax.axis_index("attn"), lax.axis_index("grp"), lax.axis_index("tp")
    x, z, y, c = attn // 2, lax.rem(attn, 2), tp // 2, lax.rem(tp, 2)
    zo, co = 1 - z, 1 - c
    zs = (z, zo)
    a = y * co + x * c
    b = x * co + y * c

    def dev(x_, z_, y_, c_):
        return (lax.rem(x_, 4) * 2 + z_, grp, lax.rem(y_, 4) * 2 + c_)

    a_other = [dev(x + k * c, z, y + k * co, c) for k in range(4)]
    b_right, b_left = dev(x + co, z, y + c, c), dev(x + 3 * co, z, y + 3 * c, c)
    z_peer, sibling = dev(x, zo, y, c), dev(x, z, y, co)
    partner = (attn, 1 - grp, tp)
    cross = (x * 2 + zo, 1 - grp, tp)
    ak = [lax.rem(a + k, 4) for k in range(4)]
    b1, b2, b3 = lax.rem(b + 1, 4), lax.rem(b + 2, 4), lax.rem(b + 3, 4)

    fetch = []
    for r in range(4):
        for src, dst in ((k_hbm, kc), (v_hbm, vc)):
            fetch.append(pltpu.make_async_copy(src.at[r], dst.at[r], kv_sem.at[len(fetch)]))
            fetch[-1].start()
    loads = [
        pltpu.make_async_copy(src, dst, w_sem.at[i])
        for i, (src, dst) in enumerate(
            ((resid_hbm, resid_ref), (gain_hbm, gain_ref), (g_hbm, wg), (u_hbm, wu), (wo_hbm, wo), (d_hbm, wd.at[pl.ds(0, FH)]))
        )
    ]
    for load in loads:
        load.start()

    barrier = pltpu.get_barrier_semaphore()
    others = [partner, cross]
    for k in range(1, 8):
        others.append((lax.rem(attn + k, 8), grp, tp))
        others.append((attn, grp, lax.rem(tp + k, 8)))
    for other in others:
        pl.semaphore_signal(barrier, inc=1, device_id=other, device_id_type=MESH)

    started = []

    def push(src, dst, s_sem, r_sem, i, to):
        copy = pltpu.make_async_remote_copy(
            src_ref=src, dst_ref=dst, send_sem=s_sem.at[i], recv_sem=r_sem.at[i],
            device_id=to, device_id_type=MESH,
        )
        copy.start()
        started.append(copy)

    def landed(dst, s_sem, r_sem, i):
        pltpu.make_async_remote_copy(
            src_ref=dst, dst_ref=dst, send_sem=s_sem.at[i], recv_sem=r_sem.at[i],
            device_id=sibling, device_id_type=MESH,
        ).wait_recv()

    wide_q = q_ref[...].astype(F32)
    for h in range(32):
        for half in range(2):
            first = h * 256 + half * 128
            qs[half, pl.ds(h, 4, stride=32), :] = wide_q[:, first : first + 128]
    slot = lax.broadcasted_iota(jnp.int32, (32, 1024), 1)
    swaps = (match_ref[0], match_ref[1])

    def attend(r):
        fetch[2 * r].wait()
        query = jnp.concatenate([qs[half, r * 32 : (r + 1) * 32] for half in range(2)], axis=1).astype(BF16)
        scores = lax.dot_general(query, kc[r], NT, preferred_element_type=F32) * (256 ** -0.5)
        scores = jnp.where(slot < len_ref[r], scores, -1e30)
        expo = jnp.exp(scores - jnp.max(scores, axis=-1, keepdims=True))
        probs = (expo / jnp.sum(expo, axis=-1, keepdims=True)).astype(BF16)
        fetch[2 * r + 1].wait()
        return jnp.dot(probs, vc[r], preferred_element_type=F32)

    contexts = [attend(r) for r in range(4)]
    for p in range(4):
        chosen = contexts[0]
        for r in range(1, 4):
            chosen = jnp.where(assign_ref[p] == r, contexts[r], chosen)
        own_b[p * 32 : p * 32 + 32] = chosen.astype(BF16)
    pl.semaphore_wait(barrier, 16)

    def gather(block, part, other, s_sem, r_sem, ready, base=0):
        def send(ref, i, to):
            push(ref, ref, s_sem, r_sem, base + i, to)

        def wait(ref, i):
            landed(ref, s_sem, r_sem, base + i)

        def ring_1(p):
            for k in (1, 3, 2):
                send(block(p, a), 3 * p + k, a_other[k])

        def ring_2(p):
            for k in (1, 3, 2):
                wait(block(p, ak[4 - k]), 3 * p + k)
            ready(p)
            first, second = ((7, b_right), (8, b_left)) if p == 0 else ((10, b_left), (9, b_right))
            send(part(p, b), *first)
            send(part(p, b), *second)
            send(part(p, b), 13 + p, sibling)

        ring_1(0)
        send(block(0, a), 0, z_peer)
        yield
        ring_2(0)
        wait(block(1, a), 0)
        ring_1(1)
        yield
        ring_2(1)
        yield
        wait(part(0, b3), 7)
        send(part(0, b3), 11, b_right)
        send(part(0, b3), 15, sibling)
        wait(part(0, b1), 8)
        send(part(0, b1), 16, sibling)
        yield
        wait(part(1, b1), 10)
        send(part(1, b1), 12, b_left)
        send(part(1, b1), 17, sibling)
        wait(part(1, b3), 9)
        send(part(1, b3), 18, sibling)
        yield
        wait(part(0, b2), 11)
        send(part(0, b2), 19, sibling)
        wait(part(1, b2), 12)
        send(part(1, b2), 20, sibling)
        yield
        for i, (zv, k) in enumerate(
            ((z, 0), (zo, 0), (z, 3), (z, 1), (zo, 1), (zo, 3), (z, 2), (zo, 2))
        ):
            wait(other(zv, ak[k]), 13 + i)
        yield

    me = ((c * 2 + z) * 4 + b) * 4 + a
    me_row = ((z * 4 + b) * 4 + a) * 4

    def residual():
        loads[0].wait()
        wide_r = resid_ref[...].astype(F32)
        ordered = []
        for p in range(4):
            chosen = wide_r[0:1]
            for r in range(1, 4):
                chosen = jnp.where(assign_ref[p] == r, wide_r[r : r + 1], chosen)
            ordered.append(chosen)
        ordered = jnp.concatenate(ordered, axis=0)
        s1f[...] = jnp.zeros_like(s1f)
        for n in range(8):
            for t in range(8):
                first = n * 896 + t * COLS
                s1f[n, (t % 4) * 4 : (t % 4) * 4 + 4, (t // 4) * 128 : (t // 4) * 128 + COLS] = ordered[
                    :, first : first + COLS
                ]
        s1[...] = s1f[...].astype(BF16)
        push(s1, s1_got, rs_sem, rr_sem, 1, partner)
        yield
        landed(s1_got, rs_sem, rr_sem, 1)
        row = lax.rem(lax.broadcasted_iota(jnp.int32, (8, 16, 256), 1), 4)
        served = jnp.where(jnp.where(row < 2, swaps[0], swaps[1]) == 1, s1_got[...], s1[...])
        s1_got[...] = served
        t1[attn] = s1_got[attn]
        for k in range(1, 8):
            to = lax.rem(attn + k, 8)
            push(s1_got.at[to], t1.at[attn], rs_sem, rr_sem, 1 + k, (to, grp, tp))
        yield
        for k in range(1, 8):
            landed(t1.at[lax.rem(attn + 8 - k, 8)], rs_sem, rr_sem, 1 + k)
        for n in range(8):
            part = t1[n].astype(F32)
            for t in range(8):
                uf[t, n * 4 : n * 4 + 4, :] = part[
                    (t % 4) * 4 : (t % 4) * 4 + 4, (t // 4) * 128 : (t // 4) * 128 + 128
                ]
        ub[...] = uf[...].astype(BF16)
        vb[tp] = ub[tp]
        for k in range(1, 8):
            to = lax.rem(tp + k, 8)
            push(ub.at[to], vb.at[tp], rs_sem, rr_sem, 8 + k, (attn, grp, to))
        yield
        for k in range(1, 8):
            landed(vb.at[lax.rem(tp + 8 - k, 8)], rs_sem, rr_sem, 8 + k)
        for t in range(8):
            part = vb[t].astype(F32)
            for n in range(8):
                plane, zv = t % 2, n % 2
                bv, av = (t // 2, n // 2) if plane else (n // 2, t // 2)
                place = (((plane * 2 + zv) * 4 + bv) * 4 + av) * 4
                wf[place : place + 4, :] = part[n * 4 : n * 4 + 4]
        wt[...] = wf[...].T
        yield

    def scaling():
        for i in (1, 2, 3):
            loads[i].wait()

        def scale(i, _):
            rows = pl.ds(pl.multiple_of(i * 16, 16), 16)
            for src, dst in ((wg, wg2), (wu, wu2)):
                wide = (src[rows, :].astype(F32) * gain_ref[...]).astype(BF16)
                for cv in range(2):
                    for xv in range(4):
                        first = [xv * 1792 + (zv * 8 + yv * 2 + cv) * COLS for zv in range(2) for yv in range(4)]
                        dst[cv, rows, xv * 896 : (xv + 1) * 896] = jnp.concatenate(
                            [wide[:, f : f + COLS] for f in first], axis=1
                        )
            return 0

        for part in range(3):
            lax.fori_loop(part * 6, part * 6 + 6, scale, 0)
            yield

    push(own_b, got_b, rs_sem, rr_sem, 0, partner)
    push(d_hbm, wd.at[pl.ds(FH, FH)], rs_sem, rr_sem, 18, sibling)
    residual_steps, scaling_steps = residual(), scaling()
    next(residual_steps)
    row = lax.broadcasted_iota(jnp.int32, (128, 256), 0)
    landed(got_b, rs_sem, rr_sem, 0)
    cb[z, a] = jnp.where(jnp.where(row < 64, swaps[0], swaps[1]) == 1, got_b[...], own_b[...])

    def ready(p):
        for half in range(2):
            sf[half] = cb[zs[p], :, :, half * 128 : (half + 1) * 128].astype(F32).reshape(512, 128)
        for h in range(32):
            for half in range(2):
                first = h * 256 + half * 128
                ctx_all[(c * 2 + zs[p]) * 4 + b, :, first : first + 128] = sf[
                    half, pl.ds(h, 16, stride=32), :
                ].astype(BF16)

    steps = gather(
        lambda p, av: cb.at[zs[p], av],
        lambda p, bv: ctx_all.at[(c * 2 + zs[p]) * 4 + bv],
        lambda zv, bv: ctx_all.at[(co * 2 + zv) * 4 + bv],
        bs_sem,
        br_sem,
        ready,
    )
    next(steps)
    next(residual_steps)
    next(steps)
    next(scaling_steps)
    next(steps)
    next(residual_steps)
    next(scaling_steps)
    next(steps)
    next(scaling_steps)
    next(steps)
    next(residual_steps)
    next(steps)
    loads[4].wait()

    def project(plane):
        def step(i, acc):
            cols = pl.ds(pl.multiple_of(i * 1024, 1024), 1024)
            rows = ctx_all[pl.ds(plane * 8, 8), :, cols].reshape(128, 1024)
            return acc + lax.dot_general(wo[:, cols], rows, NT, preferred_element_type=F32)

        total = lax.fori_loop(0, CW // 1024, step, jnp.zeros((COLS, 128), F32))
        lanes = pl.ds(pl.multiple_of(plane * 128, 128), 128)
        ht[plane, me] = (wt[:COLS, lanes] + total).astype(BF16)

    def gather_hidden(i):
        half = (c, co)[i]
        return gather(
            lambda p, av: ht.at[half, ((c * 2 + zs[p]) * 4 + b) * 4 + av],
            lambda p, bv: ht.at[half, pl.ds(((c * 2 + zs[p]) * 4 + bv) * 4, 4)],
            lambda zv, bv: ht.at[(co, c)[i], pl.ds(((co * 2 + zv) * 4 + bv) * 4, 4)],
            cs_sem,
            cr_sem,
            lambda p: None,
            21 * i,
        )

    early, late = gather_hidden(0), gather_hidden(1)

    def features(plane, half, xv):
        parts = []
        for zv in range(2):
            for yv in range(4):
                bv, av = xv * (1 - plane) + yv * plane, yv * (1 - plane) + xv * plane
                parts.append(ht[half, ((plane * 2 + zv) * 4 + bv) * 4 + av])
        return jnp.concatenate(parts, axis=0)

    def expand(plane, i):
        half = (c, co)[i]

        def step(xv, total):
            cols = pl.ds(pl.multiple_of(xv * 896, 128), 896)
            part = features(plane, half, xv)
            acc_g[i] += jnp.dot(wg2[plane, :, cols], part, preferred_element_type=F32)
            acc_u[i] += jnp.dot(wu2[plane, :, cols], part, preferred_element_type=F32)
            wide = part.astype(F32)
            return total + jnp.sum((wide * wide).reshape(112, 8, 128), axis=0)

        squares[i] += lax.fori_loop(0, 4, step, jnp.zeros((8, 128), F32))

    def activate(i):
        factor = lax.rsqrt(jnp.sum(squares[i], axis=0, keepdims=True) * (1.0 / D) + 1e-5)
        gate = acc_g[i] * factor
        act = gate / (1.0 + jnp.exp(-gate)) * (acc_u[i] * factor)
        return act.T.astype(BF16)

    project(c)
    next(early)
    next(steps)
    project(co)
    next(late)
    acc_g[...] = jnp.zeros_like(acc_g)
    acc_u[...] = jnp.zeros_like(acc_u)
    squares[...] = jnp.zeros_like(squares)
    for _ in range(4):
        next(early)
        next(late)
    next(early)
    expand(c, 0)
    next(late)
    next(early)
    expand(co, 1)
    expand(c, 1)
    act_out[...] = activate(1)
    push(act_out, act_in, rs_sem, rr_sem, 19, sibling)
    next(late)
    expand(co, 0)

    act_own = activate(0)
    loads[5].wait()
    landed(wd.at[pl.ds(FH, FH)], rs_sem, rr_sem, 18)
    landed(act_in, rs_sem, rr_sem, 19)
    lhs = jnp.concatenate([act_own, act_in[...]], axis=1)

    def reduction(h):
        for j in range(2):
            cols = pl.ds(j * 1792, 1792)
            part = jnp.dot(lhs, wd[:, pl.ds(h * 3584 + j * 1792, 1792)], preferred_element_type=F32)
            p_own[h, :, :, cols] = part.astype(BF16).reshape(8, 16, 1792)

        def slab(p, k):
            return p_own.at[h, zs[p] * 4 + k]

        def send(ref, i, to):
            push(ref, r2.at[h, i], ds_sem, dr_sem, 2 + 6 * h + i, to)

        def wait(i):
            landed(r2.at[h, i], ds_sem, dr_sem, 2 + 6 * h + i)

        send(slab(0, b2), 0, b_left)
        send(slab(1, b2), 1, b_right)
        send(slab(1, b3), 3, b_left)
        send(slab(0, b1), 4, b_right)
        yield
        for i, p, k, to, j in ((0, 0, b3, b_left, 2), (1, 1, b1, b_right, 5)):
            wait(i)
            ref = slab(p, k)
            ref[...] = (ref[...].astype(F32) + r2[h, i].astype(F32)).astype(BF16)
            send(ref, j, to)
        yield
        for i in (3, 4, 2, 5):
            wait(i)
        for p in (1, 0):
            total = (
                p_own[h, zs[p] * 4 + b].astype(F32) + r2[h, 2 + p].astype(F32) + r2[h, 4 + p].astype(F32)
            )
            for av in range(4):
                for q in range(4):
                    qf[av, q * 4 : q * 4 + 4, :] = total[av * 4 : av * 4 + 4, q * 896 : (q + 1) * 896]
            qb[h, p] = qf[...].astype(BF16)
            for k in (1, 3, 2):
                push(
                    qb.at[h, p, ak[k]], r1.at[h, p, k - 1], ds_sem, dr_sem, 13 + 6 * h + 3 * p + k, a_other[k]
                )
        yield
        sums = []
        for p in (1, 0):
            total = qb[h, p, a].astype(F32)
            for k in (1, 3, 2):
                landed(r1.at[h, p, k - 1], ds_sem, dr_sem, 13 + 6 * h + 3 * p + k)
                total = total + r1[h, p, k - 1].astype(F32)
            sums.append(total)
            if p == 1:
                tz[h] = total.astype(BF16)
                push(tz.at[h], got_peer.at[h], ds_sem, dr_sem, 26 + 3 * h, z_peer)
                push(tz.at[h], got_cross.at[h], ds_sem, dr_sem, 27 + 3 * h, cross)
        tp0[h] = sums[1].astype(BF16)
        push(tp0.at[h], got_partner.at[h], ds_sem, dr_sem, 28 + 3 * h, partner)
        t0[h] = sums[1]
        yield
        landed(got_partner.at[h], ds_sem, dr_sem, 28 + 3 * h)
        landed(got_cross.at[h], ds_sem, dr_sem, 27 + 3 * h)
        landed(got_peer.at[h], ds_sem, dr_sem, 26 + 3 * h)
        stayed = hid[h].astype(F32) + (t0[h] + got_peer[h].astype(F32))
        moved = hid_got[h].astype(F32) + (got_partner[h].astype(F32) + got_cross[h].astype(F32))
        row = lax.rem(lax.broadcasted_iota(jnp.int32, (16, 896), 0), 4)
        final = jnp.where(jnp.where(row < 2, swaps[0], swaps[1]) == 1, moved, stayed)
        request = lax.broadcasted_iota(jnp.int32, (4, 896), 0)
        for q in range(4):
            rows = jnp.zeros((4, 896), F32)
            for p in range(4):
                one = jnp.broadcast_to(final[q * 4 + p : q * 4 + p + 1], (4, 896))
                rows = jnp.where(request == assign_ref[p], one, rows)
            out_ref[:, h * 3584 + q * 896 : h * 3584 + (q + 1) * 896] = rows.astype(BF16)
        yield

    def own_hidden(h):
        lane = lax.broadcasted_iota(jnp.int32, (16, 128), 1)
        sub = lax.broadcasted_iota(jnp.int32, (16, 128), 0)
        rows = jnp.zeros((16, 896), F32)
        for q in range(4):
            pick = jnp.where(lane == me_row + sub - q * 4, 1.0, 0.0)
            pick = jnp.where((sub >= q * 4) & (sub < q * 4 + 4), pick, 0.0).astype(BF16)
            xv, zv = 2 * h + q // 2, q % 2
            parts = []
            for yv in range(4):
                parts.append(ht[c, (zv * 4 + xv) * 4 + yv])
                parts.append(ht[c, ((2 + zv) * 4 + yv) * 4 + xv])
            rows = rows + lax.dot_general(
                pick, jnp.concatenate(parts, axis=0), NT, preferred_element_type=F32
            )
        hid[h] = rows.astype(BF16)
        push(hid.at[h], hid_got.at[h], rs_sem, rr_sem, 16 + h, partner)

    halves = (reduction(0), reduction(1))
    for half in halves:
        next(half)
    own_hidden(0)
    next(halves[0])
    own_hidden(1)
    next(halves[1])
    for _ in range(2):
        for half in halves:
            next(half)
    for h in range(2):
        landed(hid_got.at[h], rs_sem, rr_sem, 16 + h)
    for half in halves:
        next(half)
    for copy in started:
        copy.wait_send()


def per_device(
    queries, keys, values, lengths, resid, assign, matching, w_out, gain, gate_w, up_w, down_w
):
    smem = pl.BlockSpec(memory_space=pltpu.SMEM)
    vmem = pl.BlockSpec(memory_space=pltpu.VMEM)
    hbm = pl.BlockSpec(memory_space=pl.ANY)
    dma = pltpu.SemaphoreType.DMA
    scratch = (
        ((4, 1024, 256), BF16),
        ((4, 1024, 256), BF16),
        ((COLS, CW), BF16),
        ((FH, D), BF16),
        ((FH, D), BF16),
        ((2, FH, D // 2), BF16),
        ((2, FH, D // 2), BF16),
        ((2 * FH, D), BF16),
        ((4, D), BF16),
        ((1, D), F32),
        ((2, 128, 128), F32),
        ((128, 256), BF16),
        ((128, 256), BF16),
        ((2, 4, 128, 256), BF16),
        ((2, 512, 128), F32),
        ((16, 16, CW), BF16),
        ((2, 64, COLS, 128), BF16),
        ((2, FH, 128), F32),
        ((2, FH, 128), F32),
        ((2, 8, 128), F32),
        ((128, FH), BF16),
        ((128, FH), BF16),
        ((8, 16, 256), F32),
        ((8, 16, 256), BF16),
        ((8, 16, 256), BF16),
        ((8, 16, 256), BF16),
        ((8, 32, 128), F32),
        ((8, 32, 128), BF16),
        ((8, 32, 128), BF16),
        ((256, 128), F32),
        ((128, 256), F32),
        ((2, 8, 16, D // 2), BF16),
        ((2, 6, 16, D // 2), BF16),
        ((4, 16, 896), F32),
        ((2, 2, 4, 16, 896), BF16),
        ((2, 2, 3, 16, 896), BF16),
        ((2, 16, 896), F32),
    ) + (((2, 16, 896), BF16),) * 7
    return pl.pallas_call(
        kernel,
        out_shape=jax.ShapeDtypeStruct((4, D), BF16),
        in_specs=[smem] * 3 + [vmem] + [hbm] * 8,
        out_specs=vmem,
        scratch_shapes=[pltpu.VMEM(shape, dtype) for shape, dtype in scratch]
        + [dma((n,)) for n in (8, 6, 21, 21, 42, 42, 32, 32, 20, 20)],
        compiler_params=pltpu.CompilerParams(
            collective_id=0, has_side_effects=True, vmem_limit_bytes=60 * 1024 * 1024
        ),
    )(
        lengths, assign[0], matching[:, 0, 0], queries, resid, gain[None],
        keys, values, w_out.T, gate_w[0].T, up_w[0].T, down_w[0],
    )


def solution(mesh):
    rows = P(("attn", "grp", "tp"), None)
    cache = P(("attn", "grp", "tp"), None, None)
    placed = (
        rows,
        cache,
        cache,
        P(("attn", "grp", "tp")),
        rows,
        rows,
        P(None, "attn", "tp"),
        P(None, ("attn", "tp")),
        P(),
        P("grp", None, ("attn", "tp")),
        P("grp", None, ("attn", "tp")),
        P("grp", ("attn", "tp"), None),
    )
    return jax.shard_map(
        per_device, mesh=mesh, in_specs=placed, out_specs=rows, check_vma=False
    )
```

```python
import jax
import jax.numpy as jnp
from jax import lax
from jax.experimental import pallas as pl
from jax.experimental.pallas import tpu as pltpu
from jax.sharding import PartitionSpec as P

D = 7168
CW = 8192
FH = 288
COLS = 112
MESH = pl.DeviceIdType.MESH
F32 = jnp.float32
BF16 = jnp.bfloat16
NT = (((1,), (1,)), ((), ()))


def kernel(
    len_ref, assign_ref, match_ref, q_ref, resid_hbm, gain_hbm, k_hbm, v_hbm, wo_hbm, g_hbm, u_hbm, d_hbm,
    out_ref,
    kc, vc, wo, wg, wu, wg2, wu2, wd, resid_ref, gain_ref,
    qs, own_b, got_b, ctx_raw, sf, ctx_all, ht, acc_g, acc_u, squares, act_out, act_in,
    s1f, s1, s1_got, t1, uf, ub, vb, wf, wt,
    p_own, r2, qf, qb, r1, t0, tp0, tz, got_peer, got_partner, got_cross, hid, hid_got,
    kv_sem, w_sem, bs_sem, br_sem, cs_sem, cr_sem, ds_sem, dr_sem, rs_sem, rr_sem,
):
    attn, grp, tp = lax.axis_index("attn"), lax.axis_index("grp"), lax.axis_index("tp")
    x, z, y, c = attn // 2, lax.rem(attn, 2), tp // 2, lax.rem(tp, 2)
    zo, co = 1 - z, 1 - c
    zs = (z, zo)
    a = x * co + y * c
    b = y * co + x * c

    def dev(x_, z_, y_, c_):
        return (lax.rem(x_, 4) * 2 + z_, grp, lax.rem(y_, 4) * 2 + c_)

    a_other = [dev(x + k * co, z, y + k * c, c) for k in range(4)]
    b_right, b_left = dev(x + c, z, y + co, c), dev(x + 3 * c, z, y + 3 * co, c)
    z_peer, sibling = dev(x, zo, y, c), dev(x, z, y, co)
    partner = (attn, 1 - grp, tp)
    cross = (x * 2 + zo, 1 - grp, tp)
    ak = [lax.rem(a + k, 4) for k in range(4)]
    bk = [lax.rem(b + k, 4) for k in range(4)]
    b1, b2, b3 = bk[1:]

    fetch = []
    for r in range(4):
        for src, dst in ((k_hbm, kc), (v_hbm, vc)):
            fetch.append(pltpu.make_async_copy(src.at[r], dst.at[r], kv_sem.at[len(fetch)]))
            fetch[-1].start()
    loads = [
        pltpu.make_async_copy(src, dst, w_sem.at[i])
        for i, (src, dst) in enumerate(
            ((resid_hbm, resid_ref), (gain_hbm, gain_ref), (g_hbm, wg), (u_hbm, wu), (wo_hbm, wo), (d_hbm, wd.at[pl.ds(0, FH)]))
        )
    ]
    for load in loads:
        load.start()

    barrier = pltpu.get_barrier_semaphore()
    others = [partner, cross]
    for k in range(1, 8):
        others.append((lax.rem(attn + k, 8), grp, tp))
        others.append((attn, grp, lax.rem(tp + k, 8)))
    for other in others:
        pl.semaphore_signal(barrier, inc=1, device_id=other, device_id_type=MESH)

    started = []

    def push(src, dst, s_sem, r_sem, i, to):
        copy = pltpu.make_async_remote_copy(
            src_ref=src, dst_ref=dst, send_sem=s_sem.at[i], recv_sem=r_sem.at[i],
            device_id=to, device_id_type=MESH,
        )
        copy.start()
        started.append(copy)

    def landed(dst, s_sem, r_sem, i):
        pltpu.make_async_remote_copy(
            src_ref=dst, dst_ref=dst, send_sem=s_sem.at[i], recv_sem=r_sem.at[i],
            device_id=sibling, device_id_type=MESH,
        ).wait_recv()

    wide_q = q_ref[...].astype(F32)
    for h in range(32):
        for half in range(2):
            first = h * 256 + half * 128
            qs[half, pl.ds(h, 4, stride=32), :] = wide_q[:, first : first + 128]
    slot = lax.broadcasted_iota(jnp.int32, (32, 1024), 1)
    swaps = (match_ref[0], match_ref[1])

    def attend(r):
        fetch[2 * r].wait()
        query = jnp.concatenate([qs[half, r * 32 : (r + 1) * 32] for half in range(2)], axis=1).astype(BF16)
        scores = lax.dot_general(query, kc[r], NT, preferred_element_type=F32) * (256 ** -0.5)
        scores = jnp.where(slot < len_ref[r], scores, -1e30)
        expo = jnp.exp(scores - jnp.max(scores, axis=-1, keepdims=True))
        probs = (expo / jnp.sum(expo, axis=-1, keepdims=True)).astype(BF16)
        fetch[2 * r + 1].wait()
        return jnp.dot(probs, vc[r], preferred_element_type=F32)

    contexts = [attend(r) for r in range(4)]
    for p in range(4):
        chosen = contexts[0]
        for r in range(1, 4):
            chosen = jnp.where(assign_ref[p] == r, contexts[r], chosen)
        own_b[p * 32 : p * 32 + 32] = chosen.astype(BF16)
    pl.semaphore_wait(barrier, 16)

    def gather(block, slab, other, s_sem, r_sem, base=0):
        def send(ref, i, to):
            push(ref, ref, s_sem, r_sem, base + i, to)

        def wait(ref, i):
            landed(ref, s_sem, r_sem, base + i)

        def along(p, j):
            ways = ((0, b_right), (1, b_left))
            for way, to in ways if j in (0, 3) else ways[::-1]:
                send(block(p, 0, j), 7 + (p * 4 + j) * 2 + way, to)

        def onward(p, j):
            if j in (0, 3):
                wait(block(p, 3, j), 7 + (p * 4 + j) * 2)
                send(block(p, 3, j), 23 + p * 4 + j, b_right)
            else:
                wait(block(p, 1, j), 7 + (p * 4 + j) * 2 + 1)
                send(block(p, 1, j), 23 + p * 4 + j, b_left)

        def rest(p):
            for j in (0, 3, 1, 2):
                if j in (0, 3):
                    wait(block(p, 1, j), 7 + (p * 4 + j) * 2 + 1)
                else:
                    wait(block(p, 3, j), 7 + (p * 4 + j) * 2)
            across(p, 3)
            across(p, 1)

        def across(p, k):
            send(slab(p, k), 31 + p * 4 + k, sibling)

        def first_ring(p):
            for k in (1, 3, 2):
                send(block(p, 0, 0), 3 * p + k, a_other[k])

        def arrive(p, j):
            wait(block(p, 0, j), 3 * p + 4 - j)
            along(p, j)

        send(block(0, 0, 0), 0, z_peer)
        along(0, 0)
        first_ring(0)
        yield
        arrive(0, 3)
        arrive(0, 1)
        yield
        onward(0, 0)
        wait(block(1, 0, 0), 0)
        first_ring(1)
        along(1, 0)
        arrive(0, 2)
        across(0, 0)
        yield
        onward(0, 3)
        onward(0, 1)
        yield
        onward(0, 2)
        arrive(1, 3)
        arrive(1, 1)
        onward(1, 0)
        arrive(1, 2)
        across(1, 0)
        yield
        rest(0)
        yield
        for j in (3, 1, 2):
            onward(1, j)
        rest(1)
        yield
        for p in range(2):
            for j in (0, 3, 1, 2):
                wait(block(p, 2, j), 23 + p * 4 + j)
            across(p, 2)
        yield
        for p, k in ((0, 0), (1, 0), (0, 3), (0, 1), (1, 3), (1, 1), (0, 2), (1, 2)):
            wait(other(p, k), 31 + p * 4 + k)
        yield

    me = ((c * 2 + z) * 4 + b) * 4 + a
    me_row = ((z * 4 + b) * 4 + a) * 4

    def residual():
        loads[0].wait()
        wide_r = resid_ref[...].astype(F32)
        ordered = []
        for p in range(4):
            chosen = wide_r[0:1]
            for r in range(1, 4):
                chosen = jnp.where(assign_ref[p] == r, wide_r[r : r + 1], chosen)
            ordered.append(chosen)
        ordered = jnp.concatenate(ordered, axis=0)
        s1f[...] = jnp.zeros_like(s1f)
        for n in range(8):
            for t in range(8):
                first = n * 896 + t * COLS
                s1f[n, (t % 4) * 4 : (t % 4) * 4 + 4, (t // 4) * 128 : (t // 4) * 128 + COLS] = ordered[
                    :, first : first + COLS
                ]
        s1[...] = s1f[...].astype(BF16)
        push(s1, s1_got, rs_sem, rr_sem, 1, partner)
        yield
        landed(s1_got, rs_sem, rr_sem, 1)
        row = lax.rem(lax.broadcasted_iota(jnp.int32, (8, 16, 256), 1), 4)
        served = jnp.where(jnp.where(row < 2, swaps[0], swaps[1]) == 1, s1_got[...], s1[...])
        s1_got[...] = served
        t1[attn] = s1_got[attn]
        for k in range(1, 8):
            to = lax.rem(attn + k, 8)
            push(s1_got.at[to], t1.at[attn], rs_sem, rr_sem, 1 + k, (to, grp, tp))
        yield
        for k in range(1, 8):
            landed(t1.at[lax.rem(attn + 8 - k, 8)], rs_sem, rr_sem, 1 + k)
        for n in range(8):
            part = t1[n].astype(F32)
            for t in range(8):
                uf[t, n * 4 : n * 4 + 4, :] = part[
                    (t % 4) * 4 : (t % 4) * 4 + 4, (t // 4) * 128 : (t // 4) * 128 + 128
                ]
        ub[...] = uf[...].astype(BF16)
        vb[tp] = ub[tp]
        for k in range(1, 8):
            to = lax.rem(tp + k, 8)
            push(ub.at[to], vb.at[tp], rs_sem, rr_sem, 8 + k, (attn, grp, to))
        yield
        for k in range(1, 8):
            landed(vb.at[lax.rem(tp + 8 - k, 8)], rs_sem, rr_sem, 8 + k)
        for t in range(8):
            part = vb[t].astype(F32)
            for n in range(8):
                plane, zv = t % 2, n % 2
                bv, av = (n // 2, t // 2) if plane else (t // 2, n // 2)
                place = (((plane * 2 + zv) * 4 + bv) * 4 + av) * 4
                wf[place : place + 4, :] = part[n * 4 : n * 4 + 4]
        wt[...] = wf[...].T
        yield

    def scaling():
        for i in (1, 2, 3):
            loads[i].wait()

        def scale(i, _):
            rows = pl.ds(pl.multiple_of(i * 16, 16), 16)
            for src, dst in ((wg, wg2), (wu, wu2)):
                wide = (src[rows, :].astype(F32) * gain_ref[...]).astype(BF16)
                for cv in range(2):
                    for xv in range(4):
                        first = [xv * 1792 + (zv * 8 + yv * 2 + cv) * COLS for zv in range(2) for yv in range(4)]
                        dst[cv, rows, xv * 896 : (xv + 1) * 896] = jnp.concatenate(
                            [wide[:, f : f + COLS] for f in first], axis=1
                        )
            return 0

        for part in range(3):
            lax.fori_loop(part * 6, part * 6 + 6, scale, 0)
            yield

    push(own_b, got_b, rs_sem, rr_sem, 0, partner)
    push(d_hbm, wd.at[pl.ds(FH, FH)], rs_sem, rr_sem, 18, sibling)
    residual_steps, scaling_steps = residual(), scaling()
    next(residual_steps)
    row = lax.broadcasted_iota(jnp.int32, (128, 256), 0)
    landed(got_b, rs_sem, rr_sem, 0)
    ctx_raw[(c * 2 + z) * 4 + b, a] = jnp.where(
        jnp.where(row < 64, swaps[0], swaps[1]) == 1, got_b[...], own_b[...]
    )

    def in_rows(place):
        for half in range(2):
            sf[half] = ctx_raw[place, :, :, half * 128 : (half + 1) * 128].astype(F32).reshape(512, 128)
        for h in range(32):
            for half in range(2):
                first = h * 256 + half * 128
                ctx_all[place, :, first : first + 128] = sf[half, pl.ds(h, 16, stride=32), :].astype(BF16)

    def own_rows(*spots):
        def step(i, _):
            p, k = spots[0][0], spots[0][1]
            if len(spots) > 1:
                p = jnp.where(i == 0, p, spots[1][0])
                k = jnp.where(i == 0, k, spots[1][1])
            in_rows((c * 2 + (z + p) % 2) * 4 + lax.rem(b + k, 4))
            return 0

        lax.fori_loop(0, len(spots), step, 0)

    steps = gather(
        lambda p, k, j: ctx_raw.at[(c * 2 + zs[p]) * 4 + bk[k], ak[j]],
        lambda p, k: ctx_raw.at[(c * 2 + zs[p]) * 4 + bk[k]],
        lambda p, k: ctx_raw.at[(co * 2 + zs[p]) * 4 + ak[k]],
        bs_sem,
        br_sem,
    )
    next(steps)
    next(residual_steps)
    next(steps)
    next(scaling_steps)
    next(steps)
    next(residual_steps)
    next(steps)
    next(scaling_steps)
    next(steps)
    own_rows((0, 0), (1, 0))
    next(steps)
    next(scaling_steps)
    next(residual_steps)
    own_rows((0, 3), (0, 1))
    next(steps)
    own_rows((1, 3), (1, 1))
    next(steps)
    own_rows((0, 2), (1, 2))
    loads[4].wait()

    def project(plane):
        def step(i, acc):
            cols = pl.ds(pl.multiple_of(i * 1024, 1024), 1024)
            rows = ctx_all[pl.ds(plane * 8, 8), :, cols].reshape(128, 1024)
            return acc + lax.dot_general(wo[:, cols], rows, NT, preferred_element_type=F32)

        total = lax.fori_loop(0, CW // 1024, step, jnp.zeros((COLS, 128), F32))
        lanes = pl.ds(pl.multiple_of(plane * 128, 128), 128)
        ht[plane, me] = (wt[:COLS, lanes] + total).astype(BF16)

    def gather_hidden(i):
        half = (c, co)[i]
        return gather(
            lambda p, k, j: ht.at[half, ((c * 2 + zs[p]) * 4 + bk[k]) * 4 + ak[j]],
            lambda p, k: ht.at[half, pl.ds(((c * 2 + zs[p]) * 4 + bk[k]) * 4, 4)],
            lambda p, k: ht.at[(co, c)[i], pl.ds(((co * 2 + zs[p]) * 4 + ak[k]) * 4, 4)],
            cs_sem,
            cr_sem,
            39 * i,
        )

    early, late = gather_hidden(0), gather_hidden(1)

    def features(plane, half, xv):
        parts = []
        for zv in range(2):
            for yv in range(4):
                bv, av = yv * (1 - plane) + xv * plane, xv * (1 - plane) + yv * plane
                parts.append(ht[half, ((plane * 2 + zv) * 4 + bv) * 4 + av])
        return jnp.concatenate(parts, axis=0)

    def expand(plane, i):
        half = (c, co)[i]

        def step(xv, total):
            cols = pl.ds(pl.multiple_of(xv * 896, 128), 896)
            part = features(plane, half, xv)
            acc_g[i] += jnp.dot(wg2[plane, :, cols], part, preferred_element_type=F32)
            acc_u[i] += jnp.dot(wu2[plane, :, cols], part, preferred_element_type=F32)
            wide = part.astype(F32)
            return total + jnp.sum((wide * wide).reshape(112, 8, 128), axis=0)

        squares[i] += lax.fori_loop(0, 4, step, jnp.zeros((8, 128), F32))

    def activate(i):
        factor = lax.rsqrt(jnp.sum(squares[i], axis=0, keepdims=True) * (1.0 / D) + 1e-5)
        gate = acc_g[i] * factor
        act = gate / (1.0 + jnp.exp(-gate)) * (acc_u[i] * factor)
        return act.T.astype(BF16)

    project(c)
    next(early)
    next(steps)
    lax.fori_loop(co * 8, co * 8 + 8, lambda i, _: (in_rows(i), 0)[1], 0)
    project(co)
    next(late)
    acc_g[...] = jnp.zeros_like(acc_g)
    acc_u[...] = jnp.zeros_like(acc_u)
    squares[...] = jnp.zeros_like(squares)
    for _ in range(6):
        next(early)
        next(late)
    next(early)
    expand(c, 0)
    next(late)
    next(early)
    expand(co, 1)
    expand(c, 1)
    act_out[...] = activate(1)
    push(act_out, act_in, rs_sem, rr_sem, 19, sibling)
    next(late)
    expand(co, 0)

    act_own = activate(0)
    loads[5].wait()
    landed(wd.at[pl.ds(FH, FH)], rs_sem, rr_sem, 18)
    landed(act_in, rs_sem, rr_sem, 19)
    lhs = jnp.concatenate([act_own, act_in[...]], axis=1)

    def reduction(h):
        for j in range(2):
            cols = pl.ds(j * 1792, 1792)
            part = jnp.dot(lhs, wd[:, pl.ds(h * 3584 + j * 1792, 1792)], preferred_element_type=F32)
            p_own[h, :, :, cols] = part.astype(BF16).reshape(8, 16, 1792)

        def slab(p, k):
            return p_own.at[h, zs[p] * 4 + k]

        def send(ref, i, to):
            push(ref, r2.at[h, i], ds_sem, dr_sem, 2 + 6 * h + i, to)

        def wait(i):
            landed(r2.at[h, i], ds_sem, dr_sem, 2 + 6 * h + i)

        send(slab(0, b2), 0, b_left)
        send(slab(1, b2), 1, b_right)
        send(slab(1, b3), 3, b_left)
        send(slab(0, b1), 4, b_right)
        yield
        for i, p, k, to, j in ((0, 0, b3, b_left, 2), (1, 1, b1, b_right, 5)):
            wait(i)
            ref = slab(p, k)
            ref[...] = (ref[...].astype(F32) + r2[h, i].astype(F32)).astype(BF16)
            send(ref, j, to)
        yield
        for i in (3, 4, 2, 5):
            wait(i)
        for p in (1, 0):
            total = (
                p_own[h, zs[p] * 4 + b].astype(F32) + r2[h, 2 + p].astype(F32) + r2[h, 4 + p].astype(F32)
            )
            for av in range(4):
                for q in range(4):
                    qf[av, q * 4 : q * 4 + 4, :] = total[av * 4 : av * 4 + 4, q * 896 : (q + 1) * 896]
            qb[h, p] = qf[...].astype(BF16)
            for k in (1, 3, 2):
                push(
                    qb.at[h, p, ak[k]], r1.at[h, p, k - 1], ds_sem, dr_sem, 13 + 6 * h + 3 * p + k, a_other[k]
                )
        yield
        sums = []
        for p in (1, 0):
            total = qb[h, p, a].astype(F32)
            for k in (1, 3, 2):
                landed(r1.at[h, p, k - 1], ds_sem, dr_sem, 13 + 6 * h + 3 * p + k)
                total = total + r1[h, p, k - 1].astype(F32)
            sums.append(total)
            if p == 1:
                tz[h] = total.astype(BF16)
                push(tz.at[h], got_peer.at[h], ds_sem, dr_sem, 26 + 3 * h, z_peer)
                push(tz.at[h], got_cross.at[h], ds_sem, dr_sem, 27 + 3 * h, cross)
        tp0[h] = sums[1].astype(BF16)
        push(tp0.at[h], got_partner.at[h], ds_sem, dr_sem, 28 + 3 * h, partner)
        t0[h] = sums[1]
        yield
        landed(got_partner.at[h], ds_sem, dr_sem, 28 + 3 * h)
        landed(got_cross.at[h], ds_sem, dr_sem, 27 + 3 * h)
        landed(got_peer.at[h], ds_sem, dr_sem, 26 + 3 * h)
        stayed = hid[h].astype(F32) + (t0[h] + got_peer[h].astype(F32))
        moved = hid_got[h].astype(F32) + (got_partner[h].astype(F32) + got_cross[h].astype(F32))
        row = lax.rem(lax.broadcasted_iota(jnp.int32, (16, 896), 0), 4)
        final = jnp.where(jnp.where(row < 2, swaps[0], swaps[1]) == 1, moved, stayed)
        request = lax.broadcasted_iota(jnp.int32, (4, 896), 0)
        for q in range(4):
            rows = jnp.zeros((4, 896), F32)
            for p in range(4):
                one = jnp.broadcast_to(final[q * 4 + p : q * 4 + p + 1], (4, 896))
                rows = jnp.where(request == assign_ref[p], one, rows)
            out_ref[:, h * 3584 + q * 896 : h * 3584 + (q + 1) * 896] = rows.astype(BF16)
        yield

    def own_hidden(h):
        lane = lax.broadcasted_iota(jnp.int32, (16, 128), 1)
        sub = lax.broadcasted_iota(jnp.int32, (16, 128), 0)
        rows = jnp.zeros((16, 896), F32)
        for q in range(4):
            pick = jnp.where(lane == me_row + sub - q * 4, 1.0, 0.0)
            pick = jnp.where((sub >= q * 4) & (sub < q * 4 + 4), pick, 0.0).astype(BF16)
            xv, zv = 2 * h + q // 2, q % 2
            parts = []
            for yv in range(4):
                parts.append(ht[c, (zv * 4 + yv) * 4 + xv])
                parts.append(ht[c, ((2 + zv) * 4 + xv) * 4 + yv])
            rows = rows + lax.dot_general(
                pick, jnp.concatenate(parts, axis=0), NT, preferred_element_type=F32
            )
        hid[h] = rows.astype(BF16)
        push(hid.at[h], hid_got.at[h], rs_sem, rr_sem, 16 + h, partner)

    halves = (reduction(0), reduction(1))
    for half in halves:
        next(half)
    own_hidden(0)
    next(halves[0])
    own_hidden(1)
    next(halves[1])
    for _ in range(2):
        for half in halves:
            next(half)
    for h in range(2):
        landed(hid_got.at[h], rs_sem, rr_sem, 16 + h)
    for half in halves:
        next(half)
    for copy in started:
        copy.wait_send()


def per_device(
    queries, keys, values, lengths, resid, assign, matching, w_out, gain, gate_w, up_w, down_w
):
    smem = pl.BlockSpec(memory_space=pltpu.SMEM)
    vmem = pl.BlockSpec(memory_space=pltpu.VMEM)
    hbm = pl.BlockSpec(memory_space=pl.ANY)
    dma = pltpu.SemaphoreType.DMA
    scratch = (
        ((4, 1024, 256), BF16),
        ((4, 1024, 256), BF16),
        ((COLS, CW), BF16),
        ((FH, D), BF16),
        ((FH, D), BF16),
        ((2, FH, D // 2), BF16),
        ((2, FH, D // 2), BF16),
        ((2 * FH, D), BF16),
        ((4, D), BF16),
        ((1, D), F32),
        ((2, 128, 128), F32),
        ((128, 256), BF16),
        ((128, 256), BF16),
        ((16, 4, 128, 256), BF16),
        ((2, 512, 128), F32),
        ((16, 16, CW), BF16),
        ((2, 64, COLS, 128), BF16),
        ((2, FH, 128), F32),
        ((2, FH, 128), F32),
        ((2, 8, 128), F32),
        ((128, FH), BF16),
        ((128, FH), BF16),
        ((8, 16, 256), F32),
        ((8, 16, 256), BF16),
        ((8, 16, 256), BF16),
        ((8, 16, 256), BF16),
        ((8, 32, 128), F32),
        ((8, 32, 128), BF16),
        ((8, 32, 128), BF16),
        ((256, 128), F32),
        ((128, 256), F32),
        ((2, 8, 16, D // 2), BF16),
        ((2, 6, 16, D // 2), BF16),
        ((4, 16, 896), F32),
        ((2, 2, 4, 16, 896), BF16),
        ((2, 2, 3, 16, 896), BF16),
        ((2, 16, 896), F32),
    ) + (((2, 16, 896), BF16),) * 7
    return pl.pallas_call(
        kernel,
        out_shape=jax.ShapeDtypeStruct((4, D), BF16),
        in_specs=[smem] * 3 + [vmem] + [hbm] * 8,
        out_specs=vmem,
        scratch_shapes=[pltpu.VMEM(shape, dtype) for shape, dtype in scratch]
        + [dma((n,)) for n in (8, 6, 39, 39, 78, 78, 32, 32, 20, 20)],
        compiler_params=pltpu.CompilerParams(
            collective_id=0, has_side_effects=True, vmem_limit_bytes=60 * 1024 * 1024
        ),
    )(
        lengths, assign[0], matching[:, 0, 0], queries, resid, gain[None],
        keys, values, w_out.T, gate_w[0].T, up_w[0].T, down_w[0],
    )


def solution(mesh):
    rows = P(("attn", "grp", "tp"), None)
    cache = P(("attn", "grp", "tp"), None, None)
    placed = (
        rows,
        cache,
        cache,
        P(("attn", "grp", "tp")),
        rows,
        rows,
        P(None, "attn", "tp"),
        P(None, ("attn", "tp")),
        P(),
        P("grp", None, ("attn", "tp")),
        P("grp", None, ("attn", "tp")),
        P("grp", ("attn", "tp"), None),
    )
    return jax.shard_map(
        per_device, mesh=mesh, in_specs=placed, out_specs=rows, check_vma=False
    )
```

```python
import jax
import jax.numpy as jnp
from jax import lax
from jax.experimental import pallas as pl
from jax.experimental.pallas import tpu as pltpu
from jax.sharding import PartitionSpec as P

D = 7168
CW = 8192
FH = 288
COLS = 112
MESH = pl.DeviceIdType.MESH
F32 = jnp.float32
BF16 = jnp.bfloat16
NT = (((1,), (1,)), ((), ()))


def kernel(
    len_ref, assign_ref, match_ref, q_ref, resid_hbm, gain_hbm, k_hbm, v_hbm, wo_hbm, g_hbm, u_hbm, d_hbm,
    out_ref,
    kc, vc, wo, wg, wu, wd, resid_ref, gain_ref,
    qs, own_b, got_b, ctx_raw, sf, ctx_all, ht, acc_g, acc_u, squares, act_out, act_in, proj_out, proj_in,
    s1f, s1, s1_got, t1, uf, ub, vb, wf, wt,
    p_own, r2, qf, qb, r1, t0, tp0, tz, got_peer, got_partner, got_cross, hid, hid_got,
    kv_sem, w_sem, bs_sem, br_sem, cs_sem, cr_sem, ds_sem, dr_sem, rs_sem, rr_sem,
):
    attn, grp, tp = lax.axis_index("attn"), lax.axis_index("grp"), lax.axis_index("tp")
    x, z, y, c = attn // 2, lax.rem(attn, 2), tp // 2, lax.rem(tp, 2)
    zo, co = 1 - z, 1 - c
    zs = (z, zo)
    a = x * co + y * c
    b = y * co + x * c

    def dev(x_, z_, y_, c_):
        return (lax.rem(x_, 4) * 2 + z_, grp, lax.rem(y_, 4) * 2 + c_)

    a_other = [dev(x + k * co, z, y + k * c, c) for k in range(4)]
    b_right, b_left = dev(x + c, z, y + co, c), dev(x + 3 * c, z, y + 3 * co, c)
    z_peer, sibling = dev(x, zo, y, c), dev(x, z, y, co)
    partner = (attn, 1 - grp, tp)
    cross = (x * 2 + zo, 1 - grp, tp)
    ak = [lax.rem(a + k, 4) for k in range(4)]
    bk = [lax.rem(b + k, 4) for k in range(4)]
    b1, b2, b3 = bk[1:]

    fetch = []
    for r in range(4):
        for src, dst in ((k_hbm, kc), (v_hbm, vc)):
            fetch.append(pltpu.make_async_copy(src.at[r], dst.at[r], kv_sem.at[len(fetch)]))
            fetch[-1].start()
    loads = [
        pltpu.make_async_copy(src, dst, w_sem.at[i])
        for i, (src, dst) in enumerate(
            ((resid_hbm, resid_ref), (gain_hbm, gain_ref), (g_hbm, wg), (u_hbm, wu), (wo_hbm, wo.at[pl.ds(0, COLS)]), (d_hbm, wd.at[pl.ds(0, FH)]))
        )
    ]
    for load in loads:
        load.start()

    barrier = pltpu.get_barrier_semaphore()
    others = [partner, cross]
    for k in range(1, 8):
        others.append((lax.rem(attn + k, 8), grp, tp))
        others.append((attn, grp, lax.rem(tp + k, 8)))
    for other in others:
        pl.semaphore_signal(barrier, inc=1, device_id=other, device_id_type=MESH)

    started = []

    def push(src, dst, s_sem, r_sem, i, to):
        copy = pltpu.make_async_remote_copy(
            src_ref=src, dst_ref=dst, send_sem=s_sem.at[i], recv_sem=r_sem.at[i],
            device_id=to, device_id_type=MESH,
        )
        copy.start()
        started.append(copy)

    def landed(dst, s_sem, r_sem, i):
        pltpu.make_async_remote_copy(
            src_ref=dst, dst_ref=dst, send_sem=s_sem.at[i], recv_sem=r_sem.at[i],
            device_id=sibling, device_id_type=MESH,
        ).wait_recv()

    wide_q = q_ref[...].astype(F32)
    for h in range(32):
        for half in range(2):
            first = h * 256 + half * 128
            qs[half, pl.ds(h, 4, stride=32), :] = wide_q[:, first : first + 128]
    slot = lax.broadcasted_iota(jnp.int32, (32, 1024), 1)
    swaps = (match_ref[0], match_ref[1])

    def attend(r):
        fetch[2 * r].wait()
        query = jnp.concatenate([qs[half, r * 32 : (r + 1) * 32] for half in range(2)], axis=1).astype(BF16)
        scores = lax.dot_general(query, kc[r], NT, preferred_element_type=F32) * (256 ** -0.5)
        scores = jnp.where(slot < len_ref[r], scores, -1e30)
        expo = jnp.exp(scores - jnp.max(scores, axis=-1, keepdims=True))
        probs = (expo / jnp.sum(expo, axis=-1, keepdims=True)).astype(BF16)
        fetch[2 * r + 1].wait()
        return jnp.dot(probs, vc[r], preferred_element_type=F32)

    contexts = [attend(r) for r in range(4)]
    for p in range(4):
        chosen = contexts[0]
        for r in range(1, 4):
            chosen = jnp.where(assign_ref[p] == r, contexts[r], chosen)
        own_b[p * 32 : p * 32 + 32] = chosen.astype(BF16)
    pl.semaphore_wait(barrier, 16)

    def gather(block, slab, other, s_sem, r_sem, base=0, share=True):
        def send(ref, i, to):
            push(ref, ref, s_sem, r_sem, base + i, to)

        def wait(ref, i):
            landed(ref, s_sem, r_sem, base + i)

        def along(p, j):
            ways = ((0, b_right), (1, b_left))
            for way, to in ways if j in (0, 3) else ways[::-1]:
                send(block(p, 0, j), 7 + (p * 4 + j) * 2 + way, to)

        def onward(p, j):
            if j in (0, 3):
                wait(block(p, 3, j), 7 + (p * 4 + j) * 2)
                send(block(p, 3, j), 23 + p * 4 + j, b_right)
            else:
                wait(block(p, 1, j), 7 + (p * 4 + j) * 2 + 1)
                send(block(p, 1, j), 23 + p * 4 + j, b_left)

        def rest(p):
            for j in (0, 3, 1, 2):
                if j in (0, 3):
                    wait(block(p, 1, j), 7 + (p * 4 + j) * 2 + 1)
                else:
                    wait(block(p, 3, j), 7 + (p * 4 + j) * 2)
            across(p, 3)
            across(p, 1)

        def across(p, k):
            if share:
                send(slab(p, k), 31 + p * 4 + k, sibling)

        def first_ring(p):
            for k in (1, 3, 2):
                send(block(p, 0, 0), 3 * p + k, a_other[k])

        def arrive(p, j):
            wait(block(p, 0, j), 3 * p + 4 - j)
            along(p, j)

        send(block(0, 0, 0), 0, z_peer)
        along(0, 0)
        first_ring(0)
        yield
        arrive(0, 3)
        arrive(0, 1)
        yield
        onward(0, 0)
        wait(block(1, 0, 0), 0)
        first_ring(1)
        along(1, 0)
        arrive(0, 2)
        across(0, 0)
        yield
        onward(0, 3)
        onward(0, 1)
        yield
        onward(0, 2)
        arrive(1, 3)
        arrive(1, 1)
        onward(1, 0)
        arrive(1, 2)
        across(1, 0)
        yield
        rest(0)
        yield
        for j in (3, 1, 2):
            onward(1, j)
        rest(1)
        yield
        for p in range(2):
            for j in (0, 3, 1, 2):
                wait(block(p, 2, j), 23 + p * 4 + j)
            across(p, 2)
        yield
        for p in range(2):
            for k in (0, 3, 1, 2):
                wait(other(p, k), 31 + p * 4 + k)
            yield

    me = ((c * 2 + z) * 4 + b) * 4 + a
    me_row = ((z * 4 + b) * 4 + a) * 4

    def residual():
        loads[0].wait()
        wide_r = resid_ref[...].astype(F32)
        ordered = []
        for p in range(4):
            chosen = wide_r[0:1]
            for r in range(1, 4):
                chosen = jnp.where(assign_ref[p] == r, wide_r[r : r + 1], chosen)
            ordered.append(chosen)
        ordered = jnp.concatenate(ordered, axis=0)
        s1f[...] = jnp.zeros_like(s1f)
        for n in range(8):
            for t in range(8):
                first = n * 896 + t * COLS
                s1f[n, (t % 4) * 4 : (t % 4) * 4 + 4, (t // 4) * 128 : (t // 4) * 128 + COLS] = ordered[
                    :, first : first + COLS
                ]
        s1[...] = s1f[...].astype(BF16)
        push(s1, s1_got, rs_sem, rr_sem, 1, partner)
        yield
        landed(s1_got, rs_sem, rr_sem, 1)
        row = lax.rem(lax.broadcasted_iota(jnp.int32, (8, 16, 256), 1), 4)
        served = jnp.where(jnp.where(row < 2, swaps[0], swaps[1]) == 1, s1_got[...], s1[...])
        s1_got[...] = served
        t1[attn] = s1_got[attn]
        for k in range(1, 8):
            to = lax.rem(attn + k, 8)
            push(s1_got.at[to], t1.at[attn], rs_sem, rr_sem, 1 + k, (to, grp, tp))
        yield
        for k in range(1, 8):
            landed(t1.at[lax.rem(attn + 8 - k, 8)], rs_sem, rr_sem, 1 + k)
        for n in range(8):
            part = t1[n].astype(F32)
            for t in range(8):
                uf[t, n * 4 : n * 4 + 4, :] = part[
                    (t % 4) * 4 : (t % 4) * 4 + 4, (t // 4) * 128 : (t // 4) * 128 + 128
                ]
        ub[...] = uf[...].astype(BF16)
        vb[tp] = ub[tp]
        for k in range(1, 8):
            to = lax.rem(tp + k, 8)
            push(ub.at[to], vb.at[tp], rs_sem, rr_sem, 8 + k, (attn, grp, to))
        yield
        for k in range(1, 8):
            landed(vb.at[lax.rem(tp + 8 - k, 8)], rs_sem, rr_sem, 8 + k)
        for t in range(8):
            part = vb[t].astype(F32)
            for n in range(8):
                plane, zv = t % 2, n % 2
                bv, av = (n // 2, t // 2) if plane else (t // 2, n // 2)
                place = (((plane * 2 + zv) * 4 + bv) * 4 + av) * 4
                wf[place : place + 4, :] = part[n * 4 : n * 4 + 4]
        wt[...] = wf[...].T
        yield

    def scaling():
        for i in (1, 2, 3):
            loads[i].wait()

        def scale(i, _):
            cols = pl.ds(pl.multiple_of(i * 512, 512), 512)
            by = gain_ref[:, cols]
            wg[:, cols] = (wg[:, cols].astype(F32) * by).astype(BF16)
            wu[:, cols] = (wu[:, cols].astype(F32) * by).astype(BF16)
            return 0

        for first, last in ((0, 3), (3, 6), (6, 10), (10, 14)):
            lax.fori_loop(first, last, scale, 0)
            yield

    push(own_b, got_b, rs_sem, rr_sem, 0, partner)
    push(wo_hbm, wo.at[pl.ds(COLS, COLS)], rs_sem, rr_sem, 20, sibling)
    push(d_hbm, wd.at[pl.ds(FH, FH)], rs_sem, rr_sem, 18, sibling)
    residual_steps, scaling_steps = residual(), scaling()
    next(residual_steps)
    row = lax.broadcasted_iota(jnp.int32, (128, 256), 0)
    landed(got_b, rs_sem, rr_sem, 0)
    ctx_raw[z * 4 + b, a] = jnp.where(
        jnp.where(row < 64, swaps[0], swaps[1]) == 1, got_b[...], own_b[...]
    )

    def in_rows(place):
        for half in range(2):
            sf[half] = ctx_raw[place, :, :, half * 128 : (half + 1) * 128].astype(F32).reshape(512, 128)
        for h in range(32):
            for half in range(2):
                first = h * 256 + half * 128
                ctx_all[place, :, first : first + 128] = sf[half, pl.ds(h, 16, stride=32), :].astype(BF16)

    def own_rows(*spots):
        def step(i, _):
            p, k = spots[0][0], spots[0][1]
            if len(spots) > 1:
                p = jnp.where(i == 0, p, spots[1][0])
                k = jnp.where(i == 0, k, spots[1][1])
            in_rows(lax.rem(z + p, 2) * 4 + lax.rem(b + k, 4))
            return 0

        lax.fori_loop(0, len(spots), step, 0)

    steps = gather(
        lambda p, k, j: ctx_raw.at[zs[p] * 4 + bk[k], ak[j]],
        lambda p, k: ctx_raw.at[zs[p] * 4 + bk[k]],
        None,
        bs_sem,
        br_sem,
        share=False,
    )
    next(steps)
    next(residual_steps)
    next(steps)
    next(scaling_steps)
    next(steps)
    next(residual_steps)
    next(steps)
    next(scaling_steps)
    next(steps)
    own_rows((0, 0), (1, 0))
    next(steps)
    next(scaling_steps)
    next(residual_steps)
    own_rows((0, 3), (0, 1))
    next(scaling_steps)
    next(steps)
    own_rows((1, 3), (1, 1))
    next(steps)
    own_rows((0, 2), (1, 2))
    loads[4].wait()

    def project():
        def step(i, acc):
            cols = pl.ds(pl.multiple_of(i * 1024, 1024), 1024)
            rows = ctx_all[:, :, cols].reshape(128, 1024)
            return acc + lax.dot_general(wo[:, cols], rows, NT, preferred_element_type=F32)

        return lax.fori_loop(0, CW // 1024, step, jnp.zeros((2 * COLS, 128), F32))

    def hidden_state(half, product):
        lanes = pl.ds(pl.multiple_of(half * 128, 128), 128)
        ht[half, me] = (wt[:COLS, lanes] + product).astype(BF16)

    def gather_hidden(i):
        half = (c, co)[i]
        return gather(
            lambda p, k, j: ht.at[half, ((c * 2 + zs[p]) * 4 + bk[k]) * 4 + ak[j]],
            lambda p, k: ht.at[half, pl.ds(((c * 2 + zs[p]) * 4 + bk[k]) * 4, 4)],
            lambda p, k: ht.at[(co, c)[i], pl.ds(((co * 2 + zs[p]) * 4 + ak[k]) * 4, 4)],
            cs_sem,
            cr_sem,
            39 * i,
        )

    early, late = gather_hidden(0), gather_hidden(1)

    def features(half, xv, zv):
        parts = []
        for yv in range(4):
            parts.append(ht[half, (zv * 4 + yv) * 4 + xv])
            parts.append(ht[half, ((2 + zv) * 4 + xv) * 4 + yv])
        return jnp.concatenate(parts, axis=0)

    def expand(i, p):
        half = (c, co)[i]

        def step(xv, total):
            cols = pl.ds(pl.multiple_of((xv * 2 + zs[p]) * 896, 128), 896)
            part = features(half, xv, zs[p])
            acc_g[i] += jnp.dot(wg[:, cols], part, preferred_element_type=F32)
            acc_u[i] += jnp.dot(wu[:, cols], part, preferred_element_type=F32)
            wide = part.astype(F32)
            return total + jnp.sum((wide * wide).reshape(112, 8, 128), axis=0)

        squares[i] += lax.fori_loop(0, 4, step, jnp.zeros((8, 128), F32))

    def activate(i):
        factor = lax.rsqrt(jnp.sum(squares[i], axis=0, keepdims=True) * (1.0 / D) + 1e-5)
        gate = acc_g[i] * factor
        act = gate / (1.0 + jnp.exp(-gate)) * (acc_u[i] * factor)
        return act.T.astype(BF16)

    landed(wo.at[pl.ds(COLS, COLS)], rs_sem, rr_sem, 20)
    product = project()
    hidden_state(c, product[:COLS])
    next(early)
    proj_out[...] = product[COLS:]
    push(proj_out, proj_in, rs_sem, rr_sem, 21, sibling)
    acc_g[...] = jnp.zeros_like(acc_g)
    acc_u[...] = jnp.zeros_like(acc_u)
    squares[...] = jnp.zeros_like(squares)
    next(early)
    landed(proj_in, rs_sem, rr_sem, 21)
    hidden_state(co, proj_in[...])
    next(late)
    for _ in range(6):
        next(early)
        next(late)
    next(late)
    next(early)
    expand(1, 0)
    next(early)
    expand(1, 1)
    act_out[...] = activate(1)
    push(act_out, act_in, rs_sem, rr_sem, 19, sibling)
    next(late)
    expand(0, 0)
    next(late)
    expand(0, 1)

    act_own = activate(0)
    loads[5].wait()
    landed(wd.at[pl.ds(FH, FH)], rs_sem, rr_sem, 18)
    landed(act_in, rs_sem, rr_sem, 19)
    lhs = jnp.concatenate([act_own, act_in[...]], axis=1)

    def reduction(h):
        for j in range(2):
            cols = pl.ds(j * 1792, 1792)
            part = jnp.dot(lhs, wd[:, pl.ds(h * 3584 + j * 1792, 1792)], preferred_element_type=F32)
            p_own[h, :, :, cols] = part.astype(BF16).reshape(8, 16, 1792)

        def slab(p, k):
            return p_own.at[h, zs[p] * 4 + k]

        def send(ref, i, to):
            push(ref, r2.at[h, i], ds_sem, dr_sem, 2 + 6 * h + i, to)

        def wait(i):
            landed(r2.at[h, i], ds_sem, dr_sem, 2 + 6 * h + i)

        send(slab(0, b2), 0, b_left)
        send(slab(1, b2), 1, b_right)
        send(slab(1, b3), 3, b_left)
        send(slab(0, b1), 4, b_right)
        yield
        for i, p, k, to, j in ((0, 0, b3, b_left, 2), (1, 1, b1, b_right, 5)):
            wait(i)
            ref = slab(p, k)
            ref[...] = (ref[...].astype(F32) + r2[h, i].astype(F32)).astype(BF16)
            send(ref, j, to)
        yield
        for i in (3, 4, 2, 5):
            wait(i)
        for p in (1, 0):
            total = (
                p_own[h, zs[p] * 4 + b].astype(F32) + r2[h, 2 + p].astype(F32) + r2[h, 4 + p].astype(F32)
            )
            for av in range(4):
                for q in range(4):
                    qf[av, q * 4 : q * 4 + 4, :] = total[av * 4 : av * 4 + 4, q * 896 : (q + 1) * 896]
            qb[h, p] = qf[...].astype(BF16)
            for k in (1, 3, 2):
                push(
                    qb.at[h, p, ak[k]], r1.at[h, p, k - 1], ds_sem, dr_sem, 13 + 6 * h + 3 * p + k, a_other[k]
                )
        yield
        sums = []
        for p in (1, 0):
            total = qb[h, p, a].astype(F32)
            for k in (1, 3, 2):
                landed(r1.at[h, p, k - 1], ds_sem, dr_sem, 13 + 6 * h + 3 * p + k)
                total = total + r1[h, p, k - 1].astype(F32)
            sums.append(total)
            if p == 1:
                tz[h] = total.astype(BF16)
                push(tz.at[h], got_peer.at[h], ds_sem, dr_sem, 26 + 3 * h, z_peer)
                push(tz.at[h], got_cross.at[h], ds_sem, dr_sem, 27 + 3 * h, cross)
        tp0[h] = sums[1].astype(BF16)
        push(tp0.at[h], got_partner.at[h], ds_sem, dr_sem, 28 + 3 * h, partner)
        t0[h] = sums[1]
        yield
        landed(got_partner.at[h], ds_sem, dr_sem, 28 + 3 * h)
        landed(got_cross.at[h], ds_sem, dr_sem, 27 + 3 * h)
        landed(got_peer.at[h], ds_sem, dr_sem, 26 + 3 * h)
        stayed = hid[h].astype(F32) + (t0[h] + got_peer[h].astype(F32))
        moved = hid_got[h].astype(F32) + (got_partner[h].astype(F32) + got_cross[h].astype(F32))
        row = lax.rem(lax.broadcasted_iota(jnp.int32, (16, 896), 0), 4)
        final = jnp.where(jnp.where(row < 2, swaps[0], swaps[1]) == 1, moved, stayed)
        request = lax.broadcasted_iota(jnp.int32, (4, 896), 0)
        for q in range(4):
            rows = jnp.zeros((4, 896), F32)
            for p in range(4):
                one = jnp.broadcast_to(final[q * 4 + p : q * 4 + p + 1], (4, 896))
                rows = jnp.where(request == assign_ref[p], one, rows)
            out_ref[:, h * 3584 + q * 896 : h * 3584 + (q + 1) * 896] = rows.astype(BF16)
        yield

    def own_hidden(h):
        lane = lax.broadcasted_iota(jnp.int32, (16, 128), 1)
        sub = lax.broadcasted_iota(jnp.int32, (16, 128), 0)
        rows = jnp.zeros((16, 896), F32)
        for q in range(4):
            pick = jnp.where(lane == me_row + sub - q * 4, 1.0, 0.0)
            pick = jnp.where((sub >= q * 4) & (sub < q * 4 + 4), pick, 0.0).astype(BF16)
            xv, zv = 2 * h + q // 2, q % 2
            rows = rows + lax.dot_general(pick, features(c, xv, zv), NT, preferred_element_type=F32)
        hid[h] = rows.astype(BF16)
        push(hid.at[h], hid_got.at[h], rs_sem, rr_sem, 16 + h, partner)

    halves = (reduction(0), reduction(1))
    for half in halves:
        next(half)
    own_hidden(0)
    next(halves[0])
    own_hidden(1)
    next(halves[1])
    for _ in range(2):
        for half in halves:
            next(half)
    for h in range(2):
        landed(hid_got.at[h], rs_sem, rr_sem, 16 + h)
    for half in halves:
        next(half)
    for copy in started:
        copy.wait_send()


def per_device(
    queries, keys, values, lengths, resid, assign, matching, w_out, gain, gate_w, up_w, down_w
):
    smem = pl.BlockSpec(memory_space=pltpu.SMEM)
    vmem = pl.BlockSpec(memory_space=pltpu.VMEM)
    hbm = pl.BlockSpec(memory_space=pl.ANY)
    dma = pltpu.SemaphoreType.DMA
    scratch = (
        ((4, 1024, 256), BF16),
        ((4, 1024, 256), BF16),
        ((2 * COLS, CW), BF16),
        ((FH, D), BF16),
        ((FH, D), BF16),
        ((2 * FH, D), BF16),
        ((4, D), BF16),
        ((1, D), F32),
        ((2, 128, 128), F32),
        ((128, 256), BF16),
        ((128, 256), BF16),
        ((8, 4, 128, 256), BF16),
        ((2, 512, 128), F32),
        ((8, 16, CW), BF16),
        ((2, 64, COLS, 128), BF16),
        ((2, FH, 128), F32),
        ((2, FH, 128), F32),
        ((2, 8, 128), F32),
        ((128, FH), BF16),
        ((128, FH), BF16),
        ((COLS, 128), F32),
        ((COLS, 128), F32),
        ((8, 16, 256), F32),
        ((8, 16, 256), BF16),
        ((8, 16, 256), BF16),
        ((8, 16, 256), BF16),
        ((8, 32, 128), F32),
        ((8, 32, 128), BF16),
        ((8, 32, 128), BF16),
        ((256, 128), F32),
        ((128, 256), F32),
        ((2, 8, 16, D // 2), BF16),
        ((2, 6, 16, D // 2), BF16),
        ((4, 16, 896), F32),
        ((2, 2, 4, 16, 896), BF16),
        ((2, 2, 3, 16, 896), BF16),
        ((2, 16, 896), F32),
    ) + (((2, 16, 896), BF16),) * 7
    return pl.pallas_call(
        kernel,
        out_shape=jax.ShapeDtypeStruct((4, D), BF16),
        in_specs=[smem] * 3 + [vmem] + [hbm] * 8,
        out_specs=vmem,
        scratch_shapes=[pltpu.VMEM(shape, dtype) for shape, dtype in scratch]
        + [dma((n,)) for n in (8, 6, 31, 31, 78, 78, 32, 32, 22, 22)],
        compiler_params=pltpu.CompilerParams(
            collective_id=0, has_side_effects=True, vmem_limit_bytes=60 * 1024 * 1024
        ),
    )(
        lengths, assign[0], matching[:, 0, 0], queries, resid, gain[None],
        keys, values, w_out.T, gate_w[0].T, up_w[0].T, down_w[0],
    )


def solution(mesh):
    rows = P(("attn", "grp", "tp"), None)
    cache = P(("attn", "grp", "tp"), None, None)
    placed = (
        rows,
        cache,
        cache,
        P(("attn", "grp", "tp")),
        rows,
        rows,
        P(None, "attn", "tp"),
        P(None, ("attn", "tp")),
        P(),
        P("grp", None, ("attn", "tp")),
        P("grp", None, ("attn", "tp")),
        P("grp", ("attn", "tp"), None),
    )
    return jax.shard_map(
        per_device, mesh=mesh, in_specs=placed, out_specs=rows, check_vma=False
    )
```

```python
import jax
import jax.numpy as jnp
from jax import lax
from jax.experimental import pallas as pl
from jax.experimental.pallas import tpu as pltpu
from jax.sharding import PartitionSpec as P

D = 7168
CW = 8192
FH = 288
COLS = 112
MESH = pl.DeviceIdType.MESH
F32 = jnp.float32
BF16 = jnp.bfloat16
NT = (((1,), (1,)), ((), ()))


def kernel(
    len_ref, assign_ref, match_ref, q_ref, resid_hbm, gain_hbm, k_hbm, v_hbm, wo_hbm, g_hbm, u_hbm, d_hbm,
    out_ref,
    kc, vc, wo, wg, wu, wd, resid_ref, gain_ref,
    qs, own_b, got_b, ctx_raw, sf, ctx_all, ht, acc_g, acc_u, squares, proj_out, proj_in, p_send, p_sib,
    s1f, s1, s1_got, t1, uf, ub, vb, wf, wt,
    p_own, r2, qf, qb, r1, t0, tp0, tz, got_peer, got_partner, got_cross, hid, hid_got,
    kv_sem, w_sem, bs_sem, br_sem, cs_sem, cr_sem, ds_sem, dr_sem, rs_sem, rr_sem,
):
    attn, grp, tp = lax.axis_index("attn"), lax.axis_index("grp"), lax.axis_index("tp")
    x, z, y, c = attn // 2, lax.rem(attn, 2), tp // 2, lax.rem(tp, 2)
    zo, co = 1 - z, 1 - c
    zs = (z, zo)
    a = x * co + y * c
    b = y * co + x * c

    def dev(x_, z_, y_, c_):
        return (lax.rem(x_, 4) * 2 + z_, grp, lax.rem(y_, 4) * 2 + c_)

    a_other = [dev(x + k * co, z, y + k * c, c) for k in range(4)]
    b_right, b_left = dev(x + c, z, y + co, c), dev(x + 3 * c, z, y + 3 * co, c)
    z_peer, sibling = dev(x, zo, y, c), dev(x, z, y, co)
    partner = (attn, 1 - grp, tp)
    cross = (x * 2 + zo, 1 - grp, tp)
    ak = [lax.rem(a + k, 4) for k in range(4)]
    bk = [lax.rem(b + k, 4) for k in range(4)]
    b1, b2, b3 = bk[1:]

    fetch = []
    for r in range(4):
        for src, dst in ((k_hbm, kc), (v_hbm, vc)):
            fetch.append(pltpu.make_async_copy(src.at[r], dst.at[r], kv_sem.at[len(fetch)]))
            fetch[-1].start()
    loads = [
        pltpu.make_async_copy(src, dst, w_sem.at[i])
        for i, (src, dst) in enumerate(
            ((resid_hbm, resid_ref), (gain_hbm, gain_ref), (g_hbm, wg), (u_hbm, wu), (wo_hbm, wo.at[pl.ds(0, COLS)]), (d_hbm, wd))
        )
    ]
    barrier = pltpu.get_barrier_semaphore()
    others = [partner, cross]
    for k in range(1, 8):
        others.append((lax.rem(attn + k, 8), grp, tp))
        others.append((attn, grp, lax.rem(tp + k, 8)))
    for other in others:
        pl.semaphore_signal(barrier, inc=1, device_id=other, device_id_type=MESH)

    started = []

    def push(src, dst, s_sem, r_sem, i, to):
        copy = pltpu.make_async_remote_copy(
            src_ref=src, dst_ref=dst, send_sem=s_sem.at[i], recv_sem=r_sem.at[i],
            device_id=to, device_id_type=MESH,
        )
        copy.start()
        started.append(copy)

    def landed(dst, s_sem, r_sem, i):
        pltpu.make_async_remote_copy(
            src_ref=dst, dst_ref=dst, send_sem=s_sem.at[i], recv_sem=r_sem.at[i],
            device_id=sibling, device_id_type=MESH,
        ).wait_recv()

    wide_q = q_ref[...].astype(F32)
    for h in range(32):
        for half in range(2):
            first = h * 256 + half * 128
            qs[half, pl.ds(h, 4, stride=32), :] = wide_q[:, first : first + 128]
    slot = lax.broadcasted_iota(jnp.int32, (32, 1024), 1)
    swaps = (match_ref[0], match_ref[1])

    def attend(r):
        fetch[2 * r].wait()
        query = jnp.concatenate([qs[half, r * 32 : (r + 1) * 32] for half in range(2)], axis=1).astype(BF16)
        scores = lax.dot_general(query, kc[r], NT, preferred_element_type=F32) * (256 ** -0.5)
        scores = jnp.where(slot < len_ref[r], scores, -1e30)
        expo = jnp.exp(scores - jnp.max(scores, axis=-1, keepdims=True))
        probs = (expo / jnp.sum(expo, axis=-1, keepdims=True)).astype(BF16)
        fetch[2 * r + 1].wait()
        return jnp.dot(probs, vc[r], preferred_element_type=F32)

    contexts = [attend(0)]
    for load in loads:
        load.start()
    contexts.append(attend(1))
    pl.semaphore_wait(barrier, 16)
    push(wo_hbm, wo.at[pl.ds(COLS, COLS)], rs_sem, rr_sem, 20, sibling)
    contexts.append(attend(2))
    contexts.append(attend(3))
    for p in range(4):
        chosen = contexts[0]
        for r in range(1, 4):
            chosen = jnp.where(assign_ref[p] == r, contexts[r], chosen)
        own_b[p * 32 : p * 32 + 32] = chosen.astype(BF16)

    def gather(block, slab, other, s_sem, r_sem, base=0, share=True):
        def send(ref, i, to):
            push(ref, ref, s_sem, r_sem, base + i, to)

        def wait(ref, i):
            landed(ref, s_sem, r_sem, base + i)

        def along(p, j):
            ways = ((0, b_right), (1, b_left))
            for way, to in ways if j in (0, 3) else ways[::-1]:
                send(block(p, 0, j), 7 + (p * 4 + j) * 2 + way, to)

        def onward(p, j):
            if j in (0, 3):
                wait(block(p, 3, j), 7 + (p * 4 + j) * 2)
                send(block(p, 3, j), 23 + p * 4 + j, b_right)
            else:
                wait(block(p, 1, j), 7 + (p * 4 + j) * 2 + 1)
                send(block(p, 1, j), 23 + p * 4 + j, b_left)

        def rest(p):
            for j in (0, 3, 1, 2):
                if j in (0, 3):
                    wait(block(p, 1, j), 7 + (p * 4 + j) * 2 + 1)
                else:
                    wait(block(p, 3, j), 7 + (p * 4 + j) * 2)
            across(p, 3)
            across(p, 1)

        def across(p, k):
            if share:
                send(slab(p, k), 31 + p * 4 + k, sibling)

        def first_ring(p):
            for k in (1, 3, 2):
                send(block(p, 0, 0), 3 * p + k, a_other[k])

        def arrive(p, j):
            wait(block(p, 0, j), 3 * p + 4 - j)
            along(p, j)

        send(block(0, 0, 0), 0, z_peer)
        along(0, 0)
        first_ring(0)
        yield
        arrive(0, 3)
        arrive(0, 1)
        yield
        onward(0, 0)
        wait(block(1, 0, 0), 0)
        first_ring(1)
        along(1, 0)
        arrive(0, 2)
        across(0, 0)
        yield
        onward(0, 3)
        onward(0, 1)
        yield
        onward(0, 2)
        arrive(1, 3)
        arrive(1, 1)
        onward(1, 0)
        arrive(1, 2)
        across(1, 0)
        yield
        rest(0)
        yield
        for j in (3, 1, 2):
            onward(1, j)
        rest(1)
        yield
        for p in range(2):
            for j in (0, 3, 1, 2):
                wait(block(p, 2, j), 23 + p * 4 + j)
            across(p, 2)
        yield
        for p in range(2):
            for k in (0, 3, 1, 2):
                wait(other(p, k), 31 + p * 4 + k)
            yield

    me = ((c * 2 + z) * 4 + b) * 4 + a
    me_row = ((z * 4 + b) * 4 + a) * 4

    def residual():
        loads[0].wait()
        wide_r = resid_ref[...].astype(F32)
        ordered = []
        for p in range(4):
            chosen = wide_r[0:1]
            for r in range(1, 4):
                chosen = jnp.where(assign_ref[p] == r, wide_r[r : r + 1], chosen)
            ordered.append(chosen)
        ordered = jnp.concatenate(ordered, axis=0)
        s1f[...] = jnp.zeros_like(s1f)
        for n in range(8):
            for t in range(8):
                first = n * 896 + t * COLS
                s1f[n, (t % 4) * 4 : (t % 4) * 4 + 4, (t // 4) * 128 : (t // 4) * 128 + COLS] = ordered[
                    :, first : first + COLS
                ]
        s1[...] = s1f[...].astype(BF16)
        push(s1, s1_got, rs_sem, rr_sem, 1, partner)
        yield
        landed(s1_got, rs_sem, rr_sem, 1)
        row = lax.rem(lax.broadcasted_iota(jnp.int32, (8, 16, 256), 1), 4)
        served = jnp.where(jnp.where(row < 2, swaps[0], swaps[1]) == 1, s1_got[...], s1[...])
        s1_got[...] = served
        t1[attn] = s1_got[attn]
        for k in range(1, 8):
            to = lax.rem(attn + k, 8)
            push(s1_got.at[to], t1.at[attn], rs_sem, rr_sem, 1 + k, (to, grp, tp))
        yield
        for k in range(1, 8):
            landed(t1.at[lax.rem(attn + 8 - k, 8)], rs_sem, rr_sem, 1 + k)
        for n in range(8):
            part = t1[n].astype(F32)
            for t in range(8):
                uf[t, n * 4 : n * 4 + 4, :] = part[
                    (t % 4) * 4 : (t % 4) * 4 + 4, (t // 4) * 128 : (t // 4) * 128 + 128
                ]
        ub[...] = uf[...].astype(BF16)
        vb[tp] = ub[tp]
        for k in range(1, 8):
            to = lax.rem(tp + k, 8)
            push(ub.at[to], vb.at[tp], rs_sem, rr_sem, 8 + k, (attn, grp, to))
        yield
        for k in range(1, 8):
            landed(vb.at[lax.rem(tp + 8 - k, 8)], rs_sem, rr_sem, 8 + k)
        for t in range(8):
            part = vb[t].astype(F32)
            for n in range(8):
                plane, zv = t % 2, n % 2
                bv, av = (n // 2, t // 2) if plane else (t // 2, n // 2)
                place = (((plane * 2 + zv) * 4 + bv) * 4 + av) * 4
                wf[place : place + 4, :] = part[n * 4 : n * 4 + 4]
        wt[...] = wf[...].T
        yield

    def scaling():
        for i in (1, 2, 3):
            loads[i].wait()

        def scale(i, _):
            cols = pl.ds(pl.multiple_of(i * 512, 512), 512)
            by = gain_ref[:, cols]
            wg[:, cols] = (wg[:, cols].astype(F32) * by).astype(BF16)
            wu[:, cols] = (wu[:, cols].astype(F32) * by).astype(BF16)
            return 0

        for first, last in ((0, 3), (3, 6), (6, 10), (10, 14)):
            lax.fori_loop(first, last, scale, 0)
            yield

    push(own_b, got_b, rs_sem, rr_sem, 0, partner)
    residual_steps, scaling_steps = residual(), scaling()
    next(residual_steps)
    row = lax.broadcasted_iota(jnp.int32, (128, 256), 0)
    landed(got_b, rs_sem, rr_sem, 0)
    ctx_raw[z * 4 + b, a] = jnp.where(
        jnp.where(row < 64, swaps[0], swaps[1]) == 1, got_b[...], own_b[...]
    )

    def in_rows(place):
        for half in range(2):
            sf[half] = ctx_raw[place, :, :, half * 128 : (half + 1) * 128].astype(F32).reshape(512, 128)
        for h in range(32):
            for half in range(2):
                first = h * 256 + half * 128
                ctx_all[place, :, first : first + 128] = sf[half, pl.ds(h, 16, stride=32), :].astype(BF16)

    def own_rows(*spots):
        def step(i, _):
            p, k = spots[0][0], spots[0][1]
            if len(spots) > 1:
                p = jnp.where(i == 0, p, spots[1][0])
                k = jnp.where(i == 0, k, spots[1][1])
            in_rows(lax.rem(z + p, 2) * 4 + lax.rem(b + k, 4))
            return 0

        lax.fori_loop(0, len(spots), step, 0)

    steps = gather(
        lambda p, k, j: ctx_raw.at[zs[p] * 4 + bk[k], ak[j]],
        lambda p, k: ctx_raw.at[zs[p] * 4 + bk[k]],
        None,
        bs_sem,
        br_sem,
        share=False,
    )
    next(steps)
    next(residual_steps)
    next(steps)
    next(scaling_steps)
    next(steps)
    next(residual_steps)
    next(steps)
    next(scaling_steps)
    next(steps)
    own_rows((0, 0), (1, 0))
    next(steps)
    next(scaling_steps)
    next(residual_steps)
    own_rows((0, 3), (0, 1))
    next(scaling_steps)
    next(steps)
    own_rows((1, 3), (1, 1))
    next(steps)
    own_rows((0, 2), (1, 2))
    loads[4].wait()

    def project():
        def step(i, acc):
            cols = pl.ds(pl.multiple_of(i * 1024, 1024), 1024)
            rows = ctx_all[:, :, cols].reshape(128, 1024)
            return acc + lax.dot_general(wo[:, cols], rows, NT, preferred_element_type=F32)

        return lax.fori_loop(0, CW // 1024, step, jnp.zeros((2 * COLS, 128), F32))

    def hidden_state(half, product):
        lanes = pl.ds(pl.multiple_of(half * 128, 128), 128)
        ht[half, me] = (wt[:COLS, lanes] + product).astype(BF16)

    def gather_hidden(i):
        half = (c, co)[i]
        return gather(
            lambda p, k, j: ht.at[half, ((c * 2 + zs[p]) * 4 + bk[k]) * 4 + ak[j]],
            lambda p, k: ht.at[half, pl.ds(((c * 2 + zs[p]) * 4 + bk[k]) * 4, 4)],
            lambda p, k: ht.at[(co, c)[i], pl.ds(((co * 2 + zs[p]) * 4 + ak[k]) * 4, 4)],
            cs_sem,
            cr_sem,
            39 * i,
        )

    early, late = gather_hidden(0), gather_hidden(1)

    def features(half, xv, zv):
        parts = []
        for yv in range(4):
            parts.append(ht[half, (zv * 4 + yv) * 4 + xv])
            parts.append(ht[half, ((2 + zv) * 4 + xv) * 4 + yv])
        return jnp.concatenate(parts, axis=0)

    def expand(i, p):
        half = (c, co)[i]

        def step(xv, total):
            cols = pl.ds(pl.multiple_of((xv * 2 + zs[p]) * 896, 128), 896)
            part = features(half, xv, zs[p])
            acc_g[i] += jnp.dot(wg[:, cols], part, preferred_element_type=F32)
            acc_u[i] += jnp.dot(wu[:, cols], part, preferred_element_type=F32)
            wide = part.astype(F32)
            return total + jnp.sum((wide * wide).reshape(112, 8, 128), axis=0)

        squares[i] += lax.fori_loop(0, 4, step, jnp.zeros((8, 128), F32))

    def activate(i):
        factor = lax.rsqrt(jnp.sum(squares[i], axis=0, keepdims=True) * (1.0 / D) + 1e-5)
        gate = acc_g[i] * factor
        act = gate / (1.0 + jnp.exp(-gate)) * (acc_u[i] * factor)
        return act.T.astype(BF16)

    landed(wo.at[pl.ds(COLS, COLS)], rs_sem, rr_sem, 20)
    product = project()
    hidden_state(c, product[:COLS])
    next(early)
    proj_out[...] = product[COLS:]
    push(proj_out, proj_in, rs_sem, rr_sem, 21, sibling)
    acc_g[...] = jnp.zeros_like(acc_g)
    acc_u[...] = jnp.zeros_like(acc_u)
    squares[...] = jnp.zeros_like(squares)
    next(early)
    landed(proj_in, rs_sem, rr_sem, 21)
    hidden_state(co, proj_in[...])
    next(late)
    for _ in range(6):
        next(early)
        next(late)
    next(late)
    next(early)
    expand(1, 0)
    next(early)
    expand(1, 1)
    loads[5].wait()
    act = activate(1)
    for h in range(2):
        for j in range(2):
            cols = pl.ds(j * 1792, 1792)
            part = jnp.dot(act, wd[:, pl.ds(h * 3584 + j * 1792, 1792)], preferred_element_type=F32)
            p_send[h, :, :, cols] = part.astype(BF16).reshape(8, 16, 1792)
        push(p_send.at[h], p_sib.at[h], ds_sem, dr_sem, h, sibling)
    next(late)
    expand(0, 0)
    next(late)
    expand(0, 1)

    act_own = activate(0)

    def reduction(h):
        landed(p_sib.at[h], ds_sem, dr_sem, h)
        for j in range(2):
            cols = pl.ds(j * 1792, 1792)
            part = jnp.dot(act_own, wd[:, pl.ds(h * 3584 + j * 1792, 1792)], preferred_element_type=F32)
            part = part.reshape(8, 16, 1792) + p_sib[h, :, :, cols].astype(F32)
            p_own[h, :, :, cols] = part.astype(BF16)

        def slab(p, k):
            return p_own.at[h, zs[p] * 4 + k]

        def send(ref, i, to):
            push(ref, r2.at[h, i], ds_sem, dr_sem, 2 + 6 * h + i, to)

        def wait(i):
            landed(r2.at[h, i], ds_sem, dr_sem, 2 + 6 * h + i)

        send(slab(0, b2), 0, b_left)
        send(slab(1, b2), 1, b_right)
        send(slab(1, b3), 3, b_left)
        send(slab(0, b1), 4, b_right)
        yield
        for i, p, k, to, j in ((0, 0, b3, b_left, 2), (1, 1, b1, b_right, 5)):
            wait(i)
            ref = slab(p, k)
            ref[...] = (ref[...].astype(F32) + r2[h, i].astype(F32)).astype(BF16)
            send(ref, j, to)
        yield
        for i in (3, 4, 2, 5):
            wait(i)
        for p in (1, 0):
            total = (
                p_own[h, zs[p] * 4 + b].astype(F32) + r2[h, 2 + p].astype(F32) + r2[h, 4 + p].astype(F32)
            )
            for av in range(4):
                for q in range(4):
                    qf[av, q * 4 : q * 4 + 4, :] = total[av * 4 : av * 4 + 4, q * 896 : (q + 1) * 896]
            qb[h, p] = qf[...].astype(BF16)
            for k in (1, 3, 2):
                push(
                    qb.at[h, p, ak[k]], r1.at[h, p, k - 1], ds_sem, dr_sem, 13 + 6 * h + 3 * p + k, a_other[k]
                )
        yield
        sums = []
        for p in (1, 0):
            total = qb[h, p, a].astype(F32)
            for k in (1, 3, 2):
                landed(r1.at[h, p, k - 1], ds_sem, dr_sem, 13 + 6 * h + 3 * p + k)
                total = total + r1[h, p, k - 1].astype(F32)
            sums.append(total)
            if p == 1:
                tz[h] = total.astype(BF16)
                push(tz.at[h], got_peer.at[h], ds_sem, dr_sem, 26 + 3 * h, z_peer)
                push(tz.at[h], got_cross.at[h], ds_sem, dr_sem, 27 + 3 * h, cross)
        tp0[h] = sums[1].astype(BF16)
        push(tp0.at[h], got_partner.at[h], ds_sem, dr_sem, 28 + 3 * h, partner)
        t0[h] = sums[1]
        yield
        landed(got_partner.at[h], ds_sem, dr_sem, 28 + 3 * h)
        landed(got_cross.at[h], ds_sem, dr_sem, 27 + 3 * h)
        landed(got_peer.at[h], ds_sem, dr_sem, 26 + 3 * h)
        stayed = hid[h].astype(F32) + (t0[h] + got_peer[h].astype(F32))
        moved = hid_got[h].astype(F32) + (got_partner[h].astype(F32) + got_cross[h].astype(F32))
        row = lax.rem(lax.broadcasted_iota(jnp.int32, (16, 896), 0), 4)
        final = jnp.where(jnp.where(row < 2, swaps[0], swaps[1]) == 1, moved, stayed)
        request = lax.broadcasted_iota(jnp.int32, (4, 896), 0)
        for q in range(4):
            rows = jnp.zeros((4, 896), F32)
            for p in range(4):
                one = jnp.broadcast_to(final[q * 4 + p : q * 4 + p + 1], (4, 896))
                rows = jnp.where(request == assign_ref[p], one, rows)
            out_ref[:, h * 3584 + q * 896 : h * 3584 + (q + 1) * 896] = rows.astype(BF16)
        yield

    def own_hidden(h):
        lane = lax.broadcasted_iota(jnp.int32, (16, 128), 1)
        sub = lax.broadcasted_iota(jnp.int32, (16, 128), 0)
        rows = jnp.zeros((16, 896), F32)
        for q in range(4):
            pick = jnp.where(lane == me_row + sub - q * 4, 1.0, 0.0)
            pick = jnp.where((sub >= q * 4) & (sub < q * 4 + 4), pick, 0.0).astype(BF16)
            xv, zv = 2 * h + q // 2, q % 2
            rows = rows + lax.dot_general(pick, features(c, xv, zv), NT, preferred_element_type=F32)
        hid[h] = rows.astype(BF16)
        push(hid.at[h], hid_got.at[h], rs_sem, rr_sem, 16 + h, partner)

    halves = (reduction(0), reduction(1))
    for half in halves:
        next(half)
    own_hidden(0)
    next(halves[0])
    own_hidden(1)
    next(halves[1])
    for _ in range(2):
        for half in halves:
            next(half)
    for h in range(2):
        landed(hid_got.at[h], rs_sem, rr_sem, 16 + h)
    for half in halves:
        next(half)
    for copy in started:
        copy.wait_send()


def per_device(
    queries, keys, values, lengths, resid, assign, matching, w_out, gain, gate_w, up_w, down_w
):
    smem = pl.BlockSpec(memory_space=pltpu.SMEM)
    vmem = pl.BlockSpec(memory_space=pltpu.VMEM)
    hbm = pl.BlockSpec(memory_space=pl.ANY)
    dma = pltpu.SemaphoreType.DMA
    scratch = (
        ((4, 1024, 256), BF16),
        ((4, 1024, 256), BF16),
        ((2 * COLS, CW), BF16),
        ((FH, D), BF16),
        ((FH, D), BF16),
        ((FH, D), BF16),
        ((4, D), BF16),
        ((1, D), F32),
        ((2, 128, 128), F32),
        ((128, 256), BF16),
        ((128, 256), BF16),
        ((8, 4, 128, 256), BF16),
        ((2, 512, 128), F32),
        ((8, 16, CW), BF16),
        ((2, 64, COLS, 128), BF16),
        ((2, FH, 128), F32),
        ((2, FH, 128), F32),
        ((2, 8, 128), F32),
        ((COLS, 128), F32),
        ((COLS, 128), F32),
        ((2, 8, 16, D // 2), BF16),
        ((2, 8, 16, D // 2), BF16),
        ((8, 16, 256), F32),
        ((8, 16, 256), BF16),
        ((8, 16, 256), BF16),
        ((8, 16, 256), BF16),
        ((8, 32, 128), F32),
        ((8, 32, 128), BF16),
        ((8, 32, 128), BF16),
        ((256, 128), F32),
        ((128, 256), F32),
        ((2, 8, 16, D // 2), BF16),
        ((2, 6, 16, D // 2), BF16),
        ((4, 16, 896), F32),
        ((2, 2, 4, 16, 896), BF16),
        ((2, 2, 3, 16, 896), BF16),
        ((2, 16, 896), F32),
    ) + (((2, 16, 896), BF16),) * 7
    return pl.pallas_call(
        kernel,
        out_shape=jax.ShapeDtypeStruct((4, D), BF16),
        in_specs=[smem] * 3 + [vmem] + [hbm] * 8,
        out_specs=vmem,
        scratch_shapes=[pltpu.VMEM(shape, dtype) for shape, dtype in scratch]
        + [dma((n,)) for n in (8, 6, 31, 31, 78, 78, 32, 32, 22, 22)],
        compiler_params=pltpu.CompilerParams(
            collective_id=0, has_side_effects=True, vmem_limit_bytes=60 * 1024 * 1024
        ),
    )(
        lengths, assign[0], matching[:, 0, 0], queries, resid, gain[None],
        keys, values, w_out.T, gate_w[0].T, up_w[0].T, down_w[0],
    )


def solution(mesh):
    rows = P(("attn", "grp", "tp"), None)
    cache = P(("attn", "grp", "tp"), None, None)
    placed = (
        rows,
        cache,
        cache,
        P(("attn", "grp", "tp")),
        rows,
        rows,
        P(None, "attn", "tp"),
        P(None, ("attn", "tp")),
        P(),
        P("grp", None, ("attn", "tp")),
        P("grp", None, ("attn", "tp")),
        P("grp", ("attn", "tp"), None),
    )
    return jax.shard_map(
        per_device, mesh=mesh, in_specs=placed, out_specs=rows, check_vma=False
    )
```

```python
import jax
import jax.numpy as jnp
from jax import lax
from jax.experimental import pallas as pl
from jax.experimental.pallas import tpu as pltpu
from jax.sharding import PartitionSpec as P

D = 7168
CW = 8192
FH = 288
COLS = 112
MESH = pl.DeviceIdType.MESH
F32 = jnp.float32
BF16 = jnp.bfloat16
NT = (((1,), (1,)), ((), ()))


def kernel(
    len_ref, assign_ref, match_ref, q_ref, resid_hbm, gain_hbm, k_hbm, v_hbm, wo_hbm, g_hbm, u_hbm, d_hbm,
    out_ref,
    kc, vc, wo, wg, wu, wg2, wu2, wd, resid_ref, gain_ref,
    qs, own_b, got_b, cb, sf, ctx_all, ht, acc_g, acc_u, squares, act_out, act_in,
    s1f, s1, s1_got, t1, uf, ub, vb, wf, wt, turned, lhs_f,
    p_own, r2, qf, qb, r1, t0, tp0, tz, got_peer, got_partner, got_cross, hid, hid_got,
    kv_sem, w_sem, bs_sem, br_sem, cs_sem, cr_sem, ds_sem, dr_sem, rs_sem, rr_sem,
):
    attn, grp, tp = lax.axis_index("attn"), lax.axis_index("grp"), lax.axis_index("tp")
    x, z, y, c = attn // 2, lax.rem(attn, 2), tp // 2, lax.rem(tp, 2)
    zo, co = 1 - z, 1 - c
    zs = (z, zo)
    def dev(x_, z_, y_, c_):
        return (lax.rem(x_, 4) * 2 + z_, grp, lax.rem(y_, 4) * 2 + c_)

    z_peer, sibling = dev(x, zo, y, c), dev(x, z, y, co)
    partner = (attn, 1 - grp, tp)
    cross = (x * 2 + zo, 1 - grp, tp)

    def axes(e):
        a, b = x * (1 - e) + y * e, y * (1 - e) + x * e
        return (
            [lax.rem(a + k, 4) for k in range(4)],
            [lax.rem(b + k, 4) for k in range(4)],
            [dev(x + k * (1 - e), z, y + k * e, c) for k in range(4)],
            [dev(x + k * e, z, y + k * (1 - e), c) for k in range(4)],
        )

    ways = (axes(c), axes(co))

    fetch = []
    for r in range(4):
        for src, dst in ((k_hbm, kc), (v_hbm, vc)):
            fetch.append(pltpu.make_async_copy(src.at[r], dst.at[r], kv_sem.at[len(fetch)]))
            fetch[-1].start()
    loads = [
        pltpu.make_async_copy(src, dst, w_sem.at[i])
        for i, (src, dst) in enumerate(
            ((resid_hbm, resid_ref), (gain_hbm, gain_ref), (g_hbm, wg), (u_hbm, wu), (wo_hbm, wo), (d_hbm, wd.at[pl.ds(0, FH)]))
        )
    ]
    for load in loads:
        load.start()

    barrier = pltpu.get_barrier_semaphore()
    others = [partner, cross]
    for k in range(1, 8):
        others.append((lax.rem(attn + k, 8), grp, tp))
        others.append((attn, grp, lax.rem(tp + k, 8)))
    for other in others:
        pl.semaphore_signal(barrier, inc=1, device_id=other, device_id_type=MESH)

    started = []

    def push(src, dst, s_sem, r_sem, i, to):
        copy = pltpu.make_async_remote_copy(
            src_ref=src, dst_ref=dst, send_sem=s_sem.at[i], recv_sem=r_sem.at[i],
            device_id=to, device_id_type=MESH,
        )
        copy.start()
        started.append(copy)

    def landed(dst, s_sem, r_sem, i):
        pltpu.make_async_remote_copy(
            src_ref=dst, dst_ref=dst, send_sem=s_sem.at[i], recv_sem=r_sem.at[i],
            device_id=sibling, device_id_type=MESH,
        ).wait_recv()

    wide_q = q_ref[...].astype(F32)
    for h in range(32):
        for half in range(2):
            first = h * 256 + half * 128
            qs[half, pl.ds(h, 4, stride=32), :] = wide_q[:, first : first + 128]
    slot = lax.broadcasted_iota(jnp.int32, (32, 1024), 1)
    swaps = (match_ref[0], match_ref[1])

    def attend(r):
        fetch[2 * r].wait()
        query = jnp.concatenate([qs[half, r * 32 : (r + 1) * 32] for half in range(2)], axis=1).astype(BF16)
        scores = lax.dot_general(query, kc[r], NT, preferred_element_type=F32) * (256 ** -0.5)
        scores = jnp.where(slot < len_ref[r], scores, -1e30)
        expo = jnp.exp(scores - jnp.max(scores, axis=-1, keepdims=True))
        probs = (expo / jnp.sum(expo, axis=-1, keepdims=True)).astype(BF16)
        fetch[2 * r + 1].wait()
        return jnp.dot(probs, vc[r], preferred_element_type=F32)

    contexts = [attend(r) for r in range(4)]
    for p in range(4):
        chosen = contexts[0]
        for r in range(1, 4):
            chosen = jnp.where(assign_ref[p] == r, contexts[r], chosen)
        for hh in range(2):
            own_b[hh * 64 + p * 16 : hh * 64 + p * 16 + 16] = chosen[hh * 16 : hh * 16 + 16].astype(BF16)
    pl.semaphore_wait(barrier, 16)

    def gather(way, block, part, other, s_sem, r_sem, ready, base):
        ak, bk, a_other, b_other = way
        a, (b, b1, b2, b3) = ak[0], bk
        b_right, b_left = b_other[1], b_other[3]

        def send(ref, i, to):
            push(ref, ref, s_sem, r_sem, base + i, to)

        def wait(ref, i):
            landed(ref, s_sem, r_sem, base + i)

        def ring_1(p):
            for k in (1, 3, 2):
                send(block(p, a), 3 * p + k, a_other[k])

        def ring_2(p):
            for k in (1, 3, 2):
                wait(block(p, ak[4 - k]), 3 * p + k)
            ready(p)
            first, second = ((7, b_right), (8, b_left)) if p == 0 else ((10, b_left), (9, b_right))
            send(part(p, b), *first)
            send(part(p, b), *second)
            send(part(p, b), 13 + p, sibling)

        ring_1(0)
        send(block(0, a), 0, z_peer)
        yield
        ring_2(0)
        wait(block(1, a), 0)
        ring_1(1)
        yield
        ring_2(1)
        yield
        wait(part(0, b3), 7)
        send(part(0, b3), 11, b_right)
        send(part(0, b3), 15, sibling)
        wait(part(0, b1), 8)
        send(part(0, b1), 16, sibling)
        yield
        wait(part(1, b1), 10)
        send(part(1, b1), 12, b_left)
        send(part(1, b1), 17, sibling)
        wait(part(1, b3), 9)
        send(part(1, b3), 18, sibling)
        yield
        wait(part(0, b2), 11)
        send(part(0, b2), 19, sibling)
        wait(part(1, b2), 12)
        send(part(1, b2), 20, sibling)
        yield
        for i, (zv, k) in enumerate(
            ((z, 0), (zo, 0), (z, 3), (z, 1), (zo, 1), (zo, 3), (z, 2), (zo, 2))
        ):
            wait(other(zv, ak[k]), 13 + i)
        yield

    a, b = ways[0][0][0], ways[0][1][0]
    me = (((c * 2 + z) * 4 + b) * 4 + a, ((c * 2 + z) * 4 + a) * 4 + b)
    me_row = ((z * 4 + b) * 4 + a) * 4

    def residual():
        loads[0].wait()
        wide_r = resid_ref[...].astype(F32)
        ordered = []
        for p in range(4):
            chosen = wide_r[0:1]
            for r in range(1, 4):
                chosen = jnp.where(assign_ref[p] == r, wide_r[r : r + 1], chosen)
            ordered.append(chosen)
        ordered = jnp.concatenate(ordered, axis=0)
        s1f[...] = jnp.zeros_like(s1f)
        for n in range(8):
            for t in range(8):
                first = n * 896 + t * COLS
                s1f[n, (t % 4) * 4 : (t % 4) * 4 + 4, (t // 4) * 128 : (t // 4) * 128 + COLS] = ordered[
                    :, first : first + COLS
                ]
        s1[...] = s1f[...].astype(BF16)
        push(s1, s1_got, rs_sem, rr_sem, 1, partner)
        yield
        landed(s1_got, rs_sem, rr_sem, 1)
        row = lax.rem(lax.broadcasted_iota(jnp.int32, (8, 16, 256), 1), 4)
        served = jnp.where(jnp.where(row < 2, swaps[0], swaps[1]) == 1, s1_got[...], s1[...])
        s1_got[...] = served
        t1[attn] = s1_got[attn]
        for k in range(1, 8):
            to = lax.rem(attn + k, 8)
            push(s1_got.at[to], t1.at[attn], rs_sem, rr_sem, 1 + k, (to, grp, tp))
        yield
        for k in range(1, 8):
            landed(t1.at[lax.rem(attn + 8 - k, 8)], rs_sem, rr_sem, 1 + k)
        for n in range(8):
            part = t1[n].astype(F32)
            for t in range(8):
                uf[t, n * 4 : n * 4 + 4, :] = part[
                    (t % 4) * 4 : (t % 4) * 4 + 4, (t // 4) * 128 : (t // 4) * 128 + 128
                ]
        ub[...] = uf[...].astype(BF16)
        vb[tp] = ub[tp]
        for k in range(1, 8):
            to = lax.rem(tp + k, 8)
            push(ub.at[to], vb.at[tp], rs_sem, rr_sem, 8 + k, (attn, grp, to))
        yield
        for k in range(1, 8):
            landed(vb.at[lax.rem(tp + 8 - k, 8)], rs_sem, rr_sem, 8 + k)
        for t in range(8):
            part = vb[t].astype(F32)
            for n in range(8):
                plane, zv = t % 2, n % 2
                bv, av = (n // 2, t // 2) if plane else (t // 2, n // 2)
                place = (((plane * 2 + zv) * 4 + bv) * 4 + av) * 4
                wf[place : place + 4, :] = part[n * 4 : n * 4 + 4]
        wt[...] = wf[...].T
        yield

    def scaling():
        for i in (1, 2, 3):
            loads[i].wait()

        def scale(i, _):
            rows = pl.ds(pl.multiple_of(i * 16, 16), 16)
            for src, dst in ((wg, wg2), (wu, wu2)):
                wide = (src[rows, :].astype(F32) * gain_ref[...]).astype(BF16)
                for cv in range(2):
                    for xv in range(4):
                        first = [xv * 1792 + (zv * 8 + yv * 2 + cv) * COLS for zv in range(2) for yv in range(4)]
                        dst[cv, rows, xv * 896 : (xv + 1) * 896] = jnp.concatenate(
                            [wide[:, f : f + COLS] for f in first], axis=1
                        )
            return 0

        for part in range(6):
            lax.fori_loop(part * 3, part * 3 + 3, scale, 0)
            yield

    push(own_b, got_b, rs_sem, rr_sem, 0, partner)
    push(d_hbm, wd.at[pl.ds(FH, FH)], rs_sem, rr_sem, 18, sibling)
    residual_steps, scaling_steps = residual(), scaling()
    next(residual_steps)
    row = lax.broadcasted_iota(jnp.int32, (128, 256), 0)
    landed(got_b, rs_sem, rr_sem, 0)
    served = jnp.where(jnp.where(row % 64 < 32, swaps[0], swaps[1]) == 1, got_b[...], own_b[...])
    for hh in range(2):
        cb[hh, z, ways[hh][0][0]] = served[hh * 64 : hh * 64 + 64]

    def gather_context(hh):
        way = ways[hh]

        def ready(p):
            for half in range(2):
                sf[half] = cb[hh, zs[p], :, :, half * 128 : (half + 1) * 128].astype(F32).reshape(256, 128)
            for h in range(16):
                for half in range(2):
                    first = h * 256 + half * 128
                    ctx_all[hh, (c * 2 + zs[p]) * 4 + way[1][0], :, first : first + 128] = sf[
                        half, pl.ds(h, 16, stride=16), :
                    ].astype(BF16)

        return gather(
            way,
            lambda p, av: cb.at[hh, zs[p], av],
            lambda p, bv: ctx_all.at[hh, (c * 2 + zs[p]) * 4 + bv],
            lambda zv, bv: ctx_all.at[hh, (co * 2 + zv) * 4 + bv],
            bs_sem,
            br_sem,
            ready,
            21 * hh,
        )

    steps = (gather_context(0), gather_context(1))

    def both(pair):
        for one in pair:
            next(one)

    both(steps)
    next(residual_steps)
    next(scaling_steps)
    both(steps)
    next(scaling_steps)
    both(steps)
    next(residual_steps)
    next(scaling_steps)
    both(steps)
    next(scaling_steps)
    both(steps)
    next(scaling_steps)
    next(residual_steps)
    next(scaling_steps)
    both(steps)
    loads[4].wait()

    def project(plane):
        def rows(hh, cols):
            return ctx_all[hh, pl.ds(plane * 8, 8), :, cols].reshape(128, 1024)

        def step(i, sums):
            cols = pl.ds(pl.multiple_of(i * 1024, 1024), 1024)
            last = pl.ds(pl.multiple_of(i * 1024 + CW // 2, 1024), 1024)
            one = lax.dot_general(wo[:, cols], rows(0, cols), NT, preferred_element_type=F32)
            two = lax.dot_general(rows(1, cols), wo[:, last], NT, preferred_element_type=F32)
            return sums[0] + one, sums[1] + two

        one, two = lax.fori_loop(
            0, CW // 2048, step, (jnp.zeros((COLS, 128), F32), jnp.zeros((128, COLS), F32))
        )
        for zv in range(2):
            for i in range(4):
                for j in range(4):
                    src, dst = ((zv * 4 + i) * 4 + j) * 4, ((zv * 4 + j) * 4 + i) * 4
                    turned[dst : dst + 4, :COLS] = two[src : src + 4]
        lanes = pl.ds(pl.multiple_of(plane * 128, 128), 128)
        return (wt[:COLS, lanes] + (one + turned[...].T[:COLS])).astype(BF16)

    def gather_hidden(i):
        half = (c, co)[i]
        return gather(
            ways[i],
            lambda p, av: ht.at[half, ((c * 2 + zs[p]) * 4 + ways[i][1][0]) * 4 + av],
            lambda p, bv: ht.at[half, pl.ds(((c * 2 + zs[p]) * 4 + bv) * 4, 4)],
            lambda zv, bv: ht.at[(co, c)[i], pl.ds(((co * 2 + zv) * 4 + bv) * 4, 4)],
            cs_sem,
            cr_sem,
            lambda p: None,
            21 * i,
        )

    early, late = gather_hidden(0), gather_hidden(1)

    def features(plane, half, xv):
        parts = []
        for zv in range(2):
            for yv in range(4):
                bv, av = yv * (1 - half) + xv * half, xv * (1 - half) + yv * half
                parts.append(ht[half, ((plane * 2 + zv) * 4 + bv) * 4 + av])
        return jnp.concatenate(parts, axis=0)

    def expand(plane, i):
        half = (c, co)[i]

        def step(xv, total):
            cols = pl.ds(pl.multiple_of(xv * 896, 128), 896)
            part = features(plane, half, xv)
            acc_g[i] += jnp.dot(wg2[plane, :, cols], part, preferred_element_type=F32)
            acc_u[i] += jnp.dot(wu2[plane, :, cols], part, preferred_element_type=F32)
            wide = part.astype(F32)
            return total + jnp.sum((wide * wide).reshape(112, 8, 128), axis=0)

        squares[i] += lax.fori_loop(0, 4, step, jnp.zeros((8, 128), F32))

    def activate(i):
        factor = lax.rsqrt(jnp.sum(squares[i], axis=0, keepdims=True) * (1.0 / D) + 1e-5)
        gate = acc_g[i] * factor
        act = gate / (1.0 + jnp.exp(-gate)) * (acc_u[i] * factor)
        return act.T.astype(BF16)

    ht[c, me[0]] = project(c)
    next(early)
    both(steps)
    ht[co, me[1]] = project(co)
    next(late)
    acc_g[...] = jnp.zeros_like(acc_g)
    acc_u[...] = jnp.zeros_like(acc_u)
    squares[...] = jnp.zeros_like(squares)
    for _ in range(4):
        next(early)
        next(late)
    next(early)
    expand(c, 0)
    next(late)
    next(early)
    expand(co, 1)
    expand(c, 1)
    act_out[...] = activate(1)
    push(act_out, act_in, rs_sem, rr_sem, 19, sibling)
    next(late)
    expand(co, 0)

    act_own = activate(0)
    loads[5].wait()
    landed(wd.at[pl.ds(FH, FH)], rs_sem, rr_sem, 18)
    landed(act_in, rs_sem, rr_sem, 19)
    lhs = jnp.concatenate([act_own, act_in[...]], axis=1)
    wide_lhs = lhs.astype(F32)
    for zv in range(2):
        for i in range(4):
            for j in range(4):
                src, dst = ((zv * 4 + i) * 4 + j) * 4, ((zv * 4 + j) * 4 + i) * 4
                lhs_f[dst : dst + 4, :] = wide_lhs[src : src + 4]
    lhs = (lhs, lhs_f[...].astype(BF16))

    def reduction(h):
        ak, (b, b1, b2, b3), a_other, b_other = ways[h]
        a, b_right, b_left = ak[0], b_other[1], b_other[3]
        for j in range(2):
            cols = pl.ds(j * 1792, 1792)
            part = jnp.dot(lhs[h], wd[:, pl.ds(h * 3584 + j * 1792, 1792)], preferred_element_type=F32)
            p_own[h, :, :, cols] = part.astype(BF16).reshape(8, 16, 1792)

        def slab(p, k):
            return p_own.at[h, zs[p] * 4 + k]

        def send(ref, i, to):
            push(ref, r2.at[h, i], ds_sem, dr_sem, 2 + 6 * h + i, to)

        def wait(i):
            landed(r2.at[h, i], ds_sem, dr_sem, 2 + 6 * h + i)

        send(slab(0, b2), 0, b_left)
        send(slab(1, b2), 1, b_right)
        send(slab(1, b3), 3, b_left)
        send(slab(0, b1), 4, b_right)
        yield
        for i, p, k, to, j in ((0, 0, b3, b_left, 2), (1, 1, b1, b_right, 5)):
            wait(i)
            ref = slab(p, k)
            ref[...] = (ref[...].astype(F32) + r2[h, i].astype(F32)).astype(BF16)
            send(ref, j, to)
        yield
        for i in (3, 4, 2, 5):
            wait(i)
        for p in (1, 0):
            total = (
                p_own[h, zs[p] * 4 + b].astype(F32) + r2[h, 2 + p].astype(F32) + r2[h, 4 + p].astype(F32)
            )
            for av in range(4):
                for q in range(4):
                    qf[av, q * 4 : q * 4 + 4, :] = total[av * 4 : av * 4 + 4, q * 896 : (q + 1) * 896]
            qb[h, p] = qf[...].astype(BF16)
            for k in (1, 3, 2):
                push(
                    qb.at[h, p, ak[k]], r1.at[h, p, k - 1], ds_sem, dr_sem, 13 + 6 * h + 3 * p + k, a_other[k]
                )
        yield
        sums = []
        for p in (1, 0):
            total = qb[h, p, a].astype(F32)
            for k in (1, 3, 2):
                landed(r1.at[h, p, k - 1], ds_sem, dr_sem, 13 + 6 * h + 3 * p + k)
                total = total + r1[h, p, k - 1].astype(F32)
            sums.append(total)
            if p == 1:
                tz[h] = total.astype(BF16)
                push(tz.at[h], got_peer.at[h], ds_sem, dr_sem, 26 + 3 * h, z_peer)
                push(tz.at[h], got_cross.at[h], ds_sem, dr_sem, 27 + 3 * h, cross)
        tp0[h] = sums[1].astype(BF16)
        push(tp0.at[h], got_partner.at[h], ds_sem, dr_sem, 28 + 3 * h, partner)
        t0[h] = sums[1]
        yield
        landed(got_partner.at[h], ds_sem, dr_sem, 28 + 3 * h)
        landed(got_cross.at[h], ds_sem, dr_sem, 27 + 3 * h)
        landed(got_peer.at[h], ds_sem, dr_sem, 26 + 3 * h)
        stayed = hid[h].astype(F32) + (t0[h] + got_peer[h].astype(F32))
        moved = hid_got[h].astype(F32) + (got_partner[h].astype(F32) + got_cross[h].astype(F32))
        row = lax.rem(lax.broadcasted_iota(jnp.int32, (16, 896), 0), 4)
        final = jnp.where(jnp.where(row < 2, swaps[0], swaps[1]) == 1, moved, stayed)
        request = lax.broadcasted_iota(jnp.int32, (4, 896), 0)
        for q in range(4):
            rows = jnp.zeros((4, 896), F32)
            for p in range(4):
                one = jnp.broadcast_to(final[q * 4 + p : q * 4 + p + 1], (4, 896))
                rows = jnp.where(request == assign_ref[p], one, rows)
            out_ref[:, h * 3584 + q * 896 : h * 3584 + (q + 1) * 896] = rows.astype(BF16)
        yield

    def own_hidden(h):
        lane = lax.broadcasted_iota(jnp.int32, (16, 128), 1)
        sub = lax.broadcasted_iota(jnp.int32, (16, 128), 0)
        rows = jnp.zeros((16, 896), F32)
        for q in range(4):
            pick = jnp.where(lane == me_row + sub - q * 4, 1.0, 0.0)
            pick = jnp.where((sub >= q * 4) & (sub < q * 4 + 4), pick, 0.0).astype(BF16)
            xv, zv = 2 * h + q // 2, q % 2
            parts = []
            for yv in range(4):
                for plane in range(2):
                    bv, av = yv * co + xv * c, xv * co + yv * c
                    parts.append(ht[c, ((plane * 2 + zv) * 4 + bv) * 4 + av])
            rows = rows + lax.dot_general(
                pick, jnp.concatenate(parts, axis=0), NT, preferred_element_type=F32
            )
        hid[h] = rows.astype(BF16)
        push(hid.at[h], hid_got.at[h], rs_sem, rr_sem, 16 + h, partner)

    halves = (reduction(0), reduction(1))
    for half in halves:
        next(half)
    own_hidden(0)
    next(halves[0])
    own_hidden(1)
    next(halves[1])
    for _ in range(2):
        for half in halves:
            next(half)
    for h in range(2):
        landed(hid_got.at[h], rs_sem, rr_sem, 16 + h)
    for half in halves:
        next(half)
    for copy in started:
        copy.wait_send()


def per_device(
    queries, keys, values, lengths, resid, assign, matching, w_out, gain, gate_w, up_w, down_w
):
    smem = pl.BlockSpec(memory_space=pltpu.SMEM)
    vmem = pl.BlockSpec(memory_space=pltpu.VMEM)
    hbm = pl.BlockSpec(memory_space=pl.ANY)
    dma = pltpu.SemaphoreType.DMA
    scratch = (
        ((4, 1024, 256), BF16),
        ((4, 1024, 256), BF16),
        ((COLS, CW), BF16),
        ((FH, D), BF16),
        ((FH, D), BF16),
        ((2, FH, D // 2), BF16),
        ((2, FH, D // 2), BF16),
        ((2 * FH, D), BF16),
        ((4, D), BF16),
        ((1, D), F32),
        ((2, 128, 128), F32),
        ((128, 256), BF16),
        ((128, 256), BF16),
        ((2, 2, 4, 64, 256), BF16),
        ((2, 256, 128), F32),
        ((2, 16, 16, CW // 2), BF16),
        ((2, 64, COLS, 128), BF16),
        ((2, FH, 128), F32),
        ((2, FH, 128), F32),
        ((2, 8, 128), F32),
        ((128, FH), BF16),
        ((128, FH), BF16),
        ((8, 16, 256), F32),
        ((8, 16, 256), BF16),
        ((8, 16, 256), BF16),
        ((8, 16, 256), BF16),
        ((8, 32, 128), F32),
        ((8, 32, 128), BF16),
        ((8, 32, 128), BF16),
        ((256, 128), F32),
        ((128, 256), F32),
        ((128, 128), F32),
        ((128, 2 * FH), F32),
        ((2, 8, 16, D // 2), BF16),
        ((2, 6, 16, D // 2), BF16),
        ((4, 16, 896), F32),
        ((2, 2, 4, 16, 896), BF16),
        ((2, 2, 3, 16, 896), BF16),
        ((2, 16, 896), F32),
    ) + (((2, 16, 896), BF16),) * 7
    return pl.pallas_call(
        kernel,
        out_shape=jax.ShapeDtypeStruct((4, D), BF16),
        in_specs=[smem] * 3 + [vmem] + [hbm] * 8,
        out_specs=vmem,
        scratch_shapes=[pltpu.VMEM(shape, dtype) for shape, dtype in scratch]
        + [dma((n,)) for n in (8, 6, 42, 42, 42, 42, 32, 32, 20, 20)],
        compiler_params=pltpu.CompilerParams(
            collective_id=0, has_side_effects=True, vmem_limit_bytes=60 * 1024 * 1024
        ),
    )(
        lengths, assign[0], matching[:, 0, 0], queries, resid, gain[None],
        keys, values, w_out.T, gate_w[0].T, up_w[0].T, down_w[0],
    )


def solution(mesh):
    rows = P(("attn", "grp", "tp"), None)
    cache = P(("attn", "grp", "tp"), None, None)
    placed = (
        rows,
        cache,
        cache,
        P(("attn", "grp", "tp")),
        rows,
        rows,
        P(None, "attn", "tp"),
        P(None, ("attn", "tp")),
        P(),
        P("grp", None, ("attn", "tp")),
        P("grp", None, ("attn", "tp")),
        P("grp", ("attn", "tp"), None),
    )
    return jax.shard_map(
        per_device, mesh=mesh, in_specs=placed, out_specs=rows, check_vma=False
    )
```

```python
import jax
import jax.numpy as jnp
from jax import lax
from jax.experimental import pallas as pl
from jax.experimental.pallas import tpu as pltpu
from jax.sharding import PartitionSpec as P

D = 7168
CW = 8192
FH = 288
COLS = 112
MESH = pl.DeviceIdType.MESH
F32 = jnp.float32
BF16 = jnp.bfloat16
NT = (((1,), (1,)), ((), ()))


def kernel(
    len_ref, assign_ref, match_ref, q_hbm, resid_hbm, gain_hbm, k_hbm, v_hbm, wo_hbm, g_hbm, u_hbm, d_hbm,
    out_ref,
    q_ref, kc, vc, wo, wg, wu, wg2, wu2, wd, resid_ref, gain_ref,
    qs, own_b, got_b, cb, sf, ctx_all, ht, acc_g, acc_u, squares, act_out, act_in,
    s1f, s1, s1_got, t1, uf, ub, vb, wf, wt, turned, lhs_f,
    p_own, r2, qf, qb, r1, t0, tp0, tz, got_peer, got_partner, got_cross, hid, hid_got,
    kv_sem, w_sem, bs_sem, br_sem, cs_sem, cr_sem, ds_sem, dr_sem, rs_sem, rr_sem,
):
    attn, grp, tp = lax.axis_index("attn"), lax.axis_index("grp"), lax.axis_index("tp")
    x, z, y, c = attn // 2, lax.rem(attn, 2), tp // 2, lax.rem(tp, 2)
    zo, co = 1 - z, 1 - c
    zs = (z, zo)
    def dev(x_, z_, y_, c_):
        return (lax.rem(x_, 4) * 2 + z_, grp, lax.rem(y_, 4) * 2 + c_)

    z_peer, sibling = dev(x, zo, y, c), dev(x, z, y, co)
    partner = (attn, 1 - grp, tp)
    cross = (x * 2 + zo, 1 - grp, tp)

    def axes(e):
        a, b = x * (1 - e) + y * e, y * (1 - e) + x * e
        return (
            [lax.rem(a + k, 4) for k in range(4)],
            [lax.rem(b + k, 4) for k in range(4)],
            [dev(x + k * (1 - e), z, y + k * e, c) for k in range(4)],
            [dev(x + k * e, z, y + k * (1 - e), c) for k in range(4)],
        )

    ways = (axes(c), axes(co))

    q_load = pltpu.make_async_copy(q_hbm, q_ref, w_sem.at[6])
    q_load.start()
    fetch = []
    for r in range(4):
        for src, dst in ((k_hbm, kc), (v_hbm, vc)):
            fetch.append(pltpu.make_async_copy(src.at[r], dst.at[r], kv_sem.at[len(fetch)]))
            fetch[-1].start()
    loads = [
        pltpu.make_async_copy(src, dst, w_sem.at[i])
        for i, (src, dst) in enumerate(
            ((resid_hbm, resid_ref), (gain_hbm, gain_ref), (g_hbm, wg), (u_hbm, wu), (wo_hbm, wo), (d_hbm, wd.at[pl.ds(0, FH)]))
        )
    ]
    barrier = pltpu.get_barrier_semaphore()
    others = [partner, cross]
    for k in range(1, 8):
        others.append((lax.rem(attn + k, 8), grp, tp))
        others.append((attn, grp, lax.rem(tp + k, 8)))
    for other in others:
        pl.semaphore_signal(barrier, inc=1, device_id=other, device_id_type=MESH)

    started = []

    def drain(keep=0):
        while len(started) > keep:
            started.pop(0).wait_send()

    def push(src, dst, s_sem, r_sem, i, to):
        copy = pltpu.make_async_remote_copy(
            src_ref=src, dst_ref=dst, send_sem=s_sem.at[i], recv_sem=r_sem.at[i],
            device_id=to, device_id_type=MESH,
        )
        copy.start()
        started.append(copy)

    def landed(dst, s_sem, r_sem, i):
        pltpu.make_async_remote_copy(
            src_ref=dst, dst_ref=dst, send_sem=s_sem.at[i], recv_sem=r_sem.at[i],
            device_id=sibling, device_id_type=MESH,
        ).wait_recv()

    q_load.wait()
    wide_q = q_ref[...].astype(F32)
    for h in range(32):
        for half in range(2):
            first = h * 256 + half * 128
            qs[half, pl.ds(h, 4, stride=32), :] = wide_q[:, first : first + 128]
    slot = lax.broadcasted_iota(jnp.int32, (32, 1024), 1)
    swaps = (match_ref[0], match_ref[1])

    def attend(r):
        fetch[2 * r].wait()
        query = jnp.concatenate([qs[half, r * 32 : (r + 1) * 32] for half in range(2)], axis=1).astype(BF16)
        scores = lax.dot_general(query, kc[r], NT, preferred_element_type=F32) * (256 ** -0.5)
        scores = jnp.where(slot < len_ref[r], scores, -1e30)
        expo = jnp.exp(scores - jnp.max(scores, axis=-1, keepdims=True))
        probs = (expo / jnp.sum(expo, axis=-1, keepdims=True)).astype(BF16)
        fetch[2 * r + 1].wait()
        return jnp.dot(probs, vc[r], preferred_element_type=F32)

    contexts = [attend(0)]
    for load in loads:
        load.start()
    contexts += [attend(r) for r in range(1, 4)]
    for p in range(4):
        chosen = contexts[0]
        for r in range(1, 4):
            chosen = jnp.where(assign_ref[p] == r, contexts[r], chosen)
        for hh in range(2):
            own_b[hh, p * 16 : p * 16 + 16] = chosen[hh * 16 : hh * 16 + 16].astype(BF16)
    pl.semaphore_wait(barrier, 16)

    def gather(way, block, part, other, s_sem, r_sem, ready, base):
        ak, bk, a_other, b_other = way
        a, (b, b1, b2, b3) = ak[0], bk
        b_right, b_left = b_other[1], b_other[3]

        def send(ref, i, to):
            push(ref, ref, s_sem, r_sem, base + i, to)

        def wait(ref, i):
            landed(ref, s_sem, r_sem, base + i)

        def ring_1(p):
            for k in (1, 3, 2):
                send(block(p, a), 3 * p + k, a_other[k])

        def ring_2(p):
            for k in (1, 3, 2):
                wait(block(p, ak[4 - k]), 3 * p + k)
            ready(p)
            first, second = ((7, b_right), (8, b_left)) if p == 0 else ((10, b_left), (9, b_right))
            send(part(p, b), *first)
            send(part(p, b), *second)
            send(part(p, b), 13 + p, sibling)

        send(block(0, a), 0, z_peer)
        ring_1(0)
        yield
        ring_2(0)
        wait(block(1, a), 0)
        ring_1(1)
        yield
        ring_2(1)
        yield
        wait(part(0, b3), 7)
        send(part(0, b3), 11, b_right)
        send(part(0, b3), 15, sibling)
        wait(part(0, b1), 8)
        send(part(0, b1), 16, sibling)
        yield
        wait(part(1, b1), 10)
        send(part(1, b1), 12, b_left)
        send(part(1, b1), 17, sibling)
        wait(part(1, b3), 9)
        send(part(1, b3), 18, sibling)
        yield
        wait(part(0, b2), 11)
        send(part(0, b2), 19, sibling)
        wait(part(1, b2), 12)
        send(part(1, b2), 20, sibling)
        yield
        for i, (zv, k) in enumerate(
            ((z, 0), (zo, 0), (z, 3), (z, 1), (zo, 1), (zo, 3), (z, 2), (zo, 2))
        ):
            wait(other(zv, ak[k]), 13 + i)
        yield

    a, b = ways[0][0][0], ways[0][1][0]
    me = (((c * 2 + z) * 4 + b) * 4 + a, ((c * 2 + z) * 4 + a) * 4 + b)
    me_row = ((z * 4 + b) * 4 + a) * 4

    def residual():
        loads[0].wait()
        wide_r = resid_ref[...].astype(F32)
        ordered = []
        for p in range(4):
            chosen = wide_r[0:1]
            for r in range(1, 4):
                chosen = jnp.where(assign_ref[p] == r, wide_r[r : r + 1], chosen)
            ordered.append(chosen)
        ordered = jnp.concatenate(ordered, axis=0)
        s1f[...] = jnp.zeros_like(s1f)
        for n in range(8):
            for t in range(8):
                first = n * 896 + t * COLS
                s1f[n, (t % 4) * 4 : (t % 4) * 4 + 4, (t // 4) * 128 : (t // 4) * 128 + COLS] = ordered[
                    :, first : first + COLS
                ]
        s1[...] = s1f[...].astype(BF16)
        push(s1, s1_got, rs_sem, rr_sem, 1, partner)
        yield
        landed(s1_got, rs_sem, rr_sem, 1)
        row = lax.rem(lax.broadcasted_iota(jnp.int32, (8, 16, 256), 1), 4)
        served = jnp.where(jnp.where(row < 2, swaps[0], swaps[1]) == 1, s1_got[...], s1[...])
        s1_got[...] = served
        t1[attn] = s1_got[attn]
        for k in range(1, 8):
            to = lax.rem(attn + k, 8)
            push(s1_got.at[to], t1.at[attn], rs_sem, rr_sem, 1 + k, (to, grp, tp))
        yield
        for k in range(1, 8):
            landed(t1.at[lax.rem(attn + 8 - k, 8)], rs_sem, rr_sem, 1 + k)
        for n in range(8):
            part = t1[n].astype(F32)
            for t in range(8):
                uf[t, n * 4 : n * 4 + 4, :] = part[
                    (t % 4) * 4 : (t % 4) * 4 + 4, (t // 4) * 128 : (t // 4) * 128 + 128
                ]
        ub[...] = uf[...].astype(BF16)
        vb[tp] = ub[tp]
        for k in range(1, 8):
            to = lax.rem(tp + k, 8)
            push(ub.at[to], vb.at[tp], rs_sem, rr_sem, 8 + k, (attn, grp, to))
        yield
        for k in range(1, 8):
            landed(vb.at[lax.rem(tp + 8 - k, 8)], rs_sem, rr_sem, 8 + k)
        for t in range(8):
            part = vb[t].astype(F32)
            for n in range(8):
                plane, zv = t % 2, n % 2
                bv, av = (n // 2, t // 2) if plane else (t // 2, n // 2)
                place = (((plane * 2 + zv) * 4 + bv) * 4 + av) * 4
                wf[place : place + 4, :] = part[n * 4 : n * 4 + 4]
        wt[...] = wf[...].T
        yield

    def scaling():
        for i in (1, 2, 3):
            loads[i].wait()

        def scale(i, _):
            rows = pl.ds(pl.multiple_of(i * 16, 16), 16)
            for src, dst in ((wg, wg2), (wu, wu2)):
                wide = (src[rows, :].astype(F32) * gain_ref[...]).astype(BF16)
                for cv in range(2):
                    for xv in range(4):
                        first = [xv * 1792 + (zv * 8 + yv * 2 + cv) * COLS for zv in range(2) for yv in range(4)]
                        dst[cv, rows, xv * 896 : (xv + 1) * 896] = jnp.concatenate(
                            [wide[:, f : f + COLS] for f in first], axis=1
                        )
            return 0

        for part in range(6):
            lax.fori_loop(part * 3, part * 3 + 3, scale, 0)
            yield

    push(own_b.at[0], got_b.at[0], rs_sem, rr_sem, 0, partner)
    push(own_b.at[1], got_b.at[1], rs_sem, rr_sem, 20, partner)
    push(d_hbm, wd.at[pl.ds(FH, FH)], rs_sem, rr_sem, 18, sibling)
    residual_steps, scaling_steps = residual(), scaling()
    next(residual_steps)
    next(scaling_steps)
    row = lax.broadcasted_iota(jnp.int32, (64, 256), 0)

    def gather_context(hh):
        way = ways[hh]

        def ready(p):
            for half in range(2):
                sf[half] = cb[hh, zs[p], :, :, half * 128 : (half + 1) * 128].astype(F32).reshape(256, 128)
            for h in range(16):
                for half in range(2):
                    first = h * 256 + half * 128
                    ctx_all[hh, (c * 2 + zs[p]) * 4 + way[1][0], :, first : first + 128] = sf[
                        half, pl.ds(h, 16, stride=16), :
                    ].astype(BF16)

        landed(got_b.at[hh], rs_sem, rr_sem, 20 * hh)
        cb[hh, z, way[0][0]] = jnp.where(
            jnp.where(row < 32, swaps[0], swaps[1]) == 1, got_b[hh], own_b[hh]
        )
        yield from gather(
            way,
            lambda p, av: cb.at[hh, zs[p], av],
            lambda p, bv: ctx_all.at[hh, (c * 2 + zs[p]) * 4 + bv],
            lambda zv, bv: ctx_all.at[hh, (co * 2 + zv) * 4 + bv],
            bs_sem,
            br_sem,
            ready,
            21 * hh,
        )

    steps = (gather_context(0), gather_context(1))

    def both(pair):
        for one in pair:
            next(one)

    both(steps)
    next(residual_steps)
    both(steps)
    next(scaling_steps)
    both(steps)
    next(residual_steps)
    next(scaling_steps)
    both(steps)
    next(scaling_steps)
    both(steps)
    next(scaling_steps)
    next(residual_steps)
    next(scaling_steps)
    both(steps)
    loads[4].wait()

    def project(plane):
        def rows(hh, cols):
            return ctx_all[hh, pl.ds(plane * 8, 8), :, cols].reshape(128, 1024)

        def step(i, sums):
            cols = pl.ds(pl.multiple_of(i * 1024, 1024), 1024)
            last = pl.ds(pl.multiple_of(i * 1024 + CW // 2, 1024), 1024)
            one = lax.dot_general(wo[:, cols], rows(0, cols), NT, preferred_element_type=F32)
            two = lax.dot_general(rows(1, cols), wo[:, last], NT, preferred_element_type=F32)
            return sums[0] + one, sums[1] + two

        one, two = lax.fori_loop(
            0, CW // 2048, step, (jnp.zeros((COLS, 128), F32), jnp.zeros((128, COLS), F32))
        )
        for zv in range(2):
            for i in range(4):
                for j in range(4):
                    src, dst = ((zv * 4 + i) * 4 + j) * 4, ((zv * 4 + j) * 4 + i) * 4
                    turned[dst : dst + 4, :COLS] = two[src : src + 4]
        lanes = pl.ds(pl.multiple_of(plane * 128, 128), 128)
        return (wt[:COLS, lanes] + (one + turned[...].T[:COLS])).astype(BF16)

    def gather_hidden(i):
        half = (c, co)[i]
        return gather(
            ways[i],
            lambda p, av: ht.at[half, ((c * 2 + zs[p]) * 4 + ways[i][1][0]) * 4 + av],
            lambda p, bv: ht.at[half, pl.ds(((c * 2 + zs[p]) * 4 + bv) * 4, 4)],
            lambda zv, bv: ht.at[(co, c)[i], pl.ds(((co * 2 + zv) * 4 + bv) * 4, 4)],
            cs_sem,
            cr_sem,
            lambda p: None,
            21 * i,
        )

    early, late = gather_hidden(0), gather_hidden(1)

    def features(plane, half, xv):
        parts = []
        for zv in range(2):
            for yv in range(4):
                bv, av = yv * (1 - half) + xv * half, xv * (1 - half) + yv * half
                parts.append(ht[half, ((plane * 2 + zv) * 4 + bv) * 4 + av])
        return jnp.concatenate(parts, axis=0)

    def expand(plane, i):
        half = (c, co)[i]

        def step(xv, total):
            cols = pl.ds(pl.multiple_of(xv * 896, 128), 896)
            part = features(plane, half, xv)
            acc_g[i] += jnp.dot(wg2[plane, :, cols], part, preferred_element_type=F32)
            acc_u[i] += jnp.dot(wu2[plane, :, cols], part, preferred_element_type=F32)
            wide = part.astype(F32)
            return total + jnp.sum((wide * wide).reshape(112, 8, 128), axis=0)

        squares[i] += lax.fori_loop(0, 4, step, jnp.zeros((8, 128), F32))

    def activate(i):
        factor = lax.rsqrt(jnp.sum(squares[i], axis=0, keepdims=True) * (1.0 / D) + 1e-5)
        gate = acc_g[i] * factor
        act = gate / (1.0 + jnp.exp(-gate)) * (acc_u[i] * factor)
        return act.T.astype(BF16)

    ht[c, me[0]] = project(c)
    next(early)
    both(steps)
    ht[co, me[1]] = project(co)
    next(late)
    acc_g[...] = jnp.zeros_like(acc_g)
    acc_u[...] = jnp.zeros_like(acc_u)
    squares[...] = jnp.zeros_like(squares)
    before = len(started)
    for i in range(4):
        next(early)
        next(late)
        if i == 0:
            drain(len(started) - before)
    next(early)
    expand(c, 0)
    next(late)
    next(early)
    expand(co, 1)
    expand(c, 1)
    act_out[...] = activate(1)
    push(act_out, act_in, rs_sem, rr_sem, 19, sibling)
    next(late)
    expand(co, 0)

    act_own = activate(0)
    loads[5].wait()
    landed(wd.at[pl.ds(FH, FH)], rs_sem, rr_sem, 18)
    landed(act_in, rs_sem, rr_sem, 19)
    lhs = jnp.concatenate([act_own, act_in[...]], axis=1)

    def other_order():
        wide_lhs = lhs.astype(F32)
        for zv in range(2):
            for i in range(4):
                for j in range(4):
                    src, dst = ((zv * 4 + i) * 4 + j) * 4, ((zv * 4 + j) * 4 + i) * 4
                    lhs_f[dst : dst + 4, :] = wide_lhs[src : src + 4]
        return lhs_f[...].astype(BF16)

    def reduction(h):
        rows = other_order() if h else lhs
        ak, (b, b1, b2, b3), a_other, b_other = ways[h]
        a, b_right, b_left = ak[0], b_other[1], b_other[3]
        for j in range(2):
            cols = pl.ds(j * 1792, 1792)
            part = jnp.dot(rows, wd[:, pl.ds(h * 3584 + j * 1792, 1792)], preferred_element_type=F32)
            p_own[h, :, :, cols] = part.astype(BF16).reshape(8, 16, 1792)

        def slab(p, k):
            return p_own.at[h, zs[p] * 4 + k]

        def send(ref, i, to):
            push(ref, r2.at[h, i], ds_sem, dr_sem, 2 + 6 * h + i, to)

        def wait(i):
            landed(r2.at[h, i], ds_sem, dr_sem, 2 + 6 * h + i)

        send(slab(0, b2), 0, b_left)
        send(slab(1, b2), 1, b_right)
        send(slab(1, b3), 3, b_left)
        send(slab(0, b1), 4, b_right)
        yield
        for i, p, k, to, j in ((0, 0, b3, b_left, 2), (1, 1, b1, b_right, 5)):
            wait(i)
            ref = slab(p, k)
            ref[...] = (ref[...].astype(F32) + r2[h, i].astype(F32)).astype(BF16)
            send(ref, j, to)
        yield
        for i in (3, 4, 2, 5):
            wait(i)
        for p in (1, 0):
            total = (
                p_own[h, zs[p] * 4 + b].astype(F32) + r2[h, 2 + p].astype(F32) + r2[h, 4 + p].astype(F32)
            )
            for av in range(4):
                for q in range(4):
                    qf[av, q * 4 : q * 4 + 4, :] = total[av * 4 : av * 4 + 4, q * 896 : (q + 1) * 896]
            qb[h, p] = qf[...].astype(BF16)
            for k in (1, 3, 2):
                push(
                    qb.at[h, p, ak[k]], r1.at[h, p, k - 1], ds_sem, dr_sem, 13 + 6 * h + 3 * p + k, a_other[k]
                )
        yield
        sums = []
        for p in (1, 0):
            total = qb[h, p, a].astype(F32)
            for k in (1, 3, 2):
                landed(r1.at[h, p, k - 1], ds_sem, dr_sem, 13 + 6 * h + 3 * p + k)
                total = total + r1[h, p, k - 1].astype(F32)
            sums.append(total)
            if p == 1:
                tz[h] = total.astype(BF16)
                push(tz.at[h], got_peer.at[h], ds_sem, dr_sem, 26 + 3 * h, z_peer)
                push(tz.at[h], got_cross.at[h], ds_sem, dr_sem, 27 + 3 * h, cross)
        tp0[h] = sums[1].astype(BF16)
        push(tp0.at[h], got_partner.at[h], ds_sem, dr_sem, 28 + 3 * h, partner)
        t0[h] = sums[1]
        yield
        landed(got_partner.at[h], ds_sem, dr_sem, 28 + 3 * h)
        landed(got_cross.at[h], ds_sem, dr_sem, 27 + 3 * h)
        landed(got_peer.at[h], ds_sem, dr_sem, 26 + 3 * h)
        stayed = hid[h].astype(F32) + (t0[h] + got_peer[h].astype(F32))
        moved = hid_got[h].astype(F32) + (got_partner[h].astype(F32) + got_cross[h].astype(F32))
        row = lax.rem(lax.broadcasted_iota(jnp.int32, (16, 896), 0), 4)
        final = jnp.where(jnp.where(row < 2, swaps[0], swaps[1]) == 1, moved, stayed)
        request = lax.broadcasted_iota(jnp.int32, (4, 896), 0)
        for q in range(4):
            rows = jnp.zeros((4, 896), F32)
            for p in range(4):
                one = jnp.broadcast_to(final[q * 4 + p : q * 4 + p + 1], (4, 896))
                rows = jnp.where(request == assign_ref[p], one, rows)
            out_ref[:, h * 3584 + q * 896 : h * 3584 + (q + 1) * 896] = rows.astype(BF16)
        yield

    def own_hidden(h):
        lane = lax.broadcasted_iota(jnp.int32, (16, 128), 1)
        sub = lax.broadcasted_iota(jnp.int32, (16, 128), 0)
        rows = jnp.zeros((16, 896), F32)
        for q in range(4):
            pick = jnp.where(lane == me_row + sub - q * 4, 1.0, 0.0)
            pick = jnp.where((sub >= q * 4) & (sub < q * 4 + 4), pick, 0.0).astype(BF16)
            xv, zv = 2 * h + q // 2, q % 2
            parts = []
            for yv in range(4):
                for plane in range(2):
                    bv, av = yv * co + xv * c, xv * co + yv * c
                    parts.append(ht[c, ((plane * 2 + zv) * 4 + bv) * 4 + av])
            rows = rows + lax.dot_general(
                pick, jnp.concatenate(parts, axis=0), NT, preferred_element_type=F32
            )
        hid[h] = rows.astype(BF16)
        push(hid.at[h], hid_got.at[h], rs_sem, rr_sem, 16 + h, partner)

    halves = (reduction(0), reduction(1))
    before = len(started)
    for half in halves:
        next(half)
    own_hidden(0)
    drain(len(started) - before)
    next(halves[0])
    own_hidden(1)
    next(halves[1])
    for _ in range(2):
        for half in halves:
            next(half)
    for h in range(2):
        landed(hid_got.at[h], rs_sem, rr_sem, 16 + h)
    for half in halves:
        next(half)
    drain()


def per_device(
    queries, keys, values, lengths, resid, assign, matching, w_out, gain, gate_w, up_w, down_w
):
    smem = pl.BlockSpec(memory_space=pltpu.SMEM)
    vmem = pl.BlockSpec(memory_space=pltpu.VMEM)
    hbm = pl.BlockSpec(memory_space=pl.ANY)
    dma = pltpu.SemaphoreType.DMA
    scratch = (
        ((4, CW), BF16),
        ((4, 1024, 256), BF16),
        ((4, 1024, 256), BF16),
        ((COLS, CW), BF16),
        ((FH, D), BF16),
        ((FH, D), BF16),
        ((2, FH, D // 2), BF16),
        ((2, FH, D // 2), BF16),
        ((2 * FH, D), BF16),
        ((4, D), BF16),
        ((1, D), F32),
        ((2, 128, 128), F32),
        ((2, 64, 256), BF16),
        ((2, 64, 256), BF16),
        ((2, 2, 4, 64, 256), BF16),
        ((2, 256, 128), F32),
        ((2, 16, 16, CW // 2), BF16),
        ((2, 64, COLS, 128), BF16),
        ((2, FH, 128), F32),
        ((2, FH, 128), F32),
        ((2, 8, 128), F32),
        ((128, FH), BF16),
        ((128, FH), BF16),
        ((8, 16, 256), F32),
        ((8, 16, 256), BF16),
        ((8, 16, 256), BF16),
        ((8, 16, 256), BF16),
        ((8, 32, 128), F32),
        ((8, 32, 128), BF16),
        ((8, 32, 128), BF16),
        ((256, 128), F32),
        ((128, 256), F32),
        ((128, 128), F32),
        ((128, 2 * FH), F32),
        ((2, 8, 16, D // 2), BF16),
        ((2, 6, 16, D // 2), BF16),
        ((4, 16, 896), F32),
        ((2, 2, 4, 16, 896), BF16),
        ((2, 2, 3, 16, 896), BF16),
        ((2, 16, 896), F32),
    ) + (((2, 16, 896), BF16),) * 7
    return pl.pallas_call(
        kernel,
        out_shape=jax.ShapeDtypeStruct((4, D), BF16),
        in_specs=[smem] * 3 + [hbm] * 9,
        out_specs=vmem,
        scratch_shapes=[pltpu.VMEM(shape, dtype) for shape, dtype in scratch]
        + [dma((n,)) for n in (8, 7, 42, 42, 42, 42, 32, 32, 21, 21)],
        compiler_params=pltpu.CompilerParams(
            collective_id=0, has_side_effects=True, vmem_limit_bytes=60 * 1024 * 1024
        ),
    )(
        lengths, assign[0], matching[:, 0, 0], queries, resid, gain[None],
        keys, values, w_out.T, gate_w[0].T, up_w[0].T, down_w[0],
    )


def solution(mesh):
    rows = P(("attn", "grp", "tp"), None)
    cache = P(("attn", "grp", "tp"), None, None)
    placed = (
        rows,
        cache,
        cache,
        P(("attn", "grp", "tp")),
        rows,
        rows,
        P(None, "attn", "tp"),
        P(None, ("attn", "tp")),
        P(),
        P("grp", None, ("attn", "tp")),
        P("grp", None, ("attn", "tp")),
        P("grp", ("attn", "tp"), None),
    )
    return jax.shard_map(
        per_device, mesh=mesh, in_specs=placed, out_specs=rows, check_vma=False
    )
```

```python
import jax
import jax.numpy as jnp
from jax import lax
from jax.experimental import pallas as pl
from jax.experimental.pallas import tpu as pltpu
from jax.sharding import PartitionSpec as P

D = 7168
CW = 8192
FH = 288
COLS = 112
MESH = pl.DeviceIdType.MESH
F32 = jnp.float32
BF16 = jnp.bfloat16
NT = (((1,), (1,)), ((), ()))


def kernel(
    len_ref, assign_ref, match_ref, q_hbm, resid_hbm, gain_hbm, k_hbm, v_hbm, wo_hbm, g_hbm, u_hbm, d_hbm,
    out_ref,
    q_ref, kc, vc, wo, wg, wu, wg2, wu2, wd, resid_ref, gain_ref,
    qs, own_b, got_b, cross_b, peer_b, flags, flag_out, flag_in, cb, sf, ctx_all, ht, acc_g, acc_u, squares, act_out, act_in,
    s1f, s1, s1_got, t1, uf, ub, vb, wf, wt, turned, lhs_f,
    p_own, r2, qf, qb, r1, t0, tp0, tz, got_peer, got_partner, got_cross, hid, hid_got,
    kv_sem, w_sem, bs_sem, br_sem, cs_sem, cr_sem, ds_sem, dr_sem, rs_sem, rr_sem,
):
    attn, grp, tp = lax.axis_index("attn"), lax.axis_index("grp"), lax.axis_index("tp")
    x, z, y, c = attn // 2, lax.rem(attn, 2), tp // 2, lax.rem(tp, 2)
    zo, co = 1 - z, 1 - c
    zs = (z, zo)
    def dev(x_, z_, y_, c_):
        return (lax.rem(x_, 4) * 2 + z_, grp, lax.rem(y_, 4) * 2 + c_)

    z_peer, sibling = dev(x, zo, y, c), dev(x, z, y, co)
    partner = (attn, 1 - grp, tp)
    cross = (x * 2 + zo, 1 - grp, tp)

    def axes(e):
        a, b = x * (1 - e) + y * e, y * (1 - e) + x * e
        return (
            [lax.rem(a + k, 4) for k in range(4)],
            [lax.rem(b + k, 4) for k in range(4)],
            [dev(x + k * (1 - e), z, y + k * e, c) for k in range(4)],
            [dev(x + k * e, z, y + k * (1 - e), c) for k in range(4)],
        )

    ways = (axes(c), axes(co))

    q_load = pltpu.make_async_copy(q_hbm, q_ref, w_sem.at[6])
    q_load.start()
    fetch = []
    for src, dst in ((k_hbm, kc), (v_hbm, vc)):
        for r in range(4):
            fetch.append(pltpu.make_async_copy(src.at[r], dst.at[r], kv_sem.at[len(fetch)]))
            fetch[-1].start()
    loads = [
        pltpu.make_async_copy(src, dst, w_sem.at[i])
        for i, (src, dst) in enumerate(
            ((resid_hbm, resid_ref), (gain_hbm, gain_ref), (g_hbm, wg), (u_hbm, wu), (wo_hbm, wo), (d_hbm, wd.at[pl.ds(0, FH)]))
        )
    ]
    barrier = pltpu.get_barrier_semaphore()
    others = [partner, cross]
    for k in range(1, 8):
        others.append((lax.rem(attn + k, 8), grp, tp))
        others.append((attn, grp, lax.rem(tp + k, 8)))
    for other in others:
        pl.semaphore_signal(barrier, inc=1, device_id=other, device_id_type=MESH)

    started = []

    def drain(keep=0):
        while len(started) > keep:
            started.pop(0).wait_send()

    def push(src, dst, s_sem, r_sem, i, to):
        copy = pltpu.make_async_remote_copy(
            src_ref=src, dst_ref=dst, send_sem=s_sem.at[i], recv_sem=r_sem.at[i],
            device_id=to, device_id_type=MESH,
        )
        copy.start()
        started.append(copy)

    def landed(dst, s_sem, r_sem, i):
        pltpu.make_async_remote_copy(
            src_ref=dst, dst_ref=dst, send_sem=s_sem.at[i], recv_sem=r_sem.at[i],
            device_id=sibling, device_id_type=MESH,
        ).wait_recv()

    q_load.wait()
    wide_q = q_ref[...].astype(F32)
    for h in range(32):
        for half in range(2):
            first = h * 256 + half * 128
            qs[half, pl.ds(h, 4, stride=32), :] = wide_q[:, first : first + 128]
    slot = lax.broadcasted_iota(jnp.int32, (32, 1024), 1)
    swaps = (match_ref[0], match_ref[1])

    def weigh(r):
        query = jnp.concatenate([qs[half, r * 32 : (r + 1) * 32] for half in range(2)], axis=1).astype(BF16)
        scores = lax.dot_general(query, kc[r], NT, preferred_element_type=F32) * (256 ** -0.5)
        scores = jnp.where(slot < len_ref[r], scores, -1e30)
        expo = jnp.exp(scores - jnp.max(scores, axis=-1, keepdims=True))
        return (expo / jnp.sum(expo, axis=-1, keepdims=True)).astype(BF16)

    for copy in fetch[:4]:
        copy.wait()
    for load in loads:
        load.start()
    probs = [weigh(r) for r in range(4)]
    for copy in fetch[4:]:
        copy.wait()
    contexts = [jnp.dot(probs[r], vc[r], preferred_element_type=F32) for r in range(4)]
    for p in range(4):
        chosen = contexts[0]
        for r in range(1, 4):
            chosen = jnp.where(assign_ref[p] == r, contexts[r], chosen)
        for hh in range(2):
            own_b[hh, p * 16 : p * 16 + 16] = chosen[hh * 16 : hh * 16 + 16].astype(BF16)
    pl.semaphore_wait(barrier, 16)

    def gather(way, block, part, other, s_sem, r_sem, ready, base, peer=None):
        ak, bk, a_other, b_other = way
        a, (b, b1, b2, b3) = ak[0], bk
        b_right, b_left = b_other[1], b_other[3]

        def send(ref, i, to):
            push(ref, ref, s_sem, r_sem, base + i, to)

        def wait(ref, i):
            landed(ref, s_sem, r_sem, base + i)

        def ring_1(p):
            for k in (1, 3, 2):
                send(block(p, a), 3 * p + k, a_other[k])

        def ring_2(p):
            for k in (1, 3, 2):
                wait(block(p, ak[4 - k]), 3 * p + k)
            ready(p)
            first, second = ((7, b_right), (8, b_left)) if p == 0 else ((10, b_left), (9, b_right))
            send(part(p, b), *first)
            send(part(p, b), *second)
            send(part(p, b), 13 + p, sibling)

        if peer is None:
            send(block(0, a), 0, z_peer)
        ring_1(0)
        yield
        if peer is None:
            ring_2(0)
            wait(block(1, a), 0)
            ring_1(1)
        else:
            peer()
            ring_1(1)
            ring_2(0)
        yield
        ring_2(1)
        yield
        wait(part(0, b3), 7)
        send(part(0, b3), 11, b_right)
        send(part(0, b3), 15, sibling)
        wait(part(0, b1), 8)
        send(part(0, b1), 16, sibling)
        yield
        wait(part(1, b1), 10)
        send(part(1, b1), 12, b_left)
        send(part(1, b1), 17, sibling)
        wait(part(1, b3), 9)
        send(part(1, b3), 18, sibling)
        yield
        wait(part(0, b2), 11)
        send(part(0, b2), 19, sibling)
        wait(part(1, b2), 12)
        send(part(1, b2), 20, sibling)
        yield
        for p, spots in enumerate((((13, 0), (15, 3), (16, 1), (19, 2)), ((14, 0), (18, 3), (17, 1), (20, 2)))):
            for i, k in spots:
                wait(other(zs[p], ak[k]), i)
            yield

    a, b = ways[0][0][0], ways[0][1][0]
    me = (((c * 2 + z) * 4 + b) * 4 + a, ((c * 2 + z) * 4 + a) * 4 + b)
    me_row = ((z * 4 + b) * 4 + a) * 4

    def residual():
        loads[0].wait()
        wide_r = resid_ref[...].astype(F32)
        ordered = []
        for p in range(4):
            chosen = wide_r[0:1]
            for r in range(1, 4):
                chosen = jnp.where(assign_ref[p] == r, wide_r[r : r + 1], chosen)
            ordered.append(chosen)
        ordered = jnp.concatenate(ordered, axis=0)
        s1f[...] = jnp.zeros_like(s1f)
        for n in range(8):
            for t in range(8):
                first = n * 896 + t * COLS
                s1f[n, (t % 4) * 4 : (t % 4) * 4 + 4, (t // 4) * 128 : (t // 4) * 128 + COLS] = ordered[
                    :, first : first + COLS
                ]
        s1[...] = s1f[...].astype(BF16)
        push(s1, s1_got, rs_sem, rr_sem, 1, partner)
        yield
        landed(s1_got, rs_sem, rr_sem, 1)
        row = lax.rem(lax.broadcasted_iota(jnp.int32, (8, 16, 256), 1), 4)
        served = jnp.where(jnp.where(row < 2, swaps[0], swaps[1]) == 1, s1_got[...], s1[...])
        s1_got[...] = served
        t1[attn] = s1_got[attn]
        for k in range(1, 8):
            to = lax.rem(attn + k, 8)
            push(s1_got.at[to], t1.at[attn], rs_sem, rr_sem, 1 + k, (to, grp, tp))
        yield
        for k in range(1, 8):
            landed(t1.at[lax.rem(attn + 8 - k, 8)], rs_sem, rr_sem, 1 + k)
        for n in range(8):
            part = t1[n].astype(F32)
            for t in range(8):
                uf[t, n * 4 : n * 4 + 4, :] = part[
                    (t % 4) * 4 : (t % 4) * 4 + 4, (t // 4) * 128 : (t // 4) * 128 + 128
                ]
        ub[...] = uf[...].astype(BF16)
        vb[tp] = ub[tp]
        for k in range(1, 8):
            to = lax.rem(tp + k, 8)
            push(ub.at[to], vb.at[tp], rs_sem, rr_sem, 8 + k, (attn, grp, to))
        yield
        for k in range(1, 8):
            landed(vb.at[lax.rem(tp + 8 - k, 8)], rs_sem, rr_sem, 8 + k)
        for t in range(8):
            part = vb[t].astype(F32)
            for n in range(8):
                plane, zv = t % 2, n % 2
                bv, av = (n // 2, t // 2) if plane else (t // 2, n // 2)
                place = (((plane * 2 + zv) * 4 + bv) * 4 + av) * 4
                wf[place : place + 4, :] = part[n * 4 : n * 4 + 4]
        wt[...] = wf[...].T
        yield

    def scaling():
        for i in (1, 2, 3):
            loads[i].wait()

        def scale(i, _):
            rows = pl.ds(pl.multiple_of(i * 16, 16), 16)
            for src, dst in ((wg, wg2), (wu, wu2)):
                wide = (src[rows, :].astype(F32) * gain_ref[...]).astype(BF16)
                for cv in range(2):
                    for xv in range(4):
                        first = [
                            ((xv // 2 * 4 + x2 * 2 + xv % 2) * 8 + yv * 2 + cv) * COLS
                            for x2 in range(2)
                            for yv in range(4)
                        ]
                        dst[cv, rows, xv * 896 : (xv + 1) * 896] = jnp.concatenate(
                            [wide[:, f : f + COLS] for f in first], axis=1
                        )
            return 0

        for part in range(6):
            lax.fori_loop(part * 3, part * 3 + 3, scale, 0)
            yield

    for m in range(2):
        flags[m * 8 : m * 8 + 8, :] = jnp.full((8, 128), swaps[m], jnp.int32).astype(F32)
    flag_out[...] = flags[...].astype(BF16)
    for hh in range(2):
        push(own_b.at[hh], got_b.at[hh], rs_sem, rr_sem, 20 * hh, partner)
    push(flag_out, flag_in, rs_sem, rr_sem, 21, z_peer)
    for hh in range(2):
        push(own_b.at[hh], cross_b.at[hh], rs_sem, rr_sem, 22 + hh, cross)
        push(own_b.at[hh], peer_b.at[hh], rs_sem, rr_sem, 24 + hh, z_peer)
    push(d_hbm, wd.at[pl.ds(FH, FH)], rs_sem, rr_sem, 18, sibling)
    residual_steps, scaling_steps = residual(), scaling()
    next(residual_steps)
    next(scaling_steps)
    row = lax.broadcasted_iota(jnp.int32, (64, 256), 0)

    def gather_context(hh):
        way = ways[hh]

        def ready(p):
            for half in range(2):
                sf[half] = cb[hh, zs[p], :, :, half * 128 : (half + 1) * 128].astype(F32).reshape(256, 128)
            for h in range(16):
                for half in range(2):
                    first = h * 256 + half * 128
                    ctx_all[hh, (c * 2 + zs[p]) * 4 + way[1][0], :, first : first + 128] = sf[
                        half, pl.ds(h, 16, stride=16), :
                    ].astype(BF16)

        landed(got_b.at[hh], rs_sem, rr_sem, 20 * hh)
        cb[hh, z, way[0][0]] = jnp.where(
            jnp.where(row < 32, swaps[0], swaps[1]) == 1, got_b[hh], own_b[hh]
        )

        def peer():
            if hh == 0:
                landed(flag_in, rs_sem, rr_sem, 21)
            landed(cross_b.at[hh], rs_sem, rr_sem, 22 + hh)
            landed(peer_b.at[hh], rs_sem, rr_sem, 24 + hh)
            wide = flag_in[...].astype(F32)
            flag = jnp.concatenate(
                [jnp.broadcast_to(wide[m * 8 : m * 8 + 1], (32, 128)) for m in range(2)], axis=0
            )
            flag = jnp.concatenate([flag, flag], axis=1)
            theirs = jnp.where(flag > 0.5, cross_b[hh].astype(F32), peer_b[hh].astype(F32))
            cb[hh, zo, way[0][0]] = theirs.astype(BF16)

        yield from gather(
            way,
            lambda p, av: cb.at[hh, zs[p], av],
            lambda p, bv: ctx_all.at[hh, (c * 2 + zs[p]) * 4 + bv],
            lambda zv, bv: ctx_all.at[hh, (co * 2 + zv) * 4 + bv],
            bs_sem,
            br_sem,
            ready,
            21 * hh,
            peer,
        )

    steps = (gather_context(0), gather_context(1))

    def both(pair):
        for one in pair:
            next(one)

    both(steps)
    next(residual_steps)
    both(steps)
    next(scaling_steps)
    both(steps)
    next(residual_steps)
    next(scaling_steps)
    both(steps)
    next(scaling_steps)
    both(steps)
    next(scaling_steps)
    next(residual_steps)
    next(scaling_steps)
    both(steps)
    loads[4].wait()

    def project(plane):
        def rows(hh, cols):
            return ctx_all[hh, pl.ds(plane * 8, 8), :, cols].reshape(128, 1024)

        def step(i, sums):
            cols = pl.ds(pl.multiple_of(i * 1024, 1024), 1024)
            last = pl.ds(pl.multiple_of(i * 1024 + CW // 2, 1024), 1024)
            one = lax.dot_general(wo[:, cols], rows(0, cols), NT, preferred_element_type=F32)
            two = lax.dot_general(rows(1, cols), wo[:, last], NT, preferred_element_type=F32)
            return sums[0] + one, sums[1] + two

        one, two = lax.fori_loop(
            0, CW // 2048, step, (jnp.zeros((COLS, 128), F32), jnp.zeros((128, COLS), F32))
        )
        for zv in range(2):
            for i in range(4):
                for j in range(4):
                    src, dst = ((zv * 4 + i) * 4 + j) * 4, ((zv * 4 + j) * 4 + i) * 4
                    turned[dst : dst + 4, :COLS] = two[src : src + 4]
        lanes = pl.ds(pl.multiple_of(plane * 128, 128), 128)
        return (wt[:COLS, lanes] + (one + turned[...].T[:COLS])).astype(BF16)

    def gather_hidden(i):
        half = (c, co)[i]
        return gather(
            ways[i],
            lambda p, av: ht.at[half, ((c * 2 + zs[p]) * 4 + ways[i][1][0]) * 4 + av],
            lambda p, bv: ht.at[half, pl.ds(((c * 2 + zs[p]) * 4 + bv) * 4, 4)],
            lambda zv, bv: ht.at[(co, c)[i], pl.ds(((co * 2 + zv) * 4 + bv) * 4, 4)],
            cs_sem,
            cr_sem,
            lambda p: None,
            21 * i,
        )

    early, late = gather_hidden(0), gather_hidden(1)

    def features(plane, half, n):
        parts = []
        for x2 in range(2):
            for yv in range(4):
                xv = n // 2 * 2 + x2
                bv, av = yv * (1 - half) + xv * half, xv * (1 - half) + yv * half
                parts.append(ht[half, ((plane * 2 + lax.rem(n, 2)) * 4 + bv) * 4 + av])
        return jnp.concatenate(parts, axis=0)

    def expand(plane, i, *ps):
        half = (c, co)[i]

        def step(k, total):
            n = (k // len(ps)) * 2 + (zs[ps[0]] if len(ps) == 1 else lax.rem(k, 2))
            cols = pl.ds(pl.multiple_of(n * 896, 128), 896)
            part = features(plane, half, n)
            acc_g[i] += jnp.dot(wg2[plane, :, cols], part, preferred_element_type=F32)
            acc_u[i] += jnp.dot(wu2[plane, :, cols], part, preferred_element_type=F32)
            wide = part.astype(F32)
            return total + jnp.sum((wide * wide).reshape(112, 8, 128), axis=0)

        squares[i] += lax.fori_loop(0, 2 * len(ps), step, jnp.zeros((8, 128), F32))

    def activate(i):
        factor = lax.rsqrt(jnp.sum(squares[i], axis=0, keepdims=True) * (1.0 / D) + 1e-5)
        gate = acc_g[i] * factor
        act = gate / (1.0 + jnp.exp(-gate)) * (acc_u[i] * factor)
        return act.T.astype(BF16)

    ht[c, me[0]] = project(c)
    next(early)
    both(steps)
    both(steps)
    ht[co, me[1]] = project(co)
    next(late)
    acc_g[...] = jnp.zeros_like(acc_g)
    acc_u[...] = jnp.zeros_like(acc_u)
    squares[...] = jnp.zeros_like(squares)
    before = len(started)
    for i in range(4):
        next(early)
        next(late)
        if i == 0:
            drain(len(started) - before)
    next(early)
    expand(c, 0, 0, 1)
    next(late)
    next(early)
    next(early)
    expand(co, 1, 0, 1)
    expand(c, 1, 0, 1)
    act_out[...] = activate(1)
    push(act_out, act_in, rs_sem, rr_sem, 19, sibling)
    next(late)
    expand(co, 0, 0)
    next(late)
    expand(co, 0, 1)

    act_own = activate(0)
    loads[5].wait()
    landed(wd.at[pl.ds(FH, FH)], rs_sem, rr_sem, 18)
    landed(act_in, rs_sem, rr_sem, 19)
    lhs = jnp.concatenate([act_own, act_in[...]], axis=1)

    def other_order():
        wide_lhs = lhs.astype(F32)
        for zv in range(2):
            for i in range(4):
                for j in range(4):
                    src, dst = ((zv * 4 + i) * 4 + j) * 4, ((zv * 4 + j) * 4 + i) * 4
                    lhs_f[dst : dst + 4, :] = wide_lhs[src : src + 4]
        return lhs_f[...].astype(BF16)

    def reduction(h):
        rows = other_order() if h else lhs
        ak, (b, b1, b2, b3), a_other, b_other = ways[h]
        a, b_right, b_left = ak[0], b_other[1], b_other[3]
        for j in range(2):
            cols = pl.ds(j * 1792, 1792)
            part = jnp.dot(rows, wd[:, pl.ds(h * 3584 + j * 1792, 1792)], preferred_element_type=F32)
            p_own[h, :, :, cols] = part.astype(BF16).reshape(8, 16, 1792)

        def slab(p, k):
            return p_own.at[h, zs[p] * 4 + k]

        def send(ref, i, to):
            push(ref, r2.at[h, i], ds_sem, dr_sem, 2 + 6 * h + i, to)

        def wait(i):
            landed(r2.at[h, i], ds_sem, dr_sem, 2 + 6 * h + i)

        send(slab(0, b2), 0, b_left)
        send(slab(1, b2), 1, b_right)
        send(slab(1, b3), 3, b_left)
        send(slab(0, b1), 4, b_right)
        yield
        for i, p, k, to, j in ((0, 0, b3, b_left, 2), (1, 1, b1, b_right, 5)):
            wait(i)
            ref = slab(p, k)
            ref[...] = (ref[...].astype(F32) + r2[h, i].astype(F32)).astype(BF16)
            send(ref, j, to)
        yield
        for i in (3, 4, 2, 5):
            wait(i)
        for p in (1, 0):
            total = (
                p_own[h, zs[p] * 4 + b].astype(F32) + r2[h, 2 + p].astype(F32) + r2[h, 4 + p].astype(F32)
            )
            for av in range(4):
                for q in range(4):
                    qf[av, q * 4 : q * 4 + 4, :] = total[av * 4 : av * 4 + 4, q * 896 : (q + 1) * 896]
            qb[h, p] = qf[...].astype(BF16)
            for k in (1, 3, 2):
                push(
                    qb.at[h, p, ak[k]], r1.at[h, p, k - 1], ds_sem, dr_sem, 13 + 6 * h + 3 * p + k, a_other[k]
                )
        yield
        sums = []
        for p in (1, 0):
            total = qb[h, p, a].astype(F32)
            for k in (1, 3, 2):
                landed(r1.at[h, p, k - 1], ds_sem, dr_sem, 13 + 6 * h + 3 * p + k)
                total = total + r1[h, p, k - 1].astype(F32)
            sums.append(total)
            if p == 1:
                tz[h] = total.astype(BF16)
                push(tz.at[h], got_peer.at[h], ds_sem, dr_sem, 26 + 3 * h, z_peer)
                push(tz.at[h], got_cross.at[h], ds_sem, dr_sem, 27 + 3 * h, cross)
        tp0[h] = sums[1].astype(BF16)
        push(tp0.at[h], got_partner.at[h], ds_sem, dr_sem, 28 + 3 * h, partner)
        t0[h] = sums[1]
        yield
        landed(got_partner.at[h], ds_sem, dr_sem, 28 + 3 * h)
        landed(got_cross.at[h], ds_sem, dr_sem, 27 + 3 * h)
        landed(got_peer.at[h], ds_sem, dr_sem, 26 + 3 * h)
        stayed = hid[h].astype(F32) + (t0[h] + got_peer[h].astype(F32))
        moved = hid_got[h].astype(F32) + (got_partner[h].astype(F32) + got_cross[h].astype(F32))
        row = lax.rem(lax.broadcasted_iota(jnp.int32, (16, 896), 0), 4)
        final = jnp.where(jnp.where(row < 2, swaps[0], swaps[1]) == 1, moved, stayed)
        request = lax.broadcasted_iota(jnp.int32, (4, 896), 0)
        for q in range(4):
            rows = jnp.zeros((4, 896), F32)
            for p in range(4):
                one = jnp.broadcast_to(final[q * 4 + p : q * 4 + p + 1], (4, 896))
                rows = jnp.where(request == assign_ref[p], one, rows)
            out_ref[:, h * 3584 + q * 896 : h * 3584 + (q + 1) * 896] = rows.astype(BF16)
        yield

    def own_hidden(h):
        lane = lax.broadcasted_iota(jnp.int32, (16, 128), 1)
        sub = lax.broadcasted_iota(jnp.int32, (16, 128), 0)
        rows = jnp.zeros((16, 896), F32)
        for q in range(4):
            pick = jnp.where(lane == me_row + sub - q * 4, 1.0, 0.0)
            pick = jnp.where((sub >= q * 4) & (sub < q * 4 + 4), pick, 0.0).astype(BF16)
            xv, zv = 2 * h + q // 2, q % 2
            parts = []
            for yv in range(4):
                for plane in range(2):
                    bv, av = yv * co + xv * c, xv * co + yv * c
                    parts.append(ht[c, ((plane * 2 + zv) * 4 + bv) * 4 + av])
            rows = rows + lax.dot_general(
                pick, jnp.concatenate(parts, axis=0), NT, preferred_element_type=F32
            )
        hid[h] = rows.astype(BF16)
        push(hid.at[h], hid_got.at[h], rs_sem, rr_sem, 16 + h, partner)

    halves = (reduction(0), reduction(1))
    before = len(started)
    for half in halves:
        next(half)
    own_hidden(0)
    drain(len(started) - before)
    next(halves[0])
    own_hidden(1)
    next(halves[1])
    for _ in range(2):
        for half in halves:
            next(half)
    for h in range(2):
        landed(hid_got.at[h], rs_sem, rr_sem, 16 + h)
    for half in halves:
        next(half)
    drain()


def per_device(
    queries, keys, values, lengths, resid, assign, matching, w_out, gain, gate_w, up_w, down_w
):
    smem = pl.BlockSpec(memory_space=pltpu.SMEM)
    vmem = pl.BlockSpec(memory_space=pltpu.VMEM)
    hbm = pl.BlockSpec(memory_space=pl.ANY)
    dma = pltpu.SemaphoreType.DMA
    scratch = (
        ((4, CW), BF16),
        ((4, 1024, 256), BF16),
        ((4, 1024, 256), BF16),
        ((COLS, CW), BF16),
        ((FH, D), BF16),
        ((FH, D), BF16),
        ((2, FH, D // 2), BF16),
        ((2, FH, D // 2), BF16),
        ((2 * FH, D), BF16),
        ((4, D), BF16),
        ((1, D), F32),
        ((2, 128, 128), F32),
        ((2, 64, 256), BF16),
        ((2, 64, 256), BF16),
        ((2, 64, 256), BF16),
        ((2, 64, 256), BF16),
        ((16, 128), F32),
        ((16, 128), BF16),
        ((16, 128), BF16),
        ((2, 2, 4, 64, 256), BF16),
        ((2, 256, 128), F32),
        ((2, 16, 16, CW // 2), BF16),
        ((2, 64, COLS, 128), BF16),
        ((2, FH, 128), F32),
        ((2, FH, 128), F32),
        ((2, 8, 128), F32),
        ((128, FH), BF16),
        ((128, FH), BF16),
        ((8, 16, 256), F32),
        ((8, 16, 256), BF16),
        ((8, 16, 256), BF16),
        ((8, 16, 256), BF16),
        ((8, 32, 128), F32),
        ((8, 32, 128), BF16),
        ((8, 32, 128), BF16),
        ((256, 128), F32),
        ((128, 256), F32),
        ((128, 128), F32),
        ((128, 2 * FH), F32),
        ((2, 8, 16, D // 2), BF16),
        ((2, 6, 16, D // 2), BF16),
        ((4, 16, 896), F32),
        ((2, 2, 4, 16, 896), BF16),
        ((2, 2, 3, 16, 896), BF16),
        ((2, 16, 896), F32),
    ) + (((2, 16, 896), BF16),) * 7
    return pl.pallas_call(
        kernel,
        out_shape=jax.ShapeDtypeStruct((4, D), BF16),
        in_specs=[smem] * 3 + [hbm] * 9,
        out_specs=vmem,
        scratch_shapes=[pltpu.VMEM(shape, dtype) for shape, dtype in scratch]
        + [dma((n,)) for n in (8, 7, 42, 42, 42, 42, 32, 32, 26, 26)],
        compiler_params=pltpu.CompilerParams(
            collective_id=0, has_side_effects=True, vmem_limit_bytes=60 * 1024 * 1024
        ),
    )(
        lengths, assign[0], matching[:, 0, 0], queries, resid, gain[None],
        keys, values, w_out.T, gate_w[0].T, up_w[0].T, down_w[0],
    )


def solution(mesh):
    rows = P(("attn", "grp", "tp"), None)
    cache = P(("attn", "grp", "tp"), None, None)
    placed = (
        rows,
        cache,
        cache,
        P(("attn", "grp", "tp")),
        rows,
        rows,
        P(None, "attn", "tp"),
        P(None, ("attn", "tp")),
        P(),
        P("grp", None, ("attn", "tp")),
        P("grp", None, ("attn", "tp")),
        P("grp", ("attn", "tp"), None),
    )
    return jax.shard_map(
        per_device, mesh=mesh, in_specs=placed, out_specs=rows, check_vma=False
    )
```

```python
import jax
import jax.numpy as jnp
from jax import lax
from jax.experimental import pallas as pl
from jax.experimental.pallas import tpu as pltpu
from jax.sharding import PartitionSpec as P

D = 7168
CW = 8192
FH = 288
COLS = 112
MESH = pl.DeviceIdType.MESH
F32 = jnp.float32
BF16 = jnp.bfloat16
NT = (((1,), (1,)), ((), ()))


def kernel(
    len_ref, assign_ref, match_ref, q_hbm, resid_hbm, gain_hbm, k_hbm, v_hbm, wo_hbm, g_hbm, u_hbm, d_hbm,
    out_ref,
    q_ref, kc, vc, wo, wg, wu, w2, wd, resid_ref, gain_ref,
    qs, own_b, got_b, cross_b, peer_b, flags, flag_out, flag_in, cb, sf, ctx_all, ht, acc, squares, act_out, act_in,
    s1f, s1, s1_got, t1, uf, ub, vb, wf, wt, turned, lhs_f,
    p_own, r2, qf, qb, r1, t0, tp0, tz, got_peer, got_partner, got_cross, hid, hid_got,
    kv_sem, w_sem, bs_sem, br_sem, cs_sem, cr_sem, ds_sem, dr_sem, rs_sem, rr_sem,
):
    attn, grp, tp = lax.axis_index("attn"), lax.axis_index("grp"), lax.axis_index("tp")
    x, z, y, c = attn // 2, lax.rem(attn, 2), tp // 2, lax.rem(tp, 2)
    zo, co = 1 - z, 1 - c
    zs = (z, zo)
    def dev(x_, z_, y_, c_):
        return (lax.rem(x_, 4) * 2 + z_, grp, lax.rem(y_, 4) * 2 + c_)

    z_peer, sibling = dev(x, zo, y, c), dev(x, z, y, co)
    partner = (attn, 1 - grp, tp)
    cross = (x * 2 + zo, 1 - grp, tp)

    def axes(e):
        a, b = x * (1 - e) + y * e, y * (1 - e) + x * e
        return (
            [lax.rem(a + k, 4) for k in range(4)],
            [lax.rem(b + k, 4) for k in range(4)],
            [dev(x + k * (1 - e), z, y + k * e, c) for k in range(4)],
            [dev(x + k * e, z, y + k * (1 - e), c) for k in range(4)],
        )

    ways = (axes(c), axes(co))

    q_load = pltpu.make_async_copy(q_hbm, q_ref, w_sem.at[6])
    q_load.start()
    fetch = []
    for src, dst in ((k_hbm, kc), (v_hbm, vc)):
        for r in range(4):
            fetch.append(pltpu.make_async_copy(src.at[r], dst.at[r], kv_sem.at[len(fetch)]))
            fetch[-1].start()
    loads = [
        pltpu.make_async_copy(src, dst, w_sem.at[i])
        for i, (src, dst) in enumerate(
            ((resid_hbm, resid_ref), (gain_hbm, gain_ref), (g_hbm, wg), (u_hbm, wu), (wo_hbm, wo), (d_hbm, wd.at[pl.ds(0, FH)]))
        )
    ]
    barrier = pltpu.get_barrier_semaphore()
    others = [partner, cross]
    for k in range(1, 8):
        others.append((lax.rem(attn + k, 8), grp, tp))
        others.append((attn, grp, lax.rem(tp + k, 8)))
    for other in others:
        pl.semaphore_signal(barrier, inc=1, device_id=other, device_id_type=MESH)

    started = []

    def drain(keep=0):
        while len(started) > keep:
            started.pop(0).wait_send()

    def push(src, dst, s_sem, r_sem, i, to):
        copy = pltpu.make_async_remote_copy(
            src_ref=src, dst_ref=dst, send_sem=s_sem.at[i], recv_sem=r_sem.at[i],
            device_id=to, device_id_type=MESH,
        )
        copy.start()
        started.append(copy)

    def landed(dst, s_sem, r_sem, i):
        pltpu.make_async_remote_copy(
            src_ref=dst, dst_ref=dst, send_sem=s_sem.at[i], recv_sem=r_sem.at[i],
            device_id=sibling, device_id_type=MESH,
        ).wait_recv()

    q_load.wait()
    wide_q = q_ref[...].astype(F32)
    for h in range(32):
        for half in range(2):
            first = h * 256 + half * 128
            qs[half, pl.ds(h, 4, stride=32), :] = wide_q[:, first : first + 128]
    slot = lax.broadcasted_iota(jnp.int32, (32, 1024), 1)
    swaps = (match_ref[0], match_ref[1])

    def weigh(r):
        query = jnp.concatenate([qs[half, r * 32 : (r + 1) * 32] for half in range(2)], axis=1).astype(BF16)
        scores = lax.dot_general(query, kc[r], NT, preferred_element_type=F32) * (256 ** -0.5)
        scores = jnp.where(slot < len_ref[r], scores, -1e30)
        expo = jnp.exp(scores - jnp.max(scores, axis=-1, keepdims=True))
        return (expo / jnp.sum(expo, axis=-1, keepdims=True)).astype(BF16)

    for copy in fetch[:4]:
        copy.wait()
    for load in loads:
        load.start()
    pl.semaphore_wait(barrier, 16)
    push(d_hbm, wd.at[pl.ds(FH, FH)], rs_sem, rr_sem, 18, sibling)
    probs = [weigh(r) for r in range(4)]
    for copy in fetch[4:]:
        copy.wait()
    contexts = [jnp.dot(probs[r], vc[r], preferred_element_type=F32) for r in range(4)]
    for p in range(4):
        chosen = contexts[0]
        for r in range(1, 4):
            chosen = jnp.where(assign_ref[p] == r, contexts[r], chosen)
        for hh in range(2):
            own_b[hh, p * 16 : p * 16 + 16] = chosen[hh * 16 : hh * 16 + 16].astype(BF16)

    def gather(way, block, part, other, s_sem, r_sem, ready, base, peer=None):
        ak, bk, a_other, b_other = way
        a, (b, b1, b2, b3) = ak[0], bk
        b_right, b_left = b_other[1], b_other[3]

        def send(ref, i, to):
            push(ref, ref, s_sem, r_sem, base + i, to)

        def wait(ref, i):
            landed(ref, s_sem, r_sem, base + i)

        def ring_1(p):
            for k in (1, 3, 2):
                send(block(p, a), 3 * p + k, a_other[k])

        def ring_2(p):
            for k in (1, 3, 2):
                wait(block(p, ak[4 - k]), 3 * p + k)
            ready(p)
            first, second = ((7, b_right), (8, b_left)) if p == 0 else ((10, b_left), (9, b_right))
            send(part(p, b), *first)
            send(part(p, b), *second)
            send(part(p, b), 13 + p, sibling)

        if peer is None:
            send(block(0, a), 0, z_peer)
        ring_1(0)
        yield
        if peer is None:
            ring_2(0)
            wait(block(1, a), 0)
            ring_1(1)
        else:
            peer()
            ring_1(1)
            ring_2(0)
        yield
        ring_2(1)
        yield
        wait(part(0, b3), 7)
        send(part(0, b3), 11, b_right)
        send(part(0, b3), 15, sibling)
        wait(part(0, b1), 8)
        send(part(0, b1), 16, sibling)
        yield
        wait(part(1, b1), 10)
        send(part(1, b1), 12, b_left)
        send(part(1, b1), 17, sibling)
        wait(part(1, b3), 9)
        send(part(1, b3), 18, sibling)
        yield
        wait(part(0, b2), 11)
        send(part(0, b2), 19, sibling)
        wait(part(1, b2), 12)
        send(part(1, b2), 20, sibling)
        yield
        for p, spots in enumerate((((13, 0), (15, 3), (16, 1), (19, 2)), ((14, 0), (18, 3), (17, 1), (20, 2)))):
            for i, k in spots:
                wait(other(zs[p], ak[k]), i)
            yield

    a, b = ways[0][0][0], ways[0][1][0]
    me = (((c * 2 + z) * 4 + b) * 4 + a, ((c * 2 + z) * 4 + a) * 4 + b)
    me_row = ((z * 4 + b) * 4 + a) * 4

    def residual():
        loads[0].wait()
        wide_r = resid_ref[...].astype(F32)
        ordered = []
        for p in range(4):
            chosen = wide_r[0:1]
            for r in range(1, 4):
                chosen = jnp.where(assign_ref[p] == r, wide_r[r : r + 1], chosen)
            ordered.append(chosen)
        ordered = jnp.concatenate(ordered, axis=0)
        s1f[...] = jnp.zeros_like(s1f)
        for n in range(8):
            for t in range(8):
                first = n * 896 + t * COLS
                s1f[n, (t % 4) * 4 : (t % 4) * 4 + 4, (t // 4) * 128 : (t // 4) * 128 + COLS] = ordered[
                    :, first : first + COLS
                ]
        s1[...] = s1f[...].astype(BF16)
        push(s1, s1_got, rs_sem, rr_sem, 1, partner)
        yield
        landed(s1_got, rs_sem, rr_sem, 1)
        row = lax.rem(lax.broadcasted_iota(jnp.int32, (8, 16, 256), 1), 4)
        served = jnp.where(jnp.where(row < 2, swaps[0], swaps[1]) == 1, s1_got[...], s1[...])
        s1_got[...] = served
        t1[attn] = s1_got[attn]
        for k in range(1, 8):
            to = lax.rem(attn + k, 8)
            push(s1_got.at[to], t1.at[attn], rs_sem, rr_sem, 1 + k, (to, grp, tp))
        yield
        for k in range(1, 8):
            landed(t1.at[lax.rem(attn + 8 - k, 8)], rs_sem, rr_sem, 1 + k)
        for n in range(8):
            part = t1[n].astype(F32)
            for t in range(8):
                uf[t, n * 4 : n * 4 + 4, :] = part[
                    (t % 4) * 4 : (t % 4) * 4 + 4, (t // 4) * 128 : (t // 4) * 128 + 128
                ]
        ub[...] = uf[...].astype(BF16)
        vb[tp] = ub[tp]
        for k in range(1, 8):
            to = lax.rem(tp + k, 8)
            push(ub.at[to], vb.at[tp], rs_sem, rr_sem, 8 + k, (attn, grp, to))
        yield
        for k in range(1, 8):
            landed(vb.at[lax.rem(tp + 8 - k, 8)], rs_sem, rr_sem, 8 + k)
        for t in range(8):
            part = vb[t].astype(F32)
            for n in range(8):
                plane, zv = t % 2, n % 2
                bv, av = (n // 2, t // 2) if plane else (t // 2, n // 2)
                place = (((plane * 2 + zv) * 4 + bv) * 4 + av) * 4
                wf[place : place + 4, :] = part[n * 4 : n * 4 + 4]
        wt[...] = wf[...].T
        yield

    def scaling():
        for i in (1, 2, 3):
            loads[i].wait()

        def scale(i, _):
            rows = pl.ds(pl.multiple_of(i * 16, 16), 16)
            for k, src in enumerate((wg, wu)):
                spot = pl.ds(pl.multiple_of(k * FH + i * 16, 16), 16)
                wide = (src[rows, :].astype(F32) * gain_ref[...]).astype(BF16)
                for cv in range(2):
                    for xv in range(4):
                        first = [
                            ((xv // 2 * 4 + x2 * 2 + xv % 2) * 8 + yv * 2 + cv) * COLS
                            for x2 in range(2)
                            for yv in range(4)
                        ]
                        w2[cv, spot, xv * 896 : (xv + 1) * 896] = jnp.concatenate(
                            [wide[:, f : f + COLS] for f in first], axis=1
                        )
            return 0

        for part in range(6):
            lax.fori_loop(part * 3, part * 3 + 3, scale, 0)
            yield

    for m in range(2):
        flags[m * 8 : m * 8 + 8, :] = jnp.full((8, 128), swaps[m], jnp.int32).astype(F32)
    flag_out[...] = flags[...].astype(BF16)
    for hh in range(2):
        push(own_b.at[hh], got_b.at[hh], rs_sem, rr_sem, 20 * hh, partner)
    push(flag_out, flag_in, rs_sem, rr_sem, 21, z_peer)
    for hh in range(2):
        push(own_b.at[hh], cross_b.at[hh], rs_sem, rr_sem, 22 + hh, cross)
        push(own_b.at[hh], peer_b.at[hh], rs_sem, rr_sem, 24 + hh, z_peer)
    residual_steps, scaling_steps = residual(), scaling()
    next(residual_steps)
    next(scaling_steps)
    row = lax.broadcasted_iota(jnp.int32, (64, 256), 0)

    def gather_context(hh):
        way = ways[hh]

        def ready(p):
            for half in range(2):
                sf[half] = cb[hh, zs[p], :, :, half * 128 : (half + 1) * 128].astype(F32).reshape(256, 128)
            for h in range(16):
                for half in range(2):
                    first = h * 256 + half * 128
                    ctx_all[hh, (c * 2 + zs[p]) * 4 + way[1][0], :, first : first + 128] = sf[
                        half, pl.ds(h, 16, stride=16), :
                    ].astype(BF16)

        landed(got_b.at[hh], rs_sem, rr_sem, 20 * hh)
        cb[hh, z, way[0][0]] = jnp.where(
            jnp.where(row < 32, swaps[0], swaps[1]) == 1, got_b[hh], own_b[hh]
        )

        def peer():
            if hh == 0:
                landed(flag_in, rs_sem, rr_sem, 21)
            landed(cross_b.at[hh], rs_sem, rr_sem, 22 + hh)
            landed(peer_b.at[hh], rs_sem, rr_sem, 24 + hh)
            wide = flag_in[...].astype(F32)
            flag = jnp.concatenate(
                [jnp.broadcast_to(wide[m * 8 : m * 8 + 1], (32, 128)) for m in range(2)], axis=0
            )
            flag = jnp.concatenate([flag, flag], axis=1)
            theirs = jnp.where(flag > 0.5, cross_b[hh].astype(F32), peer_b[hh].astype(F32))
            cb[hh, zo, way[0][0]] = theirs.astype(BF16)

        yield from gather(
            way,
            lambda p, av: cb.at[hh, zs[p], av],
            lambda p, bv: ctx_all.at[hh, (c * 2 + zs[p]) * 4 + bv],
            lambda zv, bv: ctx_all.at[hh, (co * 2 + zv) * 4 + bv],
            bs_sem,
            br_sem,
            ready,
            21 * hh,
            peer,
        )

    steps = (gather_context(0), gather_context(1))

    def both(pair):
        for one in pair:
            next(one)

    both(steps)
    next(residual_steps)
    both(steps)
    next(scaling_steps)
    both(steps)
    next(residual_steps)
    next(scaling_steps)
    both(steps)
    next(scaling_steps)
    both(steps)
    next(scaling_steps)
    next(residual_steps)
    next(scaling_steps)
    both(steps)
    loads[4].wait()

    def project(plane):
        def rows(hh, cols):
            return ctx_all[hh, pl.ds(plane * 8, 8), :, cols].reshape(128, 1024)

        def step(i, sums):
            cols = pl.ds(pl.multiple_of(i * 1024, 1024), 1024)
            last = pl.ds(pl.multiple_of(i * 1024 + CW // 2, 1024), 1024)
            one = lax.dot_general(wo[:, cols], rows(0, cols), NT, preferred_element_type=F32)
            two = lax.dot_general(rows(1, cols), wo[:, last], NT, preferred_element_type=F32)
            return sums[0] + one, sums[1] + two

        one, two = lax.fori_loop(
            0, CW // 2048, step, (jnp.zeros((COLS, 128), F32), jnp.zeros((128, COLS), F32))
        )
        for zv in range(2):
            for i in range(4):
                for j in range(4):
                    src, dst = ((zv * 4 + i) * 4 + j) * 4, ((zv * 4 + j) * 4 + i) * 4
                    turned[dst : dst + 4, :COLS] = two[src : src + 4]
        lanes = pl.ds(pl.multiple_of(plane * 128, 128), 128)
        return (wt[:COLS, lanes] + (one + turned[...].T[:COLS])).astype(BF16)

    def gather_hidden(i):
        half = (c, co)[i]
        return gather(
            ways[i],
            lambda p, av: ht.at[half, ((c * 2 + zs[p]) * 4 + ways[i][1][0]) * 4 + av],
            lambda p, bv: ht.at[half, pl.ds(((c * 2 + zs[p]) * 4 + bv) * 4, 4)],
            lambda zv, bv: ht.at[(co, c)[i], pl.ds(((co * 2 + zv) * 4 + bv) * 4, 4)],
            cs_sem,
            cr_sem,
            lambda p: None,
            21 * i,
        )

    early, late = gather_hidden(0), gather_hidden(1)

    def features(plane, half, n):
        parts = []
        for x2 in range(2):
            for yv in range(4):
                xv = n // 2 * 2 + x2
                bv, av = yv * (1 - half) + xv * half, xv * (1 - half) + yv * half
                parts.append(ht[half, ((plane * 2 + lax.rem(n, 2)) * 4 + bv) * 4 + av])
        return jnp.concatenate(parts, axis=0)

    def expand(plane, i, *ps):
        half = (c, co)[i]

        def step(k, total):
            n = (k // len(ps)) * 2 + (zs[ps[0]] if len(ps) == 1 else lax.rem(k, 2))
            cols = pl.ds(pl.multiple_of(n * 896, 128), 896)
            part = features(plane, half, n)
            acc[i] += jnp.dot(w2[plane, :, cols], part, preferred_element_type=F32)
            wide = part.astype(F32)
            return total + jnp.sum((wide * wide).reshape(112, 8, 128), axis=0)

        squares[i] += lax.fori_loop(0, 2 * len(ps), step, jnp.zeros((8, 128), F32))

    def activate(i):
        factor = lax.rsqrt(jnp.sum(squares[i], axis=0, keepdims=True) * (1.0 / D) + 1e-5)
        gate = acc[i, :FH] * factor
        act = gate / (1.0 + jnp.exp(-gate)) * (acc[i, FH:] * factor)
        return act.T.astype(BF16)

    ht[c, me[0]] = project(c)
    next(early)
    both(steps)
    both(steps)
    ht[co, me[1]] = project(co)
    next(late)
    acc[...] = jnp.zeros_like(acc)
    squares[...] = jnp.zeros_like(squares)
    before = len(started)
    for i in range(4):
        next(early)
        next(late)
        if i == 0:
            drain(len(started) - before)
    next(early)
    expand(c, 0, 0, 1)
    next(late)
    next(early)
    next(early)
    expand(co, 1, 0, 1)
    expand(c, 1, 0, 1)
    act_out[...] = activate(1)
    push(act_out, act_in, rs_sem, rr_sem, 19, sibling)
    next(late)
    expand(co, 0, 0)
    next(late)
    expand(co, 0, 1)

    act_own = activate(0)
    loads[5].wait()
    landed(wd.at[pl.ds(FH, FH)], rs_sem, rr_sem, 18)
    landed(act_in, rs_sem, rr_sem, 19)
    lhs = jnp.concatenate([act_own, act_in[...]], axis=1)

    def other_order():
        wide_lhs = lhs.astype(F32)
        for zv in range(2):
            for i in range(4):
                for j in range(4):
                    src, dst = ((zv * 4 + i) * 4 + j) * 4, ((zv * 4 + j) * 4 + i) * 4
                    lhs_f[dst : dst + 4, :] = wide_lhs[src : src + 4]
        return lhs_f[...].astype(BF16)

    def reduction(h):
        rows = other_order() if h else lhs
        ak, (b, b1, b2, b3), a_other, b_other = ways[h]
        a, b_right, b_left = ak[0], b_other[1], b_other[3]
        for j in range(2):
            cols = pl.ds(j * 1792, 1792)
            part = jnp.dot(rows, wd[:, pl.ds(h * 3584 + j * 1792, 1792)], preferred_element_type=F32)
            p_own[h, :, :, cols] = part.astype(BF16).reshape(8, 16, 1792)

        def slab(p, k):
            return p_own.at[h, zs[p] * 4 + k]

        def send(ref, i, to):
            push(ref, r2.at[h, i], ds_sem, dr_sem, 2 + 6 * h + i, to)

        def wait(i):
            landed(r2.at[h, i], ds_sem, dr_sem, 2 + 6 * h + i)

        send(slab(0, b2), 0, b_left)
        send(slab(1, b2), 1, b_right)
        send(slab(1, b3), 3, b_left)
        send(slab(0, b1), 4, b_right)
        yield
        for i, p, k, to, j in ((0, 0, b3, b_left, 2), (1, 1, b1, b_right, 5)):
            wait(i)
            ref = slab(p, k)
            ref[...] = (ref[...].astype(F32) + r2[h, i].astype(F32)).astype(BF16)
            send(ref, j, to)
        yield
        for i in (3, 4, 2, 5):
            wait(i)
        for p in (1, 0):
            total = (
                p_own[h, zs[p] * 4 + b].astype(F32) + r2[h, 2 + p].astype(F32) + r2[h, 4 + p].astype(F32)
            )
            for av in range(4):
                for q in range(4):
                    qf[av, q * 4 : q * 4 + 4, :] = total[av * 4 : av * 4 + 4, q * 896 : (q + 1) * 896]
            qb[h, p] = qf[...].astype(BF16)
            for k in (1, 3, 2):
                push(
                    qb.at[h, p, ak[k]], r1.at[h, p, k - 1], ds_sem, dr_sem, 13 + 6 * h + 3 * p + k, a_other[k]
                )
        yield
        sums = []
        for p in (1, 0):
            total = qb[h, p, a].astype(F32)
            for k in (1, 3, 2):
                landed(r1.at[h, p, k - 1], ds_sem, dr_sem, 13 + 6 * h + 3 * p + k)
                total = total + r1[h, p, k - 1].astype(F32)
            sums.append(total)
            if p == 1:
                tz[h] = total.astype(BF16)
                push(tz.at[h], got_peer.at[h], ds_sem, dr_sem, 26 + 3 * h, z_peer)
                push(tz.at[h], got_cross.at[h], ds_sem, dr_sem, 27 + 3 * h, cross)
        tp0[h] = sums[1].astype(BF16)
        push(tp0.at[h], got_partner.at[h], ds_sem, dr_sem, 28 + 3 * h, partner)
        t0[h] = sums[1]
        yield
        landed(got_partner.at[h], ds_sem, dr_sem, 28 + 3 * h)
        landed(got_cross.at[h], ds_sem, dr_sem, 27 + 3 * h)
        landed(got_peer.at[h], ds_sem, dr_sem, 26 + 3 * h)
        stayed = hid[h].astype(F32) + (t0[h] + got_peer[h].astype(F32))
        moved = hid_got[h].astype(F32) + (got_partner[h].astype(F32) + got_cross[h].astype(F32))
        row = lax.rem(lax.broadcasted_iota(jnp.int32, (16, 896), 0), 4)
        final = jnp.where(jnp.where(row < 2, swaps[0], swaps[1]) == 1, moved, stayed)
        request = lax.broadcasted_iota(jnp.int32, (4, 896), 0)
        for q in range(4):
            rows = jnp.zeros((4, 896), F32)
            for p in range(4):
                one = jnp.broadcast_to(final[q * 4 + p : q * 4 + p + 1], (4, 896))
                rows = jnp.where(request == assign_ref[p], one, rows)
            out_ref[:, h * 3584 + q * 896 : h * 3584 + (q + 1) * 896] = rows.astype(BF16)
        yield

    def own_hidden(h):
        lane = lax.broadcasted_iota(jnp.int32, (16, 128), 1)
        sub = lax.broadcasted_iota(jnp.int32, (16, 128), 0)
        rows = jnp.zeros((16, 896), F32)
        for q in range(4):
            pick = jnp.where(lane == me_row + sub - q * 4, 1.0, 0.0)
            pick = jnp.where((sub >= q * 4) & (sub < q * 4 + 4), pick, 0.0).astype(BF16)
            xv, zv = 2 * h + q // 2, q % 2
            parts = []
            for yv in range(4):
                for plane in range(2):
                    bv, av = yv * co + xv * c, xv * co + yv * c
                    parts.append(ht[c, ((plane * 2 + zv) * 4 + bv) * 4 + av])
            rows = rows + lax.dot_general(
                pick, jnp.concatenate(parts, axis=0), NT, preferred_element_type=F32
            )
        hid[h] = rows.astype(BF16)
        push(hid.at[h], hid_got.at[h], rs_sem, rr_sem, 16 + h, partner)

    halves = (reduction(0), reduction(1))
    before = len(started)
    for half in halves:
        next(half)
    own_hidden(0)
    drain(len(started) - before)
    next(halves[0])
    own_hidden(1)
    next(halves[1])
    for _ in range(2):
        for half in halves:
            next(half)
    for h in range(2):
        landed(hid_got.at[h], rs_sem, rr_sem, 16 + h)
    for half in halves:
        next(half)
    drain()


def per_device(
    queries, keys, values, lengths, resid, assign, matching, w_out, gain, gate_w, up_w, down_w
):
    smem = pl.BlockSpec(memory_space=pltpu.SMEM)
    vmem = pl.BlockSpec(memory_space=pltpu.VMEM)
    hbm = pl.BlockSpec(memory_space=pl.ANY)
    dma = pltpu.SemaphoreType.DMA
    scratch = (
        ((4, CW), BF16),
        ((4, 1024, 256), BF16),
        ((4, 1024, 256), BF16),
        ((COLS, CW), BF16),
        ((FH, D), BF16),
        ((FH, D), BF16),
        ((2, 2 * FH, D // 2), BF16),
        ((2 * FH, D), BF16),
        ((4, D), BF16),
        ((1, D), F32),
        ((2, 128, 128), F32),
        ((2, 64, 256), BF16),
        ((2, 64, 256), BF16),
        ((2, 64, 256), BF16),
        ((2, 64, 256), BF16),
        ((16, 128), F32),
        ((16, 128), BF16),
        ((16, 128), BF16),
        ((2, 2, 4, 64, 256), BF16),
        ((2, 256, 128), F32),
        ((2, 16, 16, CW // 2), BF16),
        ((2, 64, COLS, 128), BF16),
        ((2, 2 * FH, 128), F32),
        ((2, 8, 128), F32),
        ((128, FH), BF16),
        ((128, FH), BF16),
        ((8, 16, 256), F32),
        ((8, 16, 256), BF16),
        ((8, 16, 256), BF16),
        ((8, 16, 256), BF16),
        ((8, 32, 128), F32),
        ((8, 32, 128), BF16),
        ((8, 32, 128), BF16),
        ((256, 128), F32),
        ((128, 256), F32),
        ((128, 128), F32),
        ((128, 2 * FH), F32),
        ((2, 8, 16, D // 2), BF16),
        ((2, 6, 16, D // 2), BF16),
        ((4, 16, 896), F32),
        ((2, 2, 4, 16, 896), BF16),
        ((2, 2, 3, 16, 896), BF16),
        ((2, 16, 896), F32),
    ) + (((2, 16, 896), BF16),) * 7
    return pl.pallas_call(
        kernel,
        out_shape=pltpu.VMEM((4, D), BF16),
        in_specs=[smem] * 3 + [hbm] * 9,
        out_specs=vmem,
        scratch_shapes=[pltpu.VMEM(shape, dtype) for shape, dtype in scratch]
        + [dma((n,)) for n in (8, 7, 42, 42, 42, 42, 32, 32, 26, 26)],
        compiler_params=pltpu.CompilerParams(
            collective_id=0, has_side_effects=True, vmem_limit_bytes=60 * 1024 * 1024
        ),
    )(
        lengths, assign[0], matching[:, 0, 0], queries, resid, gain[None],
        keys, values, w_out.T, gate_w[0].T, up_w[0].T, down_w[0],
    )


def solution(mesh):
    rows = P(("attn", "grp", "tp"), None)
    cache = P(("attn", "grp", "tp"), None, None)
    placed = (
        rows,
        cache,
        cache,
        P(("attn", "grp", "tp")),
        rows,
        rows,
        P(None, "attn", "tp"),
        P(None, ("attn", "tp")),
        P(),
        P("grp", None, ("attn", "tp")),
        P("grp", None, ("attn", "tp")),
        P("grp", ("attn", "tp"), None),
    )
    return jax.shard_map(
        per_device, mesh=mesh, in_specs=placed, out_specs=rows, check_vma=False
    )
```

```python
import jax
import jax.numpy as jnp
from jax import lax
from jax.experimental import pallas as pl
from jax.experimental.pallas import tpu as pltpu
from jax.sharding import PartitionSpec as P

D = 7168
CW = 8192
FH = 288
COLS = 112
MESH = pl.DeviceIdType.MESH
F32 = jnp.float32
BF16 = jnp.bfloat16
NT = (((1,), (1,)), ((), ()))


def kernel(
    len_ref, assign_ref, match_ref, q_hbm, resid_hbm, gain_hbm, k_hbm, v_hbm, wo_hbm, g_hbm, u_hbm, d_hbm,
    out_ref,
    q_ref, kc, vc, wo, wg, wu, w2, wd, resid_ref, gain_ref,
    qs, own_b, got_b, cross_b, peer_b, flags, flag_out, flag_in, cb, sf, ctx_all, ht, acc, squares, act_out, act_in,
    s1f, s1, s1_got, t1, uf, ub, vb, wf, wt, turned, lhs_f,
    p_own, r2, qf, qb, r1, t0, tp0, tz, got_peer, got_partner, got_cross, hid, hid_got,
    kv_sem, w_sem, bs_sem, br_sem, cs_sem, cr_sem, ds_sem, dr_sem, rs_sem, rr_sem,
):
    attn, grp, tp = lax.axis_index("attn"), lax.axis_index("grp"), lax.axis_index("tp")
    x, z, y, c = attn // 2, lax.rem(attn, 2), tp // 2, lax.rem(tp, 2)
    zo, co = 1 - z, 1 - c
    zs = (z, zo)
    def dev(x_, z_, y_, c_):
        return (lax.rem(x_, 4) * 2 + z_, grp, lax.rem(y_, 4) * 2 + c_)

    z_peer, sibling = dev(x, zo, y, c), dev(x, z, y, co)
    partner = (attn, 1 - grp, tp)
    cross = (x * 2 + zo, 1 - grp, tp)

    def axes(e):
        a, b = x * (1 - e) + y * e, y * (1 - e) + x * e
        return (
            [lax.rem(a + k, 4) for k in range(4)],
            [lax.rem(b + k, 4) for k in range(4)],
            [dev(x + k * (1 - e), z, y + k * e, c) for k in range(4)],
            [dev(x + k * e, z, y + k * (1 - e), c) for k in range(4)],
        )

    ways = (axes(c), axes(co))

    q_load = pltpu.make_async_copy(q_hbm, q_ref, w_sem.at[6])
    q_load.start()
    fetch = []
    for src, dst in ((k_hbm, kc), (v_hbm, vc)):
        for r in range(4):
            fetch.append(pltpu.make_async_copy(src.at[r], dst.at[r], kv_sem.at[len(fetch)]))
            fetch[-1].start()
    loads = [
        pltpu.make_async_copy(src, dst, w_sem.at[i])
        for i, (src, dst) in enumerate(
            ((resid_hbm, resid_ref), (gain_hbm, gain_ref), (g_hbm, wg), (u_hbm, wu), (wo_hbm, wo), (d_hbm, wd.at[pl.ds(0, FH)]))
        )
    ]
    barrier = pltpu.get_barrier_semaphore()
    others = [partner, cross]
    for k in range(1, 8):
        others.append((lax.rem(attn + k, 8), grp, tp))
        others.append((attn, grp, lax.rem(tp + k, 8)))
    for other in others:
        pl.semaphore_signal(barrier, inc=1, device_id=other, device_id_type=MESH)

    started = []

    def drain(keep=0):
        while len(started) > keep:
            started.pop(0).wait_send()

    def push(src, dst, s_sem, r_sem, i, to):
        copy = pltpu.make_async_remote_copy(
            src_ref=src, dst_ref=dst, send_sem=s_sem.at[i], recv_sem=r_sem.at[i],
            device_id=to, device_id_type=MESH,
        )
        copy.start()
        started.append(copy)

    def landed(dst, s_sem, r_sem, i):
        pltpu.make_async_remote_copy(
            src_ref=dst, dst_ref=dst, send_sem=s_sem.at[i], recv_sem=r_sem.at[i],
            device_id=sibling, device_id_type=MESH,
        ).wait_recv()

    q_load.wait()
    wide_q = q_ref[...].astype(F32)
    for h in range(32):
        for half in range(2):
            first = h * 256 + half * 128
            qs[half, pl.ds(h, 4, stride=32), :] = wide_q[:, first : first + 128]
    slot = lax.broadcasted_iota(jnp.int32, (32, 1024), 1)
    swaps = (match_ref[0], match_ref[1])

    def weigh(r):
        query = jnp.concatenate([qs[half, r * 32 : (r + 1) * 32] for half in range(2)], axis=1).astype(BF16)
        scores = lax.dot_general(query, kc[r], NT, preferred_element_type=F32) * (256 ** -0.5)
        scores = jnp.where(slot < len_ref[r], scores, -1e30)
        expo = jnp.exp(scores - jnp.max(scores, axis=-1, keepdims=True))
        return (expo / jnp.sum(expo, axis=-1, keepdims=True)).astype(BF16)

    for copy in fetch[:4]:
        copy.wait()
    for load in loads:
        load.start()
    pl.semaphore_wait(barrier, 16)
    push(d_hbm, wd.at[pl.ds(FH, FH)], rs_sem, rr_sem, 18, sibling)
    probs = [weigh(r) for r in range(4)]
    for copy in fetch[4:]:
        copy.wait()
    contexts = [jnp.dot(probs[r], vc[r], preferred_element_type=F32) for r in range(4)]
    for p in range(4):
        chosen = contexts[0]
        for r in range(1, 4):
            chosen = jnp.where(assign_ref[p] == r, contexts[r], chosen)
        for hh in range(2):
            own_b[hh, p * 16 : p * 16 + 16] = chosen[hh * 16 : hh * 16 + 16].astype(BF16)

    def gather(way, block, part, other, s_sem, r_sem, ready, base, peer=None):
        ak, bk, a_other, b_other = way
        a, (b, b1, b2, b3) = ak[0], bk
        b_right, b_left = b_other[1], b_other[3]

        def send(ref, i, to):
            push(ref, ref, s_sem, r_sem, base + i, to)

        def wait(ref, i):
            landed(ref, s_sem, r_sem, base + i)

        def ring_1(p):
            for k in (1, 3, 2):
                send(block(p, a), 3 * p + k, a_other[k])

        def ring_2(p):
            for k in (1, 3, 2):
                wait(block(p, ak[4 - k]), 3 * p + k)
            ready(p)
            first, second = ((7, b_right), (8, b_left)) if p == 0 else ((10, b_left), (9, b_right))
            send(part(p, b), *first)
            send(part(p, b), *second)
            send(part(p, b), 13 + p, sibling)

        if peer is None:
            send(block(0, a), 0, z_peer)
        ring_1(0)
        yield
        if peer is None:
            ring_2(0)
            wait(block(1, a), 0)
            ring_1(1)
        else:
            peer()
            ring_1(1)
            ring_2(0)
        yield
        ring_2(1)
        yield
        wait(part(0, b3), 7)
        send(part(0, b3), 11, b_right)
        send(part(0, b3), 15, sibling)
        wait(part(0, b1), 8)
        send(part(0, b1), 16, sibling)
        yield
        wait(part(1, b1), 10)
        send(part(1, b1), 12, b_left)
        send(part(1, b1), 17, sibling)
        wait(part(1, b3), 9)
        send(part(1, b3), 18, sibling)
        yield
        wait(part(0, b2), 11)
        send(part(0, b2), 19, sibling)
        wait(part(1, b2), 12)
        send(part(1, b2), 20, sibling)
        yield
        for p, spots in enumerate((((13, 0), (15, 3), (16, 1), (19, 2)), ((14, 0), (18, 3), (17, 1), (20, 2)))):
            for i, k in spots:
                wait(other(zs[p], ak[k]), i)
            yield

    a, b = ways[0][0][0], ways[0][1][0]
    me = (((c * 2 + z) * 4 + b) * 4 + a, ((c * 2 + z) * 4 + a) * 4 + b)
    me_row = ((z * 4 + b) * 4 + a) * 4

    def residual():
        loads[0].wait()
        wide_r = resid_ref[...].astype(F32)
        ordered = []
        for p in range(4):
            chosen = wide_r[0:1]
            for r in range(1, 4):
                chosen = jnp.where(assign_ref[p] == r, wide_r[r : r + 1], chosen)
            ordered.append(chosen)
        ordered = jnp.concatenate(ordered, axis=0)
        s1f[...] = jnp.zeros_like(s1f)
        for n in range(8):
            for t in range(8):
                first = n * 896 + t * COLS
                s1f[n, (t % 4) * 4 : (t % 4) * 4 + 4, (t // 4) * 128 : (t // 4) * 128 + COLS] = ordered[
                    :, first : first + COLS
                ]
        s1[...] = s1f[...].astype(BF16)
        push(s1, s1_got, rs_sem, rr_sem, 1, partner)
        yield
        landed(s1_got, rs_sem, rr_sem, 1)
        row = lax.rem(lax.broadcasted_iota(jnp.int32, (8, 16, 256), 1), 4)
        served = jnp.where(jnp.where(row < 2, swaps[0], swaps[1]) == 1, s1_got[...], s1[...])
        s1_got[...] = served
        t1[attn] = s1_got[attn]
        for k in range(1, 8):
            to = lax.rem(attn + k, 8)
            push(s1_got.at[to], t1.at[attn], rs_sem, rr_sem, 1 + k, (to, grp, tp))
        yield
        for k in range(1, 8):
            landed(t1.at[lax.rem(attn + 8 - k, 8)], rs_sem, rr_sem, 1 + k)
        for n in range(8):
            part = t1[n].astype(F32)
            for t in range(8):
                uf[t, n * 4 : n * 4 + 4, :] = part[
                    (t % 4) * 4 : (t % 4) * 4 + 4, (t // 4) * 128 : (t // 4) * 128 + 128
                ]
        ub[...] = uf[...].astype(BF16)
        vb[tp] = ub[tp]
        for k in range(1, 8):
            to = lax.rem(tp + k, 8)
            push(ub.at[to], vb.at[tp], rs_sem, rr_sem, 8 + k, (attn, grp, to))
        yield
        for k in range(1, 8):
            landed(vb.at[lax.rem(tp + 8 - k, 8)], rs_sem, rr_sem, 8 + k)
        for t in range(8):
            part = vb[t].astype(F32)
            for n in range(8):
                plane, zv = t % 2, n % 2
                bv, av = (n // 2, t // 2) if plane else (t // 2, n // 2)
                place = (((plane * 2 + zv) * 4 + bv) * 4 + av) * 4
                wf[place : place + 4, :] = part[n * 4 : n * 4 + 4]
        wt[...] = wf[...].T
        yield

    def scaling():
        for i in (1, 2, 3):
            loads[i].wait()

        def scale(i, _):
            rows = pl.ds(pl.multiple_of(i * 16, 16), 16)
            for k, src in enumerate((wg, wu)):
                spot = pl.ds(pl.multiple_of(k * FH + i * 16, 16), 16)
                wide = (src[rows, :].astype(F32) * gain_ref[...]).astype(BF16)
                for cv in range(2):
                    for xv in range(4):
                        first = [
                            ((xv // 2 * 4 + x2 * 2 + xv % 2) * 8 + yv * 2 + cv) * COLS
                            for x2 in range(2)
                            for yv in range(4)
                        ]
                        w2[cv, spot, xv * 896 : (xv + 1) * 896] = jnp.concatenate(
                            [wide[:, f : f + COLS] for f in first], axis=1
                        )
            return 0

        for part in range(6):
            lax.fori_loop(part * 3, part * 3 + 3, scale, 0)
            yield

    for m in range(2):
        flags[m * 8 : m * 8 + 8, :] = jnp.full((8, 128), swaps[m], jnp.int32).astype(F32)
    flag_out[...] = flags[...].astype(BF16)
    for hh in range(2):
        push(own_b.at[hh], got_b.at[hh], rs_sem, rr_sem, 20 * hh, partner)
    push(flag_out, flag_in, rs_sem, rr_sem, 21, z_peer)
    for hh in range(2):
        push(own_b.at[hh], cross_b.at[hh], rs_sem, rr_sem, 22 + hh, cross)
        push(own_b.at[hh], peer_b.at[hh], rs_sem, rr_sem, 24 + hh, z_peer)
    residual_steps, scaling_steps = residual(), scaling()
    next(residual_steps)
    next(scaling_steps)
    row = lax.broadcasted_iota(jnp.int32, (64, 256), 0)

    def gather_context(hh):
        way = ways[hh]

        def ready(p):
            for half in range(2):
                sf[half] = cb[hh, zs[p], :, :, half * 128 : (half + 1) * 128].astype(F32).reshape(256, 128)
            for h in range(16):
                for half in range(2):
                    first = h * 256 + half * 128
                    ctx_all[hh, (c * 2 + zs[p]) * 4 + way[1][0], :, first : first + 128] = sf[
                        half, pl.ds(h, 16, stride=16), :
                    ].astype(BF16)

        landed(got_b.at[hh], rs_sem, rr_sem, 20 * hh)
        cb[hh, z, way[0][0]] = jnp.where(
            jnp.where(row < 32, swaps[0], swaps[1]) == 1, got_b[hh], own_b[hh]
        )

        def peer():
            if hh == 0:
                landed(flag_in, rs_sem, rr_sem, 21)
            landed(cross_b.at[hh], rs_sem, rr_sem, 22 + hh)
            landed(peer_b.at[hh], rs_sem, rr_sem, 24 + hh)
            wide = flag_in[...].astype(F32)
            flag = jnp.concatenate(
                [jnp.broadcast_to(wide[m * 8 : m * 8 + 1], (32, 128)) for m in range(2)], axis=0
            )
            flag = jnp.concatenate([flag, flag], axis=1)
            theirs = jnp.where(flag > 0.5, cross_b[hh].astype(F32), peer_b[hh].astype(F32))
            cb[hh, zo, way[0][0]] = theirs.astype(BF16)

        yield from gather(
            way,
            lambda p, av: cb.at[hh, zs[p], av],
            lambda p, bv: ctx_all.at[hh, (c * 2 + zs[p]) * 4 + bv],
            lambda zv, bv: ctx_all.at[hh, (co * 2 + zv) * 4 + bv],
            bs_sem,
            br_sem,
            ready,
            21 * hh,
            peer,
        )

    steps = (gather_context(0), gather_context(1))

    def both(pair):
        for one in pair:
            next(one)

    both(steps)
    next(residual_steps)
    both(steps)
    next(scaling_steps)
    both(steps)
    next(residual_steps)
    next(scaling_steps)
    both(steps)
    next(scaling_steps)
    both(steps)
    next(scaling_steps)
    next(residual_steps)
    next(scaling_steps)
    both(steps)
    loads[4].wait()

    def project(plane, arrive):
        def rows(hh, cols):
            return ctx_all[hh, pl.ds(plane * 8, 8), :, cols].reshape(128, 1024)

        def first(i, total):
            cols = pl.ds(pl.multiple_of(i * 1024, 1024), 1024)
            return total + lax.dot_general(wo[:, cols], rows(0, cols), NT, preferred_element_type=F32)

        def second(i, total):
            cols = pl.ds(pl.multiple_of(i * 1024, 1024), 1024)
            last = pl.ds(pl.multiple_of(i * 1024 + CW // 2, 1024), 1024)
            return total + lax.dot_general(rows(1, cols), wo[:, last], NT, preferred_element_type=F32)

        arrive(0)
        one = lax.fori_loop(0, CW // 2048, first, jnp.zeros((COLS, 128), F32))
        arrive(1)
        two = lax.fori_loop(0, CW // 2048, second, jnp.zeros((128, COLS), F32))
        for zv in range(2):
            for i in range(4):
                for j in range(4):
                    src, dst = ((zv * 4 + i) * 4 + j) * 4, ((zv * 4 + j) * 4 + i) * 4
                    turned[dst : dst + 4, :COLS] = two[src : src + 4]
        lanes = pl.ds(pl.multiple_of(plane * 128, 128), 128)
        return (wt[:COLS, lanes] + (one + turned[...].T[:COLS])).astype(BF16)

    def gather_hidden(i):
        half = (c, co)[i]
        return gather(
            ways[i],
            lambda p, av: ht.at[half, ((c * 2 + zs[p]) * 4 + ways[i][1][0]) * 4 + av],
            lambda p, bv: ht.at[half, pl.ds(((c * 2 + zs[p]) * 4 + bv) * 4, 4)],
            lambda zv, bv: ht.at[(co, c)[i], pl.ds(((co * 2 + zv) * 4 + bv) * 4, 4)],
            cs_sem,
            cr_sem,
            lambda p: None,
            21 * i,
        )

    early, late = gather_hidden(0), gather_hidden(1)

    def features(plane, half, n):
        parts = []
        for x2 in range(2):
            for yv in range(4):
                xv = n // 2 * 2 + x2
                bv, av = yv * (1 - half) + xv * half, xv * (1 - half) + yv * half
                parts.append(ht[half, ((plane * 2 + lax.rem(n, 2)) * 4 + bv) * 4 + av])
        return jnp.concatenate(parts, axis=0)

    def expand(plane, i, *ps):
        half = (c, co)[i]

        def step(k, total):
            n = (k // len(ps)) * 2 + (zs[ps[0]] if len(ps) == 1 else lax.rem(k, 2))
            cols = pl.ds(pl.multiple_of(n * 896, 128), 896)
            part = features(plane, half, n)
            acc[i] += jnp.dot(w2[plane, :, cols], part, preferred_element_type=F32)
            wide = part.astype(F32)
            return total + jnp.sum((wide * wide).reshape(112, 8, 128), axis=0)

        squares[i] += lax.fori_loop(0, 2 * len(ps), step, jnp.zeros((8, 128), F32))

    def activate(i):
        factor = lax.rsqrt(jnp.sum(squares[i], axis=0, keepdims=True) * (1.0 / D) + 1e-5)
        gate = acc[i, :FH] * factor
        act = gate / (1.0 + jnp.exp(-gate)) * (acc[i, FH:] * factor)
        return act.T.astype(BF16)

    ht[c, me[0]] = project(c, lambda hh: None)
    next(early)
    ht[co, me[1]] = project(co, lambda hh: (next(steps[hh]), next(steps[hh])))
    next(late)
    acc[...] = jnp.zeros_like(acc)
    squares[...] = jnp.zeros_like(squares)
    before = len(started)
    for i in range(4):
        next(early)
        next(late)
        if i == 0:
            drain(len(started) - before)
    next(early)
    expand(c, 0, 0, 1)
    next(late)
    next(early)
    next(early)
    expand(co, 1, 0, 1)
    expand(c, 1, 0, 1)
    act_out[...] = activate(1)
    push(act_out, act_in, rs_sem, rr_sem, 19, sibling)
    next(late)
    expand(co, 0, 0)
    next(late)
    expand(co, 0, 1)

    act_own = activate(0)
    loads[5].wait()
    landed(wd.at[pl.ds(FH, FH)], rs_sem, rr_sem, 18)
    landed(act_in, rs_sem, rr_sem, 19)
    lhs = jnp.concatenate([act_own, act_in[...]], axis=1)

    def other_order():
        wide_lhs = lhs.astype(F32)
        for zv in range(2):
            for i in range(4):
                for j in range(4):
                    src, dst = ((zv * 4 + i) * 4 + j) * 4, ((zv * 4 + j) * 4 + i) * 4
                    lhs_f[dst : dst + 4, :] = wide_lhs[src : src + 4]
        return lhs_f[...].astype(BF16)

    def reduction(h):
        rows = other_order() if h else lhs
        ak, (b, b1, b2, b3), a_other, b_other = ways[h]
        a, b_right, b_left = ak[0], b_other[1], b_other[3]
        def slab(p, k, j):
            return p_own.at[h, zs[p] * 4 + k, :, pl.ds(j * 1792, 1792)]

        def spot(i, j):
            return r2.at[h, i, :, pl.ds(j * 1792, 1792)]

        def send(ref, i, j, to):
            push(ref, spot(i, j), ds_sem, dr_sem, 32 + 12 * h + 6 * j + i, to)

        def wait(i, j):
            landed(spot(i, j), ds_sem, dr_sem, 32 + 12 * h + 6 * j + i)

        for j in range(2):
            cols = pl.ds(j * 1792, 1792)
            part = jnp.dot(rows, wd[:, pl.ds(h * 3584 + j * 1792, 1792)], preferred_element_type=F32)
            p_own[h, :, :, cols] = part.astype(BF16).reshape(8, 16, 1792)
            send(slab(0, b2, j), 0, j, b_left)
            send(slab(1, b2, j), 1, j, b_right)
            send(slab(1, b3, j), 3, j, b_left)
            send(slab(0, b1, j), 4, j, b_right)
        yield
        for j in range(2):
            for i, p, k, to, n in ((0, 0, b3, b_left, 2), (1, 1, b1, b_right, 5)):
                wait(i, j)
                ref = slab(p, k, j)
                ref[...] = (ref[...].astype(F32) + spot(i, j)[...].astype(F32)).astype(BF16)
                send(ref, n, j, to)
        yield
        for j in range(2):
            for i in (3, 4, 2, 5):
                wait(i, j)
        for p in (1, 0):
            total = (
                p_own[h, zs[p] * 4 + b].astype(F32) + r2[h, 2 + p].astype(F32) + r2[h, 4 + p].astype(F32)
            )
            for av in range(4):
                for q in range(4):
                    qf[av, q * 4 : q * 4 + 4, :] = total[av * 4 : av * 4 + 4, q * 896 : (q + 1) * 896]
            qb[h, p] = qf[...].astype(BF16)
            for k in (1, 3, 2):
                push(
                    qb.at[h, p, ak[k]], r1.at[h, p, k - 1], ds_sem, dr_sem, 13 + 6 * h + 3 * p + k, a_other[k]
                )
        yield
        sums = []
        for p in (1, 0):
            total = qb[h, p, a].astype(F32)
            for k in (1, 3, 2):
                landed(r1.at[h, p, k - 1], ds_sem, dr_sem, 13 + 6 * h + 3 * p + k)
                total = total + r1[h, p, k - 1].astype(F32)
            sums.append(total)
            if p == 1:
                tz[h] = total.astype(BF16)
                push(tz.at[h], got_peer.at[h], ds_sem, dr_sem, 26 + 3 * h, z_peer)
                push(tz.at[h], got_cross.at[h], ds_sem, dr_sem, 27 + 3 * h, cross)
        tp0[h] = sums[1].astype(BF16)
        push(tp0.at[h], got_partner.at[h], ds_sem, dr_sem, 28 + 3 * h, partner)
        t0[h] = sums[1]
        yield
        landed(got_partner.at[h], ds_sem, dr_sem, 28 + 3 * h)
        landed(got_cross.at[h], ds_sem, dr_sem, 27 + 3 * h)
        landed(got_peer.at[h], ds_sem, dr_sem, 26 + 3 * h)
        stayed = hid[h].astype(F32) + (t0[h] + got_peer[h].astype(F32))
        moved = hid_got[h].astype(F32) + (got_partner[h].astype(F32) + got_cross[h].astype(F32))
        row = lax.rem(lax.broadcasted_iota(jnp.int32, (16, 896), 0), 4)
        final = jnp.where(jnp.where(row < 2, swaps[0], swaps[1]) == 1, moved, stayed)
        request = lax.broadcasted_iota(jnp.int32, (4, 896), 0)
        for q in range(4):
            rows = jnp.zeros((4, 896), F32)
            for p in range(4):
                one = jnp.broadcast_to(final[q * 4 + p : q * 4 + p + 1], (4, 896))
                rows = jnp.where(request == assign_ref[p], one, rows)
            out_ref[:, h * 3584 + q * 896 : h * 3584 + (q + 1) * 896] = rows.astype(BF16)
        yield

    def own_hidden(h):
        lane = lax.broadcasted_iota(jnp.int32, (16, 128), 1)
        sub = lax.broadcasted_iota(jnp.int32, (16, 128), 0)
        rows = jnp.zeros((16, 896), F32)
        for q in range(4):
            pick = jnp.where(lane == me_row + sub - q * 4, 1.0, 0.0)
            pick = jnp.where((sub >= q * 4) & (sub < q * 4 + 4), pick, 0.0).astype(BF16)
            xv, zv = 2 * h + q // 2, q % 2
            parts = []
            for yv in range(4):
                for plane in range(2):
                    bv, av = yv * co + xv * c, xv * co + yv * c
                    parts.append(ht[c, ((plane * 2 + zv) * 4 + bv) * 4 + av])
            rows = rows + lax.dot_general(
                pick, jnp.concatenate(parts, axis=0), NT, preferred_element_type=F32
            )
        hid[h] = rows.astype(BF16)
        push(hid.at[h], hid_got.at[h], rs_sem, rr_sem, 16 + h, partner)

    halves = (reduction(0), reduction(1))
    before = len(started)
    for half in halves:
        next(half)
    own_hidden(0)
    drain(len(started) - before)
    next(halves[0])
    own_hidden(1)
    next(halves[1])
    for _ in range(2):
        for half in halves:
            next(half)
    for h in range(2):
        landed(hid_got.at[h], rs_sem, rr_sem, 16 + h)
    for half in halves:
        next(half)
    drain()


def per_device(
    queries, keys, values, lengths, resid, assign, matching, w_out, gain, gate_w, up_w, down_w
):
    smem = pl.BlockSpec(memory_space=pltpu.SMEM)
    vmem = pl.BlockSpec(memory_space=pltpu.VMEM)
    hbm = pl.BlockSpec(memory_space=pl.ANY)
    dma = pltpu.SemaphoreType.DMA
    scratch = (
        ((4, CW), BF16),
        ((4, 1024, 256), BF16),
        ((4, 1024, 256), BF16),
        ((COLS, CW), BF16),
        ((FH, D), BF16),
        ((FH, D), BF16),
        ((2, 2 * FH, D // 2), BF16),
        ((2 * FH, D), BF16),
        ((4, D), BF16),
        ((1, D), F32),
        ((2, 128, 128), F32),
        ((2, 64, 256), BF16),
        ((2, 64, 256), BF16),
        ((2, 64, 256), BF16),
        ((2, 64, 256), BF16),
        ((16, 128), F32),
        ((16, 128), BF16),
        ((16, 128), BF16),
        ((2, 2, 4, 64, 256), BF16),
        ((2, 256, 128), F32),
        ((2, 16, 16, CW // 2), BF16),
        ((2, 64, COLS, 128), BF16),
        ((2, 2 * FH, 128), F32),
        ((2, 8, 128), F32),
        ((128, FH), BF16),
        ((128, FH), BF16),
        ((8, 16, 256), F32),
        ((8, 16, 256), BF16),
        ((8, 16, 256), BF16),
        ((8, 16, 256), BF16),
        ((8, 32, 128), F32),
        ((8, 32, 128), BF16),
        ((8, 32, 128), BF16),
        ((256, 128), F32),
        ((128, 256), F32),
        ((128, 128), F32),
        ((128, 2 * FH), F32),
        ((2, 8, 16, D // 2), BF16),
        ((2, 6, 16, D // 2), BF16),
        ((4, 16, 896), F32),
        ((2, 2, 4, 16, 896), BF16),
        ((2, 2, 3, 16, 896), BF16),
        ((2, 16, 896), F32),
    ) + (((2, 16, 896), BF16),) * 7
    return pl.pallas_call(
        kernel,
        out_shape=pltpu.VMEM((4, D), BF16),
        in_specs=[smem] * 3 + [hbm] * 9,
        out_specs=vmem,
        scratch_shapes=[pltpu.VMEM(shape, dtype) for shape, dtype in scratch]
        + [dma((n,)) for n in (8, 7, 42, 42, 42, 42, 56, 56, 26, 26)],
        compiler_params=pltpu.CompilerParams(
            collective_id=0, has_side_effects=True, vmem_limit_bytes=60 * 1024 * 1024
        ),
    )(
        lengths, assign[0], matching[:, 0, 0], queries, resid, gain[None],
        keys, values, w_out.T, gate_w[0].T, up_w[0].T, down_w[0],
    )


def solution(mesh):
    rows = P(("attn", "grp", "tp"), None)
    cache = P(("attn", "grp", "tp"), None, None)
    placed = (
        rows,
        cache,
        cache,
        P(("attn", "grp", "tp")),
        rows,
        rows,
        P(None, "attn", "tp"),
        P(None, ("attn", "tp")),
        P(),
        P("grp", None, ("attn", "tp")),
        P("grp", None, ("attn", "tp")),
        P("grp", ("attn", "tp"), None),
    )
    return jax.shard_map(
        per_device, mesh=mesh, in_specs=placed, out_specs=rows, check_vma=False
    )
```

```python
import jax
import jax.numpy as jnp
from jax import lax
from jax.experimental import pallas as pl
from jax.experimental.pallas import tpu as pltpu
from jax.sharding import PartitionSpec as P

D = 7168
CW = 8192
FH = 288
COLS = 112
MESH = pl.DeviceIdType.MESH
F32 = jnp.float32
BF16 = jnp.bfloat16
NT = (((1,), (1,)), ((), ()))


def kernel(
    len_ref, assign_ref, match_ref, q_hbm, resid_hbm, gain_hbm, k_hbm, v_hbm, wo_hbm, g_hbm, u_hbm, d_hbm,
    out_ref,
    q_ref, kc, vc, wo, wg, wu, w2, wd, resid_ref, gain_ref,
    qs, own_b, got_b, cross_b, peer_b, flags, flag_out, flag_in, cb, sf, ctx_all, ht, acc, squares, act_out, act_in,
    s1f, s1, s1_got, t1, uf, ub, vb, wf, wt, turned, lhs_f,
    p_own, r2, qf, qb, r1, t0, tp0, tz, got_peer, got_partner, got_cross, hid, hid_got,
    kv_sem, w_sem, bs_sem, br_sem, cs_sem, cr_sem, ds_sem, dr_sem, rs_sem, rr_sem,
):
    attn, grp, tp = lax.axis_index("attn"), lax.axis_index("grp"), lax.axis_index("tp")
    x, z, y, c = attn // 2, lax.rem(attn, 2), tp // 2, lax.rem(tp, 2)
    zo, co = 1 - z, 1 - c
    zs = (z, zo)
    def dev(x_, z_, y_, c_):
        return (lax.rem(x_, 4) * 2 + z_, grp, lax.rem(y_, 4) * 2 + c_)

    z_peer, sibling = dev(x, zo, y, c), dev(x, z, y, co)
    partner = (attn, 1 - grp, tp)
    cross = (x * 2 + zo, 1 - grp, tp)

    def axes(e):
        a, b = x * (1 - e) + y * e, y * (1 - e) + x * e
        return (
            [lax.rem(a + k, 4) for k in range(4)],
            [lax.rem(b + k, 4) for k in range(4)],
            [dev(x + k * (1 - e), z, y + k * e, c) for k in range(4)],
            [dev(x + k * e, z, y + k * (1 - e), c) for k in range(4)],
        )

    ways = (axes(c), axes(co))

    q_load = pltpu.make_async_copy(q_hbm, q_ref, w_sem.at[6])
    q_load.start()
    fetch = [
        pltpu.make_async_copy(src, dst, kv_sem.at[i])
        for i, (src, dst) in enumerate(((k_hbm, kc), (v_hbm, vc)))
    ]
    for copy in fetch:
        copy.start()
    loads = [
        pltpu.make_async_copy(src, dst, w_sem.at[i])
        for i, (src, dst) in enumerate(
            ((resid_hbm, resid_ref), (gain_hbm, gain_ref), (g_hbm, wg), (u_hbm, wu), (wo_hbm, wo), (d_hbm, wd.at[pl.ds(0, FH)]))
        )
    ]
    barrier = pltpu.get_barrier_semaphore()
    others = [partner, cross]
    for k in range(1, 8):
        others.append((lax.rem(attn + k, 8), grp, tp))
        others.append((attn, grp, lax.rem(tp + k, 8)))
    for other in others:
        pl.semaphore_signal(barrier, inc=1, device_id=other, device_id_type=MESH)

    started = []

    def drain(keep=0):
        while len(started) > keep:
            started.pop(0).wait_send()

    def push(src, dst, s_sem, r_sem, i, to):
        copy = pltpu.make_async_remote_copy(
            src_ref=src, dst_ref=dst, send_sem=s_sem.at[i], recv_sem=r_sem.at[i],
            device_id=to, device_id_type=MESH,
        )
        copy.start()
        started.append(copy)

    def landed(dst, s_sem, r_sem, i):
        pltpu.make_async_remote_copy(
            src_ref=dst, dst_ref=dst, send_sem=s_sem.at[i], recv_sem=r_sem.at[i],
            device_id=sibling, device_id_type=MESH,
        ).wait_recv()

    q_load.wait()
    wide_q = q_ref[...].astype(F32)
    for h in range(32):
        for half in range(2):
            first = h * 256 + half * 128
            qs[half, pl.ds(h, 4, stride=32), :] = wide_q[:, first : first + 128]
    slot = lax.broadcasted_iota(jnp.int32, (32, 1024), 1)
    swaps = (match_ref[0], match_ref[1])

    def weigh(r):
        query = jnp.concatenate([qs[half, r * 32 : (r + 1) * 32] for half in range(2)], axis=1).astype(BF16)
        scores = lax.dot_general(query, kc[r], NT, preferred_element_type=F32) * (256 ** -0.5)
        scores = jnp.where(slot < len_ref[r], scores, -1e30)
        expo = jnp.exp(scores - jnp.max(scores, axis=-1, keepdims=True))
        return (expo / jnp.sum(expo, axis=-1, keepdims=True)).astype(BF16)

    fetch[0].wait()
    for load in loads:
        load.start()
    pl.semaphore_wait(barrier, 16)
    push(d_hbm, wd.at[pl.ds(FH, FH)], rs_sem, rr_sem, 18, sibling)
    probs = [weigh(r) for r in range(4)]
    fetch[1].wait()
    contexts = [jnp.dot(probs[r], vc[r], preferred_element_type=F32) for r in range(4)]
    for p in range(4):
        chosen = contexts[0]
        for r in range(1, 4):
            chosen = jnp.where(assign_ref[p] == r, contexts[r], chosen)
        for hh in range(2):
            own_b[hh, p * 16 : p * 16 + 16] = chosen[hh * 16 : hh * 16 + 16].astype(BF16)

    def gather(way, block, part, pair, other, other_pair, s_sem, r_sem, ready, base, peer=None):
        ak, bk, a_other, b_other = way
        a, (b, b1, b2, b3) = ak[0], bk
        b_right, b_left = b_other[1], b_other[3]

        def send(ref, i, to):
            push(ref, ref, s_sem, r_sem, base + i, to)

        def wait(ref, i):
            landed(ref, s_sem, r_sem, base + i)

        def ring_1(p):
            for k in (1, 3, 2):
                send(block(p, a), 3 * p + k, a_other[k])

        def ring_2(p):
            for k in (1, 3, 2):
                wait(block(p, ak[4 - k]), 3 * p + k)
            ready(p)
            first, second = ((7, b_right), (8, b_left)) if p == 0 else ((10, b_left), (9, b_right))
            send(part(p, b), *first)
            send(part(p, b), *second)

        if peer is None:
            send(block(0, a), 0, z_peer)
        ring_1(0)
        yield
        if peer is None:
            ring_2(0)
            wait(block(1, a), 0)
            ring_1(1)
        else:
            peer()
            ring_1(1)
            ring_2(0)
        yield
        ring_2(1)
        send(pair(b), 13, sibling)
        yield
        wait(part(0, b3), 7)
        send(part(0, b3), 11, b_right)
        wait(part(0, b1), 8)
        yield
        wait(part(1, b1), 10)
        send(part(1, b1), 12, b_left)
        send(pair(b1), 15, sibling)
        wait(part(1, b3), 9)
        send(pair(b3), 14, sibling)
        yield
        wait(part(0, b2), 11)
        send(part(0, b2), 16, sibling)
        wait(part(1, b2), 12)
        send(part(1, b2), 17, sibling)
        yield
        for i, k in ((13, 0), (15, 1), (14, 3)):
            wait(other_pair(ak[k]), i)
        wait(other(z, ak[2]), 16)
        yield
        wait(other(zo, ak[2]), 17)
        yield

    a, b = ways[0][0][0], ways[0][1][0]
    me_row = ((z * 4 + b) * 4 + a) * 4

    def residual():
        loads[0].wait()
        wide_r = resid_ref[...].astype(F32)
        ordered = []
        for p in range(4):
            chosen = wide_r[0:1]
            for r in range(1, 4):
                chosen = jnp.where(assign_ref[p] == r, wide_r[r : r + 1], chosen)
            ordered.append(chosen)
        ordered = jnp.concatenate(ordered, axis=0)
        s1f[...] = jnp.zeros_like(s1f)
        for n in range(8):
            for t in range(8):
                first = n * 896 + t * COLS
                s1f[n, (t % 4) * 4 : (t % 4) * 4 + 4, (t // 4) * 128 : (t // 4) * 128 + COLS] = ordered[
                    :, first : first + COLS
                ]
        s1[...] = s1f[...].astype(BF16)
        push(s1, s1_got, rs_sem, rr_sem, 1, partner)
        yield
        landed(s1_got, rs_sem, rr_sem, 1)
        row = lax.rem(lax.broadcasted_iota(jnp.int32, (8, 16, 256), 1), 4)
        served = jnp.where(jnp.where(row < 2, swaps[0], swaps[1]) == 1, s1_got[...], s1[...])
        s1_got[...] = served
        t1[attn] = s1_got[attn]
        for k in range(1, 8):
            to = lax.rem(attn + k, 8)
            push(s1_got.at[to], t1.at[attn], rs_sem, rr_sem, 1 + k, (to, grp, tp))
        yield
        for k in range(1, 8):
            landed(t1.at[lax.rem(attn + 8 - k, 8)], rs_sem, rr_sem, 1 + k)
        for n in range(8):
            part = t1[n].astype(F32)
            for t in range(8):
                uf[t, n * 4 : n * 4 + 4, :] = part[
                    (t % 4) * 4 : (t % 4) * 4 + 4, (t // 4) * 128 : (t // 4) * 128 + 128
                ]
        ub[...] = uf[...].astype(BF16)
        vb[tp] = ub[tp]
        for k in range(1, 8):
            to = lax.rem(tp + k, 8)
            push(ub.at[to], vb.at[tp], rs_sem, rr_sem, 8 + k, (attn, grp, to))
        yield
        for k in range(1, 8):
            landed(vb.at[lax.rem(tp + 8 - k, 8)], rs_sem, rr_sem, 8 + k)
        for t in range(8):
            part = vb[t].astype(F32)
            for n in range(8):
                plane, zv = t % 2, n % 2
                bv, av = (n // 2, t // 2) if plane else (t // 2, n // 2)
                place = (((plane * 2 + zv) * 4 + bv) * 4 + av) * 4
                wf[place : place + 4, :] = part[n * 4 : n * 4 + 4]
        wt[...] = wf[...].T
        yield

    def scaling():
        for i in (1, 2, 3):
            loads[i].wait()

        def scale(i, _):
            rows = pl.ds(pl.multiple_of(i * 16, 16), 16)
            for k, src in enumerate((wg, wu)):
                spot = pl.ds(pl.multiple_of(k * FH + i * 16, 16), 16)
                wide = (src[rows, :].astype(F32) * gain_ref[...]).astype(BF16)
                for cv in range(2):
                    for xv in range(4):
                        first = [
                            ((xv // 2 * 4 + x2 * 2 + xv % 2) * 8 + yv * 2 + cv) * COLS
                            for x2 in range(2)
                            for yv in range(4)
                        ]
                        w2[cv, spot, xv * 896 : (xv + 1) * 896] = jnp.concatenate(
                            [wide[:, f : f + COLS] for f in first], axis=1
                        )
            return 0

        for part in range(6):
            lax.fori_loop(part * 3, part * 3 + 3, scale, 0)
            yield

    for m in range(2):
        flags[m * 8 : m * 8 + 8, :] = jnp.full((8, 128), swaps[m], jnp.int32).astype(F32)
    flag_out[...] = flags[...].astype(BF16)
    for hh in range(2):
        push(own_b.at[hh], got_b.at[hh], rs_sem, rr_sem, 20 * hh, partner)
    push(flag_out, flag_in, rs_sem, rr_sem, 21, z_peer)
    push(own_b, cross_b, rs_sem, rr_sem, 22, cross)
    push(own_b, peer_b, rs_sem, rr_sem, 24, z_peer)
    residual_steps, scaling_steps = residual(), scaling()
    next(residual_steps)
    next(scaling_steps)
    row = lax.broadcasted_iota(jnp.int32, (64, 256), 0)

    def gather_context(hh):
        way = ways[hh]

        def ready(p):
            for half in range(2):
                sf[half] = cb[hh, zs[p], :, :, half * 128 : (half + 1) * 128].astype(F32).reshape(256, 128)
            for h in range(16):
                for half in range(2):
                    first = h * 256 + half * 128
                    ctx_all[hh, c, zs[p], way[1][0], :, first : first + 128] = sf[
                        half, pl.ds(h, 16, stride=16), :
                    ].astype(BF16)

        landed(got_b.at[hh], rs_sem, rr_sem, 20 * hh)
        cb[hh, z, way[0][0]] = jnp.where(
            jnp.where(row < 32, swaps[0], swaps[1]) == 1, got_b[hh], own_b[hh]
        )

        def peer():
            if hh == 0:
                landed(flag_in, rs_sem, rr_sem, 21)
                landed(cross_b, rs_sem, rr_sem, 22)
                landed(peer_b, rs_sem, rr_sem, 24)
            wide = flag_in[...].astype(F32)
            flag = jnp.concatenate(
                [jnp.broadcast_to(wide[m * 8 : m * 8 + 1], (32, 128)) for m in range(2)], axis=0
            )
            flag = jnp.concatenate([flag, flag], axis=1)
            theirs = jnp.where(flag > 0.5, cross_b[hh].astype(F32), peer_b[hh].astype(F32))
            cb[hh, zo, way[0][0]] = theirs.astype(BF16)

        yield from gather(
            way,
            lambda p, av: cb.at[hh, zs[p], av],
            lambda p, bv: ctx_all.at[hh, c, zs[p], bv],
            lambda bv: ctx_all.at[hh, c, :, bv],
            lambda zv, bv: ctx_all.at[hh, co, zv, bv],
            lambda bv: ctx_all.at[hh, co, :, bv],
            bs_sem,
            br_sem,
            ready,
            21 * hh,
            peer,
        )

    steps = (gather_context(0), gather_context(1))

    def both(pair):
        for one in pair:
            next(one)

    both(steps)
    next(residual_steps)
    both(steps)
    next(scaling_steps)
    both(steps)
    next(residual_steps)
    next(scaling_steps)
    both(steps)
    next(scaling_steps)
    both(steps)
    next(scaling_steps)
    next(residual_steps)
    next(scaling_steps)
    both(steps)
    loads[4].wait()

    def project(plane):
        def rows(hh, cols):
            return ctx_all[hh, plane, :, :, :, cols].reshape(128, 1024)

        def step(i, sums):
            cols = pl.ds(pl.multiple_of(i * 1024, 1024), 1024)
            last = pl.ds(pl.multiple_of(i * 1024 + CW // 2, 1024), 1024)
            one = lax.dot_general(wo[:, cols], rows(0, cols), NT, preferred_element_type=F32)
            two = lax.dot_general(rows(1, cols), wo[:, last], NT, preferred_element_type=F32)
            return sums[0] + one, sums[1] + two

        one, two = lax.fori_loop(
            0, CW // 2048, step, (jnp.zeros((COLS, 128), F32), jnp.zeros((128, COLS), F32))
        )
        for zv in range(2):
            for i in range(4):
                for j in range(4):
                    src, dst = ((zv * 4 + i) * 4 + j) * 4, ((zv * 4 + j) * 4 + i) * 4
                    turned[dst : dst + 4, :COLS] = two[src : src + 4]
        lanes = pl.ds(pl.multiple_of(plane * 128, 128), 128)
        return (wt[:COLS, lanes] + (one + turned[...].T[:COLS])).astype(BF16)

    def gather_hidden(i):
        half = (c, co)[i]
        return gather(
            ways[i],
            lambda p, av: ht.at[half, c, zs[p], ways[i][1][0], av],
            lambda p, bv: ht.at[half, c, zs[p], bv],
            lambda bv: ht.at[half, c, :, bv],
            lambda zv, bv: ht.at[(co, c)[i], co, zv, bv],
            lambda bv: ht.at[(co, c)[i], co, :, bv],
            cs_sem,
            cr_sem,
            lambda p: None,
            21 * i,
        )

    early, late = gather_hidden(0), gather_hidden(1)

    def features(plane, half, n):
        parts = []
        for x2 in range(2):
            for yv in range(4):
                xv = n // 2 * 2 + x2
                bv, av = yv * (1 - half) + xv * half, xv * (1 - half) + yv * half
                parts.append(ht[half, plane, lax.rem(n, 2), bv, av])
        return jnp.concatenate(parts, axis=0)

    def expand(plane, i, *ps):
        half = (c, co)[i]

        def step(k, total):
            n = (k // len(ps)) * 2 + (zs[ps[0]] if len(ps) == 1 else lax.rem(k, 2))
            cols = pl.ds(pl.multiple_of(n * 896, 128), 896)
            part = features(plane, half, n)
            acc[i] += jnp.dot(w2[plane, :, cols], part, preferred_element_type=F32)
            wide = part.astype(F32)
            return total + jnp.sum((wide * wide).reshape(112, 8, 128), axis=0)

        squares[i] += lax.fori_loop(0, 2 * len(ps), step, jnp.zeros((8, 128), F32))

    def activate(i):
        factor = lax.rsqrt(jnp.sum(squares[i], axis=0, keepdims=True) * (1.0 / D) + 1e-5)
        gate = acc[i, :FH] * factor
        act = gate / (1.0 + jnp.exp(-gate)) * (acc[i, FH:] * factor)
        return act.T.astype(BF16)

    ht[c, c, z, b, a] = project(c)
    next(early)
    both(steps)
    both(steps)
    ht[co, c, z, a, b] = project(co)
    next(late)
    acc[...] = jnp.zeros_like(acc)
    squares[...] = jnp.zeros_like(squares)
    before = len(started)
    for i in range(4):
        next(early)
        next(late)
        if i == 0:
            drain(len(started) - before)
    next(early)
    expand(c, 0, 0, 1)
    next(late)
    next(early)
    next(early)
    expand(co, 1, 0, 1)
    expand(c, 1, 0, 1)
    act_out[...] = activate(1)
    push(act_out, act_in, rs_sem, rr_sem, 19, sibling)
    next(late)
    expand(co, 0, 0)
    next(late)
    expand(co, 0, 1)

    act_own = activate(0)
    loads[5].wait()
    landed(wd.at[pl.ds(FH, FH)], rs_sem, rr_sem, 18)
    landed(act_in, rs_sem, rr_sem, 19)
    lhs = jnp.concatenate([act_own, act_in[...]], axis=1)

    def other_order():
        wide_lhs = lhs.astype(F32)
        for zv in range(2):
            for i in range(4):
                for j in range(4):
                    src, dst = ((zv * 4 + i) * 4 + j) * 4, ((zv * 4 + j) * 4 + i) * 4
                    lhs_f[dst : dst + 4, :] = wide_lhs[src : src + 4]
        return lhs_f[...].astype(BF16)

    def reduction(h):
        rows = other_order() if h else lhs
        ak, (b, b1, b2, b3), a_other, b_other = ways[h]
        a, b_right, b_left = ak[0], b_other[1], b_other[3]
        for j in range(2):
            cols = pl.ds(j * 1792, 1792)
            part = jnp.dot(rows, wd[:, pl.ds(h * 3584 + j * 1792, 1792)], preferred_element_type=F32)
            p_own[h, :, :, cols] = part.astype(BF16).reshape(8, 16, 1792)

        def slab(p, k):
            return p_own.at[h, zs[p] * 4 + k]

        def send(ref, i, to):
            push(ref, r2.at[h, i], ds_sem, dr_sem, 2 + 6 * h + i, to)

        def wait(i):
            landed(r2.at[h, i], ds_sem, dr_sem, 2 + 6 * h + i)

        send(slab(0, b2), 0, b_left)
        send(slab(1, b2), 1, b_right)
        send(slab(1, b3), 3, b_left)
        send(slab(0, b1), 4, b_right)
        yield
        for i, p, k, to, j in ((0, 0, b3, b_left, 2), (1, 1, b1, b_right, 5)):
            wait(i)
            ref = slab(p, k)
            ref[...] = (ref[...].astype(F32) + r2[h, i].astype(F32)).astype(BF16)
            send(ref, j, to)
        yield
        for i in (3, 4, 2, 5):
            wait(i)
        for p in (1, 0):
            total = (
                p_own[h, zs[p] * 4 + b].astype(F32) + r2[h, 2 + p].astype(F32) + r2[h, 4 + p].astype(F32)
            )
            for av in range(4):
                for q in range(4):
                    qf[av, q * 4 : q * 4 + 4, :] = total[av * 4 : av * 4 + 4, q * 896 : (q + 1) * 896]
            qb[h, p] = qf[...].astype(BF16)
        for k in (1, 3, 2):
            push(qb.at[h, :, ak[k]], r1.at[h, k - 1], ds_sem, dr_sem, 13 + 6 * h + k, a_other[k])
        yield
        for k in (1, 3, 2):
            landed(r1.at[h, k - 1], ds_sem, dr_sem, 13 + 6 * h + k)
        sums = []
        for p in (1, 0):
            total = qb[h, p, a].astype(F32)
            for k in (1, 3, 2):
                total = total + r1[h, k - 1, p].astype(F32)
            sums.append(total)
            if p == 1:
                tz[h] = total.astype(BF16)
                push(tz.at[h], got_peer.at[h], ds_sem, dr_sem, 26 + 3 * h, z_peer)
                push(tz.at[h], got_cross.at[h], ds_sem, dr_sem, 27 + 3 * h, cross)
        tp0[h] = sums[1].astype(BF16)
        push(tp0.at[h], got_partner.at[h], ds_sem, dr_sem, 28 + 3 * h, partner)
        t0[h] = sums[1]
        yield
        landed(got_partner.at[h], ds_sem, dr_sem, 28 + 3 * h)
        landed(got_cross.at[h], ds_sem, dr_sem, 27 + 3 * h)
        landed(got_peer.at[h], ds_sem, dr_sem, 26 + 3 * h)
        stayed = hid[h].astype(F32) + (t0[h] + got_peer[h].astype(F32))
        moved = hid_got[h].astype(F32) + (got_partner[h].astype(F32) + got_cross[h].astype(F32))
        row = lax.rem(lax.broadcasted_iota(jnp.int32, (16, 896), 0), 4)
        final = jnp.where(jnp.where(row < 2, swaps[0], swaps[1]) == 1, moved, stayed)
        request = lax.broadcasted_iota(jnp.int32, (4, 896), 0)
        for q in range(4):
            rows = jnp.zeros((4, 896), F32)
            for p in range(4):
                one = jnp.broadcast_to(final[q * 4 + p : q * 4 + p + 1], (4, 896))
                rows = jnp.where(request == assign_ref[p], one, rows)
            out_ref[:, h * 3584 + q * 896 : h * 3584 + (q + 1) * 896] = rows.astype(BF16)
        yield

    def own_hidden(h):
        lane = lax.broadcasted_iota(jnp.int32, (16, 128), 1)
        sub = lax.broadcasted_iota(jnp.int32, (16, 128), 0)
        rows = jnp.zeros((16, 896), F32)
        for q in range(4):
            pick = jnp.where(lane == me_row + sub - q * 4, 1.0, 0.0)
            pick = jnp.where((sub >= q * 4) & (sub < q * 4 + 4), pick, 0.0).astype(BF16)
            xv, zv = 2 * h + q // 2, q % 2
            parts = []
            for yv in range(4):
                for plane in range(2):
                    bv, av = yv * co + xv * c, xv * co + yv * c
                    parts.append(ht[c, plane, zv, bv, av])
            rows = rows + lax.dot_general(
                pick, jnp.concatenate(parts, axis=0), NT, preferred_element_type=F32
            )
        hid[h] = rows.astype(BF16)
        if h:
            push(hid, hid_got, rs_sem, rr_sem, 16, partner)

    halves = (reduction(0), reduction(1))
    before = len(started)
    for half in halves:
        next(half)
    own_hidden(0)
    drain(len(started) - before)
    next(halves[0])
    own_hidden(1)
    next(halves[1])
    for _ in range(2):
        for half in halves:
            next(half)
    landed(hid_got, rs_sem, rr_sem, 16)
    for half in halves:
        next(half)
    drain()


def per_device(
    queries, keys, values, lengths, resid, assign, matching, w_out, gain, gate_w, up_w, down_w
):
    smem = pl.BlockSpec(memory_space=pltpu.SMEM)
    vmem = pl.BlockSpec(memory_space=pltpu.VMEM)
    hbm = pl.BlockSpec(memory_space=pl.ANY)
    dma = pltpu.SemaphoreType.DMA
    scratch = (
        ((4, CW), BF16),
        ((4, 1024, 256), BF16),
        ((4, 1024, 256), BF16),
        ((COLS, CW), BF16),
        ((FH, D), BF16),
        ((FH, D), BF16),
        ((2, 2 * FH, D // 2), BF16),
        ((2 * FH, D), BF16),
        ((4, D), BF16),
        ((1, D), F32),
        ((2, 128, 128), F32),
        ((2, 64, 256), BF16),
        ((2, 64, 256), BF16),
        ((2, 64, 256), BF16),
        ((2, 64, 256), BF16),
        ((16, 128), F32),
        ((16, 128), BF16),
        ((16, 128), BF16),
        ((2, 2, 4, 64, 256), BF16),
        ((2, 256, 128), F32),
        ((2, 2, 2, 4, 16, CW // 2), BF16),
        ((2, 2, 2, 4, 4, COLS, 128), BF16),
        ((2, 2 * FH, 128), F32),
        ((2, 8, 128), F32),
        ((128, FH), BF16),
        ((128, FH), BF16),
        ((8, 16, 256), F32),
        ((8, 16, 256), BF16),
        ((8, 16, 256), BF16),
        ((8, 16, 256), BF16),
        ((8, 32, 128), F32),
        ((8, 32, 128), BF16),
        ((8, 32, 128), BF16),
        ((256, 128), F32),
        ((128, 256), F32),
        ((128, 128), F32),
        ((128, 2 * FH), F32),
        ((2, 8, 16, D // 2), BF16),
        ((2, 6, 16, D // 2), BF16),
        ((4, 16, 896), F32),
        ((2, 2, 4, 16, 896), BF16),
        ((2, 3, 2, 16, 896), BF16),
        ((2, 16, 896), F32),
    ) + (((2, 16, 896), BF16),) * 7
    return pl.pallas_call(
        kernel,
        out_shape=pltpu.VMEM((4, D), BF16),
        in_specs=[smem] * 3 + [hbm] * 9,
        out_specs=vmem,
        scratch_shapes=[pltpu.VMEM(shape, dtype) for shape, dtype in scratch]
        + [dma((n,)) for n in (8, 7, 42, 42, 42, 42, 32, 32, 26, 26)],
        compiler_params=pltpu.CompilerParams(
            collective_id=0, has_side_effects=True, vmem_limit_bytes=60 * 1024 * 1024
        ),
    )(
        lengths, assign[0], matching[:, 0, 0], queries, resid, gain[None],
        keys, values, w_out.T, gate_w[0].T, up_w[0].T, down_w[0],
    )


def solution(mesh):
    rows = P(("attn", "grp", "tp"), None)
    cache = P(("attn", "grp", "tp"), None, None)
    placed = (
        rows,
        cache,
        cache,
        P(("attn", "grp", "tp")),
        rows,
        rows,
        P(None, "attn", "tp"),
        P(None, ("attn", "tp")),
        P(),
        P("grp", None, ("attn", "tp")),
        P("grp", None, ("attn", "tp")),
        P("grp", ("attn", "tp"), None),
    )
    return jax.shard_map(
        per_device, mesh=mesh, in_specs=placed, out_specs=rows, check_vma=False
    )
```

```python
import jax
import jax.numpy as jnp
from jax import lax
from jax.experimental import pallas as pl
from jax.experimental.pallas import tpu as pltpu
from jax.sharding import PartitionSpec as P

D = 7168
CW = 8192
FH = 288
COLS = 112
MESH = pl.DeviceIdType.MESH
F32 = jnp.float32
BF16 = jnp.bfloat16
NT = (((1,), (1,)), ((), ()))


def kernel(
    len_ref, assign_ref, match_ref, q_hbm, resid_hbm, gain_hbm, k_hbm, v_hbm, wo_hbm, g_hbm, u_hbm, d_hbm,
    out_ref,
    q_ref, kc, vc, wo, wg, wu, w2, wd, resid_ref, gain_ref,
    qs, own_b, got_b, cross_b, peer_b, flags, flag_out, flag_in, cb, sf, ctx_all, ht, acc, squares, act_out, act_in,
    s1f, s1, s1_got, t1, uf, ub, vb, wf, wt, turned, lhs_f,
    p_own, r2, qf, qb, r1, t0, tp0, tz, got_peer, got_partner, got_cross, hid, hid_got,
    kv_sem, w_sem, bs_sem, br_sem, cs_sem, cr_sem, ds_sem, dr_sem, rs_sem, rr_sem,
):
    attn, grp, tp = lax.axis_index("attn"), lax.axis_index("grp"), lax.axis_index("tp")
    x, z, y, c = attn // 2, lax.rem(attn, 2), tp // 2, lax.rem(tp, 2)
    zo, co = 1 - z, 1 - c
    zs = (z, zo)
    def dev(x_, z_, y_, c_):
        return (lax.rem(x_, 4) * 2 + z_, grp, lax.rem(y_, 4) * 2 + c_)

    z_peer, sibling = dev(x, zo, y, c), dev(x, z, y, co)
    partner = (attn, 1 - grp, tp)
    cross = (x * 2 + zo, 1 - grp, tp)

    def axes(e):
        a, b = x * (1 - e) + y * e, y * (1 - e) + x * e
        return (
            [lax.rem(a + k, 4) for k in range(4)],
            [lax.rem(b + k, 4) for k in range(4)],
            [dev(x + k * (1 - e), z, y + k * e, c) for k in range(4)],
            [dev(x + k * e, z, y + k * (1 - e), c) for k in range(4)],
        )

    ways = (axes(c), axes(co))

    q_load = pltpu.make_async_copy(q_hbm, q_ref, w_sem.at[6])
    q_load.start()
    fetch = []
    for src, dst in ((k_hbm, kc), (v_hbm, vc)):
        for r in range(4):
            fetch.append(pltpu.make_async_copy(src.at[r], dst.at[r], kv_sem.at[len(fetch)]))
            fetch[-1].start()
    loads = [
        pltpu.make_async_copy(src, dst, w_sem.at[i])
        for i, (src, dst) in enumerate(
            ((resid_hbm, resid_ref), (gain_hbm, gain_ref), (g_hbm, wg), (u_hbm, wu), (wo_hbm, wo), (d_hbm, wd.at[pl.ds(0, FH)]))
        )
    ]
    barrier = pltpu.get_barrier_semaphore()
    others = [partner, cross]
    for k in range(1, 8):
        others.append((lax.rem(attn + k, 8), grp, tp))
        others.append((attn, grp, lax.rem(tp + k, 8)))
    for other in others:
        pl.semaphore_signal(barrier, inc=1, device_id=other, device_id_type=MESH)

    started = []

    def drain(keep=0):
        while len(started) > keep:
            started.pop(0).wait_send()

    def push(src, dst, s_sem, r_sem, i, to):
        copy = pltpu.make_async_remote_copy(
            src_ref=src, dst_ref=dst, send_sem=s_sem.at[i], recv_sem=r_sem.at[i],
            device_id=to, device_id_type=MESH,
        )
        copy.start()
        started.append(copy)

    def landed(dst, s_sem, r_sem, i):
        pltpu.make_async_remote_copy(
            src_ref=dst, dst_ref=dst, send_sem=s_sem.at[i], recv_sem=r_sem.at[i],
            device_id=sibling, device_id_type=MESH,
        ).wait_recv()

    q_load.wait()
    wide_q = q_ref[...].astype(F32)
    for h in range(32):
        for half in range(2):
            first = h * 256 + half * 128
            qs[half, pl.ds(h, 4, stride=32), :] = wide_q[:, first : first + 128]
    slot = lax.broadcasted_iota(jnp.int32, (32, 1024), 1)
    swaps = (match_ref[0], match_ref[1])

    def weigh(r):
        query = jnp.concatenate([qs[half, r * 32 : (r + 1) * 32] for half in range(2)], axis=1).astype(BF16)
        scores = lax.dot_general(query, kc[r], NT, preferred_element_type=F32) * (256 ** -0.5)
        scores = jnp.where(slot < len_ref[r], scores, -1e30)
        expo = jnp.exp(scores - jnp.max(scores, axis=-1, keepdims=True))
        return (expo / jnp.sum(expo, axis=-1, keepdims=True)).astype(BF16)

    for copy in fetch[:4]:
        copy.wait()
    for load in loads:
        load.start()
    pl.semaphore_wait(barrier, 16)
    push(d_hbm, wd.at[pl.ds(FH, FH)], rs_sem, rr_sem, 18, sibling)
    probs = [weigh(r) for r in range(4)]
    for copy in fetch[4:]:
        copy.wait()
    contexts = [jnp.dot(probs[r], vc[r], preferred_element_type=F32) for r in range(4)]
    for p in range(4):
        chosen = contexts[0]
        for r in range(1, 4):
            chosen = jnp.where(assign_ref[p] == r, contexts[r], chosen)
        for hh in range(2):
            own_b[hh, p * 16 : p * 16 + 16] = chosen[hh * 16 : hh * 16 + 16].astype(BF16)

    def gather(way, block, part, other, s_sem, r_sem, ready, base, peer=None):
        ak, bk, a_other, b_other = way
        a, (b, b1, b2, b3) = ak[0], bk
        b_right, b_left = b_other[1], b_other[3]

        def send(ref, i, to):
            push(ref, ref, s_sem, r_sem, base + i, to)

        def wait(ref, i):
            landed(ref, s_sem, r_sem, base + i)

        def ring_1(p):
            for k in (1, 3, 2):
                send(block(p, a), 3 * p + k, a_other[k])

        def ring_2(p):
            for k in (1, 3, 2):
                wait(block(p, ak[4 - k]), 3 * p + k)
            ready(p)
            first, second = ((7, b_right), (8, b_left)) if p == 0 else ((10, b_left), (9, b_right))
            send(part(p, b), *first)
            send(part(p, b), *second)
            send(part(p, b), 13 + p, sibling)

        if peer is None:
            send(block(0, a), 0, z_peer)
        ring_1(0)
        yield
        if peer is None:
            ring_2(0)
            wait(block(1, a), 0)
            ring_1(1)
        else:
            peer()
            ring_1(1)
            ring_2(0)
        yield
        ring_2(1)
        yield
        wait(part(0, b3), 7)
        send(part(0, b3), 11, b_right)
        send(part(0, b3), 15, sibling)
        wait(part(0, b1), 8)
        send(part(0, b1), 16, sibling)
        yield
        wait(part(1, b1), 10)
        send(part(1, b1), 12, b_left)
        send(part(1, b1), 17, sibling)
        wait(part(1, b3), 9)
        send(part(1, b3), 18, sibling)
        yield
        wait(part(0, b2), 11)
        send(part(0, b2), 19, sibling)
        wait(part(1, b2), 12)
        send(part(1, b2), 20, sibling)
        yield
        for p, spots in enumerate((((13, 0), (15, 3), (16, 1), (19, 2)), ((14, 0), (18, 3), (17, 1), (20, 2)))):
            for i, k in spots:
                wait(other(zs[p], ak[k]), i)
            yield

    a, b = ways[0][0][0], ways[0][1][0]
    me = (((c * 2 + z) * 4 + b) * 4 + a, ((c * 2 + z) * 4 + a) * 4 + b)
    me_row = ((z * 4 + b) * 4 + a) * 4

    def residual():
        loads[0].wait()
        wide_r = resid_ref[...].astype(F32)
        ordered = []
        for p in range(4):
            chosen = wide_r[0:1]
            for r in range(1, 4):
                chosen = jnp.where(assign_ref[p] == r, wide_r[r : r + 1], chosen)
            ordered.append(chosen)
        ordered = jnp.concatenate(ordered, axis=0)
        s1f[...] = jnp.zeros_like(s1f)
        for n in range(8):
            for t in range(8):
                first = n * 896 + t * COLS
                s1f[n, (t % 4) * 4 : (t % 4) * 4 + 4, (t // 4) * 128 : (t // 4) * 128 + COLS] = ordered[
                    :, first : first + COLS
                ]
        s1[...] = s1f[...].astype(BF16)
        push(s1, s1_got, rs_sem, rr_sem, 1, partner)
        yield
        landed(s1_got, rs_sem, rr_sem, 1)
        row = lax.rem(lax.broadcasted_iota(jnp.int32, (8, 16, 256), 1), 4)
        served = jnp.where(jnp.where(row < 2, swaps[0], swaps[1]) == 1, s1_got[...], s1[...])
        s1_got[...] = served
        t1[attn] = s1_got[attn]
        for k in range(1, 8):
            to = lax.rem(attn + k, 8)
            push(s1_got.at[to], t1.at[attn], rs_sem, rr_sem, 1 + k, (to, grp, tp))
        yield
        for k in range(1, 8):
            landed(t1.at[lax.rem(attn + 8 - k, 8)], rs_sem, rr_sem, 1 + k)
        for n in range(8):
            part = t1[n].astype(F32)
            for t in range(8):
                uf[t, n * 4 : n * 4 + 4, :] = part[
                    (t % 4) * 4 : (t % 4) * 4 + 4, (t // 4) * 128 : (t // 4) * 128 + 128
                ]
        ub[...] = uf[...].astype(BF16)
        vb[tp] = ub[tp]
        for k in range(1, 8):
            to = lax.rem(tp + k, 8)
            push(ub.at[to], vb.at[tp], rs_sem, rr_sem, 8 + k, (attn, grp, to))
        yield
        for k in range(1, 8):
            landed(vb.at[lax.rem(tp + 8 - k, 8)], rs_sem, rr_sem, 8 + k)
        for t in range(8):
            part = vb[t].astype(F32)
            for n in range(8):
                plane, zv = t % 2, n % 2
                bv, av = (n // 2, t // 2) if plane else (t // 2, n // 2)
                place = (((plane * 2 + zv) * 4 + bv) * 4 + av) * 4
                wf[place : place + 4, :] = part[n * 4 : n * 4 + 4]
        wt[...] = wf[...].T
        yield

    def scaling():
        for i in (1, 2, 3):
            loads[i].wait()

        def scale(i, _):
            rows = pl.ds(pl.multiple_of(i * 16, 16), 16)
            for k, src in enumerate((wg, wu)):
                spot = pl.ds(pl.multiple_of(k * FH + i * 16, 16), 16)
                wide = (src[rows, :].astype(F32) * gain_ref[...]).astype(BF16)
                for cv in range(2):
                    for xv in range(4):
                        first = [
                            ((xv // 2 * 4 + x2 * 2 + xv % 2) * 8 + yv * 2 + cv) * COLS
                            for x2 in range(2)
                            for yv in range(4)
                        ]
                        w2[cv, spot, xv * 896 : (xv + 1) * 896] = jnp.concatenate(
                            [wide[:, f : f + COLS] for f in first], axis=1
                        )
            return 0

        for part in range(6):
            lax.fori_loop(part * 3, part * 3 + 3, scale, 0)
            yield

    for m in range(2):
        flags[m * 8 : m * 8 + 8, :] = jnp.full((8, 128), swaps[m], jnp.int32).astype(F32)
    flag_out[...] = flags[...].astype(BF16)
    for hh in range(2):
        push(own_b.at[hh], got_b.at[hh], rs_sem, rr_sem, 20 * hh, partner)
    push(flag_out, flag_in, rs_sem, rr_sem, 21, z_peer)
    for hh in range(2):
        push(own_b.at[hh], cross_b.at[hh], rs_sem, rr_sem, 22 + hh, cross)
        push(own_b.at[hh], peer_b.at[hh], rs_sem, rr_sem, 24 + hh, z_peer)
    residual_steps, scaling_steps = residual(), scaling()
    next(residual_steps)
    next(scaling_steps)
    row = lax.broadcasted_iota(jnp.int32, (64, 256), 0)

    def gather_context(hh):
        way = ways[hh]

        def ready(p):
            for half in range(2):
                sf[half] = cb[hh, zs[p], :, :, half * 128 : (half + 1) * 128].astype(F32).reshape(256, 128)
            for h in range(16):
                for half in range(2):
                    first = h * 256 + half * 128
                    ctx_all[hh, (c * 2 + zs[p]) * 4 + way[1][0], :, first : first + 128] = sf[
                        half, pl.ds(h, 16, stride=16), :
                    ].astype(BF16)

        landed(got_b.at[hh], rs_sem, rr_sem, 20 * hh)
        cb[hh, z, way[0][0]] = jnp.where(
            jnp.where(row < 32, swaps[0], swaps[1]) == 1, got_b[hh], own_b[hh]
        )

        def peer():
            if hh == 0:
                landed(flag_in, rs_sem, rr_sem, 21)
            landed(cross_b.at[hh], rs_sem, rr_sem, 22 + hh)
            landed(peer_b.at[hh], rs_sem, rr_sem, 24 + hh)
            wide = flag_in[...].astype(F32)
            flag = jnp.concatenate(
                [jnp.broadcast_to(wide[m * 8 : m * 8 + 1], (32, 128)) for m in range(2)], axis=0
            )
            flag = jnp.concatenate([flag, flag], axis=1)
            theirs = jnp.where(flag > 0.5, cross_b[hh].astype(F32), peer_b[hh].astype(F32))
            cb[hh, zo, way[0][0]] = theirs.astype(BF16)

        yield from gather(
            way,
            lambda p, av: cb.at[hh, zs[p], av],
            lambda p, bv: ctx_all.at[hh, (c * 2 + zs[p]) * 4 + bv],
            lambda zv, bv: ctx_all.at[hh, (co * 2 + zv) * 4 + bv],
            bs_sem,
            br_sem,
            ready,
            21 * hh,
            peer,
        )

    steps = (gather_context(0), gather_context(1))

    def both(pair):
        for one in pair:
            next(one)

    both(steps)
    next(residual_steps)
    next(scaling_steps)
    both(steps)
    both(steps)
    next(residual_steps)
    next(scaling_steps)
    next(scaling_steps)
    both(steps)
    both(steps)
    next(residual_steps)
    next(scaling_steps)
    next(scaling_steps)
    both(steps)
    loads[4].wait()

    def project(plane):
        def rows(hh, cols):
            return ctx_all[hh, pl.ds(plane * 8, 8), :, cols].reshape(128, 1024)

        def step(i, sums):
            cols = pl.ds(pl.multiple_of(i * 1024, 1024), 1024)
            last = pl.ds(pl.multiple_of(i * 1024 + CW // 2, 1024), 1024)
            one = lax.dot_general(wo[:, cols], rows(0, cols), NT, preferred_element_type=F32)
            two = lax.dot_general(rows(1, cols), wo[:, last], NT, preferred_element_type=F32)
            return sums[0] + one, sums[1] + two

        one, two = lax.fori_loop(
            0, CW // 2048, step, (jnp.zeros((COLS, 128), F32), jnp.zeros((128, COLS), F32))
        )
        for zv in range(2):
            for i in range(4):
                for j in range(4):
                    src, dst = ((zv * 4 + i) * 4 + j) * 4, ((zv * 4 + j) * 4 + i) * 4
                    turned[dst : dst + 4, :COLS] = two[src : src + 4]
        lanes = pl.ds(pl.multiple_of(plane * 128, 128), 128)
        return (wt[:COLS, lanes] + (one + turned[...].T[:COLS])).astype(BF16)

    def gather_hidden(i):
        half = (c, co)[i]
        return gather(
            ways[i],
            lambda p, av: ht.at[half, ((c * 2 + zs[p]) * 4 + ways[i][1][0]) * 4 + av],
            lambda p, bv: ht.at[half, pl.ds(((c * 2 + zs[p]) * 4 + bv) * 4, 4)],
            lambda zv, bv: ht.at[(co, c)[i], pl.ds(((co * 2 + zv) * 4 + bv) * 4, 4)],
            cs_sem,
            cr_sem,
            lambda p: None,
            21 * i,
        )

    early, late = gather_hidden(0), gather_hidden(1)

    def features(plane, half, n):
        parts = []
        for x2 in range(2):
            for yv in range(4):
                xv = n // 2 * 2 + x2
                bv, av = yv * (1 - half) + xv * half, xv * (1 - half) + yv * half
                parts.append(ht[half, ((plane * 2 + lax.rem(n, 2)) * 4 + bv) * 4 + av])
        return jnp.concatenate(parts, axis=0)

    def expand(plane, i, *ps):
        half = (c, co)[i]

        def step(k, total):
            n = (k // len(ps)) * 2 + (zs[ps[0]] if len(ps) == 1 else lax.rem(k, 2))
            cols = pl.ds(pl.multiple_of(n * 896, 128), 896)
            part = features(plane, half, n)
            acc[i] += jnp.dot(w2[plane, :, cols], part, preferred_element_type=F32)
            wide = part.astype(F32)
            return total + jnp.sum((wide * wide).reshape(112, 8, 128), axis=0)

        squares[i] += lax.fori_loop(0, 2 * len(ps), step, jnp.zeros((8, 128), F32))

    def activate(i):
        factor = lax.rsqrt(jnp.sum(squares[i], axis=0, keepdims=True) * (1.0 / D) + 1e-5)
        gate = acc[i, :FH] * factor
        act = gate / (1.0 + jnp.exp(-gate)) * (acc[i, FH:] * factor)
        return act.T.astype(BF16)

    ht[c, me[0]] = project(c)
    next(early)
    both(steps)
    both(steps)
    ht[co, me[1]] = project(co)
    next(late)
    acc[...] = jnp.zeros_like(acc)
    squares[...] = jnp.zeros_like(squares)
    before = len(started)
    for i in range(4):
        next(early)
        next(late)
        if i == 0:
            drain(len(started) - before)
    next(early)
    expand(c, 0, 0, 1)
    next(late)
    next(early)
    next(early)
    expand(co, 1, 0, 1)
    expand(c, 1, 0, 1)
    act_out[...] = activate(1)
    push(act_out, act_in, rs_sem, rr_sem, 19, sibling)
    next(late)
    expand(co, 0, 0)
    next(late)
    expand(co, 0, 1)

    act_own = activate(0)
    loads[5].wait()
    landed(wd.at[pl.ds(FH, FH)], rs_sem, rr_sem, 18)
    landed(act_in, rs_sem, rr_sem, 19)
    lhs = jnp.concatenate([act_own, act_in[...]], axis=1)

    def other_order():
        wide_lhs = lhs.astype(F32)
        for zv in range(2):
            for i in range(4):
                for j in range(4):
                    src, dst = ((zv * 4 + i) * 4 + j) * 4, ((zv * 4 + j) * 4 + i) * 4
                    lhs_f[dst : dst + 4, :] = wide_lhs[src : src + 4]
        return lhs_f[...].astype(BF16)

    def reduction(h):
        rows = other_order() if h else lhs
        ak, (b, b1, b2, b3), a_other, b_other = ways[h]
        a, b_right, b_left = ak[0], b_other[1], b_other[3]
        for j in range(2):
            cols = pl.ds(j * 1792, 1792)
            part = jnp.dot(rows, wd[:, pl.ds(h * 3584 + j * 1792, 1792)], preferred_element_type=F32)
            p_own[h, :, :, cols] = part.astype(BF16).reshape(8, 16, 1792)

        def slab(p, k):
            return p_own.at[h, zs[p] * 4 + k]

        def send(ref, i, to):
            push(ref, r2.at[h, i], ds_sem, dr_sem, 2 + 6 * h + i, to)

        def wait(i):
            landed(r2.at[h, i], ds_sem, dr_sem, 2 + 6 * h + i)

        send(slab(0, b2), 0, b_left)
        send(slab(1, b2), 1, b_right)
        send(slab(1, b3), 3, b_left)
        send(slab(0, b1), 4, b_right)
        yield
        for i, p, k, to, j in ((0, 0, b3, b_left, 2), (1, 1, b1, b_right, 5)):
            wait(i)
            ref = slab(p, k)
            ref[...] = (ref[...].astype(F32) + r2[h, i].astype(F32)).astype(BF16)
            send(ref, j, to)
        yield
        for i in (3, 4, 2, 5):
            wait(i)
        for p in (1, 0):
            total = (
                p_own[h, zs[p] * 4 + b].astype(F32) + r2[h, 2 + p].astype(F32) + r2[h, 4 + p].astype(F32)
            )
            for av in range(4):
                for q in range(4):
                    qf[av, q * 4 : q * 4 + 4, :] = total[av * 4 : av * 4 + 4, q * 896 : (q + 1) * 896]
            qb[h, p] = qf[...].astype(BF16)
            for k in (1, 3, 2):
                push(
                    qb.at[h, p, ak[k]], r1.at[h, p, k - 1], ds_sem, dr_sem, 13 + 6 * h + 3 * p + k, a_other[k]
                )
        yield
        sums = []
        for p in (1, 0):
            total = qb[h, p, a].astype(F32)
            for k in (1, 3, 2):
                landed(r1.at[h, p, k - 1], ds_sem, dr_sem, 13 + 6 * h + 3 * p + k)
                total = total + r1[h, p, k - 1].astype(F32)
            sums.append(total)
            if p == 1:
                tz[h] = total.astype(BF16)
                push(tz.at[h], got_peer.at[h], ds_sem, dr_sem, 26 + 3 * h, z_peer)
                push(tz.at[h], got_cross.at[h], ds_sem, dr_sem, 27 + 3 * h, cross)
        tp0[h] = sums[1].astype(BF16)
        push(tp0.at[h], got_partner.at[h], ds_sem, dr_sem, 28 + 3 * h, partner)
        t0[h] = sums[1]
        yield
        landed(got_partner.at[h], ds_sem, dr_sem, 28 + 3 * h)
        landed(got_cross.at[h], ds_sem, dr_sem, 27 + 3 * h)
        landed(got_peer.at[h], ds_sem, dr_sem, 26 + 3 * h)
        stayed = hid[h].astype(F32) + (t0[h] + got_peer[h].astype(F32))
        moved = hid_got[h].astype(F32) + (got_partner[h].astype(F32) + got_cross[h].astype(F32))
        row = lax.rem(lax.broadcasted_iota(jnp.int32, (16, 896), 0), 4)
        final = jnp.where(jnp.where(row < 2, swaps[0], swaps[1]) == 1, moved, stayed)
        request = lax.broadcasted_iota(jnp.int32, (4, 896), 0)
        for q in range(4):
            rows = jnp.zeros((4, 896), F32)
            for p in range(4):
                one = jnp.broadcast_to(final[q * 4 + p : q * 4 + p + 1], (4, 896))
                rows = jnp.where(request == assign_ref[p], one, rows)
            out_ref[:, h * 3584 + q * 896 : h * 3584 + (q + 1) * 896] = rows.astype(BF16)
        yield

    def own_hidden(h):
        lane = lax.broadcasted_iota(jnp.int32, (16, 128), 1)
        sub = lax.broadcasted_iota(jnp.int32, (16, 128), 0)
        rows = jnp.zeros((16, 896), F32)
        for q in range(4):
            pick = jnp.where(lane == me_row + sub - q * 4, 1.0, 0.0)
            pick = jnp.where((sub >= q * 4) & (sub < q * 4 + 4), pick, 0.0).astype(BF16)
            xv, zv = 2 * h + q // 2, q % 2
            parts = []
            for yv in range(4):
                for plane in range(2):
                    bv, av = yv * co + xv * c, xv * co + yv * c
                    parts.append(ht[c, ((plane * 2 + zv) * 4 + bv) * 4 + av])
            rows = rows + lax.dot_general(
                pick, jnp.concatenate(parts, axis=0), NT, preferred_element_type=F32
            )
        hid[h] = rows.astype(BF16)
        push(hid.at[h], hid_got.at[h], rs_sem, rr_sem, 16 + h, partner)

    halves = (reduction(0), reduction(1))
    before = len(started)
    for half in halves:
        next(half)
    own_hidden(0)
    drain(len(started) - before)
    next(halves[0])
    own_hidden(1)
    next(halves[1])
    for _ in range(2):
        for half in halves:
            next(half)
    for h in range(2):
        landed(hid_got.at[h], rs_sem, rr_sem, 16 + h)
    for half in halves:
        next(half)
    drain()


def per_device(
    queries, keys, values, lengths, resid, assign, matching, w_out, gain, gate_w, up_w, down_w
):
    smem = pl.BlockSpec(memory_space=pltpu.SMEM)
    vmem = pl.BlockSpec(memory_space=pltpu.VMEM)
    hbm = pl.BlockSpec(memory_space=pl.ANY)
    dma = pltpu.SemaphoreType.DMA
    scratch = (
        ((4, CW), BF16),
        ((4, 1024, 256), BF16),
        ((4, 1024, 256), BF16),
        ((COLS, CW), BF16),
        ((FH, D), BF16),
        ((FH, D), BF16),
        ((2, 2 * FH, D // 2), BF16),
        ((2 * FH, D), BF16),
        ((4, D), BF16),
        ((1, D), F32),
        ((2, 128, 128), F32),
        ((2, 64, 256), BF16),
        ((2, 64, 256), BF16),
        ((2, 64, 256), BF16),
        ((2, 64, 256), BF16),
        ((16, 128), F32),
        ((16, 128), BF16),
        ((16, 128), BF16),
        ((2, 2, 4, 64, 256), BF16),
        ((2, 256, 128), F32),
        ((2, 16, 16, CW // 2), BF16),
        ((2, 64, COLS, 128), BF16),
        ((2, 2 * FH, 128), F32),
        ((2, 8, 128), F32),
        ((128, FH), BF16),
        ((128, FH), BF16),
        ((8, 16, 256), F32),
        ((8, 16, 256), BF16),
        ((8, 16, 256), BF16),
        ((8, 16, 256), BF16),
        ((8, 32, 128), F32),
        ((8, 32, 128), BF16),
        ((8, 32, 128), BF16),
        ((256, 128), F32),
        ((128, 256), F32),
        ((128, 128), F32),
        ((128, 2 * FH), F32),
        ((2, 8, 16, D // 2), BF16),
        ((2, 6, 16, D // 2), BF16),
        ((4, 16, 896), F32),
        ((2, 2, 4, 16, 896), BF16),
        ((2, 2, 3, 16, 896), BF16),
        ((2, 16, 896), F32),
    ) + (((2, 16, 896), BF16),) * 7
    return pl.pallas_call(
        kernel,
        out_shape=pltpu.VMEM((4, D), BF16),
        in_specs=[smem] * 3 + [hbm] * 9,
        out_specs=vmem,
        scratch_shapes=[pltpu.VMEM(shape, dtype) for shape, dtype in scratch]
        + [dma((n,)) for n in (8, 7, 42, 42, 42, 42, 32, 32, 26, 26)],
        compiler_params=pltpu.CompilerParams(
            collective_id=0, has_side_effects=True, vmem_limit_bytes=60 * 1024 * 1024
        ),
    )(
        lengths, assign[0], matching[:, 0, 0], queries, resid, gain[None],
        keys, values, w_out.T, gate_w[0].T, up_w[0].T, down_w[0],
    )


def solution(mesh):
    rows = P(("attn", "grp", "tp"), None)
    cache = P(("attn", "grp", "tp"), None, None)
    placed = (
        rows,
        cache,
        cache,
        P(("attn", "grp", "tp")),
        rows,
        rows,
        P(None, "attn", "tp"),
        P(None, ("attn", "tp")),
        P(),
        P("grp", None, ("attn", "tp")),
        P("grp", None, ("attn", "tp")),
        P("grp", ("attn", "tp"), None),
    )
    return jax.shard_map(
        per_device, mesh=mesh, in_specs=placed, out_specs=rows, check_vma=False
    )
```

```python
import jax
import jax.numpy as jnp
from jax import lax
from jax.experimental import pallas as pl
from jax.experimental.pallas import tpu as pltpu
from jax.sharding import PartitionSpec as P

D = 7168
CW = 8192
FH = 288
COLS = 112
MESH = pl.DeviceIdType.MESH
F32 = jnp.float32
BF16 = jnp.bfloat16
NT = (((1,), (1,)), ((), ()))


def kernel(
    len_ref, assign_ref, match_ref, q_hbm, resid_hbm, gain_hbm, k_hbm, v_hbm, wo_hbm, g_hbm, u_hbm, d_hbm,
    out_ref,
    q_ref, kc, vc, wo, wg, wu, w2, wd, resid_ref, gain_ref,
    qs, own_b, got_b, cross_b, peer_b, flags, flag_out, flag_in, cb, sf, ctx_all, ht, acc, squares, act_out, act_in,
    s1f, s1, s1_got, t1, uf, ub, vb, wf, wt, turned, lhs_f,
    p_own, r2, qf, qb, r1, t0, tp0, tz, got_peer, got_partner, got_cross, hid, hid_got,
    kv_sem, w_sem, bs_sem, br_sem, cs_sem, cr_sem, ds_sem, dr_sem, rs_sem, rr_sem,
):
    attn, grp, tp = lax.axis_index("attn"), lax.axis_index("grp"), lax.axis_index("tp")
    x, z, y, c = attn // 2, lax.rem(attn, 2), tp // 2, lax.rem(tp, 2)
    zo, co = 1 - z, 1 - c
    zs = (z, zo)
    def dev(x_, z_, y_, c_):
        return (lax.rem(x_, 4) * 2 + z_, grp, lax.rem(y_, 4) * 2 + c_)

    z_peer, sibling = dev(x, zo, y, c), dev(x, z, y, co)
    partner = (attn, 1 - grp, tp)
    cross = (x * 2 + zo, 1 - grp, tp)

    def axes(e):
        a, b = x * (1 - e) + y * e, y * (1 - e) + x * e
        return (
            [lax.rem(a + k, 4) for k in range(4)],
            [lax.rem(b + k, 4) for k in range(4)],
            [dev(x + k * (1 - e), z, y + k * e, c) for k in range(4)],
            [dev(x + k * e, z, y + k * (1 - e), c) for k in range(4)],
        )

    ways = (axes(c), axes(co))

    q_load = pltpu.make_async_copy(q_hbm, q_ref, w_sem.at[6])
    q_load.start()
    fetch = []
    for src, dst in ((k_hbm, kc), (v_hbm, vc)):
        for r in range(4):
            fetch.append(pltpu.make_async_copy(src.at[r], dst.at[r], kv_sem.at[len(fetch)]))
            fetch[-1].start()
    loads = [
        pltpu.make_async_copy(src, dst, w_sem.at[i])
        for i, (src, dst) in enumerate(
            ((resid_hbm, resid_ref), (gain_hbm, gain_ref), (g_hbm, wg), (u_hbm, wu), (wo_hbm, wo), (d_hbm, wd.at[pl.ds(0, FH)]))
        )
    ]
    barrier = pltpu.get_barrier_semaphore()
    others = [partner, cross]
    for k in range(1, 8):
        others.append((lax.rem(attn + k, 8), grp, tp))
        others.append((attn, grp, lax.rem(tp + k, 8)))
    for other in others:
        pl.semaphore_signal(barrier, inc=1, device_id=other, device_id_type=MESH)

    started = []

    def drain(keep=0):
        while len(started) > keep:
            started.pop(0).wait_send()

    def push(src, dst, s_sem, r_sem, i, to):
        copy = pltpu.make_async_remote_copy(
            src_ref=src, dst_ref=dst, send_sem=s_sem.at[i], recv_sem=r_sem.at[i],
            device_id=to, device_id_type=MESH,
        )
        copy.start()
        started.append(copy)

    def landed(dst, s_sem, r_sem, i):
        pltpu.make_async_remote_copy(
            src_ref=dst, dst_ref=dst, send_sem=s_sem.at[i], recv_sem=r_sem.at[i],
            device_id=sibling, device_id_type=MESH,
        ).wait_recv()

    q_load.wait()
    wide_q = q_ref[...].astype(F32)
    for h in range(32):
        for half in range(2):
            first = h * 256 + half * 128
            qs[half, pl.ds(h, 4, stride=32), :] = wide_q[:, first : first + 128]
    slot = lax.broadcasted_iota(jnp.int32, (32, 1024), 1)
    swaps = (match_ref[0], match_ref[1])

    def weigh(r):
        query = jnp.concatenate([qs[half, r * 32 : (r + 1) * 32] for half in range(2)], axis=1).astype(BF16)
        scores = lax.dot_general(query, kc[r], NT, preferred_element_type=F32) * (256 ** -0.5)
        scores = jnp.where(slot < len_ref[r], scores, -1e30)
        expo = jnp.exp(scores - jnp.max(scores, axis=-1, keepdims=True))
        return (expo / jnp.sum(expo, axis=-1, keepdims=True)).astype(BF16)

    for copy in fetch[:4]:
        copy.wait()
    for load in loads:
        load.start()
    probs = [weigh(r) for r in range(4)]
    for copy in fetch[4:]:
        copy.wait()
    contexts = [jnp.dot(probs[r], vc[r], preferred_element_type=F32) for r in range(4)]
    for p in range(4):
        chosen = contexts[0]
        for r in range(1, 4):
            chosen = jnp.where(assign_ref[p] == r, contexts[r], chosen)
        for hh in range(2):
            own_b[hh, p * 16 : p * 16 + 16] = chosen[hh * 16 : hh * 16 + 16].astype(BF16)
    pl.semaphore_wait(barrier, 16)

    def gather(way, block, part, other, s_sem, r_sem, ready, base, peer=None):
        ak, bk, a_other, b_other = way
        a, (b, b1, b2, b3) = ak[0], bk
        b_right, b_left = b_other[1], b_other[3]

        def send(ref, i, to):
            push(ref, ref, s_sem, r_sem, base + i, to)

        def wait(ref, i):
            landed(ref, s_sem, r_sem, base + i)

        def ring_1(p):
            for k in (1, 3, 2):
                send(block(p, a), 3 * p + k, a_other[k])

        def ring_2(p):
            for k in (1, 3, 2):
                wait(block(p, ak[4 - k]), 3 * p + k)
            ready(p)
            first, second = ((7, b_right), (8, b_left)) if p == 0 else ((10, b_left), (9, b_right))
            send(part(p, b), *first)
            send(part(p, b), *second)
            send(part(p, b), 13 + p, sibling)

        if peer is None:
            send(block(0, a), 0, z_peer)
        ring_1(0)
        yield
        if peer is None:
            ring_2(0)
            wait(block(1, a), 0)
            ring_1(1)
        else:
            peer()
            ring_1(1)
            ring_2(0)
        yield
        ring_2(1)
        yield
        wait(part(0, b3), 7)
        send(part(0, b3), 11, b_right)
        send(part(0, b3), 15, sibling)
        wait(part(0, b1), 8)
        send(part(0, b1), 16, sibling)
        yield
        wait(part(1, b1), 10)
        send(part(1, b1), 12, b_left)
        send(part(1, b1), 17, sibling)
        wait(part(1, b3), 9)
        send(part(1, b3), 18, sibling)
        yield
        wait(part(0, b2), 11)
        send(part(0, b2), 19, sibling)
        wait(part(1, b2), 12)
        send(part(1, b2), 20, sibling)
        yield
        for p, spots in enumerate((((13, 0), (15, 3), (16, 1), (19, 2)), ((14, 0), (18, 3), (17, 1), (20, 2)))):
            for i, k in spots:
                wait(other(zs[p], ak[k]), i)
            yield

    a, b = ways[0][0][0], ways[0][1][0]
    me = (((c * 2 + z) * 4 + b) * 4 + a, ((c * 2 + z) * 4 + a) * 4 + b)
    me_row = ((z * 4 + b) * 4 + a) * 4

    def residual():
        loads[0].wait()
        wide_r = resid_ref[...].astype(F32)
        ordered = []
        for p in range(4):
            chosen = wide_r[0:1]
            for r in range(1, 4):
                chosen = jnp.where(assign_ref[p] == r, wide_r[r : r + 1], chosen)
            ordered.append(chosen)
        ordered = jnp.concatenate(ordered, axis=0)
        s1f[...] = jnp.zeros_like(s1f)
        for n in range(8):
            for t in range(8):
                first = n * 896 + t * COLS
                s1f[n, (t % 4) * 4 : (t % 4) * 4 + 4, (t // 4) * 128 : (t // 4) * 128 + COLS] = ordered[
                    :, first : first + COLS
                ]
        s1[...] = s1f[...].astype(BF16)
        push(s1, s1_got, rs_sem, rr_sem, 1, partner)
        yield
        landed(s1_got, rs_sem, rr_sem, 1)
        row = lax.rem(lax.broadcasted_iota(jnp.int32, (8, 16, 256), 1), 4)
        served = jnp.where(jnp.where(row < 2, swaps[0], swaps[1]) == 1, s1_got[...], s1[...])
        s1_got[...] = served
        t1[attn] = s1_got[attn]
        for k in range(1, 8):
            to = lax.rem(attn + k, 8)
            push(s1_got.at[to], t1.at[attn], rs_sem, rr_sem, 1 + k, (to, grp, tp))
        yield
        for k in range(1, 8):
            landed(t1.at[lax.rem(attn + 8 - k, 8)], rs_sem, rr_sem, 1 + k)
        for n in range(8):
            part = t1[n].astype(F32)
            for t in range(8):
                uf[t, n * 4 : n * 4 + 4, :] = part[
                    (t % 4) * 4 : (t % 4) * 4 + 4, (t // 4) * 128 : (t // 4) * 128 + 128
                ]
        ub[...] = uf[...].astype(BF16)
        vb[tp] = ub[tp]
        for k in range(1, 8):
            to = lax.rem(tp + k, 8)
            push(ub.at[to], vb.at[tp], rs_sem, rr_sem, 8 + k, (attn, grp, to))
        yield
        for k in range(1, 8):
            landed(vb.at[lax.rem(tp + 8 - k, 8)], rs_sem, rr_sem, 8 + k)
        for t in range(8):
            part = vb[t].astype(F32)
            for n in range(8):
                plane, zv = t % 2, n % 2
                bv, av = (n // 2, t // 2) if plane else (t // 2, n // 2)
                place = (((plane * 2 + zv) * 4 + bv) * 4 + av) * 4
                wf[place : place + 4, :] = part[n * 4 : n * 4 + 4]
        wt[...] = wf[...].T
        yield

    def scaling():
        for i in (1, 2, 3):
            loads[i].wait()

        def scale(i, _):
            rows = pl.ds(pl.multiple_of(i * 16, 16), 16)
            for k, src in enumerate((wg, wu)):
                spot = pl.ds(pl.multiple_of(k * FH + i * 16, 16), 16)
                wide = (src[rows, :].astype(F32) * gain_ref[...]).astype(BF16)
                for cv in range(2):
                    for xv in range(4):
                        first = [
                            ((xv // 2 * 4 + x2 * 2 + xv % 2) * 8 + yv * 2 + cv) * COLS
                            for x2 in range(2)
                            for yv in range(4)
                        ]
                        w2[cv, spot, xv * 896 : (xv + 1) * 896] = jnp.concatenate(
                            [wide[:, f : f + COLS] for f in first], axis=1
                        )
            return 0

        for part in range(6):
            lax.fori_loop(part * 3, part * 3 + 3, scale, 0)
            yield

    for m in range(2):
        flags[m * 8 : m * 8 + 8, :] = jnp.full((8, 128), swaps[m], jnp.int32).astype(F32)
    flag_out[...] = flags[...].astype(BF16)
    for hh in range(2):
        push(own_b.at[hh], got_b.at[hh], rs_sem, rr_sem, 20 * hh, partner)
    push(flag_out, flag_in, rs_sem, rr_sem, 21, z_peer)
    for hh in range(2):
        push(own_b.at[hh], cross_b.at[hh], rs_sem, rr_sem, 22 + hh, cross)
        push(own_b.at[hh], peer_b.at[hh], rs_sem, rr_sem, 24 + hh, z_peer)
    push(d_hbm, wd.at[pl.ds(FH, FH)], rs_sem, rr_sem, 18, sibling)
    residual_steps, scaling_steps = residual(), scaling()
    next(residual_steps)
    next(scaling_steps)
    row = lax.broadcasted_iota(jnp.int32, (64, 256), 0)

    def gather_context(hh):
        way = ways[hh]

        def ready(p):
            for half in range(2):
                sf[half] = cb[hh, zs[p], :, :, half * 128 : (half + 1) * 128].astype(F32).reshape(256, 128)
            for h in range(16):
                for half in range(2):
                    first = h * 256 + half * 128
                    ctx_all[hh, (c * 2 + zs[p]) * 4 + way[1][0], :, first : first + 128] = sf[
                        half, pl.ds(h, 16, stride=16), :
                    ].astype(BF16)

        landed(got_b.at[hh], rs_sem, rr_sem, 20 * hh)
        cb[hh, z, way[0][0]] = jnp.where(
            jnp.where(row < 32, swaps[0], swaps[1]) == 1, got_b[hh], own_b[hh]
        )

        def peer():
            if hh == 0:
                landed(flag_in, rs_sem, rr_sem, 21)
            landed(cross_b.at[hh], rs_sem, rr_sem, 22 + hh)
            landed(peer_b.at[hh], rs_sem, rr_sem, 24 + hh)
            wide = flag_in[...].astype(F32)
            flag = jnp.concatenate(
                [jnp.broadcast_to(wide[m * 8 : m * 8 + 1], (32, 128)) for m in range(2)], axis=0
            )
            flag = jnp.concatenate([flag, flag], axis=1)
            theirs = jnp.where(flag > 0.5, cross_b[hh].astype(F32), peer_b[hh].astype(F32))
            cb[hh, zo, way[0][0]] = theirs.astype(BF16)

        yield from gather(
            way,
            lambda p, av: cb.at[hh, zs[p], av],
            lambda p, bv: ctx_all.at[hh, (c * 2 + zs[p]) * 4 + bv],
            lambda zv, bv: ctx_all.at[hh, (co * 2 + zv) * 4 + bv],
            bs_sem,
            br_sem,
            ready,
            21 * hh,
            peer,
        )

    steps = (gather_context(0), gather_context(1))

    def both(pair):
        for one in pair:
            next(one)

    both(steps)
    next(residual_steps)
    both(steps)
    next(scaling_steps)
    both(steps)
    next(residual_steps)
    next(scaling_steps)
    both(steps)
    next(scaling_steps)
    both(steps)
    next(scaling_steps)
    next(residual_steps)
    next(scaling_steps)
    both(steps)
    loads[4].wait()

    def project(plane):
        def rows(hh, cols):
            return ctx_all[hh, pl.ds(plane * 8, 8), :, cols].reshape(128, 1024)

        def step(i, sums):
            cols = pl.ds(pl.multiple_of(i * 1024, 1024), 1024)
            last = pl.ds(pl.multiple_of(i * 1024 + CW // 2, 1024), 1024)
            one = lax.dot_general(wo[:, cols], rows(0, cols), NT, preferred_element_type=F32)
            two = lax.dot_general(rows(1, cols), wo[:, last], NT, preferred_element_type=F32)
            return sums[0] + one, sums[1] + two

        one, two = lax.fori_loop(
            0, CW // 2048, step, (jnp.zeros((COLS, 128), F32), jnp.zeros((128, COLS), F32))
        )
        for zv in range(2):
            for i in range(4):
                for j in range(4):
                    src, dst = ((zv * 4 + i) * 4 + j) * 4, ((zv * 4 + j) * 4 + i) * 4
                    turned[dst : dst + 4, :COLS] = two[src : src + 4]
        lanes = pl.ds(pl.multiple_of(plane * 128, 128), 128)
        return (wt[:COLS, lanes] + (one + turned[...].T[:COLS])).astype(BF16)

    def gather_hidden(i):
        half = (c, co)[i]
        return gather(
            ways[i],
            lambda p, av: ht.at[half, ((c * 2 + zs[p]) * 4 + ways[i][1][0]) * 4 + av],
            lambda p, bv: ht.at[half, pl.ds(((c * 2 + zs[p]) * 4 + bv) * 4, 4)],
            lambda zv, bv: ht.at[(co, c)[i], pl.ds(((co * 2 + zv) * 4 + bv) * 4, 4)],
            cs_sem,
            cr_sem,
            lambda p: None,
            21 * i,
        )

    early, late = gather_hidden(0), gather_hidden(1)

    def features(plane, half, n):
        parts = []
        for x2 in range(2):
            for yv in range(4):
                xv = n // 2 * 2 + x2
                bv, av = yv * (1 - half) + xv * half, xv * (1 - half) + yv * half
                parts.append(ht[half, ((plane * 2 + lax.rem(n, 2)) * 4 + bv) * 4 + av])
        return jnp.concatenate(parts, axis=0)

    def expand(plane, i, *ps):
        half = (c, co)[i]

        def step(k, total):
            n = (k // len(ps)) * 2 + (zs[ps[0]] if len(ps) == 1 else lax.rem(k, 2))
            cols = pl.ds(pl.multiple_of(n * 896, 128), 896)
            part = features(plane, half, n)
            acc[i] += jnp.dot(w2[plane, :, cols], part, preferred_element_type=F32)
            wide = part.astype(F32)
            return total + jnp.sum((wide * wide).reshape(112, 8, 128), axis=0)

        squares[i] += lax.fori_loop(0, 2 * len(ps), step, jnp.zeros((8, 128), F32))

    def activate(i):
        factor = lax.rsqrt(jnp.sum(squares[i], axis=0, keepdims=True) * (1.0 / D) + 1e-5)
        gate = acc[i, :FH] * factor
        act = gate / (1.0 + jnp.exp(-gate)) * (acc[i, FH:] * factor)
        return act.T.astype(BF16)

    ht[c, me[0]] = project(c)
    next(early)
    both(steps)
    both(steps)
    ht[co, me[1]] = project(co)
    next(late)
    acc[...] = jnp.zeros_like(acc)
    squares[...] = jnp.zeros_like(squares)
    before = len(started)
    for i in range(4):
        next(early)
        next(late)
        if i == 0:
            drain(len(started) - before)
    next(early)
    expand(c, 0, 0, 1)
    next(late)
    next(early)
    next(early)
    expand(co, 1, 0, 1)
    expand(c, 1, 0, 1)
    act_out[...] = activate(1)
    push(act_out, act_in, rs_sem, rr_sem, 19, sibling)
    next(late)
    expand(co, 0, 0)
    next(late)
    expand(co, 0, 1)

    act_own = activate(0)
    loads[5].wait()
    landed(wd.at[pl.ds(FH, FH)], rs_sem, rr_sem, 18)
    landed(act_in, rs_sem, rr_sem, 19)
    lhs = jnp.concatenate([act_own, act_in[...]], axis=1)

    def other_order():
        wide_lhs = lhs.astype(F32)
        for zv in range(2):
            for i in range(4):
                for j in range(4):
                    src, dst = ((zv * 4 + i) * 4 + j) * 4, ((zv * 4 + j) * 4 + i) * 4
                    lhs_f[dst : dst + 4, :] = wide_lhs[src : src + 4]
        return lhs_f[...].astype(BF16)

    def reduction(h):
        rows = other_order() if h else lhs
        ak, (b, b1, b2, b3), a_other, b_other = ways[h]
        a, b_right, b_left = ak[0], b_other[1], b_other[3]
        for j in range(2):
            cols = pl.ds(j * 1792, 1792)
            part = jnp.dot(rows, wd[:, pl.ds(h * 3584 + j * 1792, 1792)], preferred_element_type=F32)
            p_own[h, :, :, cols] = part.astype(BF16).reshape(8, 16, 1792)

        def slab(p, k):
            return p_own.at[h, zs[p] * 4 + k]

        def send(ref, i, to):
            push(ref, r2.at[h, i], ds_sem, dr_sem, 2 + 6 * h + i, to)

        def wait(i):
            landed(r2.at[h, i], ds_sem, dr_sem, 2 + 6 * h + i)

        send(slab(0, b2), 0, b_left)
        send(slab(1, b2), 1, b_right)
        send(slab(1, b3), 3, b_left)
        send(slab(0, b1), 4, b_right)
        yield
        for i, p, k, to, j in ((0, 0, b3, b_left, 2), (1, 1, b1, b_right, 5)):
            wait(i)
            ref = slab(p, k)
            ref[...] = (ref[...].astype(F32) + r2[h, i].astype(F32)).astype(BF16)
            send(ref, j, to)
        yield
        for i in (3, 4, 2, 5):
            wait(i)
        for p in (1, 0):
            total = (
                p_own[h, zs[p] * 4 + b].astype(F32) + r2[h, 2 + p].astype(F32) + r2[h, 4 + p].astype(F32)
            )
            for av in range(4):
                for q in range(4):
                    qf[av, q * 4 : q * 4 + 4, :] = total[av * 4 : av * 4 + 4, q * 896 : (q + 1) * 896]
            qb[h, p] = qf[...].astype(BF16)
            for k in (1, 3, 2):
                push(
                    qb.at[h, p, ak[k]], r1.at[h, p, k - 1], ds_sem, dr_sem, 13 + 6 * h + 3 * p + k, a_other[k]
                )
        yield
        sums = []
        for p in (1, 0):
            total = qb[h, p, a].astype(F32)
            for k in (1, 3, 2):
                landed(r1.at[h, p, k - 1], ds_sem, dr_sem, 13 + 6 * h + 3 * p + k)
                total = total + r1[h, p, k - 1].astype(F32)
            sums.append(total)
            if p == 1:
                tz[h] = total.astype(BF16)
                push(tz.at[h], got_peer.at[h], ds_sem, dr_sem, 26 + 3 * h, z_peer)
                push(tz.at[h], got_cross.at[h], ds_sem, dr_sem, 27 + 3 * h, cross)
        tp0[h] = sums[1].astype(BF16)
        push(tp0.at[h], got_partner.at[h], ds_sem, dr_sem, 28 + 3 * h, partner)
        t0[h] = sums[1]
        yield
        landed(got_partner.at[h], ds_sem, dr_sem, 28 + 3 * h)
        landed(got_cross.at[h], ds_sem, dr_sem, 27 + 3 * h)
        landed(got_peer.at[h], ds_sem, dr_sem, 26 + 3 * h)
        stayed = hid[h].astype(F32) + (t0[h] + got_peer[h].astype(F32))
        moved = hid_got[h].astype(F32) + (got_partner[h].astype(F32) + got_cross[h].astype(F32))
        row = lax.rem(lax.broadcasted_iota(jnp.int32, (16, 896), 0), 4)
        final = jnp.where(jnp.where(row < 2, swaps[0], swaps[1]) == 1, moved, stayed)
        request = lax.broadcasted_iota(jnp.int32, (4, 896), 0)
        for q in range(4):
            rows = jnp.zeros((4, 896), F32)
            for p in range(4):
                one = jnp.broadcast_to(final[q * 4 + p : q * 4 + p + 1], (4, 896))
                rows = jnp.where(request == assign_ref[p], one, rows)
            out_ref[:, h * 3584 + q * 896 : h * 3584 + (q + 1) * 896] = rows.astype(BF16)
        yield

    def own_hidden(h):
        lane = lax.broadcasted_iota(jnp.int32, (16, 128), 1)
        sub = lax.broadcasted_iota(jnp.int32, (16, 128), 0)
        rows = jnp.zeros((16, 896), F32)
        for q in range(4):
            pick = jnp.where(lane == me_row + sub - q * 4, 1.0, 0.0)
            pick = jnp.where((sub >= q * 4) & (sub < q * 4 + 4), pick, 0.0).astype(BF16)
            xv, zv = 2 * h + q // 2, q % 2
            parts = []
            for yv in range(4):
                for plane in range(2):
                    bv, av = yv * co + xv * c, xv * co + yv * c
                    parts.append(ht[c, ((plane * 2 + zv) * 4 + bv) * 4 + av])
            rows = rows + lax.dot_general(
                pick, jnp.concatenate(parts, axis=0), NT, preferred_element_type=F32
            )
        hid[h] = rows.astype(BF16)
        push(hid.at[h], hid_got.at[h], rs_sem, rr_sem, 16 + h, partner)

    halves = (reduction(0), reduction(1))
    before = len(started)
    for half in halves:
        next(half)
    own_hidden(0)
    drain(len(started) - before)
    next(halves[0])
    own_hidden(1)
    next(halves[1])
    for _ in range(2):
        for half in halves:
            next(half)
    for h in range(2):
        landed(hid_got.at[h], rs_sem, rr_sem, 16 + h)
    for half in halves:
        next(half)
    drain()


def per_device(
    queries, keys, values, lengths, resid, assign, matching, w_out, gain, gate_w, up_w, down_w
):
    smem = pl.BlockSpec(memory_space=pltpu.SMEM)
    vmem = pl.BlockSpec(memory_space=pltpu.VMEM)
    hbm = pl.BlockSpec(memory_space=pl.ANY)
    dma = pltpu.SemaphoreType.DMA
    scratch = (
        ((4, CW), BF16),
        ((4, 1024, 256), BF16),
        ((4, 1024, 256), BF16),
        ((COLS, CW), BF16),
        ((FH, D), BF16),
        ((FH, D), BF16),
        ((2, 2 * FH, D // 2), BF16),
        ((2 * FH, D), BF16),
        ((4, D), BF16),
        ((1, D), F32),
        ((2, 128, 128), F32),
        ((2, 64, 256), BF16),
        ((2, 64, 256), BF16),
        ((2, 64, 256), BF16),
        ((2, 64, 256), BF16),
        ((16, 128), F32),
        ((16, 128), BF16),
        ((16, 128), BF16),
        ((2, 2, 4, 64, 256), BF16),
        ((2, 256, 128), F32),
        ((2, 16, 16, CW // 2), BF16),
        ((2, 64, COLS, 128), BF16),
        ((2, 2 * FH, 128), F32),
        ((2, 8, 128), F32),
        ((128, FH), BF16),
        ((128, FH), BF16),
        ((8, 16, 256), F32),
        ((8, 16, 256), BF16),
        ((8, 16, 256), BF16),
        ((8, 16, 256), BF16),
        ((8, 32, 128), F32),
        ((8, 32, 128), BF16),
        ((8, 32, 128), BF16),
        ((256, 128), F32),
        ((128, 256), F32),
        ((128, 128), F32),
        ((128, 2 * FH), F32),
        ((2, 8, 16, D // 2), BF16),
        ((2, 6, 16, D // 2), BF16),
        ((4, 16, 896), F32),
        ((2, 2, 4, 16, 896), BF16),
        ((2, 2, 3, 16, 896), BF16),
        ((2, 16, 896), F32),
    ) + (((2, 16, 896), BF16),) * 7
    return pl.pallas_call(
        kernel,
        out_shape=pltpu.VMEM((4, D), BF16),
        in_specs=[smem] * 3 + [hbm] * 9,
        out_specs=vmem,
        scratch_shapes=[pltpu.VMEM(shape, dtype) for shape, dtype in scratch]
        + [dma((n,)) for n in (8, 7, 42, 42, 42, 42, 32, 32, 26, 26)],
        compiler_params=pltpu.CompilerParams(
            collective_id=0, has_side_effects=True, vmem_limit_bytes=60 * 1024 * 1024
        ),
    )(
        lengths, assign[0], matching[:, 0, 0], queries, resid, gain[None],
        keys, values, w_out.T, gate_w[0].T, up_w[0].T, down_w[0],
    )


def solution(mesh):
    rows = P(("attn", "grp", "tp"), None)
    cache = P(("attn", "grp", "tp"), None, None)
    placed = (
        rows,
        cache,
        cache,
        P(("attn", "grp", "tp")),
        rows,
        rows,
        P(None, "attn", "tp"),
        P(None, ("attn", "tp")),
        P(),
        P("grp", None, ("attn", "tp")),
        P("grp", None, ("attn", "tp")),
        P("grp", ("attn", "tp"), None),
    )
    return jax.shard_map(
        per_device, mesh=mesh, in_specs=placed, out_specs=rows, check_vma=False
    )
```

```python
import jax
import jax.numpy as jnp
from jax import lax
from jax.experimental import pallas as pl
from jax.experimental.pallas import tpu as pltpu
from jax.sharding import PartitionSpec as P

D = 7168
CW = 8192
FH = 288
COLS = 112
MESH = pl.DeviceIdType.MESH
F32 = jnp.float32
BF16 = jnp.bfloat16
NT = (((1,), (1,)), ((), ()))


def kernel(
    len_ref, assign_ref, match_ref, q_hbm, resid_hbm, gain_hbm, k_hbm, v_hbm, wo_hbm, g_hbm, u_hbm, d_hbm,
    out_ref,
    q_ref, kc, vc, wo, wg, wu, w2, wd, resid_ref, gain_ref,
    qs, own_b, got_b, cross_b, peer_b, flags, flag_out, flag_in, cb, sf, ctx_all, ht, acc, squares, act_out, act_in,
    s1f, s1, s1_got, t1, uf, ub, vb, wf, wt, turned, lhs_f,
    p_own, r2, qf, qb, r1, t0, tp0, tz, got_peer, got_partner, got_cross, hid, hid_got,
    kv_sem, w_sem, bs_sem, br_sem, cs_sem, cr_sem, ds_sem, dr_sem, rs_sem, rr_sem,
):
    attn, grp, tp = lax.axis_index("attn"), lax.axis_index("grp"), lax.axis_index("tp")
    x, z, y, c = attn // 2, lax.rem(attn, 2), tp // 2, lax.rem(tp, 2)
    zo, co = 1 - z, 1 - c
    zs = (z, zo)
    def dev(x_, z_, y_, c_):
        return (lax.rem(x_, 4) * 2 + z_, grp, lax.rem(y_, 4) * 2 + c_)

    z_peer, sibling = dev(x, zo, y, c), dev(x, z, y, co)
    partner = (attn, 1 - grp, tp)
    cross = (x * 2 + zo, 1 - grp, tp)

    def axes(e):
        a, b = x * (1 - e) + y * e, y * (1 - e) + x * e
        return (
            [lax.rem(a + k, 4) for k in range(4)],
            [lax.rem(b + k, 4) for k in range(4)],
            [dev(x + k * (1 - e), z, y + k * e, c) for k in range(4)],
            [dev(x + k * e, z, y + k * (1 - e), c) for k in range(4)],
        )

    ways = (axes(c), axes(co))

    q_load = pltpu.make_async_copy(q_hbm, q_ref, w_sem.at[6])
    q_load.start()
    fetch = []
    for src, dst in ((k_hbm, kc), (v_hbm, vc)):
        for r in range(4):
            fetch.append(pltpu.make_async_copy(src.at[r], dst.at[r], kv_sem.at[len(fetch)]))
            fetch[-1].start()
    loads = [
        pltpu.make_async_copy(src, dst, w_sem.at[i])
        for i, (src, dst) in enumerate(
            ((resid_hbm, resid_ref), (gain_hbm, gain_ref), (g_hbm, wg), (u_hbm, wu), (wo_hbm, wo), (d_hbm, wd.at[pl.ds(0, FH)]))
        )
    ]
    barrier = pltpu.get_barrier_semaphore()
    others = [partner, cross]
    for k in range(1, 8):
        others.append((lax.rem(attn + k, 8), grp, tp))
        others.append((attn, grp, lax.rem(tp + k, 8)))
    for other in others:
        pl.semaphore_signal(barrier, inc=1, device_id=other, device_id_type=MESH)

    started = []

    def drain(keep=0):
        while len(started) > keep:
            started.pop(0).wait_send()

    def push(src, dst, s_sem, r_sem, i, to):
        copy = pltpu.make_async_remote_copy(
            src_ref=src, dst_ref=dst, send_sem=s_sem.at[i], recv_sem=r_sem.at[i],
            device_id=to, device_id_type=MESH,
        )
        copy.start()
        started.append(copy)

    def landed(dst, s_sem, r_sem, i):
        pltpu.make_async_remote_copy(
            src_ref=dst, dst_ref=dst, send_sem=s_sem.at[i], recv_sem=r_sem.at[i],
            device_id=sibling, device_id_type=MESH,
        ).wait_recv()

    q_load.wait()
    wide_q = q_ref[...].astype(F32)
    for h in range(32):
        for half in range(2):
            first = h * 256 + half * 128
            qs[half, pl.ds(h, 4, stride=32), :] = wide_q[:, first : first + 128]
    slot = lax.broadcasted_iota(jnp.int32, (32, 1024), 1)
    swaps = (match_ref[0], match_ref[1])

    def weigh(r):
        query = jnp.concatenate([qs[half, r * 32 : (r + 1) * 32] for half in range(2)], axis=1).astype(BF16)
        scores = lax.dot_general(query, kc[r], NT, preferred_element_type=F32) * (256 ** -0.5)
        scores = jnp.where(slot < len_ref[r], scores, -1e30)
        expo = jnp.exp(scores - jnp.max(scores, axis=-1, keepdims=True))
        return (expo / jnp.sum(expo, axis=-1, keepdims=True)).astype(BF16)

    for copy in fetch[:4]:
        copy.wait()
    for load in loads:
        load.start()
    probs = [weigh(r) for r in range(4)]
    for copy in fetch[4:]:
        copy.wait()
    contexts = [jnp.dot(probs[r], vc[r], preferred_element_type=F32) for r in range(4)]
    for p in range(4):
        chosen = contexts[0]
        for r in range(1, 4):
            chosen = jnp.where(assign_ref[p] == r, contexts[r], chosen)
        for hh in range(2):
            own_b[hh, p * 16 : p * 16 + 16] = chosen[hh * 16 : hh * 16 + 16].astype(BF16)
    pl.semaphore_wait(barrier, 16)

    def gather(way, block, part, other, s_sem, r_sem, ready, base, peer=None):
        ak, bk, a_other, b_other = way
        a, (b, b1, b2, b3) = ak[0], bk
        b_right, b_left = b_other[1], b_other[3]

        def send(ref, i, to):
            push(ref, ref, s_sem, r_sem, base + i, to)

        def wait(ref, i):
            landed(ref, s_sem, r_sem, base + i)

        def ring_1(p):
            for k in (1, 3, 2):
                send(block(p, a), 3 * p + k, a_other[k])

        def ring_2(p):
            for k in (1, 3, 2):
                wait(block(p, ak[4 - k]), 3 * p + k)
            ready(p)
            first, second = ((7, b_right), (8, b_left)) if p == 0 else ((10, b_left), (9, b_right))
            send(part(p, b), *first)
            send(part(p, b), *second)
            send(part(p, b), 13 + p, sibling)

        if peer is None:
            send(block(0, a), 0, z_peer)
        ring_1(0)
        yield
        if peer is None:
            ring_2(0)
            wait(block(1, a), 0)
            ring_1(1)
        else:
            peer()
            ring_1(1)
            ring_2(0)
        yield
        ring_2(1)
        yield
        wait(part(0, b3), 7)
        send(part(0, b3), 11, b_right)
        send(part(0, b3), 15, sibling)
        wait(part(0, b1), 8)
        send(part(0, b1), 16, sibling)
        yield
        wait(part(1, b1), 10)
        send(part(1, b1), 12, b_left)
        send(part(1, b1), 17, sibling)
        wait(part(1, b3), 9)
        send(part(1, b3), 18, sibling)
        yield
        wait(part(0, b2), 11)
        send(part(0, b2), 19, sibling)
        wait(part(1, b2), 12)
        send(part(1, b2), 20, sibling)
        yield
        for p, spots in enumerate((((13, 0), (15, 3), (16, 1), (19, 2)), ((14, 0), (18, 3), (17, 1), (20, 2)))):
            for i, k in spots:
                wait(other(zs[p], ak[k]), i)
            yield

    a, b = ways[0][0][0], ways[0][1][0]
    me = (((c * 2 + z) * 4 + b) * 4 + a, ((c * 2 + z) * 4 + a) * 4 + b)
    me_row = ((z * 4 + b) * 4 + a) * 4

    def residual():
        loads[0].wait()
        wide_r = resid_ref[...].astype(F32)
        ordered = []
        for p in range(4):
            chosen = wide_r[0:1]
            for r in range(1, 4):
                chosen = jnp.where(assign_ref[p] == r, wide_r[r : r + 1], chosen)
            ordered.append(chosen)
        ordered = jnp.concatenate(ordered, axis=0)
        s1f[...] = jnp.zeros_like(s1f)
        for n in range(8):
            for t in range(8):
                first = n * 896 + t * COLS
                s1f[n, (t % 4) * 4 : (t % 4) * 4 + 4, (t // 4) * 128 : (t // 4) * 128 + COLS] = ordered[
                    :, first : first + COLS
                ]
        s1[...] = s1f[...].astype(BF16)
        push(s1, s1_got, rs_sem, rr_sem, 1, partner)
        yield
        landed(s1_got, rs_sem, rr_sem, 1)
        row = lax.rem(lax.broadcasted_iota(jnp.int32, (8, 16, 256), 1), 4)
        served = jnp.where(jnp.where(row < 2, swaps[0], swaps[1]) == 1, s1_got[...], s1[...])
        s1_got[...] = served
        t1[attn] = s1_got[attn]
        for k in range(1, 8):
            to = lax.rem(attn + k, 8)
            push(s1_got.at[to], t1.at[attn], rs_sem, rr_sem, 1 + k, (to, grp, tp))
        yield
        for k in range(1, 8):
            landed(t1.at[lax.rem(attn + 8 - k, 8)], rs_sem, rr_sem, 1 + k)
        for n in range(8):
            part = t1[n].astype(F32)
            for t in range(8):
                uf[t, n * 4 : n * 4 + 4, :] = part[
                    (t % 4) * 4 : (t % 4) * 4 + 4, (t // 4) * 128 : (t // 4) * 128 + 128
                ]
        ub[...] = uf[...].astype(BF16)
        vb[tp] = ub[tp]
        for k in range(1, 8):
            to = lax.rem(tp + k, 8)
            push(ub.at[to], vb.at[tp], rs_sem, rr_sem, 8 + k, (attn, grp, to))
        yield
        for k in range(1, 8):
            landed(vb.at[lax.rem(tp + 8 - k, 8)], rs_sem, rr_sem, 8 + k)
        for t in range(8):
            part = vb[t].astype(F32)
            for n in range(8):
                plane, zv = t % 2, n % 2
                bv, av = (n // 2, t // 2) if plane else (t // 2, n // 2)
                place = (((plane * 2 + zv) * 4 + bv) * 4 + av) * 4
                wf[place : place + 4, :] = part[n * 4 : n * 4 + 4]
        wt[...] = wf[...].T
        yield

    def scaling():
        for i in (1, 2, 3):
            loads[i].wait()

        def scale(i, _):
            rows = pl.ds(pl.multiple_of(i * 16, 16), 16)
            for k, src in enumerate((wg, wu)):
                spot = pl.ds(pl.multiple_of(k * FH + i * 16, 16), 16)
                wide = (src[rows, :].astype(F32) * gain_ref[...]).astype(BF16)
                for cv in range(2):
                    for xv in range(4):
                        first = [
                            ((xv // 2 * 4 + x2 * 2 + xv % 2) * 8 + yv * 2 + cv) * COLS
                            for x2 in range(2)
                            for yv in range(4)
                        ]
                        w2[cv, spot, xv * 896 : (xv + 1) * 896] = jnp.concatenate(
                            [wide[:, f : f + COLS] for f in first], axis=1
                        )
            return 0

        for part in range(6):
            lax.fori_loop(part * 3, part * 3 + 3, scale, 0)
            yield

    for m in range(2):
        flags[m * 8 : m * 8 + 8, :] = jnp.full((8, 128), swaps[m], jnp.int32).astype(F32)
    flag_out[...] = flags[...].astype(BF16)
    for hh in range(2):
        push(own_b.at[hh], got_b.at[hh], rs_sem, rr_sem, 20 * hh, partner)
    push(flag_out, flag_in, rs_sem, rr_sem, 21, z_peer)
    for hh in range(2):
        push(own_b.at[hh], cross_b.at[hh], rs_sem, rr_sem, 22 + hh, cross)
        push(own_b.at[hh], peer_b.at[hh], rs_sem, rr_sem, 24 + hh, z_peer)
    push(d_hbm, wd.at[pl.ds(FH, FH)], rs_sem, rr_sem, 18, sibling)
    residual_steps, scaling_steps = residual(), scaling()
    next(residual_steps)
    next(scaling_steps)
    row = lax.broadcasted_iota(jnp.int32, (64, 256), 0)

    def gather_context(hh):
        way = ways[hh]

        def ready(p):
            for half in range(2):
                sf[half] = cb[hh, zs[p], :, :, half * 128 : (half + 1) * 128].astype(F32).reshape(256, 128)
            for h in range(16):
                for half in range(2):
                    first = h * 256 + half * 128
                    ctx_all[hh, (c * 2 + zs[p]) * 4 + way[1][0], :, first : first + 128] = sf[
                        half, pl.ds(h, 16, stride=16), :
                    ].astype(BF16)

        landed(got_b.at[hh], rs_sem, rr_sem, 20 * hh)
        cb[hh, z, way[0][0]] = jnp.where(
            jnp.where(row < 32, swaps[0], swaps[1]) == 1, got_b[hh], own_b[hh]
        )

        def peer():
            if hh == 0:
                landed(flag_in, rs_sem, rr_sem, 21)
            landed(cross_b.at[hh], rs_sem, rr_sem, 22 + hh)
            landed(peer_b.at[hh], rs_sem, rr_sem, 24 + hh)
            wide = flag_in[...].astype(F32)
            flag = jnp.concatenate(
                [jnp.broadcast_to(wide[m * 8 : m * 8 + 1], (32, 128)) for m in range(2)], axis=0
            )
            flag = jnp.concatenate([flag, flag], axis=1)
            theirs = jnp.where(flag > 0.5, cross_b[hh].astype(F32), peer_b[hh].astype(F32))
            cb[hh, zo, way[0][0]] = theirs.astype(BF16)

        yield from gather(
            way,
            lambda p, av: cb.at[hh, zs[p], av],
            lambda p, bv: ctx_all.at[hh, (c * 2 + zs[p]) * 4 + bv],
            lambda zv, bv: ctx_all.at[hh, (co * 2 + zv) * 4 + bv],
            bs_sem,
            br_sem,
            ready,
            21 * hh,
            peer,
        )

    steps = (gather_context(0), gather_context(1))

    def both(pair):
        for one in pair:
            next(one)

    both(steps)
    next(residual_steps)
    both(steps)
    next(scaling_steps)
    both(steps)
    next(residual_steps)
    next(scaling_steps)
    both(steps)
    next(scaling_steps)
    both(steps)
    next(scaling_steps)
    next(residual_steps)
    next(scaling_steps)
    both(steps)
    loads[4].wait()

    def project(plane):
        def rows(hh, cols):
            return ctx_all[hh, pl.ds(plane * 8, 8), :, cols].reshape(128, 1024)

        def step(i, sums):
            cols = pl.ds(pl.multiple_of(i * 1024, 1024), 1024)
            last = pl.ds(pl.multiple_of(i * 1024 + CW // 2, 1024), 1024)
            one = lax.dot_general(wo[:, cols], rows(0, cols), NT, preferred_element_type=F32)
            two = lax.dot_general(rows(1, cols), wo[:, last], NT, preferred_element_type=F32)
            return sums[0] + one, sums[1] + two

        one, two = lax.fori_loop(
            0, CW // 2048, step, (jnp.zeros((COLS, 128), F32), jnp.zeros((128, COLS), F32))
        )
        for zv in range(2):
            for i in range(4):
                for j in range(4):
                    src, dst = ((zv * 4 + i) * 4 + j) * 4, ((zv * 4 + j) * 4 + i) * 4
                    turned[dst : dst + 4, :COLS] = two[src : src + 4]
        lanes = pl.ds(pl.multiple_of(plane * 128, 128), 128)
        return (wt[:COLS, lanes] + (one + turned[...].T[:COLS])).astype(BF16)

    def gather_hidden(i):
        half = (c, co)[i]
        return gather(
            ways[i],
            lambda p, av: ht.at[half, ((c * 2 + zs[p]) * 4 + ways[i][1][0]) * 4 + av],
            lambda p, bv: ht.at[half, pl.ds(((c * 2 + zs[p]) * 4 + bv) * 4, 4)],
            lambda zv, bv: ht.at[(co, c)[i], pl.ds(((co * 2 + zv) * 4 + bv) * 4, 4)],
            cs_sem,
            cr_sem,
            lambda p: None,
            21 * i,
        )

    early, late = gather_hidden(0), gather_hidden(1)

    def features(plane, half, n):
        parts = []
        for x2 in range(2):
            for yv in range(4):
                xv = n // 2 * 2 + x2
                bv, av = yv * (1 - half) + xv * half, xv * (1 - half) + yv * half
                parts.append(ht[half, ((plane * 2 + lax.rem(n, 2)) * 4 + bv) * 4 + av])
        return jnp.concatenate(parts, axis=0)

    def expand(plane, i, *ps):
        half = (c, co)[i]

        def step(k, total):
            n = (k // len(ps)) * 2 + (zs[ps[0]] if len(ps) == 1 else lax.rem(k, 2))
            cols = pl.ds(pl.multiple_of(n * 896, 128), 896)
            part = features(plane, half, n)
            acc[i] += jnp.dot(w2[plane, :, cols], part, preferred_element_type=F32)
            wide = part.astype(F32)
            return total + jnp.sum((wide * wide).reshape(112, 8, 128), axis=0)

        squares[i] += lax.fori_loop(0, 2 * len(ps), step, jnp.zeros((8, 128), F32))

    def activate(i):
        factor = lax.rsqrt(jnp.sum(squares[i], axis=0, keepdims=True) * (1.0 / D) + 1e-5)
        gate = acc[i, :FH] * factor
        act = gate / (1.0 + jnp.exp(-gate)) * (acc[i, FH:] * factor)
        return act.T.astype(BF16)

    ht[c, me[0]] = project(c)
    next(early)
    both(steps)
    both(steps)
    ht[co, me[1]] = project(co)
    next(late)
    acc[...] = jnp.zeros_like(acc)
    squares[...] = jnp.zeros_like(squares)
    before = len(started)
    for i in range(4):
        next(early)
        next(late)
        if i == 0:
            drain(len(started) - before)
    next(early)
    expand(c, 0, 0, 1)
    next(late)
    next(early)
    next(early)
    expand(co, 1, 0, 1)
    expand(c, 1, 0, 1)
    act_out[...] = activate(1)
    push(act_out, act_in, rs_sem, rr_sem, 19, sibling)
    next(late)
    expand(co, 0, 0)
    next(late)
    expand(co, 0, 1)

    act_own = activate(0)
    loads[5].wait()
    landed(wd.at[pl.ds(FH, FH)], rs_sem, rr_sem, 18)
    landed(act_in, rs_sem, rr_sem, 19)
    lhs = jnp.concatenate([act_own, act_in[...]], axis=1)

    def other_order():
        wide_lhs = lhs.astype(F32)
        for zv in range(2):
            for i in range(4):
                for j in range(4):
                    src, dst = ((zv * 4 + i) * 4 + j) * 4, ((zv * 4 + j) * 4 + i) * 4
                    lhs_f[dst : dst + 4, :] = wide_lhs[src : src + 4]
        return lhs_f[...].astype(BF16)

    def reduction(h):
        rows = other_order() if h else lhs
        ak, (b, b1, b2, b3), a_other, b_other = ways[h]
        a, b_right, b_left = ak[0], b_other[1], b_other[3]
        for j in range(2):
            cols = pl.ds(j * 1792, 1792)
            part = jnp.dot(rows, wd[:, pl.ds(h * 3584 + j * 1792, 1792)], preferred_element_type=F32)
            p_own[h, :, :, cols] = part.astype(BF16).reshape(8, 16, 1792)

        def slab(p, k):
            return p_own.at[h, zs[p] * 4 + k]

        def send(ref, i, to):
            push(ref, r2.at[h, i], ds_sem, dr_sem, 2 + 6 * h + i, to)

        def wait(i):
            landed(r2.at[h, i], ds_sem, dr_sem, 2 + 6 * h + i)

        send(slab(0, b2), 0, b_left)
        send(slab(1, b2), 1, b_right)
        send(slab(1, b3), 3, b_left)
        send(slab(0, b1), 4, b_right)
        yield
        for i, p, k, to, j in ((0, 0, b3, b_left, 2), (1, 1, b1, b_right, 5)):
            wait(i)
            ref = slab(p, k)
            ref[...] = (ref[...].astype(F32) + r2[h, i].astype(F32)).astype(BF16)
            send(ref, j, to)
        yield
        for i in (3, 4, 2, 5):
            wait(i)
        for p in (1, 0):
            total = (
                p_own[h, zs[p] * 4 + b].astype(F32) + r2[h, 2 + p].astype(F32) + r2[h, 4 + p].astype(F32)
            )
            for av in range(4):
                for q in range(4):
                    qf[av, q * 4 : q * 4 + 4, :] = total[av * 4 : av * 4 + 4, q * 896 : (q + 1) * 896]
            qb[h, p] = qf[...].astype(BF16)
        for k in (1, 3, 2):
            push(qb.at[h, :, ak[k]], r1.at[h, k - 1], ds_sem, dr_sem, 13 + 6 * h + k, a_other[k])
        yield
        for k in (1, 3, 2):
            landed(r1.at[h, k - 1], ds_sem, dr_sem, 13 + 6 * h + k)
        sums = []
        for p in (1, 0):
            total = qb[h, p, a].astype(F32)
            for k in (1, 3, 2):
                total = total + r1[h, k - 1, p].astype(F32)
            sums.append(total)
            if p == 1:
                tz[h] = total.astype(BF16)
                push(tz.at[h], got_peer.at[h], ds_sem, dr_sem, 26 + 3 * h, z_peer)
                push(tz.at[h], got_cross.at[h], ds_sem, dr_sem, 27 + 3 * h, cross)
        tp0[h] = sums[1].astype(BF16)
        push(tp0.at[h], got_partner.at[h], ds_sem, dr_sem, 28 + 3 * h, partner)
        t0[h] = sums[1]
        yield
        landed(got_partner.at[h], ds_sem, dr_sem, 28 + 3 * h)
        landed(got_cross.at[h], ds_sem, dr_sem, 27 + 3 * h)
        landed(got_peer.at[h], ds_sem, dr_sem, 26 + 3 * h)
        stayed = hid[h].astype(F32) + (t0[h] + got_peer[h].astype(F32))
        moved = hid_got[h].astype(F32) + (got_partner[h].astype(F32) + got_cross[h].astype(F32))
        row = lax.rem(lax.broadcasted_iota(jnp.int32, (16, 896), 0), 4)
        final = jnp.where(jnp.where(row < 2, swaps[0], swaps[1]) == 1, moved, stayed)
        request = lax.broadcasted_iota(jnp.int32, (4, 896), 0)
        for q in range(4):
            rows = jnp.zeros((4, 896), F32)
            for p in range(4):
                one = jnp.broadcast_to(final[q * 4 + p : q * 4 + p + 1], (4, 896))
                rows = jnp.where(request == assign_ref[p], one, rows)
            out_ref[:, h * 3584 + q * 896 : h * 3584 + (q + 1) * 896] = rows.astype(BF16)
        yield

    def own_hidden(h):
        lane = lax.broadcasted_iota(jnp.int32, (16, 128), 1)
        sub = lax.broadcasted_iota(jnp.int32, (16, 128), 0)
        rows = jnp.zeros((16, 896), F32)
        for q in range(4):
            pick = jnp.where(lane == me_row + sub - q * 4, 1.0, 0.0)
            pick = jnp.where((sub >= q * 4) & (sub < q * 4 + 4), pick, 0.0).astype(BF16)
            xv, zv = 2 * h + q // 2, q % 2
            parts = []
            for yv in range(4):
                for plane in range(2):
                    bv, av = yv * co + xv * c, xv * co + yv * c
                    parts.append(ht[c, ((plane * 2 + zv) * 4 + bv) * 4 + av])
            rows = rows + lax.dot_general(
                pick, jnp.concatenate(parts, axis=0), NT, preferred_element_type=F32
            )
        hid[h] = rows.astype(BF16)
        push(hid.at[h], hid_got.at[h], rs_sem, rr_sem, 16 + h, partner)

    halves = (reduction(0), reduction(1))
    before = len(started)
    for half in halves:
        next(half)
    own_hidden(0)
    drain(len(started) - before)
    next(halves[0])
    own_hidden(1)
    next(halves[1])
    for _ in range(2):
        for half in halves:
            next(half)
    for h in range(2):
        landed(hid_got.at[h], rs_sem, rr_sem, 16 + h)
    for half in halves:
        next(half)
    drain()


def per_device(
    queries, keys, values, lengths, resid, assign, matching, w_out, gain, gate_w, up_w, down_w
):
    smem = pl.BlockSpec(memory_space=pltpu.SMEM)
    vmem = pl.BlockSpec(memory_space=pltpu.VMEM)
    hbm = pl.BlockSpec(memory_space=pl.ANY)
    dma = pltpu.SemaphoreType.DMA
    scratch = (
        ((4, CW), BF16),
        ((4, 1024, 256), BF16),
        ((4, 1024, 256), BF16),
        ((COLS, CW), BF16),
        ((FH, D), BF16),
        ((FH, D), BF16),
        ((2, 2 * FH, D // 2), BF16),
        ((2 * FH, D), BF16),
        ((4, D), BF16),
        ((1, D), F32),
        ((2, 128, 128), F32),
        ((2, 64, 256), BF16),
        ((2, 64, 256), BF16),
        ((2, 64, 256), BF16),
        ((2, 64, 256), BF16),
        ((16, 128), F32),
        ((16, 128), BF16),
        ((16, 128), BF16),
        ((2, 2, 4, 64, 256), BF16),
        ((2, 256, 128), F32),
        ((2, 16, 16, CW // 2), BF16),
        ((2, 64, COLS, 128), BF16),
        ((2, 2 * FH, 128), F32),
        ((2, 8, 128), F32),
        ((128, FH), BF16),
        ((128, FH), BF16),
        ((8, 16, 256), F32),
        ((8, 16, 256), BF16),
        ((8, 16, 256), BF16),
        ((8, 16, 256), BF16),
        ((8, 32, 128), F32),
        ((8, 32, 128), BF16),
        ((8, 32, 128), BF16),
        ((256, 128), F32),
        ((128, 256), F32),
        ((128, 128), F32),
        ((128, 2 * FH), F32),
        ((2, 8, 16, D // 2), BF16),
        ((2, 6, 16, D // 2), BF16),
        ((4, 16, 896), F32),
        ((2, 2, 4, 16, 896), BF16),
        ((2, 3, 2, 16, 896), BF16),
        ((2, 16, 896), F32),
    ) + (((2, 16, 896), BF16),) * 7
    return pl.pallas_call(
        kernel,
        out_shape=pltpu.VMEM((4, D), BF16),
        in_specs=[smem] * 3 + [hbm] * 9,
        out_specs=vmem,
        scratch_shapes=[pltpu.VMEM(shape, dtype) for shape, dtype in scratch]
        + [dma((n,)) for n in (8, 7, 42, 42, 42, 42, 32, 32, 26, 26)],
        compiler_params=pltpu.CompilerParams(
            collective_id=0, has_side_effects=True, vmem_limit_bytes=60 * 1024 * 1024
        ),
    )(
        lengths, assign[0], matching[:, 0, 0], queries, resid, gain[None],
        keys, values, w_out.T, gate_w[0].T, up_w[0].T, down_w[0],
    )


def solution(mesh):
    rows = P(("attn", "grp", "tp"), None)
    cache = P(("attn", "grp", "tp"), None, None)
    placed = (
        rows,
        cache,
        cache,
        P(("attn", "grp", "tp")),
        rows,
        rows,
        P(None, "attn", "tp"),
        P(None, ("attn", "tp")),
        P(),
        P("grp", None, ("attn", "tp")),
        P("grp", None, ("attn", "tp")),
        P("grp", ("attn", "tp"), None),
    )
    return jax.shard_map(
        per_device, mesh=mesh, in_specs=placed, out_specs=rows, check_vma=False
    )
```
